32 devices in a mesh: section: 2 (over core), dp: 16 (over z, y, x).
Axes of the slice: x: 2, y: 2, z: 4, core: 2. Of those that a mesh axis runs over, the one named last changes fastest.
Arguments:
- patches: bfloat16 [128, 196, 768], P('dp'), may hold values from -6 to 6
- labels: int32 [128], P('dp'), may hold values from 0 to 999
- replay: int32 [128], P('dp'), may hold values from 0 to 1, as said below
- old_logits: float32 [128, 1000], P('dp'), may hold values from -10 to 10
- basis_count: int32 [2], replicated, may hold values from 20 to 200, as said below
- master: float32 [2, 638976], P('section', 'dp')
- first_moment: float32 [2, 638976], P('section', 'dp'), may hold values from -3.0517578e-05 to 3.0517578e-05
- second_moment: float32 [2, 638976], P('section', 'dp'), may hold values from 1.565004e-13 to 2.5040063e-12
- basis: bfloat16 [400, 2, 638976], P(None, 'section', 'dp'), may hold values from -6 to 6
Outputs:
- loss_parts: float32 [3], replicated
- grad_norm: float32 [], replicated
- coefficients: float32 [2, 200], replicated
- new_master: float32 [2, 638976], P('section', 'dp')
- new_first: float32 [2, 638976], P('section', 'dp')
- new_second: float32 [2, 638976], P('section', 'dp')
The draws below stay inside these ranges and needn't reach their ends.
Inputs may be any that keep to these rules, and one draw needn't show every extreme that they name: `basis_count`: one task has exactly 200 basis vectors. At least one image is a replay example.
All inputs are finite; a program needn't handle non-finite values.
Results may differ from the reference program's by a relative error of at most 0.012.
The reference program's roundings to bfloat16 on the way count: a program that leaves them out, or rounds other values in their place, can miss the bound.
Values may be sent and summed in bfloat16 or wider, within the bound.
No kernel may reach another device: no remote copies, remote signals or barrier semaphores. Data moves between devices by JAX's collectives and lax.ppermute only.
A program may use at most 192 MiB of HBM per device.

```python
import math
import jax
import jax.numpy as jnp
from jax import lax

HEADS = 3
HD = 64
D = 192
FF = 768
PDIM = 768
PATCHES = 196
CLASSES = 1000
IMG_MB = 4
TASKS = 2
KMAX = 200
STEP = 10
IMAGES = 128
KB = 400
KMIN = 20
BLOCK_P = 444672
FIRST_P = 185664
LAST_P = 193384
PS = 638976
PALL = 1277952


def segment_scales(shapes_scales):
    scale_parts = []
    offset_parts = []
    for entries, spread, centre in shapes_scales:
        scale_parts.append(jnp.full((entries,), spread, jnp.float32))
        offset_parts.append(jnp.full((entries,), centre, jnp.float32))
    return (jnp.concatenate(scale_parts), jnp.concatenate(offset_parts))


def block_table():
    return [(D, 0.1, 1.0), (D, 0.1, 0.0), (3 * D * D, D ** (-0.5), 0.0), (2 * D, 0.1, 0.0), (D * D, 4.0 * D ** (-0.5), 0.0), (D, 0.1, 0.0), (D, 0.1, 1.0), (D, 0.1, 0.0), (D * FF, D ** (-0.5), 0.0), (FF, 0.1, 0.0), (FF * D, FF ** (-0.5), 0.0), (D, 0.1, 0.0)]


def draw_master(key, part):
    key = jax.random.fold_in(key, 11)
    first_table = block_table() + [(PDIM * D, PDIM ** (-0.5), 0.0), (D, 0.1, 0.0), (D, 1.0, 0.0), ((PATCHES + 1) * D, 0.5, 0.0)]
    first_table = first_table + [(PS - BLOCK_P - FIRST_P, 0.02, 0.0)]
    last_table = block_table() + [(D, 0.1, 1.0), (D, 0.1, 0.0), (D * CLASSES, 2.0 * D ** (-0.5), 0.0), (CLASSES, 0.1, 0.0)]
    last_table = last_table + [(PS - BLOCK_P - LAST_P, 0.02, 0.0)]
    scale_zero, centre_zero = segment_scales(first_table)
    scale_one, centre_one = segment_scales(last_table)
    spreads = jnp.stack([scale_zero, scale_one])
    centres = jnp.stack([centre_zero, centre_one])
    normal_draw = jax.random.normal(key, (2, PS), jnp.float32)
    return normal_draw * spreads + centres


def draw_replay(key, part):
    key = jax.random.fold_in(key, 5)
    key_draw, key_pick = jax.random.split(key)
    drawn = jax.random.randint(key_draw, (IMAGES,), 0, 1000)
    limits = 200 + 600 * jnp.arange(IMAGES) // IMAGES
    picked = jax.random.randint(key_pick, (), 0, IMAGES)
    chosen = jnp.logical_or(drawn < limits, jnp.arange(IMAGES) == picked)
    return chosen.astype(jnp.int32)


def draw_basis_count(key, part):
    key = jax.random.fold_in(key, 7)
    key_counts, key_pick = jax.random.split(key)
    counts = jax.random.randint(key_counts, (TASKS,), KMIN, KMAX + 1)
    picked = jax.random.randint(key_pick, (), 0, TASKS)
    return jnp.where(jnp.arange(TASKS) == picked, KMAX, counts).astype(jnp.int32)


def with_ends(values, stream_key, smallest, largest):
    extent = values.shape
    index_at = [jax.random.randint(jax.random.fold_in(stream_key, axis), (), 0, extent[axis]) for axis in range(len(extent))]
    values = values.at[tuple(index_at)].set(smallest)
    longest = extent.index(max(extent))
    index_at[longest] = (index_at[longest] + 1) % extent[longest]
    return values.at[tuple(index_at)].set(largest)


def shard_levels(rng, shape, shards, low, high):
    def one(position, blocks):
        heights = jax.random.uniform(jax.random.fold_in(jax.random.fold_in(rng, 6), position), (blocks,), jnp.float32, low / len(shards), high / len(shards))
        return jnp.repeat(jnp.exp(heights), shape[position] // blocks).reshape((-1,) + (1,) * (len(shape) - position - 1))

    gain = one(*shards[0])
    for cut in shards[1:]:
        gain = gain * one(*cut)
    return gain


def bell_draw(key, shape, width, limit, cuts=(), kind=jnp.bfloat16):
    array = width * jax.random.normal(key, shape, jnp.float32)
    if cuts:
        array = array * shard_levels(key, shape, cuts, -0.22, 0.18)
    return jnp.clip(array, -limit, limit).astype(kind)


def setup_inputs(seed: int = 0) -> dict:
    key_list = jax.random.split(jax.random.key(seed), 10)
    return {
        "patches": bell_draw(key_list[0], (IMAGES, PATCHES, PDIM), 1.0, 6.0, ((0, 16),)),
        "labels": with_ends(jax.random.randint(key_list[1], (IMAGES,), 0, CLASSES), jax.random.fold_in(key_list[1], 1), 0, CLASSES - 1).astype(jnp.int32),
        "replay": draw_replay(jax.random.fold_in(key_list[9], 71), 0),
        "old_logits": bell_draw(key_list[3], (IMAGES, CLASSES), 2.0, 10.0, ((0, 16),), jnp.float32),
        "basis_count": draw_basis_count(jax.random.fold_in(key_list[9], 71), 0),
        "master": draw_master(jax.random.fold_in(key_list[9], 71), 0),
        "first_moment": bell_draw(key_list[6], (2, PS), (0.0022 / PALL ** 0.5), 3.0517578125e-05, ((0, 2), (1, 16)), jnp.float32),
        "second_moment": jnp.clip(jnp.exp(math.log(2.5040063338782614e-12) - 2.7725887 * jax.random.uniform(key_list[7], (2, PS), jnp.float32) ** shard_levels(key_list[7], (2, PS), ((0, 2), (1, 16)), -0.2, 0.2)), 1.5650039586739134e-13, 2.5040063338782614e-12),
        "basis": bell_draw(key_list[8], (KB, 2, PS), 1.0, 6.0, ((1, 2), (2, 16))),
    }


HIGHEST_PREC = lax.Precision.HIGHEST
NORM_EPS = 1e-06
CLIP_NORM = 0.02
LEARN_RATE = 0.05
BETA_ONE = 0.9
BETA_TWO = 0.999
ADAM_EPS = 1e-08
WEIGHT_DECAY = 0.05

@jax.custom_vjp
def low(v):
    return lax.optimization_barrier(v.astype(jnp.bfloat16)).astype(jnp.float32)

@jax.custom_vjp
def low_back(v):
    return v

def low_keep(v):
    return (low(v), None)

def low_pass(kept, grad):
    return (grad,)

def back_keep(v):
    return (v, None)

def back_low(kept, grad):
    return (low(grad),)
low.defvjp(low_keep, low_pass)
low_back.defvjp(back_keep, back_low)

def block_shapes():
    return [(D,), (D,), (D, 3 * D), (2 * D,), (D, D), (D,), (D,), (D,), (D, FF), (FF,), (FF, D), (D,)]

def first_shapes():
    return [(PDIM, D), (D,), (D,), (PATCHES + 1, D)]

def last_shapes():
    return [(D,), (D,), (D, CLASSES), (CLASSES,)]

def unpack(flat_vec, shapes):
    pieces = []
    offset = 0
    for dims in shapes:
        entries = math.prod(dims)
        pieces.append(flat_vec[offset:offset + entries].reshape(dims))
        offset += entries
    return pieces

def norm_rows(rows_in, gain_vec, bias_vec):
    mean_row = lax.optimization_barrier(jnp.mean(rows_in, -1, keepdims=True))
    centred = rows_in - mean_row
    variance = lax.optimization_barrier(jnp.mean(centred * centred, -1, keepdims=True))
    return centred * lax.rsqrt(variance + NORM_EPS) * gain_vec + bias_vec

def block_ref(residual, params):
    gain_one, bias_one, w_qkv, b_qkv, w_out, b_out, gain_two, bias_two, w_up, b_up, w_down, b_down = params
    images, seq_len, model_width = residual.shape
    normed = low(norm_rows(residual, gain_one, bias_one))
    bias_full = jnp.concatenate([b_qkv[:D], jnp.zeros((D,), jnp.float32), b_qkv[D:]])
    qkv = low(low_back(jnp.einsum('bsd,de->bse', normed, w_qkv, precision=HIGHEST_PREC) + bias_full))
    heads = qkv.reshape(images, seq_len, 3, HEADS, HD)
    queries, key_heads, values = (heads[:, :, 0], heads[:, :, 1], heads[:, :, 2])
    scores = low_back(jnp.einsum('bqhe,bkhe->bhqk', queries, key_heads, precision=HIGHEST_PREC) * HD ** (-0.5))
    soft_weights = jax.nn.softmax(scores, -1)
    mixed = jnp.einsum('bhqk,bkhe->bqhe', low(soft_weights), values, precision=HIGHEST_PREC)
    mixed = low_back(low(mixed.reshape(images, seq_len, model_width)))
    branch = low_back(jnp.einsum('bsd,de->bse', mixed, w_out, precision=HIGHEST_PREC) + b_out)
    hidden = residual + branch
    normed_two = low(norm_rows(hidden, gain_two, bias_two))
    pre_act = low_back(jnp.einsum('bsd,df->bsf', normed_two, w_up, precision=HIGHEST_PREC) + b_up)
    activated = low(jax.nn.gelu(pre_act, approximate=False))
    branch_two = low_back(jnp.einsum('bsf,fd->bsd', activated, w_down, precision=HIGHEST_PREC) + b_down)
    return hidden + branch_two

def embed_ref(patch_blk, first_edge):
    w_patch, b_patch, cls_token, pos_embed = first_edge
    embedded = low_back(jnp.einsum('bpc,cd->bpd', patch_blk, w_patch, precision=HIGHEST_PREC) + b_patch)
    cls_rows = jnp.broadcast_to(cls_token[None, None, :], (patch_blk.shape[0], 1, D))
    return jnp.concatenate([cls_rows, embedded], 1) + pos_embed[None]

def head_ref(final, last_edge, label_blk, replay_blk, old_blk):
    gain_last, bias_last, w_head, b_head = last_edge
    top_rows = low(norm_rows(final[:, 0], gain_last, bias_last))
    logits = low_back(jnp.dot(top_rows, w_head, precision=HIGHEST_PREC) + b_head)
    log_total = jax.nn.logsumexp(logits, -1)
    onehot = (label_blk[:, None] == jnp.arange(CLASSES)[None, :]).astype(jnp.float32)
    entropy_sum = jnp.sum(log_total - lax.optimization_barrier(jnp.sum(logits * onehot, -1)))
    distance = logits - old_blk
    replay_sum = jnp.sum(replay_blk.astype(jnp.float32) * lax.optimization_barrier(jnp.mean(distance * distance, -1)))
    return (entropy_sum, replay_sum)

def loss_fn(master, patches, labels, replay, old_logits, replay_count):
    weights = low(master)
    block_zero = unpack(weights[0, :BLOCK_P], block_shapes())
    block_one = unpack(weights[1, :BLOCK_P], block_shapes())
    first_edge = unpack(weights[0, BLOCK_P:BLOCK_P + FIRST_P], first_shapes())
    last_edge = unpack(weights[1, BLOCK_P:BLOCK_P + LAST_P], last_shapes())
    groups = IMAGES // IMG_MB

    def piece(totals, batch):
        patch_blk, label_blk, replay_blk, old_blk = batch
        tokens = embed_ref(patch_blk.astype(jnp.float32), first_edge)
        middle = low_back(low(block_ref(tokens, block_zero)))
        final = block_ref(middle, block_one)
        entropy_sum, replay_sum = head_ref(final, last_edge, label_blk, replay_blk, old_blk)
        return ((totals[0] + entropy_sum, totals[1] + replay_sum), None)
    batches = (patches.reshape(groups, IMG_MB, PATCHES, PDIM), labels.reshape(groups, IMG_MB), replay.reshape(groups, IMG_MB), old_logits.reshape(groups, IMG_MB, CLASSES))
    start = (jnp.zeros((), jnp.float32), jnp.zeros((), jnp.float32))
    totals, _ = lax.scan(jax.checkpoint(piece), start, batches)
    loss = totals[0] / IMAGES + totals[1] / replay_count
    return (loss, totals)

def reference(patches, labels, replay, old_logits, basis_count, master, first_moment, second_moment, basis):
    replay_count = jnp.sum(replay).astype(jnp.float32)
    loss, pull, totals = jax.vjp(lambda weights: loss_fn(weights, patches, labels, replay, old_logits, replay_count), master, has_aux=True)
    gradient = pull(jnp.ones((), jnp.float32))[0]
    grad_norm = jnp.sqrt(jnp.sum(gradient * gradient))
    clipped = gradient * jnp.minimum(1.0, CLIP_NORM / (grad_norm + 1e-06))
    row_mask = (jnp.arange(KMAX)[None, :] < basis_count[:, None]).astype(jnp.float32).reshape(KB)
    clipped_flat = clipped.reshape(PALL)

    def one_row(summed, inputs):
        basis_row, row_valid = inputs
        basis_vec = basis_row.reshape(PALL).astype(jnp.float32)
        coefficient = row_valid * jnp.dot(basis_vec, clipped_flat, precision=HIGHEST_PREC)
        return (summed + coefficient * basis_vec, coefficient)
    summed, coefficients = lax.scan(one_row, jnp.zeros((PALL,), jnp.float32), (basis, row_mask))
    projected = clipped - (summed / PALL).reshape(2, PS)
    new_first = BETA_ONE * first_moment + (1.0 - BETA_ONE) * projected
    new_second = BETA_TWO * second_moment + (1.0 - BETA_TWO) * projected * projected
    ratio = new_first / (1.0 - BETA_ONE ** STEP) / (jnp.sqrt(new_second / (1.0 - BETA_TWO ** STEP)) + ADAM_EPS)
    new_master = master - LEARN_RATE * (ratio + WEIGHT_DECAY * master)
    loss_parts = jnp.stack([totals[0], totals[1], replay_count])
    return (loss_parts, grad_norm, coefficients.reshape(TASKS, KMAX), new_master, new_first, new_second)
```

```python
import functools
import math

import jax
import jax.numpy as jnp
from jax import lax
from jax.experimental import pallas as pl
from jax.experimental.pallas import tpu as pltpu
from jax.sharding import PartitionSpec as P

HEADS = 3
HD = 64
D = 192
FF = 768
PDIM = 768
PATCHES = 196
TOKENS = PATCHES + 1
ROWS = 208
CLS = PATCHES
CLASSES = 1000
CPAD = 1024
TASKS = 2
KMAX = 200
KB = TASKS * KMAX
STEP = 10
LANES = 128
HALF = 64
SPARE = 512
SUMS = 512

NORM_EPS = 1e-06
CLIP_NORM = 0.02
LEARN_RATE = 0.05
BETA_ONE = 0.9
BETA_TWO = 0.999
ADAM_EPS = 1e-08
WEIGHT_DECAY = 0.05
SCALE = HD ** (-0.5)
MASKED = -1e30

BLOCK_AT = dict(
    gain_one=0,
    bias_one=3,
    w_qkv=6,
    b_qkv=1734,
    w_out=1740,
    b_out=2316,
    gain_two=2319,
    bias_two=2322,
    w_up=2325,
    b_up=4629,
    w_down=4641,
    b_down=6945,
)
W_PATCH, B_PATCH, CLS_TOKEN, POS_EMBED = 6948, 9252, 9255, 9258
GAIN_LAST, BIAS_LAST, W_HEAD, B_HEAD = 6948, 6951, 6954, 9954
VECTORS = ("gain_one", "bias_one", "b_q", "b_v", "b_out", "gain_two", "bias_two", "b_up", "b_down")
VEC_ROWS = 16

f32 = jnp.float32
bf16 = jnp.bfloat16


def dot(left, right, left_dim=1, right_dim=0):
    return lax.dot_general(
        left, right, (((left_dim,), (right_dim,)), ((), ())), preferred_element_type=f32
    )


def low_lanes(shape):
    return lax.broadcasted_iota(jnp.int32, shape, 1) < HALF


def swap_halves(value):
    return pltpu.roll(value, HALF, 1)


def head_masks():
    lane = lax.broadcasted_iota(jnp.int32, (1, D), 1)
    return [jnp.logical_and(lane >= h * HD, lane < (h + 1) * HD) for h in range(HEADS)]


def by_head(value):
    return jnp.concatenate([jnp.where(m, value, 0.0) for m in head_masks()], 0)


def from_heads(value):
    rows = value.shape[0] // HEADS
    parts = [value[h * rows : (h + 1) * rows] for h in range(HEADS)]
    masks = head_masks()
    return jnp.where(masks[0], parts[0], jnp.where(masks[1], parts[1], parts[2]))


def normalise(rows_in):
    mean = jnp.sum(rows_in, -1, keepdims=True) * (1.0 / D)
    centred = rows_in - mean
    variance = jnp.sum(centred * centred, -1, keepdims=True) * (1.0 / D)
    scale = lax.rsqrt(variance + NORM_EPS)
    return centred * scale, scale


def normalise_back(grad, gain, unit, scale):
    grad_unit = grad * gain
    first = jnp.sum(grad_unit, -1, keepdims=True) * (1.0 / D)
    second = jnp.sum(grad_unit * unit, -1, keepdims=True) * (1.0 / D)
    return scale * (grad_unit - first - unit * second)


def gelu_parts(pre):
    cdf = 0.5 * (1.0 + lax.erf(pre * math.sqrt(0.5)))
    slope = cdf + pre * (jnp.exp(-0.5 * pre * pre) * (1.0 / math.sqrt(2.0 * math.pi)))
    return pre * cdf, slope


def column_sums(value):
    return jnp.sum(value.astype(f32), 0, keepdims=True)


def strided(ref, start, count, stride):
    if count == 1 or stride == 1:
        return ref[pl.ds(start, count), :]
    return ref[pl.ds(start, count, stride=stride), :]


class Flat:
    def __init__(self, even, odd, mix, rows):
        self.even, self.odd, self.mix, self.rows = even, odd, mix, rows

    def shift(self):
        step = 192
        for at in range(0, self.rows, step):
            here = swap_halves(self.even[at : at + step, :])
            after = swap_halves(self.even[at + 1 : at + 1 + step, :])
            self.odd[at : at + step, :] = jnp.where(low_lanes(here.shape), here, after)

    def rows_at(self, half, count, stride):
        return strided(self.odd if half % 2 else self.even, half // 2, count, stride)

    def blocks(self, half, width, rows, cols):
        for at in range(0, cols, LANES):
            start = half + at // HALF
            if rows == 1 or width % 2 == 0:
                value = self.rows_at(start, rows, width // 2)
            else:
                pairs = (rows + 1) // 2
                self.mix[pl.ds(0, pairs, stride=2), :] = self.rows_at(start, pairs, width)
                self.mix[pl.ds(1, pairs, stride=2), :] = self.rows_at(start + width, pairs, width)
                value = self.mix[0:rows, :]
            yield at, min(LANES, cols - at), value

    def read(self, dest, half, width, rows, cols):
        for at, wide, value in self.blocks(half, width, rows, cols):
            dest[0:rows, at : at + wide] = value[:, :wide].astype(dest.dtype)

    def read_row(self, dest, row, half, cols):
        for at, wide, value in self.blocks(half, 2, 1, cols):
            dest[row : row + 1, at : at + wide] = value[:, :wide]

    def clear(self):
        self.even[...] = jnp.zeros(self.even.shape, f32)
        self.odd[...] = jnp.zeros(self.odd.shape, f32)

    def put_rows(self, half, count, stride, value):
        ref, start = (self.odd, half // 2 + 8) if half % 2 else (self.even, half // 2)
        if count == 1 or stride == 1:
            ref[pl.ds(start, count), :] = value
        else:
            ref[pl.ds(start, count, stride=stride), :] = value

    def write(self, value, half, width, cols):
        rows = value.shape[0]
        for at in range(0, cols, LANES):
            wide = min(LANES, cols - at)
            part = value[:, at : at + wide]
            if wide < LANES:
                part = jnp.concatenate([part, jnp.zeros((rows, LANES - wide), f32)], 1)
            start = half + at // HALF
            if rows == 1 or width % 2 == 0:
                self.put_rows(start, rows, width // 2, part)
            else:
                pairs = (rows + 1) // 2
                self.mix[0:rows, :] = part
                self.put_rows(start, pairs, width, self.mix[pl.ds(0, pairs, stride=2), :])
                self.put_rows(start + width, pairs, width, self.mix[pl.ds(1, pairs, stride=2), :])

    def merged(self, at, count):
        here = swap_halves(self.odd[at + 8 : at + 8 + count, :])
        before = swap_halves(self.odd[at + 7 : at + 7 + count, :])
        return self.even[at : at + count, :] + jnp.where(low_lanes(here.shape), before, here)


class Place:
    def __init__(self, dims, shard_rows):
        self.z, self.y, self.x = dims
        self.count = self.z * self.y * self.x
        self.shard_rows = shard_rows
        self.sent_rows = -(-(shard_rows + 1) // 16) * 16

    def split(self, index):
        plane = self.y * self.x
        return index // plane, lax.rem(index, plane) // self.x, lax.rem(index, self.x)

    def turns(self):
        return [(a, b) for a in range(self.y) for b in range(self.x)]


def load_section(place, info, pieces, wanted, flat):
    own, other = pieces
    section = info[0]
    zed, why, ex = place.split(info[1])
    rows = place.shard_rows

    def copy(refs):
        for turn, (a, b) in enumerate(place.turns()):
            for d in range(place.z):
                shard = lax.rem(zed + (place.z - d), place.z) * (place.y * place.x)
                shard = shard + lax.rem(why + (place.y - a), place.y) * place.x
                shard = shard + lax.rem(ex + (place.x - b), place.x)
                start = shard * rows
                if rows % 8 == 0:
                    start = pl.multiple_of(start, 8)
                value = refs[turn][d].astype(f32)
                flat.even[pl.ds(start, rows), :] = value[:rows]

    @pl.when(section == wanted)
    def _():
        copy(own)

    @pl.when(section != wanted)
    def _():
        copy(other)

    flat.shift()


def read_block(flat, weights, vec):
    at = BLOCK_AT
    w_q, w_k, w_v, w_out, w_up, w_down = weights
    for place, dest in enumerate((w_q, w_k, w_v)):
        flat.read(dest, at["w_qkv"] + 3 * place, 9, D, D)
    flat.read(w_out, at["w_out"], 3, D, D)
    flat.read(w_up, at["w_up"], 12, D, FF)
    flat.read(w_down, at["w_down"], 3, FF, D)
    starts = dict(at, b_q=at["b_qkv"], b_v=at["b_qkv"] + 3)
    for row, name in enumerate(VECTORS):
        flat.read_row(vec, row, starts[name], FF if name == "b_up" else D)


def vector(vec, name):
    row = VECTORS.index(name)
    return vec[row : row + 1, 0 : FF if name == "b_up" else D]


def write_vectors(flat, sums):
    at = BLOCK_AT
    starts = dict(at, b_q=at["b_qkv"], b_v=at["b_qkv"] + 3)
    for name, value in sums.items():
        flat.write(value, starts[name], 2, value.shape[1])


def send_out(place, info, flat, out_ref):
    zed, why, ex = place.split(info[1])
    rows, spare = place.shard_rows, place.sent_rows - place.shard_rows
    for shard in range(place.count):
        zk, yk, xk = shard // (place.y * place.x), shard // place.x % place.y, shard % place.x
        d = lax.rem(zk + place.z - zed, place.z)
        a = lax.rem(yk + place.y - why, place.y)
        b = lax.rem(xk + place.x - ex, place.x)
        value = flat.merged(shard * rows, rows)
        value = jnp.concatenate([value, jnp.zeros((spare, LANES), f32)], 0)
        out_ref[(a * place.x + b) * place.z + d] = value.astype(bf16)


def front_kernel(place, info, *refs):
    turns = len(place.turns())
    own, other, refs = refs[:turns], refs[turns : 2 * turns], refs[2 * turns :]
    patches, refs = refs[0], refs[1:]
    (x_out, q_out, k_out, v_out, probs_out, mixed_out, hidden_out, act_out, slope_out, middle_out) = refs[:10]
    w_q, w_k, w_v, w_out, w_up, w_down, vec = refs[10:17]
    even, odd, mix, w_patch, added, tokens = refs[17:]
    flat = Flat(even, odd, mix, place.count * place.shard_rows)

    @pl.when(pl.program_id(0) == 0)
    def _():
        load_section(place, info, (own, other), 0, flat)
        read_block(flat, (w_q, w_k, w_v, w_out, w_up, w_down), vec)
        flat.read(w_patch, W_PATCH, 3, PDIM, D)
        flat.read_row(vec, 9, B_PATCH, D)
        flat.read_row(vec, 10, CLS_TOKEN, D)
        added[...] = jnp.zeros(added.shape, f32)
        tokens[...] = jnp.zeros(tokens.shape, f32)
        for at, wide, value in flat.blocks(POS_EMBED, 3, TOKENS + 1, D):
            bias = vec[9:10, at : at + wide]
            token = vec[10:11, at : at + wide]
            added[0:PATCHES, at : at + wide] = value[1:TOKENS, :wide] + bias
            added[CLS : CLS + 1, at : at + wide] = value[0:1, :wide] + token

    tokens[0:PATCHES, :] = dot(patches[...], w_patch[...])
    x = tokens[...] + added[...]
    x_out[...] = x
    unit, _ = normalise(x)
    normed = (unit * vector(vec, "gain_one") + vector(vec, "bias_one")).astype(bf16)
    q = (dot(normed, w_q[...]) + vector(vec, "b_q")).astype(bf16)
    k = dot(normed, w_k[...]).astype(bf16)
    v = (dot(normed, w_v[...]) + vector(vec, "b_v")).astype(bf16)
    q_out[...], k_out[...], v_out[...] = q, k, v
    scores = dot(by_head(q.astype(f32) * SCALE).astype(bf16), k, 1, 1)
    column = lax.broadcasted_iota(jnp.int32, scores.shape, 1)
    scores = jnp.where(column < TOKENS, scores, MASKED)
    raised = jnp.exp(scores - jnp.max(scores, -1, keepdims=True))
    probs = raised / jnp.sum(raised, -1, keepdims=True)
    probs_out[...] = probs
    mixed = from_heads(dot(probs.astype(bf16), v)).astype(bf16)
    mixed_out[...] = mixed
    hidden = x + dot(mixed, w_out[...]) + vector(vec, "b_out")
    hidden_out[...] = hidden
    unit, _ = normalise(hidden)
    normed = (unit * vector(vec, "gain_two") + vector(vec, "bias_two")).astype(bf16)
    pre = dot(normed, w_up[...]) + vector(vec, "b_up")
    act, slope = gelu_parts(pre)
    act = act.astype(bf16)
    act_out[...], slope_out[...] = act, slope
    middle = hidden + dot(act, w_down[...]) + vector(vec, "b_down")
    middle_out[...] = middle.astype(bf16)


def read_head(flat, wide, w_head, b_head):
    first = W_HEAD // 2
    lane = lax.broadcasted_iota(jnp.int32, (16, LANES), 1)
    for phase in range(16):
        start, off = first + CLASSES * phase // LANES, CLASSES * phase % LANES
        got = [strided(flat.even, start + j, 16, 125) for j in range(9 if off else 8)]
        if off:
            got = [pltpu.roll(g, LANES - off, 1) for g in got]
        for j in range(8):
            value = jnp.where(lane < LANES - off, got[j], got[j + 1]) if off else got[j]
            wide[j, pl.ds(phase, 16, stride=16), :] = value
    lane = lax.broadcasted_iota(jnp.int32, (1, LANES), 1)
    for j in range(8):
        keep = lane + j * LANES < CLASSES
        w_head[:, j * LANES : (j + 1) * LANES] = jnp.where(keep, wide[j, 0:D, :], 0.0).astype(bf16)
        value = flat.even[B_HEAD // 2 + j : B_HEAD // 2 + j + 1, :]
        b_head[0:1, j * LANES : (j + 1) * LANES] = jnp.where(keep, value, 0.0)


def write_head(flat, wide, grad_w, grad_b):
    first = W_HEAD // 2
    for j in range(8):
        wide[j, 0:D, :] = grad_w[:, j * LANES : (j + 1) * LANES]
        wide[j, D:, :] = jnp.zeros((wide.shape[1] - D, LANES), f32)
    lane = lax.broadcasted_iota(jnp.int32, (16, LANES), 1)
    for phase in range(16):
        start, off = first + CLASSES * phase // LANES, CLASSES * phase % LANES
        got = [wide[j, pl.ds(phase, 16, stride=16), :] for j in range(8)]
        if off:
            got = [pltpu.roll(g, off, 1) for g in got]
        for j in range(9 if off else 8):
            if not off:
                value = got[j]
            else:
                before = got[j - 1] if j else jnp.zeros((16, LANES), f32)
                value = jnp.where(lane < off, before, got[j] if j < 8 else 0.0)
            flat.even[pl.ds(start + j, 16, stride=125), :] += value
    for j in range(8):
        row = B_HEAD // 2 + j
        flat.even[row : row + 1, :] += grad_b[:, j * LANES : (j + 1) * LANES]


def late_kernel(place, per, image_total, info, labels, replay, *refs):
    turns = len(place.turns())
    own, other, refs = refs[:turns], refs[turns : 2 * turns], refs[2 * turns :]
    middle, old_logits, back_out, grad_out, loss_out = refs[:5]
    even, odd, mix, wide, w_q, w_k, w_v, w_out, w_up, w_down, vec, w_head, b_head, few, many = refs[5:]
    flat = Flat(even, odd, mix, place.count * place.shard_rows)
    load_section(place, info, (own, other), 1, flat)
    read_block(flat, (w_q, w_k, w_v, w_out, w_up, w_down), vec)
    flat.read_row(vec, 9, GAIN_LAST, D)
    flat.read_row(vec, 10, BIAS_LAST, D)
    read_head(flat, wide, w_head, b_head)
    gain_last, bias_last = vec[9:10, 0:D], vec[10:11, 0:D]
    carried = jnp.zeros((1, LANES), f32)
    for ref in own:
        for d in range(place.z):
            carried = carried + ref[d].astype(f32)[place.shard_rows : place.shard_rows + 1]
    replay_count = carried[:, 0:1]

    x = middle[...].astype(f32)
    unit, scale = normalise(x)
    normed_f = unit * vector(vec, "gain_one") + vector(vec, "bias_one")
    normed = normed_f.astype(bf16)
    k = dot(normed, w_k[...]).astype(bf16)
    v = (dot(normed, w_v[...]) + vector(vec, "b_v")).astype(bf16)

    def class_rows(value):
        few[...] = jnp.zeros(few.shape, f32)
        for i in range(per):
            few[i : i + 1, :] = value[i * ROWS + CLS : i * ROWS + CLS + 1, :]
        return few[...]

    eight = few.shape[0]
    image = lax.broadcasted_iota(jnp.int32, (eight, 1), 0)
    real = image < per
    x_top = class_rows(x)
    top_normed = class_rows(normed_f).astype(bf16)
    q = (dot(top_normed, w_q[...]) + vector(vec, "b_q")).astype(bf16)
    q_heads = by_head(jnp.where(real, q.astype(f32) * SCALE, 0.0)).astype(bf16)
    scores = dot(q_heads, k, 1, 1)
    column = lax.broadcasted_iota(jnp.int32, scores.shape, 1)
    owner = lax.rem(lax.broadcasted_iota(jnp.int32, scores.shape, 0), eight) * ROWS
    inside = jnp.logical_and(column >= owner, column < owner + TOKENS)
    scores = jnp.where(inside, scores, MASKED)
    raised = jnp.where(inside, jnp.exp(scores - jnp.max(scores, -1, keepdims=True)), 0.0)
    total = jnp.sum(raised, -1, keepdims=True)
    probs = raised / jnp.where(total > 0.0, total, 1.0)
    probs_low = probs.astype(bf16)
    mixed = from_heads(dot(probs_low, v)).astype(bf16)
    hidden = x_top + dot(mixed, w_out[...]) + vector(vec, "b_out")
    unit_two, scale_two = normalise(hidden)
    normed_two = (unit_two * vector(vec, "gain_two") + vector(vec, "bias_two")).astype(bf16)
    act, slope = gelu_parts(dot(normed_two, w_up[...]) + vector(vec, "b_up"))
    act = act.astype(bf16)
    final = hidden + dot(act, w_down[...]) + vector(vec, "b_down")

    unit_last, scale_last = normalise(final)
    top = (unit_last * gain_last + bias_last).astype(bf16)
    classes = lax.broadcasted_iota(jnp.int32, (eight, CPAD), 1)
    logits = dot(top, w_head[...]) + b_head[...]
    logits = jnp.where(classes < CLASSES, logits, MASKED)
    highest = jnp.max(logits, -1, keepdims=True)
    log_total = highest + jnp.log(jnp.sum(jnp.exp(logits - highest), -1, keepdims=True))
    label = jnp.zeros((eight, 1), jnp.int32)
    again = jnp.zeros((eight, 1), f32)
    for i in range(per):
        label = jnp.where(image == i, labels[info[0] * per + i], label)
        again = jnp.where(image == i, replay[info[0] * per + i].astype(f32), again)
    picked = jnp.logical_and(classes == label, real)
    entropy = jnp.where(real, log_total, 0.0) - jnp.sum(jnp.where(picked, logits, 0.0), -1, keepdims=True)
    wanted = jnp.where(info[0] == 0, old_logits[0:per, :], old_logits[per : 2 * per, :])
    if per < eight:
        wanted = jnp.concatenate([wanted, jnp.zeros((eight - per, CLASSES), f32)], 0)
    wanted = jnp.concatenate([wanted, jnp.zeros((eight, CPAD - CLASSES), f32)], 1)
    distance = jnp.where(jnp.logical_and(classes < CLASSES, real), logits - wanted, 0.0)
    squares = again * (jnp.sum(distance * distance, -1, keepdims=True) * (1.0 / CLASSES))
    lane = lax.broadcasted_iota(jnp.int32, (1, LANES), 1)
    entropy_sum = jnp.sum(entropy, 0, keepdims=True)
    replay_sum = jnp.sum(squares, 0, keepdims=True)
    loss_out[...] = jnp.where(lane == 0, entropy_sum, jnp.where(lane == 1, replay_sum, replay_count))

    grad = (jnp.exp(logits - log_total) - jnp.where(picked, 1.0, 0.0)) * (1.0 / image_total)
    grad = grad + again * 2.0 * distance / (CLASSES * replay_count)
    grad = jnp.where(jnp.logical_and(classes < CLASSES, real), grad, 0.0)
    grad_low = grad.astype(bf16)
    flat.clear()
    write_head(flat, wide, dot(top, grad_low, 0, 0), column_sums(grad_low))
    sums = {}
    grad = dot(grad_low, w_head[...], 1, 1)
    flat.write(column_sums(grad * unit_last), GAIN_LAST, 2, D)
    flat.write(column_sums(grad), BIAS_LAST, 2, D)
    grad = normalise_back(grad, gain_last, unit_last, scale_last)

    at = BLOCK_AT
    grad_down = grad.astype(bf16)
    flat.write(dot(act, grad_down, 0, 0), at["w_down"], 3, D)
    sums["b_down"] = column_sums(grad_down)
    grad_up = (dot(grad_down, w_down[...], 1, 1) * slope).astype(bf16)
    flat.write(dot(normed_two, grad_up, 0, 0), at["w_up"], 12, FF)
    sums["b_up"] = column_sums(grad_up)
    grad_two = dot(grad_up, w_up[...], 1, 1)
    sums["gain_two"], sums["bias_two"] = column_sums(grad_two * unit_two), column_sums(grad_two)
    grad_hidden = grad + normalise_back(grad_two, vector(vec, "gain_two"), unit_two, scale_two)
    branch = grad_hidden.astype(bf16)
    flat.write(dot(mixed, branch, 0, 0), at["w_out"], 3, D)
    sums["b_out"] = column_sums(branch)
    mixed_heads = by_head(dot(branch, w_out[...], 1, 1).astype(bf16).astype(f32)).astype(bf16)
    grad_probs = dot(mixed_heads, v, 1, 1)
    grad_v = dot(probs_low, mixed_heads, 0, 0).astype(bf16)
    inner = jnp.sum(grad_probs * probs, -1, keepdims=True)
    grad_scores = (probs * (grad_probs - inner)).astype(bf16)
    grad_q = (from_heads(dot(grad_scores, k)) * SCALE).astype(bf16)
    grad_k = dot(grad_scores, q_heads, 0, 0).astype(bf16)
    flat.write(dot(top_normed, grad_q, 0, 0), at["w_qkv"], 9, D)
    flat.write(dot(normed, grad_k, 0, 0), at["w_qkv"] + 3, 9, D)
    flat.write(dot(normed, grad_v, 0, 0), at["w_qkv"] + 6, 9, D)
    sums["b_q"], sums["b_v"] = column_sums(grad_q), column_sums(grad_v)
    many[...] = dot(grad_k, w_k[...], 1, 1) + dot(grad_v, w_v[...], 1, 1)
    top_back = dot(grad_q, w_q[...], 1, 1)
    for i in range(per):
        many[i * ROWS + CLS : i * ROWS + CLS + 1, :] += top_back[i : i + 1, :]
    grad_one = many[...]
    sums["gain_one"], sums["bias_one"] = column_sums(grad_one * unit), column_sums(grad_one)
    many[...] = normalise_back(grad_one, vector(vec, "gain_one"), unit, scale)
    for i in range(per):
        many[i * ROWS + CLS : i * ROWS + CLS + 1, :] += grad_hidden[i : i + 1, :]
    back_out[...] = many[...].astype(bf16)
    write_vectors(flat, sums)
    send_out(place, info, flat, grad_out)


def back_kernel(place, info, *refs):
    (grad_in, x_in, q_in, k_in, v_in, probs_in, mixed_in, hidden_in, act_in, slope_in, patches) = refs[:11]
    w_q, w_k, w_v, w_out, w_up, w_down, vec, grad_out = refs[11:19]
    even, odd, mix, g_q, g_k, g_v, g_out, g_up, g_down, g_patch, g_pos, rows = refs[19:]
    step = pl.program_id(0)
    sums_at = {name: row for row, name in enumerate(VECTORS)}

    @pl.when(step == 0)
    def _():
        for ref in (g_q, g_k, g_v, g_out, g_up, g_down, g_patch, g_pos, rows):
            ref[...] = jnp.zeros(ref.shape, f32)

    def add_row(row, value):
        rows[row : row + 1, 0 : value.shape[1]] += value

    grad_low = grad_in[...]
    g_down[...] += dot(act_in[...], grad_low, 0, 0)
    add_row(sums_at["b_down"], column_sums(grad_low))
    grad_up = (dot(grad_low, w_down[...], 1, 1) * slope_in[...]).astype(bf16)
    unit, scale = normalise(hidden_in[...])
    normed = (unit * vector(vec, "gain_two") + vector(vec, "bias_two")).astype(bf16)
    g_up[...] += dot(normed, grad_up, 0, 0)
    add_row(sums_at["b_up"], column_sums(grad_up))
    grad_two = dot(grad_up, w_up[...], 1, 1)
    add_row(sums_at["gain_two"], column_sums(grad_two * unit))
    add_row(sums_at["bias_two"], column_sums(grad_two))
    grad_hidden = grad_low.astype(f32) + normalise_back(grad_two, vector(vec, "gain_two"), unit, scale)
    branch = grad_hidden.astype(bf16)
    g_out[...] += dot(mixed_in[...], branch, 0, 0)
    add_row(sums_at["b_out"], column_sums(branch))
    mixed_heads = by_head(dot(branch, w_out[...], 1, 1).astype(bf16).astype(f32)).astype(bf16)
    q_heads = by_head(q_in[...].astype(f32) * SCALE).astype(bf16)
    probs = probs_in[...]
    grad_probs = dot(mixed_heads, v_in[...], 1, 1)
    grad_v = dot(probs.astype(bf16), mixed_heads, 0, 0).astype(bf16)
    inner = jnp.sum(grad_probs * probs, -1, keepdims=True)
    grad_scores = (probs * (grad_probs - inner)).astype(bf16)
    grad_q = (from_heads(dot(grad_scores, k_in[...])) * SCALE).astype(bf16)
    grad_k = dot(grad_scores, q_heads, 0, 0).astype(bf16)
    unit, scale = normalise(x_in[...])
    normed = (unit * vector(vec, "gain_one") + vector(vec, "bias_one")).astype(bf16)
    g_q[...] += dot(normed, grad_q, 0, 0)
    g_k[...] += dot(normed, grad_k, 0, 0)
    g_v[...] += dot(normed, grad_v, 0, 0)
    add_row(sums_at["b_q"], column_sums(grad_q))
    add_row(sums_at["b_v"], column_sums(grad_v))
    grad_one = dot(grad_q, w_q[...], 1, 1) + dot(grad_k, w_k[...], 1, 1) + dot(grad_v, w_v[...], 1, 1)
    add_row(sums_at["gain_one"], column_sums(grad_one * unit))
    add_row(sums_at["bias_one"], column_sums(grad_one))
    grad_x = grad_hidden + normalise_back(grad_one, vector(vec, "gain_one"), unit, scale)
    g_pos[...] += grad_x
    grad_emb = grad_x[0:PATCHES].astype(bf16)
    g_patch[...] += dot(patches[...], grad_emb, 0, 0)
    add_row(9, column_sums(grad_emb))

    @pl.when(step == pl.num_programs(0) - 1)
    def _():
        at = BLOCK_AT
        flat = Flat(even, odd, mix, place.count * place.shard_rows)
        flat.clear()
        for part, ref in enumerate((g_q, g_k, g_v)):
            flat.write(ref[...], at["w_qkv"] + 3 * part, 9, D)
        flat.write(g_out[...], at["w_out"], 3, D)
        flat.write(g_up[...], at["w_up"], 12, FF)
        flat.write(g_down[...], at["w_down"], 3, D)
        flat.write(g_patch[...], W_PATCH, 3, D)
        names = {name: rows[row : row + 1, 0 : FF if name == "b_up" else D] for name, row in sums_at.items()}
        write_vectors(flat, names)
        flat.write(rows[9:10, 0:D], B_PATCH, 2, D)
        token = g_pos[CLS : CLS + 1, :]
        flat.write(token, CLS_TOKEN, 2, D)
        natural = jnp.concatenate([token, g_pos[0:PATCHES, :], jnp.zeros((1, D), f32)], 0)
        flat.write(natural, POS_EMBED, 3, D)
        send_out(place, info, flat, grad_out)


def inner_kernel(blocks, first, *refs):
    pieces, basis, loss, grad_out, sums_out, total = refs[:-5], *refs[-5:]
    step = pl.program_id(0)
    shard_rows = grad_out.shape[0]

    @pl.when(step == 0)
    def _():
        value = first[...]
        for ref in pieces:
            value = value + ref[...].astype(f32)
        grad_out[...] = value[:shard_rows]
        total[...] = jnp.zeros(total.shape, f32)

    base = step * blocks
    for at in range(0, KB, 16):
        acc = jnp.zeros((16, LANES), f32)
        for j in range(blocks):
            part = basis[at : at + 16, j * LANES : (j + 1) * LANES].astype(f32)
            acc = acc + part * grad_out[pl.ds(base + j, 1), :]
        total[at : at + 16, :] += acc

    @pl.when(step == pl.num_programs(0) - 1)
    def _():
        coefs = jnp.sum(total[...].T, 0, keepdims=True)
        grad = grad_out[...]
        squares = jnp.sum(jnp.sum(grad * grad, 0, keepdims=True), 1, keepdims=True)
        lane = lax.broadcasted_iota(jnp.int32, (1, SUMS - KB), 1)
        rest = jnp.where(lane == 0, squares, 0.0)
        rest = rest + jnp.where(lane == 1, loss[0:1, 0:1], 0.0) + jnp.where(lane == 2, loss[0:1, 1:2], 0.0)
        sums_out[:, 0:KB] = coefs
        sums_out[:, KB:SUMS] = rest


def update_kernel(blocks, whole_len, counts, sums, basis, grad, loss, master, first, second, *refs):
    loss_out, norm_out, coef_out, master_out, first_out, second_out, coef, removed = refs
    step = pl.program_id(0)

    def clip_factor():
        norm = jnp.sqrt(sums[0:1, KB : KB + 1])
        return norm, jnp.minimum(1.0, CLIP_NORM / (norm + 1e-06))

    @pl.when(step == 0)
    def _():
        norm, factor = clip_factor()
        lane = lax.broadcasted_iota(jnp.int32, (1, KB), 1)
        limit = jnp.where(lane < KMAX, counts[0], counts[1] + KMAX)
        row = jnp.where(lane < limit, sums[:, 0:KB] * factor, 0.0)
        coef_out[0:1, :] = row[:, 0:KMAX]
        coef_out[1:2, :] = row[:, KMAX:KB]
        coef[...] = jnp.broadcast_to(row, (LANES, KB)).T
        norm_out[0] = jnp.sum(norm)
        loss_out[0] = jnp.sum(sums[0:1, KB + 1 : KB + 2])
        loss_out[1] = jnp.sum(sums[0:1, KB + 2 : KB + 3])
        loss_out[2] = jnp.sum(loss[0:1, 2:3])

    acc = [jnp.zeros((8, LANES), f32) for _ in range(blocks)]
    for at in range(0, KB, 16):
        weight = coef[at : at + 16, :]
        for j in range(blocks):
            part = basis[at : at + 16, j * LANES : (j + 1) * LANES].astype(f32) * weight
            acc[j] = acc[j] + (part[0:8] + part[8:16])
    base = step * blocks
    for j in range(blocks):
        removed[pl.ds(base + j, 1), :] = jnp.sum(acc[j], 0, keepdims=True)

    @pl.when(step == pl.num_programs(0) - 1)
    def _():
        _, factor = clip_factor()
        rows = grad.shape[0]
        projected = grad[...] * factor - removed[0:rows, :] * (1.0 / whole_len)
        new_first = BETA_ONE * first[...] + (1.0 - BETA_ONE) * projected
        new_second = BETA_TWO * second[...] + (1.0 - BETA_TWO) * projected * projected
        ratio = (
            new_first
            / (1.0 - BETA_ONE**STEP)
            / (jnp.sqrt(new_second / (1.0 - BETA_TWO**STEP)) + ADAM_EPS)
        )
        old = master[...]
        master_out[...] = old - LEARN_RATE * (ratio + WEIGHT_DECAY * old)
        first_out[...] = new_first
        second_out[...] = new_second


def dp_dims(count):
    zed = 4 if count % 4 == 0 else 1
    plane = count // zed
    ex = max(side for side in range(1, math.isqrt(plane) + 1) if plane % side == 0)
    return zed, plane // ex, ex


def moved(value, place, turn=(0, 0, 0), core=0, sections=(0, 1)):
    pairs = []
    for section in sections:
        for zed in range(place.z):
            for why in range(place.y):
                for ex in range(place.x):
                    source = (section * place.z + zed) * place.y * place.x + why * place.x + ex
                    there = ((section + core) % 2) * place.z + (zed + turn[0]) % place.z
                    target = (there * place.y + (why + turn[1]) % place.y) * place.x
                    pairs.append((source, target + (ex + turn[2]) % place.x))
    return lax.ppermute(value, ("section", "dp"), pairs)


def butterfly(value, place):
    value = value + moved(value, place, core=1)
    for axis, size in ((2, place.x), (1, place.y), (0, place.z)):
        span = 1
        while span < size:
            pairs = []
            for index in range(2 * place.count):
                section, rest = divmod(index, place.count)
                at = [rest // (place.y * place.x), rest // place.x % place.y, rest % place.x]
                at[axis] ^= span
                pairs.append((index, section * place.count + (at[0] * place.y + at[1]) * place.x + at[2]))
            value = value + lax.ppermute(value, ("section", "dp"), pairs)
            span *= 2
    return value


def whole(shape):
    return pl.BlockSpec(shape, lambda *_: (0,) * len(shape))


def params(megabytes):
    return pltpu.CompilerParams(
        vmem_limit_bytes=megabytes * 1024 * 1024, dimension_semantics=("arbitrary",)
    )


def body(
    patches, labels, replay, old_logits, basis_count, master, first_moment, second_moment, basis
):
    chips = lax.axis_size("dp")
    shard_len = master.shape[1]
    shard_rows = shard_len // LANES
    place = Place(dp_dims(chips), shard_rows)
    images = patches.shape[0]
    per = images // 2
    section = lax.axis_index("section")
    info = jnp.stack([section, lax.axis_index("dp")]).astype(jnp.int32)
    flat_rows = chips * shard_rows + SPARE
    turns = place.turns()

    shard = master[0].astype(bf16).reshape(shard_rows, LANES)
    count = jnp.sum(replay).astype(bf16)
    tail = jnp.full((place.sent_rows - shard_rows, LANES), count, bf16)
    shard = jnp.concatenate([shard, tail], 0)
    line = jnp.stack([shard] + [moved(shard, place, (d, 0, 0)) for d in range(1, place.z)])
    own = [moved(line, place, (0, a, b)) if a + b else line for a, b in turns]
    other = [moved(piece, place, core=1) for piece in own]

    flat_scratch = [
        pltpu.VMEM((flat_rows, LANES), f32),
        pltpu.VMEM((flat_rows, LANES), f32),
        pltpu.VMEM((FF + 32, LANES), f32),
    ]
    piece_specs = [whole(piece.shape) for piece in own + other]
    block_shapes = [(D, D)] * 4 + [(D, FF), (FF, D)]
    row_of = lambda i, *_: (i, 0)
    saved = [
        ((ROWS, D), f32),
        ((ROWS, D), bf16),
        ((ROWS, D), bf16),
        ((ROWS, D), bf16),
        ((HEADS * ROWS, ROWS), f32),
        ((ROWS, D), bf16),
        ((ROWS, D), f32),
        ((ROWS, FF), bf16),
        ((ROWS, FF), f32),
    ]
    middle_kind = ((ROWS, D), bf16)
    patch_spec = pl.BlockSpec((None, PATCHES, PDIM), lambda i, info: (info[0] * per + i, 0, 0))
    outs = pl.pallas_call(
        functools.partial(front_kernel, place),
        grid_spec=pltpu.PrefetchScalarGridSpec(
            num_scalar_prefetch=1,
            grid=(per,),
            in_specs=piece_specs + [patch_spec],
            out_specs=[pl.BlockSpec(shape, row_of) for shape, _ in saved + [middle_kind]]
            + [whole(shape) for shape in block_shapes]
            + [whole((VEC_ROWS, FF))],
            scratch_shapes=flat_scratch
            + [pltpu.VMEM((PDIM, D), bf16), pltpu.VMEM((ROWS, D), f32), pltpu.VMEM((ROWS, D), f32)],
        ),
        out_shape=[
            jax.ShapeDtypeStruct((per * shape[0], shape[1]), kind) for shape, kind in saved + [middle_kind]
        ]
        + [jax.ShapeDtypeStruct(shape, bf16) for shape in block_shapes]
        + [jax.ShapeDtypeStruct((VEC_ROWS, FF), f32)],
        compiler_params=params(40),
        name="front",
    )(info, *own, *other, patches)
    kept, middle, weights = outs[:9], outs[9], outs[10:]

    grad_shape = jax.ShapeDtypeStruct((chips, place.sent_rows, LANES), bf16)
    smem = pl.BlockSpec(memory_space=pltpu.SMEM)
    vmem = pl.BlockSpec(memory_space=pltpu.VMEM)
    eight = -(-per // 8) * 8
    back, late_grad, loss = pl.pallas_call(
        functools.partial(late_kernel, place, per, float(images * chips)),
        in_specs=[smem] * 3 + [vmem] * (2 * len(turns) + 2),
        out_specs=[vmem] * 3,
        out_shape=[
            jax.ShapeDtypeStruct((per * ROWS, D), bf16),
            grad_shape,
            jax.ShapeDtypeStruct((1, LANES), f32),
        ],
        scratch_shapes=flat_scratch
        + [pltpu.VMEM((8, 256, LANES), f32)]
        + [pltpu.VMEM(shape, bf16) for shape in block_shapes]
        + [
            pltpu.VMEM((VEC_ROWS, FF), f32),
            pltpu.VMEM((D, CPAD), bf16),
            pltpu.VMEM((1, CPAD), f32),
            pltpu.VMEM((eight, D), f32),
            pltpu.VMEM((per * ROWS, D), f32),
        ],
        compiler_params=pltpu.CompilerParams(vmem_limit_bytes=40 * 1024 * 1024),
        name="late",
    )(info, labels, replay, *own, *other, middle, old_logits)

    early_grad = pl.pallas_call(
        functools.partial(back_kernel, place),
        grid_spec=pltpu.PrefetchScalarGridSpec(
            num_scalar_prefetch=1,
            grid=(per,),
            in_specs=[pl.BlockSpec(shape, row_of) for shape, _ in [middle_kind] + saved]
            + [patch_spec]
            + [whole(shape) for shape in block_shapes]
            + [whole((VEC_ROWS, FF))],
            out_specs=whole(grad_shape.shape),
            scratch_shapes=flat_scratch
            + [pltpu.VMEM(shape, f32) for shape in block_shapes]
            + [
                pltpu.VMEM((PDIM, D), f32),
                pltpu.VMEM((ROWS, D), f32),
                pltpu.VMEM((VEC_ROWS, FF), f32),
            ],
        ),
        out_shape=grad_shape,
        compiler_params=params(48),
        name="back",
    )(info, back, *kept, patches, *weights)

    late_here = moved(late_grad, place, core=1, sections=(0,))
    early_here = moved(early_grad, place, core=1, sections=(1,))

    def paired(turn):
        cut = slice(turn * place.z, (turn + 1) * place.z)
        early = early_grad[cut].astype(f32) + early_here[cut].astype(f32)
        late = late_grad[cut].astype(f32) + late_here[cut].astype(f32)
        return jnp.where(section == 0, early, late)

    summed = paired(0)
    arrived = [
        moved(paired(turn).astype(bf16), place, (0, a, b)) for turn, (a, b) in enumerate(turns) if turn
    ]
    for piece in arrived:
        summed = summed + piece.astype(f32)
    pieces = [moved(summed[d].astype(bf16), place, (d, 0, 0)) for d in range(1, place.z)]

    rows_basis = basis.reshape(KB, shard_len)
    blocks = max(n for n in range(1, 27) if shard_rows % n == 0)
    steps = shard_rows // blocks
    basis_spec = pl.BlockSpec((KB, blocks * LANES), lambda i, *_: (0, i))
    flat_kind = jax.ShapeDtypeStruct((shard_rows, LANES), f32)
    grad, sums = pl.pallas_call(
        functools.partial(inner_kernel, blocks),
        grid=(steps,),
        in_specs=[whole((place.sent_rows, LANES))] * place.z + [basis_spec, whole((1, LANES))],
        out_specs=[whole((shard_rows, LANES)), whole((1, SUMS))],
        out_shape=[flat_kind, jax.ShapeDtypeStruct((1, SUMS), f32)],
        scratch_shapes=[pltpu.VMEM((KB, LANES), f32)],
        compiler_params=params(24),
        name="inner",
    )(summed[0], *pieces, rows_basis, loss)
    sums = butterfly(sums, place)
    flat_spec = whole((shard_rows, LANES))
    padded_rows = -(-shard_rows // 8) * 8
    loss_parts, norm, coefficients, new_master, new_first, new_second = pl.pallas_call(
        functools.partial(update_kernel, blocks, float(2 * shard_len * chips)),
        grid_spec=pltpu.PrefetchScalarGridSpec(
            num_scalar_prefetch=1,
            grid=(steps,),
            in_specs=[whole((1, SUMS)), basis_spec, flat_spec, whole((1, LANES))] + [flat_spec] * 3,
            out_specs=[smem, smem, whole((TASKS, KMAX))] + [flat_spec] * 3,
            scratch_shapes=[pltpu.VMEM((KB, LANES), f32), pltpu.VMEM((padded_rows, LANES), f32)],
        ),
        out_shape=[
            jax.ShapeDtypeStruct((3,), f32),
            jax.ShapeDtypeStruct((1,), f32),
            jax.ShapeDtypeStruct((TASKS, KMAX), f32),
        ]
        + [flat_kind] * 3,
        compiler_params=params(24),
        name="update",
    )(
        basis_count,
        sums,
        rows_basis,
        grad,
        loss,
        master.reshape(shard_rows, LANES),
        first_moment.reshape(shard_rows, LANES),
        second_moment.reshape(shard_rows, LANES),
    )
    return (
        loss_parts,
        norm[0],
        coefficients,
        new_master.reshape(1, shard_len),
        new_first.reshape(1, shard_len),
        new_second.reshape(1, shard_len),
    )


def solution(mesh):
    in_specs = (
        P("dp", None, None),
        P("dp"),
        P("dp"),
        P("dp", None),
        P(),
        P("section", "dp"),
        P("section", "dp"),
        P("section", "dp"),
        P(None, "section", "dp"),
    )
    out_specs = (P(), P(), P(), P("section", "dp"), P("section", "dp"), P("section", "dp"))
    return jax.shard_map(body, mesh=mesh, in_specs=in_specs, out_specs=out_specs, check_vma=False)
```

```python
import functools
import math

import jax
import jax.numpy as jnp
from jax import lax
from jax.experimental import pallas as pl
from jax.experimental.pallas import tpu as pltpu
from jax.sharding import PartitionSpec as P

HEADS = 3
HD = 64
D = 192
FF = 768
PDIM = 768
PATCHES = 196
TOKENS = PATCHES + 1
ROWS = 208
CLS = PATCHES
CLASSES = 1000
CPAD = 1024
TASKS = 2
KMAX = 200
KB = TASKS * KMAX
UPPER = 208
STEP = 10
LANES = 128
HALF = 64
SPARE = 512
SUMS = 512

NORM_EPS = 1e-06
CLIP_NORM = 0.02
LEARN_RATE = 0.05
BETA_ONE = 0.9
BETA_TWO = 0.999
ADAM_EPS = 1e-08
WEIGHT_DECAY = 0.05
SCALE = HD ** (-0.5)
MASKED = -1e30

BLOCK_AT = dict(
    gain_one=0,
    bias_one=3,
    w_qkv=6,
    b_qkv=1734,
    w_out=1740,
    b_out=2316,
    gain_two=2319,
    bias_two=2322,
    w_up=2325,
    b_up=4629,
    w_down=4641,
    b_down=6945,
)
W_PATCH, B_PATCH, CLS_TOKEN, POS_EMBED = 6948, 9252, 9255, 9258
GAIN_LAST, BIAS_LAST, W_HEAD, B_HEAD = 6948, 6951, 6954, 9954
VECTORS = ("gain_one", "bias_one", "b_q", "b_v", "b_out", "gain_two", "bias_two", "b_up", "b_down")
VEC_ROWS = 16

f32 = jnp.float32
bf16 = jnp.bfloat16


def dot(left, right, left_dim=1, right_dim=0):
    return lax.dot_general(
        left, right, (((left_dim,), (right_dim,)), ((), ())), preferred_element_type=f32
    )


def low_lanes(shape):
    return lax.broadcasted_iota(jnp.int32, shape, 1) < HALF


def swap_halves(value):
    return pltpu.roll(value, HALF, 1)


def head_masks():
    lane = lax.broadcasted_iota(jnp.int32, (1, D), 1)
    return [jnp.logical_and(lane >= h * HD, lane < (h + 1) * HD) for h in range(HEADS)]


def by_head(value):
    return jnp.concatenate([jnp.where(m, value, 0.0) for m in head_masks()], 0)


def from_heads(value):
    rows = value.shape[0] // HEADS
    parts = [value[h * rows : (h + 1) * rows] for h in range(HEADS)]
    masks = head_masks()
    return jnp.where(masks[0], parts[0], jnp.where(masks[1], parts[1], parts[2]))


def normalise(rows_in):
    mean = jnp.sum(rows_in, -1, keepdims=True) * (1.0 / D)
    centred = rows_in - mean
    variance = jnp.sum(centred * centred, -1, keepdims=True) * (1.0 / D)
    scale = lax.rsqrt(variance + NORM_EPS)
    return centred * scale, scale


def normalise_back(grad, gain, unit, scale):
    grad_unit = grad * gain
    first = jnp.sum(grad_unit, -1, keepdims=True) * (1.0 / D)
    second = jnp.sum(grad_unit * unit, -1, keepdims=True) * (1.0 / D)
    return scale * (grad_unit - first - unit * second)


def gelu_parts(pre):
    cdf = 0.5 * (1.0 + lax.erf(pre * math.sqrt(0.5)))
    slope = cdf + pre * (jnp.exp(-0.5 * pre * pre) * (1.0 / math.sqrt(2.0 * math.pi)))
    return pre * cdf, slope


def column_sums(value):
    return jnp.sum(value.astype(f32), 0, keepdims=True)


def strided(ref, start, count, stride):
    if count == 1 or stride == 1:
        return ref[pl.ds(start, count), :]
    return ref[pl.ds(start, count, stride=stride), :]


class Flat:
    def __init__(self, even, odd, mix, rows):
        self.even, self.odd, self.mix, self.rows = even, odd, mix, rows

    def shift(self):
        step = 192
        for at in range(0, self.rows, step):
            here = swap_halves(self.even[at : at + step, :])
            after = swap_halves(self.even[at + 1 : at + 1 + step, :])
            self.odd[at : at + step, :] = jnp.where(low_lanes(here.shape), here, after)

    def rows_at(self, half, count, stride):
        return strided(self.odd if half % 2 else self.even, half // 2, count, stride)

    def blocks(self, half, width, rows, cols):
        for at in range(0, cols, LANES):
            start = half + at // HALF
            if rows == 1 or width % 2 == 0:
                value = self.rows_at(start, rows, width // 2)
            else:
                pairs = (rows + 1) // 2
                self.mix[pl.ds(0, pairs, stride=2), :] = self.rows_at(start, pairs, width)
                self.mix[pl.ds(1, pairs, stride=2), :] = self.rows_at(start + width, pairs, width)
                value = self.mix[0:rows, :]
            yield at, min(LANES, cols - at), value

    def read(self, dest, half, width, rows, cols):
        for at, wide, value in self.blocks(half, width, rows, cols):
            dest[0:rows, at : at + wide] = value[:, :wide].astype(dest.dtype)

    def read_row(self, dest, row, half, cols):
        for at, wide, value in self.blocks(half, 2, 1, cols):
            dest[row : row + 1, at : at + wide] = value[:, :wide]

    def clear(self):
        self.even[...] = jnp.zeros(self.even.shape, f32)
        self.odd[...] = jnp.zeros(self.odd.shape, f32)

    def put_rows(self, half, count, stride, value):
        ref, start = (self.odd, half // 2 + 8) if half % 2 else (self.even, half // 2)
        if count == 1 or stride == 1:
            ref[pl.ds(start, count), :] = value
        else:
            ref[pl.ds(start, count, stride=stride), :] = value

    def write(self, value, half, width, cols):
        rows = value.shape[0]
        for at in range(0, cols, LANES):
            wide = min(LANES, cols - at)
            part = value[:, at : at + wide]
            if wide < LANES:
                part = jnp.concatenate([part, jnp.zeros((rows, LANES - wide), f32)], 1)
            start = half + at // HALF
            if rows == 1 or width % 2 == 0:
                self.put_rows(start, rows, width // 2, part)
            else:
                pairs = (rows + 1) // 2
                self.mix[0:rows, :] = part
                self.put_rows(start, pairs, width, self.mix[pl.ds(0, pairs, stride=2), :])
                self.put_rows(start + width, pairs, width, self.mix[pl.ds(1, pairs, stride=2), :])

    def merged(self, at, count):
        here = swap_halves(self.odd[at + 8 : at + 8 + count, :])
        before = swap_halves(self.odd[at + 7 : at + 7 + count, :])
        return self.even[at : at + count, :] + jnp.where(low_lanes(here.shape), before, here)


class Place:
    def __init__(self, dims, shard_rows):
        self.z, self.y, self.x = dims
        self.count = self.z * self.y * self.x
        self.shard_rows = shard_rows
        self.sent_rows = -(-(shard_rows + 1) // 16) * 16

    def split(self, index):
        plane = self.y * self.x
        return index // plane, lax.rem(index, plane) // self.x, lax.rem(index, self.x)

    def turns(self):
        return [(a, b) for a in range(self.y) for b in range(self.x)]


def load_section(place, info, pieces, wanted, flat):
    own, other = pieces
    section = info[0]
    zed, why, ex = place.split(info[1])
    rows = place.shard_rows

    def copy(refs):
        for turn, (a, b) in enumerate(place.turns()):
            for d in range(place.z):
                shard = lax.rem(zed + (place.z - d), place.z) * (place.y * place.x)
                shard = shard + lax.rem(why + (place.y - a), place.y) * place.x
                shard = shard + lax.rem(ex + (place.x - b), place.x)
                start = shard * rows
                if rows % 8 == 0:
                    start = pl.multiple_of(start, 8)
                value = refs[turn][d].astype(f32)
                flat.even[pl.ds(start, rows), :] = value[:rows]

    @pl.when(section == wanted)
    def _():
        copy(own)

    @pl.when(section != wanted)
    def _():
        copy(other)

    flat.shift()


def read_block(flat, weights, vec):
    at = BLOCK_AT
    w_q, w_k, w_v, w_out, w_up, w_down = weights
    for place, dest in enumerate((w_q, w_k, w_v)):
        flat.read(dest, at["w_qkv"] + 3 * place, 9, D, D)
    flat.read(w_out, at["w_out"], 3, D, D)
    flat.read(w_up, at["w_up"], 12, D, FF)
    flat.read(w_down, at["w_down"], 3, FF, D)
    starts = dict(at, b_q=at["b_qkv"], b_v=at["b_qkv"] + 3)
    for row, name in enumerate(VECTORS):
        flat.read_row(vec, row, starts[name], FF if name == "b_up" else D)


def vector(vec, name):
    row = VECTORS.index(name)
    return vec[row : row + 1, 0 : FF if name == "b_up" else D]


def write_vectors(flat, sums):
    at = BLOCK_AT
    starts = dict(at, b_q=at["b_qkv"], b_v=at["b_qkv"] + 3)
    for name, value in sums.items():
        flat.write(value, starts[name], 2, value.shape[1])


def send_out(place, info, flat, out_ref):
    zed, why, ex = place.split(info[1])
    rows, spare = place.shard_rows, place.sent_rows - place.shard_rows
    for shard in range(place.count):
        zk, yk, xk = shard // (place.y * place.x), shard // place.x % place.y, shard % place.x
        d = lax.rem(zk + place.z - zed, place.z)
        a = lax.rem(yk + place.y - why, place.y)
        b = lax.rem(xk + place.x - ex, place.x)
        value = flat.merged(shard * rows, rows)
        value = jnp.concatenate([value, jnp.zeros((spare, LANES), f32)], 0)
        out_ref[(a * place.x + b) * place.z + d] = value.astype(bf16)


def front_kernel(place, info, *refs):
    turns = len(place.turns())
    own, other, refs = refs[:turns], refs[turns : 2 * turns], refs[2 * turns :]
    patches, refs = refs[0], refs[1:]
    (x_out, q_out, k_out, v_out, probs_out, mixed_out, hidden_out, act_out, slope_out, middle_out) = refs[:10]
    w_q, w_k, w_v, w_out, w_up, w_down, vec = refs[10:17]
    even, odd, mix, w_patch, added, tokens = refs[17:]
    flat = Flat(even, odd, mix, place.count * place.shard_rows)

    @pl.when(pl.program_id(0) == 0)
    def _():
        load_section(place, info, (own, other), 0, flat)
        read_block(flat, (w_q, w_k, w_v, w_out, w_up, w_down), vec)
        flat.read(w_patch, W_PATCH, 3, PDIM, D)
        flat.read_row(vec, 9, B_PATCH, D)
        flat.read_row(vec, 10, CLS_TOKEN, D)
        added[...] = jnp.zeros(added.shape, f32)
        tokens[...] = jnp.zeros(tokens.shape, f32)
        for at, wide, value in flat.blocks(POS_EMBED, 3, TOKENS + 1, D):
            bias = vec[9:10, at : at + wide]
            token = vec[10:11, at : at + wide]
            added[0:PATCHES, at : at + wide] = value[1:TOKENS, :wide] + bias
            added[CLS : CLS + 1, at : at + wide] = value[0:1, :wide] + token

    tokens[0:PATCHES, :] = dot(patches[...], w_patch[...])
    x = tokens[...] + added[...]
    x_out[...] = x
    unit, _ = normalise(x)
    normed = (unit * vector(vec, "gain_one") + vector(vec, "bias_one")).astype(bf16)
    q = (dot(normed, w_q[...]) + vector(vec, "b_q")).astype(bf16)
    k = dot(normed, w_k[...]).astype(bf16)
    v = (dot(normed, w_v[...]) + vector(vec, "b_v")).astype(bf16)
    q_out[...], k_out[...], v_out[...] = q, k, v
    scores = dot(by_head(q.astype(f32) * SCALE).astype(bf16), k, 1, 1)
    column = lax.broadcasted_iota(jnp.int32, scores.shape, 1)
    scores = jnp.where(column < TOKENS, scores, MASKED)
    raised = jnp.exp(scores - jnp.max(scores, -1, keepdims=True))
    probs = raised / jnp.sum(raised, -1, keepdims=True)
    probs_out[...] = probs
    mixed = from_heads(dot(probs.astype(bf16), v)).astype(bf16)
    mixed_out[...] = mixed
    hidden = x + dot(mixed, w_out[...]) + vector(vec, "b_out")
    hidden_out[...] = hidden
    unit, _ = normalise(hidden)
    normed = (unit * vector(vec, "gain_two") + vector(vec, "bias_two")).astype(bf16)
    pre = dot(normed, w_up[...]) + vector(vec, "b_up")
    act, slope = gelu_parts(pre)
    act = act.astype(bf16)
    act_out[...], slope_out[...] = act, slope
    middle = hidden + dot(act, w_down[...]) + vector(vec, "b_down")
    middle_out[...] = middle.astype(bf16)


def read_head(flat, wide, w_head, b_head):
    first = W_HEAD // 2
    lane = lax.broadcasted_iota(jnp.int32, (16, LANES), 1)
    for phase in range(16):
        start, off = first + CLASSES * phase // LANES, CLASSES * phase % LANES
        got = [strided(flat.even, start + j, 16, 125) for j in range(9 if off else 8)]
        if off:
            got = [pltpu.roll(g, LANES - off, 1) for g in got]
        for j in range(8):
            value = jnp.where(lane < LANES - off, got[j], got[j + 1]) if off else got[j]
            wide[j, pl.ds(phase, 16, stride=16), :] = value
    lane = lax.broadcasted_iota(jnp.int32, (1, LANES), 1)
    for j in range(8):
        keep = lane + j * LANES < CLASSES
        w_head[:, j * LANES : (j + 1) * LANES] = jnp.where(keep, wide[j, 0:D, :], 0.0).astype(bf16)
        value = flat.even[B_HEAD // 2 + j : B_HEAD // 2 + j + 1, :]
        b_head[0:1, j * LANES : (j + 1) * LANES] = jnp.where(keep, value, 0.0)


def write_head(flat, wide, grad_w, grad_b):
    first = W_HEAD // 2
    for j in range(8):
        wide[j, 0:D, :] = grad_w[:, j * LANES : (j + 1) * LANES]
        wide[j, D:, :] = jnp.zeros((wide.shape[1] - D, LANES), f32)
    lane = lax.broadcasted_iota(jnp.int32, (16, LANES), 1)
    for phase in range(16):
        start, off = first + CLASSES * phase // LANES, CLASSES * phase % LANES
        got = [wide[j, pl.ds(phase, 16, stride=16), :] for j in range(8)]
        if off:
            got = [pltpu.roll(g, off, 1) for g in got]
        for j in range(9 if off else 8):
            if not off:
                value = got[j]
            else:
                before = got[j - 1] if j else jnp.zeros((16, LANES), f32)
                value = jnp.where(lane < off, before, got[j] if j < 8 else 0.0)
            flat.even[pl.ds(start + j, 16, stride=125), :] += value
    for j in range(8):
        row = B_HEAD // 2 + j
        flat.even[row : row + 1, :] += grad_b[:, j * LANES : (j + 1) * LANES]


def late_kernel(place, per, image_total, info, labels, replay, *refs):
    turns = len(place.turns())
    own, other, refs = refs[:turns], refs[turns : 2 * turns], refs[2 * turns :]
    middle, old_logits, back_out, grad_out, loss_out = refs[:5]
    even, odd, mix, wide, w_q, w_k, w_v, w_out, w_up, w_down, vec, w_head, b_head, few, many = refs[5:]
    flat = Flat(even, odd, mix, place.count * place.shard_rows)
    load_section(place, info, (own, other), 1, flat)
    read_block(flat, (w_q, w_k, w_v, w_out, w_up, w_down), vec)
    flat.read_row(vec, 9, GAIN_LAST, D)
    flat.read_row(vec, 10, BIAS_LAST, D)
    read_head(flat, wide, w_head, b_head)
    gain_last, bias_last = vec[9:10, 0:D], vec[10:11, 0:D]
    carried = jnp.zeros((1, LANES), f32)
    for ref in own:
        for d in range(place.z):
            carried = carried + ref[d].astype(f32)[place.shard_rows : place.shard_rows + 1]
    replay_count = carried[:, 0:1]

    x = middle[...].astype(f32)
    unit, scale = normalise(x)
    normed_f = unit * vector(vec, "gain_one") + vector(vec, "bias_one")
    normed = normed_f.astype(bf16)
    k = dot(normed, w_k[...]).astype(bf16)
    v = (dot(normed, w_v[...]) + vector(vec, "b_v")).astype(bf16)

    def class_rows(value):
        few[...] = jnp.zeros(few.shape, f32)
        for i in range(per):
            few[i : i + 1, :] = value[i * ROWS + CLS : i * ROWS + CLS + 1, :]
        return few[...]

    eight = few.shape[0]
    image = lax.broadcasted_iota(jnp.int32, (eight, 1), 0)
    real = image < per
    x_top = class_rows(x)
    top_normed = class_rows(normed_f).astype(bf16)
    q = (dot(top_normed, w_q[...]) + vector(vec, "b_q")).astype(bf16)
    q_heads = by_head(jnp.where(real, q.astype(f32) * SCALE, 0.0)).astype(bf16)
    scores = dot(q_heads, k, 1, 1)
    column = lax.broadcasted_iota(jnp.int32, scores.shape, 1)
    owner = lax.rem(lax.broadcasted_iota(jnp.int32, scores.shape, 0), eight) * ROWS
    inside = jnp.logical_and(column >= owner, column < owner + TOKENS)
    scores = jnp.where(inside, scores, MASKED)
    raised = jnp.where(inside, jnp.exp(scores - jnp.max(scores, -1, keepdims=True)), 0.0)
    total = jnp.sum(raised, -1, keepdims=True)
    probs = raised / jnp.where(total > 0.0, total, 1.0)
    probs_low = probs.astype(bf16)
    mixed = from_heads(dot(probs_low, v)).astype(bf16)
    hidden = x_top + dot(mixed, w_out[...]) + vector(vec, "b_out")
    unit_two, scale_two = normalise(hidden)
    normed_two = (unit_two * vector(vec, "gain_two") + vector(vec, "bias_two")).astype(bf16)
    act, slope = gelu_parts(dot(normed_two, w_up[...]) + vector(vec, "b_up"))
    act = act.astype(bf16)
    final = hidden + dot(act, w_down[...]) + vector(vec, "b_down")

    unit_last, scale_last = normalise(final)
    top = (unit_last * gain_last + bias_last).astype(bf16)
    classes = lax.broadcasted_iota(jnp.int32, (eight, CPAD), 1)
    logits = dot(top, w_head[...]) + b_head[...]
    logits = jnp.where(classes < CLASSES, logits, MASKED)
    highest = jnp.max(logits, -1, keepdims=True)
    log_total = highest + jnp.log(jnp.sum(jnp.exp(logits - highest), -1, keepdims=True))
    label = jnp.zeros((eight, 1), jnp.int32)
    again = jnp.zeros((eight, 1), f32)
    for i in range(per):
        label = jnp.where(image == i, labels[info[0] * per + i], label)
        again = jnp.where(image == i, replay[info[0] * per + i].astype(f32), again)
    picked = jnp.logical_and(classes == label, real)
    entropy = jnp.where(real, log_total, 0.0) - jnp.sum(jnp.where(picked, logits, 0.0), -1, keepdims=True)
    wanted = jnp.where(info[0] == 0, old_logits[0:per, :], old_logits[per : 2 * per, :])
    if per < eight:
        wanted = jnp.concatenate([wanted, jnp.zeros((eight - per, CLASSES), f32)], 0)
    wanted = jnp.concatenate([wanted, jnp.zeros((eight, CPAD - CLASSES), f32)], 1)
    distance = jnp.where(jnp.logical_and(classes < CLASSES, real), logits - wanted, 0.0)
    squares = again * (jnp.sum(distance * distance, -1, keepdims=True) * (1.0 / CLASSES))
    lane = lax.broadcasted_iota(jnp.int32, (1, LANES), 1)
    entropy_sum = jnp.sum(entropy, 0, keepdims=True)
    replay_sum = jnp.sum(squares, 0, keepdims=True)
    loss_out[...] = jnp.where(lane == 0, entropy_sum, jnp.where(lane == 1, replay_sum, replay_count))

    grad = (jnp.exp(logits - log_total) - jnp.where(picked, 1.0, 0.0)) * (1.0 / image_total)
    grad = grad + again * 2.0 * distance / (CLASSES * replay_count)
    grad = jnp.where(jnp.logical_and(classes < CLASSES, real), grad, 0.0)
    grad_low = grad.astype(bf16)
    flat.clear()
    write_head(flat, wide, dot(top, grad_low, 0, 0), column_sums(grad_low))
    sums = {}
    grad = dot(grad_low, w_head[...], 1, 1)
    flat.write(column_sums(grad * unit_last), GAIN_LAST, 2, D)
    flat.write(column_sums(grad), BIAS_LAST, 2, D)
    grad = normalise_back(grad, gain_last, unit_last, scale_last)

    at = BLOCK_AT
    grad_down = grad.astype(bf16)
    flat.write(dot(act, grad_down, 0, 0), at["w_down"], 3, D)
    sums["b_down"] = column_sums(grad_down)
    grad_up = (dot(grad_down, w_down[...], 1, 1) * slope).astype(bf16)
    flat.write(dot(normed_two, grad_up, 0, 0), at["w_up"], 12, FF)
    sums["b_up"] = column_sums(grad_up)
    grad_two = dot(grad_up, w_up[...], 1, 1)
    sums["gain_two"], sums["bias_two"] = column_sums(grad_two * unit_two), column_sums(grad_two)
    grad_hidden = grad + normalise_back(grad_two, vector(vec, "gain_two"), unit_two, scale_two)
    branch = grad_hidden.astype(bf16)
    flat.write(dot(mixed, branch, 0, 0), at["w_out"], 3, D)
    sums["b_out"] = column_sums(branch)
    mixed_heads = by_head(dot(branch, w_out[...], 1, 1).astype(bf16).astype(f32)).astype(bf16)
    grad_probs = dot(mixed_heads, v, 1, 1)
    grad_v = dot(probs_low, mixed_heads, 0, 0).astype(bf16)
    inner = jnp.sum(grad_probs * probs, -1, keepdims=True)
    grad_scores = (probs * (grad_probs - inner)).astype(bf16)
    grad_q = (from_heads(dot(grad_scores, k)) * SCALE).astype(bf16)
    grad_k = dot(grad_scores, q_heads, 0, 0).astype(bf16)
    flat.write(dot(top_normed, grad_q, 0, 0), at["w_qkv"], 9, D)
    flat.write(dot(normed, grad_k, 0, 0), at["w_qkv"] + 3, 9, D)
    flat.write(dot(normed, grad_v, 0, 0), at["w_qkv"] + 6, 9, D)
    sums["b_q"], sums["b_v"] = column_sums(grad_q), column_sums(grad_v)
    many[...] = dot(grad_k, w_k[...], 1, 1) + dot(grad_v, w_v[...], 1, 1)
    top_back = dot(grad_q, w_q[...], 1, 1)
    for i in range(per):
        many[i * ROWS + CLS : i * ROWS + CLS + 1, :] += top_back[i : i + 1, :]
    grad_one = many[...]
    sums["gain_one"], sums["bias_one"] = column_sums(grad_one * unit), column_sums(grad_one)
    many[...] = normalise_back(grad_one, vector(vec, "gain_one"), unit, scale)
    for i in range(per):
        many[i * ROWS + CLS : i * ROWS + CLS + 1, :] += grad_hidden[i : i + 1, :]
    back_out[...] = many[...].astype(bf16)
    write_vectors(flat, sums)
    send_out(place, info, flat, grad_out)


def back_kernel(place, info, *refs):
    (grad_in, x_in, q_in, k_in, v_in, probs_in, mixed_in, hidden_in, act_in, slope_in, patches) = refs[:11]
    w_q, w_k, w_v, w_out, w_up, w_down, vec, grad_out = refs[11:19]
    even, odd, mix, g_q, g_k, g_v, g_out, g_up, g_down, g_patch, g_pos, rows = refs[19:]
    step = pl.program_id(0)
    sums_at = {name: row for row, name in enumerate(VECTORS)}

    @pl.when(step == 0)
    def _():
        for ref in (g_q, g_k, g_v, g_out, g_up, g_down, g_patch, g_pos, rows):
            ref[...] = jnp.zeros(ref.shape, f32)

    def add_row(row, value):
        rows[row : row + 1, 0 : value.shape[1]] += value

    grad_low = grad_in[...]
    g_down[...] += dot(act_in[...], grad_low, 0, 0)
    add_row(sums_at["b_down"], column_sums(grad_low))
    grad_up = (dot(grad_low, w_down[...], 1, 1) * slope_in[...]).astype(bf16)
    unit, scale = normalise(hidden_in[...])
    normed = (unit * vector(vec, "gain_two") + vector(vec, "bias_two")).astype(bf16)
    g_up[...] += dot(normed, grad_up, 0, 0)
    add_row(sums_at["b_up"], column_sums(grad_up))
    grad_two = dot(grad_up, w_up[...], 1, 1)
    add_row(sums_at["gain_two"], column_sums(grad_two * unit))
    add_row(sums_at["bias_two"], column_sums(grad_two))
    grad_hidden = grad_low.astype(f32) + normalise_back(grad_two, vector(vec, "gain_two"), unit, scale)
    branch = grad_hidden.astype(bf16)
    g_out[...] += dot(mixed_in[...], branch, 0, 0)
    add_row(sums_at["b_out"], column_sums(branch))
    mixed_heads = by_head(dot(branch, w_out[...], 1, 1).astype(bf16).astype(f32)).astype(bf16)
    q_heads = by_head(q_in[...].astype(f32) * SCALE).astype(bf16)
    probs = probs_in[...]
    grad_probs = dot(mixed_heads, v_in[...], 1, 1)
    grad_v = dot(probs.astype(bf16), mixed_heads, 0, 0).astype(bf16)
    inner = jnp.sum(grad_probs * probs, -1, keepdims=True)
    grad_scores = (probs * (grad_probs - inner)).astype(bf16)
    grad_q = (from_heads(dot(grad_scores, k_in[...])) * SCALE).astype(bf16)
    grad_k = dot(grad_scores, q_heads, 0, 0).astype(bf16)
    unit, scale = normalise(x_in[...])
    normed = (unit * vector(vec, "gain_one") + vector(vec, "bias_one")).astype(bf16)
    g_q[...] += dot(normed, grad_q, 0, 0)
    g_k[...] += dot(normed, grad_k, 0, 0)
    g_v[...] += dot(normed, grad_v, 0, 0)
    add_row(sums_at["b_q"], column_sums(grad_q))
    add_row(sums_at["b_v"], column_sums(grad_v))
    grad_one = dot(grad_q, w_q[...], 1, 1) + dot(grad_k, w_k[...], 1, 1) + dot(grad_v, w_v[...], 1, 1)
    add_row(sums_at["gain_one"], column_sums(grad_one * unit))
    add_row(sums_at["bias_one"], column_sums(grad_one))
    grad_x = grad_hidden + normalise_back(grad_one, vector(vec, "gain_one"), unit, scale)
    g_pos[...] += grad_x
    grad_emb = grad_x[0:PATCHES].astype(bf16)
    g_patch[...] += dot(patches[...], grad_emb, 0, 0)
    add_row(9, column_sums(grad_emb))

    @pl.when(step == pl.num_programs(0) - 1)
    def _():
        at = BLOCK_AT
        flat = Flat(even, odd, mix, place.count * place.shard_rows)
        flat.clear()
        for part, ref in enumerate((g_q, g_k, g_v)):
            flat.write(ref[...], at["w_qkv"] + 3 * part, 9, D)
        flat.write(g_out[...], at["w_out"], 3, D)
        flat.write(g_up[...], at["w_up"], 12, FF)
        flat.write(g_down[...], at["w_down"], 3, D)
        flat.write(g_patch[...], W_PATCH, 3, D)
        names = {name: rows[row : row + 1, 0 : FF if name == "b_up" else D] for name, row in sums_at.items()}
        write_vectors(flat, names)
        flat.write(rows[9:10, 0:D], B_PATCH, 2, D)
        token = g_pos[CLS : CLS + 1, :]
        flat.write(token, CLS_TOKEN, 2, D)
        natural = jnp.concatenate([token, g_pos[0:PATCHES, :], jnp.zeros((1, D), f32)], 0)
        flat.write(natural, POS_EMBED, 3, D)
        send_out(place, info, flat, grad_out)


def fetch_kernel(first, last, _, basis, kept, sem):
    copy = pltpu.make_async_copy(basis.at[pl.ds(first, last - first)], kept, sem)
    copy.start()
    copy.wait()


def add_kernel(left, right, _, __, total):
    total[...] = left[...] + right[...]


def plane_kernel(depth, info, early, early_here, late, late_here, _, *refs):
    arrived, (whole_out, *outs) = refs[:-depth], refs[-depth:]
    for d in range(depth):
        first = early[d].astype(f32) + early_here[d].astype(f32)
        second = late[d].astype(f32) + late_here[d].astype(f32)
        total = jnp.where(info[0] == 0, first, second)
        for ref in arrived:
            total = total + ref[d].astype(f32)
        if d == 0:
            whole_out[...] = total
        else:
            outs[d - 1][...] = total.astype(bf16)


def inner_kernel(blocks, *refs):
    first, pieces, (upper, lower, loss, grad_out, sums_out, total) = refs[0], refs[1:-6], refs[-6:]
    shard_rows = grad_out.shape[0]
    value = first[...]
    for ref in pieces:
        value = value + ref[...].astype(f32)
    grad_out[...] = value[:shard_rows]
    total[...] = jnp.zeros(total.shape, f32)

    def step(i, carry):
        base = i * blocks
        rows = [jnp.broadcast_to(grad_out[pl.ds(base + j, 1), :], (8, LANES)) for j in range(blocks)]
        start = pl.multiple_of(base * LANES, LANES)
        for at in range(0, KB, 16):
            basis, row = (upper, at) if at < UPPER else (lower, at - UPPER)
            part = basis[row : row + 16, pl.ds(start, blocks * LANES)].astype(f32)
            for half in range(0, 16, 8):
                acc = total[at + half : at + half + 8, :]
                for j in range(blocks):
                    acc = acc + part[half : half + 8, j * LANES : (j + 1) * LANES] * rows[j]
                total[at + half : at + half + 8, :] = acc
        return carry

    lax.fori_loop(0, shard_rows // blocks, step, 0)
    coefs = jnp.sum(total[...].T, 0, keepdims=True)
    grad = grad_out[...]
    squares = jnp.sum(jnp.sum(grad * grad, 0, keepdims=True), 1, keepdims=True)
    lane = lax.broadcasted_iota(jnp.int32, (1, SUMS - KB), 1)
    rest = jnp.where(lane == 0, squares, 0.0)
    rest = rest + jnp.where(lane == 1, loss[0:1, 0:1], 0.0) + jnp.where(lane == 2, loss[0:1, 1:2], 0.0)
    sums_out[:, 0:KB] = coefs
    sums_out[:, KB:SUMS] = rest


def update_kernel(blocks, whole_len, counts, sums, upper, lower, grad, loss, master, first, second, *refs):
    loss_out, norm_out, coef_out, master_out, first_out, second_out, removed = refs
    norm = jnp.sqrt(sums[0:1, KB : KB + 1])
    factor = jnp.minimum(1.0, CLIP_NORM / (norm + 1e-06))
    lane = lax.broadcasted_iota(jnp.int32, (1, KB), 1)
    limit = jnp.where(lane < KMAX, counts[0], counts[1] + KMAX)
    row = jnp.where(lane < limit, sums[:, 0:KB] * factor, 0.0)
    coef_out[0:1, :] = row[:, 0:KMAX]
    coef_out[1:2, :] = row[:, KMAX:KB]
    norm_out[0] = jnp.sum(norm)
    loss_out[0] = jnp.sum(sums[0:1, KB + 1 : KB + 2])
    loss_out[1] = jnp.sum(sums[0:1, KB + 2 : KB + 3])
    loss_out[2] = jnp.sum(loss[0:1, 2:3])
    high = row.astype(bf16).astype(f32)
    mid = (row - high).astype(bf16).astype(f32)
    low = row - high - mid
    place = lax.broadcasted_iota(jnp.int32, (16, KB), 0)
    split = jnp.where(place == 0, high, jnp.where(place == 1, mid, jnp.where(place == 2, low, 0.0)))
    split = split.astype(bf16)
    rows = grad.shape[0]

    def step(i, carry):
        base = i * blocks
        start = pl.multiple_of(base * LANES, LANES)
        part = dot(split[:, :UPPER], upper[:, pl.ds(start, blocks * LANES)])
        part = part + dot(split[:, UPPER:], lower[:, pl.ds(start, blocks * LANES)])
        part = jnp.sum(part, 0, keepdims=True)
        for j in range(blocks):
            removed[pl.ds(base + j, 1), :] = part[:, j * LANES : (j + 1) * LANES]
        return carry

    lax.fori_loop(0, rows // blocks, step, 0)
    projected = grad[...] * factor - removed[0:rows, :] * (1.0 / whole_len)
    new_first = BETA_ONE * first[...] + (1.0 - BETA_ONE) * projected
    new_second = BETA_TWO * second[...] + (1.0 - BETA_TWO) * projected * projected
    ratio = (
        new_first
        / (1.0 - BETA_ONE**STEP)
        / (jnp.sqrt(new_second / (1.0 - BETA_TWO**STEP)) + ADAM_EPS)
    )
    old = master[...]
    master_out[...] = old - LEARN_RATE * (ratio + WEIGHT_DECAY * old)
    first_out[...] = new_first
    second_out[...] = new_second


def dp_dims(count):
    zed = 4 if count % 4 == 0 else 1
    plane = count // zed
    ex = max(side for side in range(1, math.isqrt(plane) + 1) if plane % side == 0)
    return zed, plane // ex, ex


def moved(value, place, turn=(0, 0, 0), core=0, sections=(0, 1)):
    pairs = []
    for section in sections:
        for zed in range(place.z):
            for why in range(place.y):
                for ex in range(place.x):
                    source = (section * place.z + zed) * place.y * place.x + why * place.x + ex
                    there = ((section + core) % 2) * place.z + (zed + turn[0]) % place.z
                    target = (there * place.y + (why + turn[1]) % place.y) * place.x
                    pairs.append((source, target + (ex + turn[2]) % place.x))
    return lax.ppermute(value, ("section", "dp"), pairs)


def add(left, right, resident):
    vmem = pl.BlockSpec(memory_space=pltpu.VMEM)
    return pl.pallas_call(
        add_kernel,
        in_specs=[vmem, vmem] + [pl.BlockSpec(memory_space=pl.ANY)] * 2,
        out_specs=vmem,
        out_shape=jax.ShapeDtypeStruct(left.shape, left.dtype),
        compiler_params=pltpu.CompilerParams(vmem_limit_bytes=2 * 1024 * 1024),
        name="add",
    )(left, right, *resident)


def butterfly(value, place, resident):
    value = add(value, moved(value, place, core=1), resident)
    for axis, size in ((2, place.x), (1, place.y), (0, place.z)):
        span = 1
        while span < size:
            pairs = []
            for index in range(2 * place.count):
                section, rest = divmod(index, place.count)
                at = [rest // (place.y * place.x), rest // place.x % place.y, rest % place.x]
                at[axis] ^= span
                pairs.append((index, section * place.count + (at[0] * place.y + at[1]) * place.x + at[2]))
            value = add(value, lax.ppermute(value, ("section", "dp"), pairs), resident)
            span *= 2
    return value


def whole(shape):
    return pl.BlockSpec(shape, lambda *_: (0,) * len(shape))


def params(megabytes):
    return pltpu.CompilerParams(
        vmem_limit_bytes=megabytes * 1024 * 1024, dimension_semantics=("arbitrary",)
    )


def body(
    patches, labels, replay, old_logits, basis_count, master, first_moment, second_moment, basis
):
    chips = lax.axis_size("dp")
    shard_len = master.shape[1]
    shard_rows = shard_len // LANES
    place = Place(dp_dims(chips), shard_rows)
    images = patches.shape[0]
    per = images // 2
    section = lax.axis_index("section")
    info = jnp.stack([section, lax.axis_index("dp")]).astype(jnp.int32)
    flat_rows = chips * shard_rows + SPARE
    turns = place.turns()

    shard = master[0].astype(bf16).reshape(shard_rows, LANES)
    count = jnp.sum(replay).astype(bf16)
    tail = jnp.full((place.sent_rows - shard_rows, LANES), count, bf16)
    shard = jnp.concatenate([shard, tail], 0)
    line = jnp.stack([shard] + [moved(shard, place, (d, 0, 0)) for d in range(1, place.z)])
    own = [moved(line, place, (0, a, b)) if a + b else line for a, b in turns]
    other = [moved(piece, place, core=1) for piece in own]

    flat_scratch = [
        pltpu.VMEM((flat_rows, LANES), f32),
        pltpu.VMEM((flat_rows, LANES), f32),
        pltpu.VMEM((FF + 32, LANES), f32),
    ]
    piece_specs = [whole(piece.shape) for piece in own + other]
    block_shapes = [(D, D)] * 4 + [(D, FF), (FF, D)]
    row_of = lambda i, *_: (i, 0)
    saved = [
        ((ROWS, D), f32),
        ((ROWS, D), bf16),
        ((ROWS, D), bf16),
        ((ROWS, D), bf16),
        ((HEADS * ROWS, ROWS), f32),
        ((ROWS, D), bf16),
        ((ROWS, D), f32),
        ((ROWS, FF), bf16),
        ((ROWS, FF), f32),
    ]
    middle_kind = ((ROWS, D), bf16)
    patch_spec = pl.BlockSpec((None, PATCHES, PDIM), lambda i, info: (info[0] * per + i, 0, 0))
    outs = pl.pallas_call(
        functools.partial(front_kernel, place),
        grid_spec=pltpu.PrefetchScalarGridSpec(
            num_scalar_prefetch=1,
            grid=(per,),
            in_specs=piece_specs + [patch_spec],
            out_specs=[pl.BlockSpec(shape, row_of) for shape, _ in saved + [middle_kind]]
            + [whole(shape) for shape in block_shapes]
            + [whole((VEC_ROWS, FF))],
            scratch_shapes=flat_scratch
            + [pltpu.VMEM((PDIM, D), bf16), pltpu.VMEM((ROWS, D), f32), pltpu.VMEM((ROWS, D), f32)],
        ),
        out_shape=[
            jax.ShapeDtypeStruct((per * shape[0], shape[1]), kind) for shape, kind in saved + [middle_kind]
        ]
        + [jax.ShapeDtypeStruct(shape, bf16) for shape in block_shapes]
        + [jax.ShapeDtypeStruct((VEC_ROWS, FF), f32)],
        compiler_params=params(40),
        name="front",
    )(info, *own, *other, patches)
    kept, middle, weights = outs[:9], outs[9], outs[10:]

    grad_shape = jax.ShapeDtypeStruct((chips, place.sent_rows, LANES), bf16)
    smem = pl.BlockSpec(memory_space=pltpu.SMEM)
    vmem = pl.BlockSpec(memory_space=pltpu.VMEM)
    eight = -(-per // 8) * 8
    back, late_grad, loss = pl.pallas_call(
        functools.partial(late_kernel, place, per, float(images * chips)),
        in_specs=[smem] * 3 + [vmem] * (2 * len(turns) + 2),
        out_specs=[vmem] * 3,
        out_shape=[
            jax.ShapeDtypeStruct((per * ROWS, D), bf16),
            grad_shape,
            jax.ShapeDtypeStruct((1, LANES), f32),
        ],
        scratch_shapes=flat_scratch
        + [pltpu.VMEM((8, 256, LANES), f32)]
        + [pltpu.VMEM(shape, bf16) for shape in block_shapes]
        + [
            pltpu.VMEM((VEC_ROWS, FF), f32),
            pltpu.VMEM((D, CPAD), bf16),
            pltpu.VMEM((1, CPAD), f32),
            pltpu.VMEM((eight, D), f32),
            pltpu.VMEM((per * ROWS, D), f32),
        ],
        compiler_params=pltpu.CompilerParams(vmem_limit_bytes=40 * 1024 * 1024),
        name="late",
    )(info, labels, replay, *own, *other, middle, old_logits)

    early_grad = pl.pallas_call(
        functools.partial(back_kernel, place),
        grid_spec=pltpu.PrefetchScalarGridSpec(
            num_scalar_prefetch=1,
            grid=(per,),
            in_specs=[pl.BlockSpec(shape, row_of) for shape, _ in [middle_kind] + saved]
            + [patch_spec]
            + [whole(shape) for shape in block_shapes]
            + [whole((VEC_ROWS, FF))],
            out_specs=whole(grad_shape.shape),
            scratch_shapes=flat_scratch
            + [pltpu.VMEM(shape, f32) for shape in block_shapes]
            + [
                pltpu.VMEM((PDIM, D), f32),
                pltpu.VMEM((ROWS, D), f32),
                pltpu.VMEM((VEC_ROWS, FF), f32),
            ],
        ),
        out_shape=grad_shape,
        compiler_params=params(48),
        name="back",
    )(info, back, *kept, patches, *weights)

    late_here = moved(late_grad, place, core=1, sections=(0,))
    early_here = moved(early_grad, place, core=1, sections=(1,))

    def paired(turn):
        cut = slice(turn * place.z, (turn + 1) * place.z)
        early = early_grad[cut].astype(f32) + early_here[cut].astype(f32)
        late = late_grad[cut].astype(f32) + late_here[cut].astype(f32)
        return jnp.where(section == 0, early, late)

    leaving = [paired(turn).astype(bf16) for turn in range(1, len(turns))]
    rows_basis = pltpu.with_memory_space_constraint(basis.reshape(KB, shard_len), pltpu.HBM)
    hbm = pl.BlockSpec(memory_space=pl.ANY)

    def fetch(first, last, after):
        return pl.pallas_call(
            functools.partial(fetch_kernel, first, last),
            in_specs=[hbm, pl.BlockSpec(memory_space=pltpu.HBM)],
            out_specs=hbm,
            out_shape=pltpu.VMEM((last - first, shard_len), bf16),
            scratch_shapes=[pltpu.SemaphoreType.DMA],
            compiler_params=pltpu.CompilerParams(vmem_limit_bytes=2 * 1024 * 1024),
            cost_estimate=pl.CostEstimate(
                flops=0, bytes_accessed=4 * (last - first) * shard_len, transcendentals=0
            ),
            name="fetch",
        )(after, rows_basis)

    upper = fetch(0, UPPER, leaving[0])
    arrived = [moved(leaving[turn - 1], place, (0, *turns[turn])) for turn in range(1, len(turns))]
    piece_shape = (place.sent_rows, LANES)
    first, *rest = pl.pallas_call(
        functools.partial(plane_kernel, place.z),
        in_specs=[smem] + [vmem] * 4 + [hbm] + [vmem] * (len(turns) - 1),
        out_specs=[vmem] * place.z,
        out_shape=[jax.ShapeDtypeStruct(piece_shape, bf16 if d else f32) for d in range(place.z)],
        compiler_params=pltpu.CompilerParams(vmem_limit_bytes=2 * 1024 * 1024),
        name="plane",
    )(info, early_grad, early_here, late_grad, late_here, upper, *arrived)
    resident = (upper, fetch(UPPER, KB, rest[0]))
    pieces = [moved(rest[d - 1], place, (d, 0, 0)) for d in range(1, place.z)]

    def divisor(most):
        return max(n for n in range(1, most + 1) if shard_rows % n == 0)

    flat_kind = jax.ShapeDtypeStruct((shard_rows, LANES), f32)
    grad, sums = pl.pallas_call(
        functools.partial(inner_kernel, divisor(26)),
        in_specs=[vmem] * (place.z + 3),
        out_specs=[vmem] * 2,
        out_shape=[flat_kind, jax.ShapeDtypeStruct((1, SUMS), f32)],
        scratch_shapes=[pltpu.VMEM((KB, LANES), f32)],
        compiler_params=pltpu.CompilerParams(vmem_limit_bytes=2 * 1024 * 1024),
        name="inner",
    )(first, *pieces, *resident, loss)
    sums = butterfly(sums, place, resident)
    padded_rows = -(-shard_rows // 8) * 8
    loss_parts, norm, coefficients, new_master, new_first, new_second = pl.pallas_call(
        functools.partial(update_kernel, divisor(78), float(2 * shard_len * chips)),
        in_specs=[smem] + [vmem] * 8,
        out_specs=[smem, smem] + [vmem] * 4,
        out_shape=[
            jax.ShapeDtypeStruct((3,), f32),
            jax.ShapeDtypeStruct((1,), f32),
            jax.ShapeDtypeStruct((TASKS, KMAX), f32),
        ]
        + [flat_kind] * 3,
        scratch_shapes=[pltpu.VMEM((padded_rows, LANES), f32)],
        compiler_params=pltpu.CompilerParams(vmem_limit_bytes=2 * 1024 * 1024),
        name="update",
    )(
        basis_count,
        sums,
        *resident,
        grad,
        loss,
        master.reshape(shard_rows, LANES),
        first_moment.reshape(shard_rows, LANES),
        second_moment.reshape(shard_rows, LANES),
    )
    return (
        loss_parts,
        norm[0],
        coefficients,
        new_master.reshape(1, shard_len),
        new_first.reshape(1, shard_len),
        new_second.reshape(1, shard_len),
    )


def solution(mesh):
    in_specs = (
        P("dp", None, None),
        P("dp"),
        P("dp"),
        P("dp", None),
        P(),
        P("section", "dp"),
        P("section", "dp"),
        P("section", "dp"),
        P(None, "section", "dp"),
    )
    out_specs = (P(), P(), P(), P("section", "dp"), P("section", "dp"), P("section", "dp"))
    return jax.shard_map(body, mesh=mesh, in_specs=in_specs, out_specs=out_specs, check_vma=False)
```

```python
import functools
import math

import jax
import jax.numpy as jnp
from jax import lax
from jax.experimental import pallas as pl
from jax.experimental.pallas import tpu as pltpu
from jax.sharding import PartitionSpec as P

HEADS = 3
HD = 64
D = 192
FF = 768
PDIM = 768
PATCHES = 196
TOKENS = PATCHES + 1
ROWS = 208
CLS = PATCHES
GROUP = 2
CLASSES = 1000
CPAD = 1024
TASKS = 2
KMAX = 200
KB = TASKS * KMAX
UPPER = 208
STEP = 10
LANES = 128
HALF = 64
SPARE = 512
SUMS = 512

NORM_EPS = 1e-06
CLIP_NORM = 0.02
LEARN_RATE = 0.05
BETA_ONE = 0.9
BETA_TWO = 0.999
ADAM_EPS = 1e-08
WEIGHT_DECAY = 0.05
SCALE = HD ** (-0.5)
MASKED = -1e30

BLOCK_AT = dict(
    gain_one=0,
    bias_one=3,
    w_qkv=6,
    b_qkv=1734,
    w_out=1740,
    b_out=2316,
    gain_two=2319,
    bias_two=2322,
    w_up=2325,
    b_up=4629,
    w_down=4641,
    b_down=6945,
)
W_PATCH, B_PATCH, CLS_TOKEN, POS_EMBED = 6948, 9252, 9255, 9258
GAIN_LAST, BIAS_LAST, W_HEAD, B_HEAD = 6948, 6951, 6954, 9954
VECTORS = ("gain_one", "bias_one", "b_q", "b_v", "b_out", "gain_two", "bias_two", "b_up", "b_down")
VEC_ROWS = 16

f32 = jnp.float32
bf16 = jnp.bfloat16


def dot(left, right, left_dim=1, right_dim=0):
    return lax.dot_general(
        left, right, (((left_dim,), (right_dim,)), ((), ())), preferred_element_type=f32
    )


def low_lanes(shape):
    return lax.broadcasted_iota(jnp.int32, shape, 1) < HALF


def swap_halves(value):
    return pltpu.roll(value, HALF, 1)


def head_masks():
    lane = lax.broadcasted_iota(jnp.int32, (1, D), 1)
    return [jnp.logical_and(lane >= h * HD, lane < (h + 1) * HD) for h in range(HEADS)]


def by_head(value):
    return jnp.concatenate([jnp.where(m, value, 0.0) for m in head_masks()], 0)


def from_heads(value):
    rows = value.shape[0] // HEADS
    parts = [value[h * rows : (h + 1) * rows] for h in range(HEADS)]
    masks = head_masks()
    return jnp.where(masks[0], parts[0], jnp.where(masks[1], parts[1], parts[2]))


def normalise(rows_in):
    mean = jnp.sum(rows_in, -1, keepdims=True) * (1.0 / D)
    centred = rows_in - mean
    variance = jnp.sum(centred * centred, -1, keepdims=True) * (1.0 / D)
    scale = lax.rsqrt(variance + NORM_EPS)
    return centred * scale, scale


def normalise_back(grad, gain, unit, scale):
    grad_unit = grad * gain
    first = jnp.sum(grad_unit, -1, keepdims=True) * (1.0 / D)
    second = jnp.sum(grad_unit * unit, -1, keepdims=True) * (1.0 / D)
    return scale * (grad_unit - first - unit * second)


def gelu_parts(pre):
    cdf = 0.5 * (1.0 + lax.erf(pre * math.sqrt(0.5)))
    slope = cdf + pre * (jnp.exp(-0.5 * pre * pre) * (1.0 / math.sqrt(2.0 * math.pi)))
    return pre * cdf, slope


def column_sums(value):
    return jnp.sum(value.astype(f32), 0, keepdims=True)


def strided(ref, start, count, stride):
    if count == 1 or stride == 1:
        return ref[pl.ds(start, count), :]
    return ref[pl.ds(start, count, stride=stride), :]


class Flat:
    def __init__(self, even, odd, mix, rows):
        self.even, self.odd, self.mix, self.rows = even, odd, mix, rows

    def shift(self):
        step = 192
        for at in range(0, self.rows, step):
            here = self.even[at : at + step, :]
            after = self.even[at + 1 : at + 1 + step, :]
            self.odd[at : at + step, :] = swap_halves(jnp.where(low_lanes(here.shape), after, here))

    def rows_at(self, half, count, stride):
        return strided(self.odd if half % 2 else self.even, half // 2, count, stride)

    def blocks(self, half, width, rows, cols):
        for at in range(0, cols, LANES):
            start = half + at // HALF
            if rows == 1 or width % 2 == 0:
                value = self.rows_at(start, rows, width // 2)
            else:
                pairs = (rows + 1) // 2
                self.mix[pl.ds(0, pairs, stride=2), :] = self.rows_at(start, pairs, width)
                self.mix[pl.ds(1, pairs, stride=2), :] = self.rows_at(start + width, pairs, width)
                value = self.mix[0:rows, :]
            yield at, min(LANES, cols - at), value

    def read(self, dest, half, width, rows, cols):
        for at, wide, value in self.blocks(half, width, rows, cols):
            dest[0:rows, at : at + wide] = value[:, :wide].astype(dest.dtype)

    def read_row(self, dest, row, half, cols):
        for at, wide, value in self.blocks(half, 2, 1, cols):
            dest[row : row + 1, at : at + wide] = value[:, :wide]

    def clear(self):
        self.even[...] = jnp.zeros(self.even.shape, f32)
        self.odd[...] = jnp.zeros(self.odd.shape, f32)

    def put_rows(self, half, count, stride, value):
        ref, start = (self.odd, half // 2 + 8) if half % 2 else (self.even, half // 2)
        if count == 1 or stride == 1:
            ref[pl.ds(start, count), :] = value
        else:
            ref[pl.ds(start, count, stride=stride), :] = value

    def write(self, value, half, width, cols):
        rows = value.shape[0]
        for at in range(0, cols, LANES):
            wide = min(LANES, cols - at)
            part = value[:, at : at + wide]
            if wide < LANES:
                part = jnp.concatenate([part, jnp.zeros((rows, LANES - wide), f32)], 1)
            start = half + at // HALF
            if rows == 1 or width % 2 == 0:
                self.put_rows(start, rows, width // 2, part)
            else:
                pairs = (rows + 1) // 2
                self.mix[0:rows, :] = part
                self.put_rows(start, pairs, width, self.mix[pl.ds(0, pairs, stride=2), :])
                self.put_rows(start + width, pairs, width, self.mix[pl.ds(1, pairs, stride=2), :])

    def merged(self, at, count):
        here = self.odd[at + 8 : at + 8 + count, :]
        before = self.odd[at + 7 : at + 7 + count, :]
        moved_back = swap_halves(jnp.where(low_lanes(here.shape), here, before))
        return self.even[at : at + count, :] + moved_back


class Place:
    def __init__(self, dims, shard_rows):
        self.z, self.y, self.x = dims
        self.count = self.z * self.y * self.x
        self.shard_rows = shard_rows
        self.sent_rows = -(-(shard_rows + 1) // 16) * 16
        self.first_rows = self.sent_rows * 13 // 20 // 16 * 16

    def split(self, index):
        plane = self.y * self.x
        return index // plane, lax.rem(index, plane) // self.x, lax.rem(index, self.x)

    def turns(self):
        return [(a, b) for a in range(self.y) for b in range(self.x)]


def load_section(place, pieces, wanted, flat):
    own, other = pieces
    section = lax.axis_index("section")
    zed, why, ex = place.split(lax.axis_index("dp"))
    rows = place.shard_rows

    def copy(refs):
        for turn, (a, b) in enumerate(place.turns()):
            for d in range(place.z):
                shard = lax.rem(zed + (place.z - d), place.z) * (place.y * place.x)
                shard = shard + lax.rem(why + (place.y - a), place.y) * place.x
                shard = shard + lax.rem(ex + (place.x - b), place.x)
                start = shard * rows
                if rows % 8 == 0:
                    start = pl.multiple_of(start, 8)
                cut = place.first_rows
                flat.even[pl.ds(start, cut), :] = refs[turn][d].astype(f32)
                value = refs[len(place.turns()) + d][turn].astype(f32)
                after = start + cut
                if rows % 8 == 0:
                    after = pl.multiple_of(after, 8)
                flat.even[pl.ds(after, rows - cut), :] = value[: rows - cut]

    @pl.when(section == wanted)
    def _():
        copy(own)

    @pl.when(section != wanted)
    def _():
        copy(other)

    flat.shift()


def read_block(flat, weights, vec):
    at = BLOCK_AT
    w_q, w_k, w_v, w_out, w_up, w_down = weights
    for place, dest in enumerate((w_q, w_k, w_v)):
        flat.read(dest, at["w_qkv"] + 3 * place, 9, D, D)
    flat.read(w_out, at["w_out"], 3, D, D)
    flat.read(w_up, at["w_up"], 12, D, FF)
    flat.read(w_down, at["w_down"], 3, FF, D)
    starts = dict(at, b_q=at["b_qkv"], b_v=at["b_qkv"] + 3)
    for row, name in enumerate(VECTORS):
        flat.read_row(vec, row, starts[name], FF if name == "b_up" else D)


def vector(vec, name):
    row = VECTORS.index(name)
    return vec[row : row + 1, 0 : FF if name == "b_up" else D]


def write_vectors(flat, sums):
    at = BLOCK_AT
    starts = dict(at, b_q=at["b_qkv"], b_v=at["b_qkv"] + 3)
    for name, value in sums.items():
        flat.write(value, starts[name], 2, value.shape[1])


def send_out(place, flat, write):
    zed, why, ex = place.split(lax.axis_index("dp"))
    rows, spare = place.shard_rows, place.sent_rows - place.shard_rows
    for shard in range(place.count):
        zk, yk, xk = shard // (place.y * place.x), shard // place.x % place.y, shard % place.x
        d = lax.rem(zk + place.z - zed, place.z)
        a = lax.rem(yk + place.y - why, place.y)
        b = lax.rem(xk + place.x - ex, place.x)
        value = flat.merged(shard * rows, rows)
        value = jnp.concatenate([value, jnp.zeros((spare, LANES), f32)], 0)
        write((a * place.x + b) * place.z + d, value.astype(bf16))


def shard_kernel(replay, master, out):
    rows = master.shape[0]
    count = sum(replay[i].astype(f32) for i in range(replay.shape[0]))
    tail = jnp.full((out.shape[0] - rows, LANES), count, f32)
    out[...] = jnp.concatenate([master[...], tail], 0).astype(bf16)


def front_kernel(place, *refs):
    section = lax.axis_index("section")
    parts = len(place.turns()) + place.z
    own, other, refs = refs[:parts], refs[parts : 2 * parts], refs[2 * parts :]
    patches, refs = refs[0], refs[1:]
    (x_out, q_out, k_out, v_out, probs_out, mixed_out, hidden_out, act_out, slope_out, middle_out) = refs[:10]
    w_q, w_k, w_v, w_out, w_up, w_down, vec = refs[10:17]
    even, odd, mix, w_patch, added, tokens = refs[17:]
    flat = Flat(even, odd, mix, place.count * place.shard_rows)

    @pl.when(pl.program_id(0) == 0)
    def _():
        load_section(place, (own, other), 0, flat)
        read_block(flat, (w_q, w_k, w_v, w_out, w_up, w_down), vec)
        flat.read(w_patch, W_PATCH, 3, PDIM, D)
        flat.read_row(vec, 9, B_PATCH, D)
        flat.read_row(vec, 10, CLS_TOKEN, D)
        added[...] = jnp.zeros(added.shape, f32)
        tokens[...] = jnp.zeros(tokens.shape, f32)
        for at, wide, value in flat.blocks(POS_EMBED, 3, TOKENS + 1, D):
            bias = vec[9:10, at : at + wide]
            token = vec[10:11, at : at + wide]
            for top in range(0, added.shape[0], ROWS):
                added[top : top + PATCHES, at : at + wide] = value[1:TOKENS, :wide] + bias
                added[top + CLS : top + CLS + 1, at : at + wide] = value[0:1, :wide] + token

    group = patches.shape[0]
    spans = [slice(i * ROWS, (i + 1) * ROWS) for i in range(group)]
    for i in range(group):
        tokens[i * ROWS : i * ROWS + PATCHES, :] = dot(patches[i], w_patch[...])
    x = tokens[...] + added[...]
    x_out[...] = x
    unit, _ = normalise(x)
    normed = (unit * vector(vec, "gain_one") + vector(vec, "bias_one")).astype(bf16)
    q = (dot(normed, w_q[...]) + vector(vec, "b_q")).astype(bf16)
    k = dot(normed, w_k[...]).astype(bf16)
    v = (dot(normed, w_v[...]) + vector(vec, "b_v")).astype(bf16)
    q_out[...], k_out[...], v_out[...] = q, k, v
    q_scaled = q.astype(f32) * SCALE
    column = lax.broadcasted_iota(jnp.int32, (1, ROWS), 1)
    scores = [dot(by_head(q_scaled[at]).astype(bf16), k[at], 1, 1) for at in spans]
    scores = [jnp.where(column < TOKENS, value, MASKED) for value in scores]
    raised = [jnp.exp(value - jnp.max(value, -1, keepdims=True)) for value in scores]
    probs = [value * (1.0 / jnp.sum(value, -1, keepdims=True)) for value in raised]
    for i, value in enumerate(probs):
        probs_out[i * HEADS * ROWS : (i + 1) * HEADS * ROWS, :] = value
    mixed = [from_heads(dot(value.astype(bf16), v[at])) for value, at in zip(probs, spans)]
    mixed = jnp.concatenate(mixed, 0).astype(bf16)
    mixed_out[...] = mixed
    hidden = x + dot(mixed, w_out[...]) + vector(vec, "b_out")
    hidden_out[...] = hidden
    unit, _ = normalise(hidden)
    normed = (unit * vector(vec, "gain_two") + vector(vec, "bias_two")).astype(bf16)
    pre = dot(normed, w_up[...]) + vector(vec, "b_up")
    act, slope = gelu_parts(pre)
    act = act.astype(bf16)
    act_out[...], slope_out[...] = act, slope
    middle = hidden + dot(act, w_down[...]) + vector(vec, "b_down")
    middle_out[...] = middle.astype(bf16)


def read_head(flat, wide, w_head, b_head):
    first = W_HEAD // 2
    lane = lax.broadcasted_iota(jnp.int32, (16, LANES), 1)
    for phase in range(16):
        start, off = first + CLASSES * phase // LANES, CLASSES * phase % LANES
        got = [strided(flat.even, start + j, 16, 125) for j in range(9 if off else 8)]
        if off:
            got = [pltpu.roll(g, LANES - off, 1) for g in got]
        for j in range(8):
            value = jnp.where(lane < LANES - off, got[j], got[j + 1]) if off else got[j]
            wide[j, pl.ds(phase, 16, stride=16), :] = value
    lane = lax.broadcasted_iota(jnp.int32, (1, LANES), 1)
    for j in range(8):
        keep = lane + j * LANES < CLASSES
        w_head[:, j * LANES : (j + 1) * LANES] = jnp.where(keep, wide[j, 0:D, :], 0.0).astype(bf16)
        value = flat.even[B_HEAD // 2 + j : B_HEAD // 2 + j + 1, :]
        b_head[0:1, j * LANES : (j + 1) * LANES] = jnp.where(keep, value, 0.0)


def write_head(flat, wide, grad_w, grad_b):
    first = W_HEAD // 2
    for j in range(8):
        wide[j, 0:D, :] = grad_w[:, j * LANES : (j + 1) * LANES]
        wide[j, D:, :] = jnp.zeros((wide.shape[1] - D, LANES), f32)
    lane = lax.broadcasted_iota(jnp.int32, (16, LANES), 1)
    for phase in range(16):
        start, off = first + CLASSES * phase // LANES, CLASSES * phase % LANES
        got = [wide[j, pl.ds(phase, 16, stride=16), :] for j in range(8)]
        if off:
            got = [pltpu.roll(g, off, 1) for g in got]
        for j in range(9 if off else 8):
            if not off:
                value = got[j]
            else:
                before = got[j - 1] if j else jnp.zeros((16, LANES), f32)
                value = jnp.where(lane < off, before, got[j] if j < 8 else 0.0)
            flat.even[pl.ds(start + j, 16, stride=125), :] += value
    for j in range(8):
        row = B_HEAD // 2 + j
        flat.even[row : row + 1, :] += grad_b[:, j * LANES : (j + 1) * LANES]


def late_kernel(place, per, image_total, labels, replay, *refs):
    section = lax.axis_index("section")
    parts = len(place.turns()) + place.z
    own, other, refs = refs[:parts], refs[parts : 2 * parts], refs[2 * parts :]
    middle, old_logits, back_out, grad_out, loss_out = refs[:5]
    even, odd, mix, wide, w_q, w_k, w_v, w_out, w_up, w_down, vec, w_head, b_head, few, many = refs[5:]
    flat = Flat(even, odd, mix, place.count * place.shard_rows)
    load_section(place, (own, other), 1, flat)
    read_block(flat, (w_q, w_k, w_v, w_out, w_up, w_down), vec)
    flat.read_row(vec, 9, GAIN_LAST, D)
    flat.read_row(vec, 10, BIAS_LAST, D)
    read_head(flat, wide, w_head, b_head)
    gain_last, bias_last = vec[9:10, 0:D], vec[10:11, 0:D]
    carried = jnp.zeros((1, LANES), f32)
    carrier = place.shard_rows - place.first_rows
    for ref in own[len(place.turns()) :]:
        for turn in range(len(place.turns())):
            carried = carried + ref[turn].astype(f32)[carrier : carrier + 1]
    replay_count = carried[:, 0:1]

    x = middle[...].astype(f32)
    unit, scale = normalise(x)
    normed_f = unit * vector(vec, "gain_one") + vector(vec, "bias_one")
    normed = normed_f.astype(bf16)
    k = dot(normed, w_k[...]).astype(bf16)
    v = (dot(normed, w_v[...]) + vector(vec, "b_v")).astype(bf16)

    def class_rows(value):
        few[...] = jnp.zeros(few.shape, f32)
        for i in range(per):
            few[i : i + 1, :] = value[i * ROWS + CLS : i * ROWS + CLS + 1, :]
        return few[...]

    eight = few.shape[0]
    image = lax.broadcasted_iota(jnp.int32, (eight, 1), 0)
    real = image < per
    x_top = class_rows(x)
    top_normed = class_rows(normed_f).astype(bf16)
    q = (dot(top_normed, w_q[...]) + vector(vec, "b_q")).astype(bf16)
    q_heads = by_head(jnp.where(real, q.astype(f32) * SCALE, 0.0)).astype(bf16)
    scores = dot(q_heads, k, 1, 1)
    column = lax.broadcasted_iota(jnp.int32, scores.shape, 1)
    owner = lax.rem(lax.broadcasted_iota(jnp.int32, scores.shape, 0), eight) * ROWS
    inside = jnp.logical_and(column >= owner, column < owner + TOKENS)
    scores = jnp.where(inside, scores, MASKED)
    raised = jnp.where(inside, jnp.exp(scores - jnp.max(scores, -1, keepdims=True)), 0.0)
    total = jnp.sum(raised, -1, keepdims=True)
    probs = raised * (1.0 / jnp.where(total > 0.0, total, 1.0))
    probs_low = probs.astype(bf16)
    mixed = from_heads(dot(probs_low, v)).astype(bf16)
    hidden = x_top + dot(mixed, w_out[...]) + vector(vec, "b_out")
    unit_two, scale_two = normalise(hidden)
    normed_two = (unit_two * vector(vec, "gain_two") + vector(vec, "bias_two")).astype(bf16)
    act, slope = gelu_parts(dot(normed_two, w_up[...]) + vector(vec, "b_up"))
    act = act.astype(bf16)
    final = hidden + dot(act, w_down[...]) + vector(vec, "b_down")

    unit_last, scale_last = normalise(final)
    top = (unit_last * gain_last + bias_last).astype(bf16)
    classes = lax.broadcasted_iota(jnp.int32, (eight, CPAD), 1)
    logits = dot(top, w_head[...]) + b_head[...]
    logits = jnp.where(classes < CLASSES, logits, MASKED)
    highest = jnp.max(logits, -1, keepdims=True)
    log_total = highest + jnp.log(jnp.sum(jnp.exp(logits - highest), -1, keepdims=True))
    label = jnp.zeros((eight, 1), jnp.int32)
    again = jnp.zeros((eight, 1), f32)
    for i in range(per):
        label = jnp.where(image == i, labels[section * per + i], label)
        again = jnp.where(image == i, replay[section * per + i].astype(f32), again)
    picked = jnp.logical_and(classes == label, real)
    entropy = jnp.where(real, log_total, 0.0) - jnp.sum(jnp.where(picked, logits, 0.0), -1, keepdims=True)
    wanted = jnp.where(section == 0, old_logits[0:per, :], old_logits[per : 2 * per, :])
    if per < eight:
        wanted = jnp.concatenate([wanted, jnp.zeros((eight - per, CLASSES), f32)], 0)
    wanted = jnp.concatenate([wanted, jnp.zeros((eight, CPAD - CLASSES), f32)], 1)
    distance = jnp.where(jnp.logical_and(classes < CLASSES, real), logits - wanted, 0.0)
    squares = again * (jnp.sum(distance * distance, -1, keepdims=True) * (1.0 / CLASSES))
    lane = lax.broadcasted_iota(jnp.int32, (1, LANES), 1)
    entropy_sum = jnp.sum(entropy, 0, keepdims=True)
    replay_sum = jnp.sum(squares, 0, keepdims=True)
    loss_out[...] = jnp.where(lane == 0, entropy_sum, jnp.where(lane == 1, replay_sum, replay_count))

    grad = (jnp.exp(logits - log_total) - jnp.where(picked, 1.0, 0.0)) * (1.0 / image_total)
    grad = grad + again * 2.0 * distance / (CLASSES * replay_count)
    grad = jnp.where(jnp.logical_and(classes < CLASSES, real), grad, 0.0)
    grad_low = grad.astype(bf16)
    flat.clear()
    write_head(flat, wide, dot(top, grad_low, 0, 0), column_sums(grad_low))
    sums = {}
    grad = dot(grad_low, w_head[...], 1, 1)
    flat.write(column_sums(grad * unit_last), GAIN_LAST, 2, D)
    flat.write(column_sums(grad), BIAS_LAST, 2, D)
    grad = normalise_back(grad, gain_last, unit_last, scale_last)

    at = BLOCK_AT
    grad_down = grad.astype(bf16)
    flat.write(dot(act, grad_down, 0, 0), at["w_down"], 3, D)
    sums["b_down"] = column_sums(grad_down)
    grad_up = (dot(grad_down, w_down[...], 1, 1) * slope).astype(bf16)
    flat.write(dot(normed_two, grad_up, 0, 0), at["w_up"], 12, FF)
    sums["b_up"] = column_sums(grad_up)
    grad_two = dot(grad_up, w_up[...], 1, 1)
    sums["gain_two"], sums["bias_two"] = column_sums(grad_two * unit_two), column_sums(grad_two)
    grad_hidden = grad + normalise_back(grad_two, vector(vec, "gain_two"), unit_two, scale_two)
    branch = grad_hidden.astype(bf16)
    flat.write(dot(mixed, branch, 0, 0), at["w_out"], 3, D)
    sums["b_out"] = column_sums(branch)
    mixed_heads = by_head(dot(branch, w_out[...], 1, 1).astype(bf16).astype(f32)).astype(bf16)
    grad_probs = dot(mixed_heads, v, 1, 1)
    grad_v = dot(probs_low, mixed_heads, 0, 0).astype(bf16)
    inner = jnp.sum(grad_probs * probs, -1, keepdims=True)
    grad_scores = (probs * (grad_probs - inner)).astype(bf16)
    grad_q = (from_heads(dot(grad_scores, k)) * SCALE).astype(bf16)
    grad_k = dot(grad_scores, q_heads, 0, 0).astype(bf16)
    flat.write(dot(top_normed, grad_q, 0, 0), at["w_qkv"], 9, D)
    flat.write(dot(normed, grad_k, 0, 0), at["w_qkv"] + 3, 9, D)
    flat.write(dot(normed, grad_v, 0, 0), at["w_qkv"] + 6, 9, D)
    sums["b_q"], sums["b_v"] = column_sums(grad_q), column_sums(grad_v)
    many[...] = dot(grad_k, w_k[...], 1, 1) + dot(grad_v, w_v[...], 1, 1)
    top_back = dot(grad_q, w_q[...], 1, 1)
    for i in range(per):
        many[i * ROWS + CLS : i * ROWS + CLS + 1, :] += top_back[i : i + 1, :]
    grad_one = many[...]
    sums["gain_one"], sums["bias_one"] = column_sums(grad_one * unit), column_sums(grad_one)
    many[...] = normalise_back(grad_one, vector(vec, "gain_one"), unit, scale)
    for i in range(per):
        many[i * ROWS + CLS : i * ROWS + CLS + 1, :] += grad_hidden[i : i + 1, :]
    back_out[...] = many[...].astype(bf16)
    write_vectors(flat, sums)

    def store(at, value):
        grad_out[at] = value

    send_out(place, flat, store)


def back_kernel(place, *refs):
    (grad_in, x_in, q_in, k_in, v_in, probs_in, mixed_in, hidden_in, act_in, slope_in, patches) = refs[:11]
    w_q, w_k, w_v, w_out, w_up, w_down, vec, late_grad, keep_out, give_out = refs[11:21]
    even, odd, mix, g_q, g_k, g_v, g_out, g_up, g_down, g_patch, g_pos, rows = refs[21:]
    step = pl.program_id(0)
    sums_at = {name: row for row, name in enumerate(VECTORS)}

    @pl.when(step == 0)
    def _():
        for ref in (g_q, g_k, g_v, g_out, g_up, g_down, g_patch, g_pos, rows):
            ref[...] = jnp.zeros(ref.shape, f32)

    def add_row(row, value):
        rows[row : row + 1, 0 : value.shape[1]] += value

    grad_low = grad_in[...]
    g_down[...] += dot(act_in[...], grad_low, 0, 0)
    add_row(sums_at["b_down"], column_sums(grad_low))
    grad_up = (dot(grad_low, w_down[...], 1, 1) * slope_in[...]).astype(bf16)
    unit, scale = normalise(hidden_in[...])
    normed = (unit * vector(vec, "gain_two") + vector(vec, "bias_two")).astype(bf16)
    g_up[...] += dot(normed, grad_up, 0, 0)
    add_row(sums_at["b_up"], column_sums(grad_up))
    grad_two = dot(grad_up, w_up[...], 1, 1)
    add_row(sums_at["gain_two"], column_sums(grad_two * unit))
    add_row(sums_at["bias_two"], column_sums(grad_two))
    grad_hidden = grad_low.astype(f32) + normalise_back(grad_two, vector(vec, "gain_two"), unit, scale)
    branch = grad_hidden.astype(bf16)
    g_out[...] += dot(mixed_in[...], branch, 0, 0)
    add_row(sums_at["b_out"], column_sums(branch))
    group = patches.shape[0]
    spans = [slice(i * ROWS, (i + 1) * ROWS) for i in range(group)]
    grad_mixed = dot(branch, w_out[...], 1, 1).astype(bf16).astype(f32)
    mixed_heads = [by_head(grad_mixed[at]).astype(bf16) for at in spans]
    q_scaled = q_in[...].astype(f32) * SCALE
    q_heads = [by_head(q_scaled[at]).astype(bf16) for at in spans]
    probs = [probs_in[i * HEADS * ROWS : (i + 1) * HEADS * ROWS, :] for i in range(group)]
    grad_probs = [dot(value, v_in[at, :], 1, 1) for value, at in zip(mixed_heads, spans)]
    grad_v = [dot(value.astype(bf16), right, 0, 0) for value, right in zip(probs, mixed_heads)]
    inner = [jnp.sum(one * two, -1, keepdims=True) for one, two in zip(grad_probs, probs)]
    grad_scores = [(two * (one - less)).astype(bf16) for one, two, less in zip(grad_probs, probs, inner)]
    grad_q = [from_heads(dot(value, k_in[at, :])) * SCALE for value, at in zip(grad_scores, spans)]
    grad_k = [dot(value, right, 0, 0) for value, right in zip(grad_scores, q_heads)]
    grad_q, grad_k, grad_v = [jnp.concatenate(value, 0).astype(bf16) for value in (grad_q, grad_k, grad_v)]
    unit, scale = normalise(x_in[...])
    normed = (unit * vector(vec, "gain_one") + vector(vec, "bias_one")).astype(bf16)
    g_q[...] += dot(normed, grad_q, 0, 0)
    g_k[...] += dot(normed, grad_k, 0, 0)
    g_v[...] += dot(normed, grad_v, 0, 0)
    add_row(sums_at["b_q"], column_sums(grad_q))
    add_row(sums_at["b_v"], column_sums(grad_v))
    grad_one = dot(grad_q, w_q[...], 1, 1) + dot(grad_k, w_k[...], 1, 1) + dot(grad_v, w_v[...], 1, 1)
    add_row(sums_at["gain_one"], column_sums(grad_one * unit))
    add_row(sums_at["bias_one"], column_sums(grad_one))
    grad_x = grad_hidden + normalise_back(grad_one, vector(vec, "gain_one"), unit, scale)
    grad_emb = [grad_x[at.start : at.start + PATCHES].astype(bf16) for at in spans]
    for i, at in enumerate(spans):
        g_pos[...] += grad_x[at]
        g_patch[...] += dot(patches[i], grad_emb[i], 0, 0)
        add_row(9, column_sums(grad_emb[i]))

    @pl.when(step == pl.num_programs(0) - 1)
    def _():
        at = BLOCK_AT
        flat = Flat(even, odd, mix, place.count * place.shard_rows)
        flat.clear()
        for part, ref in enumerate((g_q, g_k, g_v)):
            flat.write(ref[...], at["w_qkv"] + 3 * part, 9, D)
        flat.write(g_out[...], at["w_out"], 3, D)
        flat.write(g_up[...], at["w_up"], 12, FF)
        flat.write(g_down[...], at["w_down"], 3, D)
        flat.write(g_patch[...], W_PATCH, 3, D)
        names = {name: rows[row : row + 1, 0 : FF if name == "b_up" else D] for name, row in sums_at.items()}
        write_vectors(flat, names)
        flat.write(rows[9:10, 0:D], B_PATCH, 2, D)
        token = g_pos[CLS : CLS + 1, :]
        flat.write(token, CLS_TOKEN, 2, D)
        natural = jnp.concatenate([token, g_pos[0:PATCHES, :], jnp.zeros((1, D), f32)], 0)
        flat.write(natural, POS_EMBED, 3, D)

        section = lax.axis_index("section")

        @pl.when(section == 0)
        def _():
            def store(at, value):
                keep_out[at] = value
                give_out[at] = late_grad[at]

            send_out(place, flat, store)

        @pl.when(section != 0)
        def _():
            def store(at, value):
                give_out[at] = value
                keep_out[at] = late_grad[at]

            send_out(place, flat, store)


def fetch_kernel(first, last, _, basis, kept, sem):
    copy = pltpu.make_async_copy(basis.at[pl.ds(first, last - first)], kept, sem)
    copy.start()
    copy.wait()


def add_kernel(left, right, _, __, total):
    total[...] = left[...] + right[...]


def plane_kernel(depth, own, _, *refs):
    arrived, (whole_out, *outs) = refs[:-depth], refs[-depth:]
    for d in range(depth):
        total = own[d]
        for ref in arrived:
            total = total + ref[d].astype(f32)
        if d == 0:
            whole_out[...] = total
        else:
            outs[d - 1][...] = total.astype(bf16)


def inner_kernel(blocks, *refs):
    first, pieces, (upper, lower, loss, grad_out, sums_out, total) = refs[0], refs[1:-6], refs[-6:]
    shard_rows = grad_out.shape[0]
    value = first[...]
    for ref in pieces:
        value = value + ref[...].astype(f32)
    grad_out[...] = value[:shard_rows]
    total[...] = jnp.zeros(total.shape, f32)

    def step(i, carry):
        base = i * blocks
        rows = [jnp.broadcast_to(grad_out[pl.ds(base + j, 1), :], (8, LANES)) for j in range(blocks)]
        start = pl.multiple_of(base * LANES, LANES)
        for at in range(0, KB, 16):
            basis, row = (upper, at) if at < UPPER else (lower, at - UPPER)
            part = basis[row : row + 16, pl.ds(start, blocks * LANES)].astype(f32)
            for half in range(0, 16, 8):
                acc = total[at + half : at + half + 8, :]
                for j in range(blocks):
                    acc = acc + part[half : half + 8, j * LANES : (j + 1) * LANES] * rows[j]
                total[at + half : at + half + 8, :] = acc
        return carry

    lax.fori_loop(0, shard_rows // blocks, step, 0)
    coefs = jnp.sum(total[...].T, 0, keepdims=True)
    grad = grad_out[...]
    squares = jnp.sum(jnp.sum(grad * grad, 0, keepdims=True), 1, keepdims=True)
    lane = lax.broadcasted_iota(jnp.int32, (1, SUMS - KB), 1)
    rest = jnp.where(lane == 0, squares, 0.0)
    rest = rest + jnp.where(lane == 1, loss[0:1, 0:1], 0.0) + jnp.where(lane == 2, loss[0:1, 1:2], 0.0)
    sums_out[:, 0:KB] = coefs
    sums_out[:, KB:SUMS] = rest


def update_kernel(blocks, whole_len, counts, sums, upper, lower, grad, loss, master, first, second, *refs):
    loss_out, norm_out, coef_out, master_out, first_out, second_out, removed = refs
    norm = jnp.sqrt(sums[0:1, KB : KB + 1])
    factor = jnp.minimum(1.0, CLIP_NORM / (norm + 1e-06))
    lane = lax.broadcasted_iota(jnp.int32, (1, KB), 1)
    limit = jnp.where(lane < KMAX, counts[0], counts[1] + KMAX)
    row = jnp.where(lane < limit, sums[:, 0:KB] * factor, 0.0)
    coef_out[0:1, :] = row[:, 0:KMAX]
    coef_out[1:2, :] = row[:, KMAX:KB]
    norm_out[0] = jnp.sum(norm)
    loss_out[0] = jnp.sum(sums[0:1, KB + 1 : KB + 2])
    loss_out[1] = jnp.sum(sums[0:1, KB + 2 : KB + 3])
    loss_out[2] = jnp.sum(loss[0:1, 2:3])
    high = row.astype(bf16).astype(f32)
    mid = (row - high).astype(bf16).astype(f32)
    low = row - high - mid
    place = lax.broadcasted_iota(jnp.int32, (16, KB), 0)
    split = jnp.where(place == 0, high, jnp.where(place == 1, mid, jnp.where(place == 2, low, 0.0)))
    split = split.astype(bf16)
    rows = grad.shape[0]

    def step(i, carry):
        base = i * blocks
        start = pl.multiple_of(base * LANES, LANES)
        part = dot(split[:, :UPPER], upper[:, pl.ds(start, blocks * LANES)])
        part = part + dot(split[:, UPPER:], lower[:, pl.ds(start, blocks * LANES)])
        part = jnp.sum(part, 0, keepdims=True)
        for j in range(blocks):
            removed[pl.ds(base + j, 1), :] = part[:, j * LANES : (j + 1) * LANES]
        return carry

    lax.fori_loop(0, rows // blocks, step, 0)
    projected = grad[...] * factor - removed[0:rows, :] * (1.0 / whole_len)
    new_first = BETA_ONE * first[...] + (1.0 - BETA_ONE) * projected
    new_second = BETA_TWO * second[...] + (1.0 - BETA_TWO) * projected * projected
    ratio = (
        new_first
        / (1.0 - BETA_ONE**STEP)
        / (jnp.sqrt(new_second / (1.0 - BETA_TWO**STEP)) + ADAM_EPS)
    )
    old = master[...]
    master_out[...] = old - LEARN_RATE * (ratio + WEIGHT_DECAY * old)
    first_out[...] = new_first
    second_out[...] = new_second


def dp_dims(count):
    zed = 4 if count % 4 == 0 else 1
    plane = count // zed
    ex = max(side for side in range(1, math.isqrt(plane) + 1) if plane % side == 0)
    return zed, plane // ex, ex


def moved(value, place, turn=(0, 0, 0), core=0, sections=(0, 1)):
    pairs = []
    for section in sections:
        for zed in range(place.z):
            for why in range(place.y):
                for ex in range(place.x):
                    source = (section * place.z + zed) * place.y * place.x + why * place.x + ex
                    there = ((section + core) % 2) * place.z + (zed + turn[0]) % place.z
                    target = (there * place.y + (why + turn[1]) % place.y) * place.x
                    pairs.append((source, target + (ex + turn[2]) % place.x))
    return lax.ppermute(value, ("section", "dp"), pairs)


def add(left, right, resident):
    vmem = pl.BlockSpec(memory_space=pltpu.VMEM)
    return pl.pallas_call(
        add_kernel,
        in_specs=[vmem, vmem] + [pl.BlockSpec(memory_space=pl.ANY)] * 2,
        out_specs=vmem,
        out_shape=jax.ShapeDtypeStruct(left.shape, left.dtype),
        compiler_params=pltpu.CompilerParams(vmem_limit_bytes=2 * 1024 * 1024),
        name="add",
    )(left, right, *resident)


def butterfly(value, place, resident):
    value = add(value, moved(value, place, core=1), resident)
    for axis, size in ((2, place.x), (1, place.y), (0, place.z)):
        span = 1
        while span < size:
            pairs = []
            for index in range(2 * place.count):
                section, rest = divmod(index, place.count)
                at = [rest // (place.y * place.x), rest // place.x % place.y, rest % place.x]
                at[axis] ^= span
                pairs.append((index, section * place.count + (at[0] * place.y + at[1]) * place.x + at[2]))
            value = add(value, lax.ppermute(value, ("section", "dp"), pairs), resident)
            span *= 2
    return value


def whole(shape):
    return pl.BlockSpec(shape, lambda *_: (0,) * len(shape))


def params(megabytes):
    return pltpu.CompilerParams(
        vmem_limit_bytes=megabytes * 1024 * 1024, dimension_semantics=("arbitrary",)
    )


BLOCK_SHAPES = [(D, D)] * 4 + [(D, FF), (FF, D)]
SAVED = [
    ((ROWS, D), f32),
    ((ROWS, D), bf16),
    ((ROWS, D), bf16),
    ((ROWS, D), bf16),
    ((HEADS * ROWS, ROWS), f32),
    ((ROWS, D), bf16),
    ((ROWS, D), f32),
    ((ROWS, FF), bf16),
    ((ROWS, FF), f32),
]
MIDDLE = ((ROWS, D), bf16)
WORK = pl.CostEstimate(flops=3_000_000_000, bytes_accessed=30_000_000, transcendentals=1_000_000)
VMEM = pl.BlockSpec(memory_space=pltpu.VMEM)
SMEM = pl.BlockSpec(memory_space=pltpu.SMEM)
ANY = pl.BlockSpec(memory_space=pl.ANY)


def group_of(per):
    return GROUP if per % GROUP == 0 else 1


def row_block(shape, per):
    return pl.BlockSpec((group_of(per) * shape[0], shape[1]), lambda i, *_: (i, 0))


def flat_scratch(place):
    flat_rows = place.count * place.shard_rows + SPARE
    return [
        pltpu.VMEM((flat_rows, LANES), f32),
        pltpu.VMEM((flat_rows, LANES), f32),
        pltpu.VMEM((FF + 32, LANES), f32),
    ]


def patch_block(per):
    return pl.BlockSpec((group_of(per), PATCHES, PDIM), lambda i, *_: (i, 0, 0))


def front(place, per, own, other, patches):
    outs = pl.pallas_call(
        functools.partial(front_kernel, place),
        grid_spec=pltpu.PrefetchScalarGridSpec(
            num_scalar_prefetch=0,
            grid=(per // group_of(per),),
            in_specs=[whole(piece.shape) for piece in own + other] + [patch_block(per)],
            out_specs=[row_block(shape, per) for shape, _ in SAVED + [MIDDLE]]
            + [whole(shape) for shape in BLOCK_SHAPES]
            + [whole((VEC_ROWS, FF))],
            scratch_shapes=flat_scratch(place)
            + [pltpu.VMEM((PDIM, D), bf16)]
            + [pltpu.VMEM((group_of(per) * ROWS, D), f32)] * 2,
        ),
        out_shape=[
            jax.ShapeDtypeStruct((per * shape[0], shape[1]), kind) for shape, kind in SAVED + [MIDDLE]
        ]
        + [jax.ShapeDtypeStruct(shape, bf16) for shape in BLOCK_SHAPES]
        + [jax.ShapeDtypeStruct((VEC_ROWS, FF), f32)],
        compiler_params=params(20),
        cost_estimate=WORK,
        name="front",
    )(*own, *other, patches)
    return outs[:9], outs[9], outs[10:]


def grad_kind(place):
    return jax.ShapeDtypeStruct((place.count, place.sent_rows, LANES), bf16)


def late(place, per, image_total, labels, replay, own, other, middle, old_logits):
    eight = -(-per // 8) * 8
    return pl.pallas_call(
        functools.partial(late_kernel, place, per, image_total),
        in_specs=[SMEM] * 2 + [VMEM] * (len(own) + len(other) + 2),
        out_specs=[VMEM] * 3,
        out_shape=[
            jax.ShapeDtypeStruct((per * ROWS, D), bf16),
            grad_kind(place),
            jax.ShapeDtypeStruct((1, LANES), f32),
        ],
        scratch_shapes=flat_scratch(place)
        + [pltpu.VMEM((8, 256, LANES), f32)]
        + [pltpu.VMEM(shape, bf16) for shape in BLOCK_SHAPES]
        + [
            pltpu.VMEM((VEC_ROWS, FF), f32),
            pltpu.VMEM((D, CPAD), bf16),
            pltpu.VMEM((1, CPAD), f32),
            pltpu.VMEM((eight, D), f32),
            pltpu.VMEM((per * ROWS, D), f32),
        ],
        compiler_params=pltpu.CompilerParams(vmem_limit_bytes=16 * 1024 * 1024),
        cost_estimate=WORK,
        name="late",
    )(labels, replay, *own, *other, middle, old_logits)


def back(place, per, grad_middle, kept, patches, weights, late_grad):
    return pl.pallas_call(
        functools.partial(back_kernel, place),
        grid_spec=pltpu.PrefetchScalarGridSpec(
            num_scalar_prefetch=0,
            grid=(per // group_of(per),),
            in_specs=[row_block(shape, per) for shape, _ in [MIDDLE] + SAVED]
            + [patch_block(per)]
            + [whole(shape) for shape in BLOCK_SHAPES]
            + [whole((VEC_ROWS, FF)), whole(grad_kind(place).shape)],
            out_specs=[whole(grad_kind(place).shape)] * 2,
            scratch_shapes=flat_scratch(place)
            + [pltpu.VMEM(shape, f32) for shape in BLOCK_SHAPES]
            + [
                pltpu.VMEM((PDIM, D), f32),
                pltpu.VMEM((ROWS, D), f32),
                pltpu.VMEM((VEC_ROWS, FF), f32),
            ],
        ),
        out_shape=[grad_kind(place)] * 2,
        compiler_params=params(20),
        cost_estimate=WORK,
        name="back",
    )(grad_middle, *kept, patches, *weights, late_grad)


def body(
    patches, labels, replay, old_logits, basis_count, master, first_moment, second_moment, basis
):
    chips = lax.axis_size("dp")
    shard_len = master.shape[1]
    shard_rows = shard_len // LANES
    place = Place(dp_dims(chips), shard_rows)
    images = patches.shape[0]
    per = images // 2
    section = lax.axis_index("section")
    turns = place.turns()

    shard = pl.pallas_call(
        shard_kernel,
        grid=(1,),
        in_specs=[SMEM, whole((shard_rows, LANES))],
        out_specs=whole((place.sent_rows, LANES)),
        out_shape=jax.ShapeDtypeStruct((place.sent_rows, LANES), bf16),
        compiler_params=pltpu.CompilerParams(vmem_limit_bytes=2 * 1024 * 1024),
        name="shard",
    )(replay, master.reshape(shard_rows, LANES))
    mine = lax.dynamic_slice_in_dim(patches, section * per, per, 0)
    early, late_part = shard[: place.first_rows], shard[place.first_rows :]
    column = [early] + [moved(early, place, (d, 0, 0)) for d in range(1, place.z)]
    plane = [moved(late_part, place, (0, a, b)) if a + b else late_part for a, b in turns]
    column[-1], mine = lax.optimization_barrier((column[-1], mine))
    column, plane = jnp.stack(column), jnp.stack(plane)
    own = [moved(column, place, (0, a, b)) if a + b else column for a, b in turns]
    own += [moved(plane, place, (d, 0, 0)) if d else plane for d in range(place.z)]
    other = [moved(piece, place, core=1) for piece in own]

    kept, middle, weights = front(place, per, own, other, mine)
    grad_middle, late_grad, loss = late(
        place, per, float(images * chips), labels, replay, own, other, middle, old_logits
    )
    keep, give = back(place, per, grad_middle, kept, mine, weights, late_grad)

    given = moved(give, place, core=1)

    def paired(turn):
        cut = slice(turn * place.z, (turn + 1) * place.z)
        return keep[cut].astype(f32) + given[cut].astype(f32)

    staying, leaving = paired(0), [paired(turn).astype(bf16) for turn in range(1, len(turns))]
    rows_basis = pltpu.with_memory_space_constraint(basis.reshape(KB, shard_len), pltpu.HBM)

    def fetch(first, last, after):
        return pl.pallas_call(
            functools.partial(fetch_kernel, first, last),
            in_specs=[ANY, ANY],
            out_specs=ANY,
            out_shape=pltpu.VMEM((last - first, shard_len), bf16),
            scratch_shapes=[pltpu.SemaphoreType.DMA],
            compiler_params=pltpu.CompilerParams(vmem_limit_bytes=2 * 1024 * 1024),
            cost_estimate=pl.CostEstimate(
                flops=0, bytes_accessed=4 * (last - first) * shard_len, transcendentals=0
            ),
            name="fetch",
        )(after, rows_basis)

    upper = fetch(0, UPPER, leaving[0])
    arrived = [moved(leaving[turn - 1], place, (0, *turns[turn])) for turn in range(1, len(turns))]
    piece_shape = (place.sent_rows, LANES)
    first, *rest = pl.pallas_call(
        functools.partial(plane_kernel, place.z),
        in_specs=[VMEM, ANY] + [VMEM] * (len(turns) - 1),
        out_specs=[VMEM] * place.z,
        out_shape=[jax.ShapeDtypeStruct(piece_shape, bf16 if d else f32) for d in range(place.z)],
        compiler_params=pltpu.CompilerParams(vmem_limit_bytes=2 * 1024 * 1024),
        name="plane",
    )(staying, upper, *arrived)
    resident = (upper, fetch(UPPER, KB, rest[0]))
    pieces = [moved(rest[d - 1], place, (d, 0, 0)) for d in range(1, place.z)]

    def divisor(most):
        return max(n for n in range(1, most + 1) if shard_rows % n == 0)

    flat_kind = jax.ShapeDtypeStruct((shard_rows, LANES), f32)
    grad, sums = pl.pallas_call(
        functools.partial(inner_kernel, divisor(26)),
        in_specs=[VMEM] * (place.z + 3),
        out_specs=[VMEM] * 2,
        out_shape=[flat_kind, jax.ShapeDtypeStruct((1, SUMS), f32)],
        scratch_shapes=[pltpu.VMEM((KB, LANES), f32)],
        compiler_params=pltpu.CompilerParams(vmem_limit_bytes=2 * 1024 * 1024),
        name="inner",
    )(first, *pieces, *resident, loss)
    sums = butterfly(sums, place, resident)
    padded_rows = -(-shard_rows // 8) * 8
    loss_parts, norm, coefficients, new_master, new_first, new_second = pl.pallas_call(
        functools.partial(update_kernel, divisor(78), float(2 * shard_len * chips)),
        in_specs=[SMEM] + [VMEM] * 8,
        out_specs=[SMEM, SMEM] + [VMEM] * 4,
        out_shape=[
            jax.ShapeDtypeStruct((3,), f32),
            jax.ShapeDtypeStruct((1,), f32),
            jax.ShapeDtypeStruct((TASKS, KMAX), f32),
        ]
        + [flat_kind] * 3,
        scratch_shapes=[pltpu.VMEM((padded_rows, LANES), f32)],
        compiler_params=pltpu.CompilerParams(vmem_limit_bytes=2 * 1024 * 1024),
        name="update",
    )(
        basis_count,
        sums,
        *resident,
        grad,
        loss,
        master.reshape(shard_rows, LANES),
        first_moment.reshape(shard_rows, LANES),
        second_moment.reshape(shard_rows, LANES),
    )
    return (
        loss_parts,
        norm[0],
        coefficients,
        new_master.reshape(1, shard_len),
        new_first.reshape(1, shard_len),
        new_second.reshape(1, shard_len),
    )


def solution(mesh):
    in_specs = (
        P("dp", None, None),
        P("dp"),
        P("dp"),
        P("dp", None),
        P(),
        P("section", "dp"),
        P("section", "dp"),
        P("section", "dp"),
        P(None, "section", "dp"),
    )
    out_specs = (P(), P(), P(), P("section", "dp"), P("section", "dp"), P("section", "dp"))
    return jax.shard_map(body, mesh=mesh, in_specs=in_specs, out_specs=out_specs, check_vma=False)
```

```python
import functools
import math

import jax
import jax.numpy as jnp
from jax import lax
from jax.experimental import pallas as pl
from jax.experimental.pallas import tpu as pltpu
from jax.sharding import PartitionSpec as P

HEADS = 3
HD = 64
D = 192
FF = 768
PDIM = 768
PATCHES = 196
TOKENS = PATCHES + 1
ROWS = 208
CLS = PATCHES
GROUP = 4
CLASSES = 1000
CPAD = 1024
TASKS = 2
KMAX = 200
KB = TASKS * KMAX
UPPER = 208
STEP = 10
LANES = 128
HALF = 64
SPARE = 512
SUMS = 512

NORM_EPS = 1e-06
CLIP_NORM = 0.02
LEARN_RATE = 0.05
BETA_ONE = 0.9
BETA_TWO = 0.999
ADAM_EPS = 1e-08
WEIGHT_DECAY = 0.05
SCALE = HD ** (-0.5)
MASKED = -1e30

BLOCK_AT = dict(
    gain_one=0,
    bias_one=3,
    w_qkv=6,
    b_qkv=1734,
    w_out=1740,
    b_out=2316,
    gain_two=2319,
    bias_two=2322,
    w_up=2325,
    b_up=4629,
    w_down=4641,
    b_down=6945,
)
W_PATCH, B_PATCH, CLS_TOKEN, POS_EMBED = 6948, 9252, 9255, 9258
GAIN_LAST, BIAS_LAST, W_HEAD, B_HEAD = 6948, 6951, 6954, 9954
VECTORS = ("gain_one", "bias_one", "b_q", "b_v", "b_out", "gain_two", "bias_two", "b_up", "b_down")
VEC_ROWS = 16

f32 = jnp.float32
bf16 = jnp.bfloat16


def dot(left, right, left_dim=1, right_dim=0):
    return lax.dot_general(
        left, right, (((left_dim,), (right_dim,)), ((), ())), preferred_element_type=f32
    )


def low_lanes(shape):
    return lax.broadcasted_iota(jnp.int32, shape, 1) < HALF


def swap_halves(value):
    return pltpu.roll(value, HALF, 1)


def head_masks():
    lane = lax.broadcasted_iota(jnp.int32, (1, D), 1)
    return [jnp.logical_and(lane >= h * HD, lane < (h + 1) * HD) for h in range(HEADS)]


def by_head(value):
    return jnp.concatenate([jnp.where(m, value, 0.0) for m in head_masks()], 0)


def from_heads(value):
    rows = value.shape[0] // HEADS
    parts = [value[h * rows : (h + 1) * rows] for h in range(HEADS)]
    masks = head_masks()
    return jnp.where(masks[0], parts[0], jnp.where(masks[1], parts[1], parts[2]))


def normalise(rows_in):
    mean = jnp.sum(rows_in, -1, keepdims=True) * (1.0 / D)
    centred = rows_in - mean
    variance = jnp.sum(centred * centred, -1, keepdims=True) * (1.0 / D)
    scale = lax.rsqrt(variance + NORM_EPS)
    return centred * scale, scale


def normalise_back(grad, gain, unit, scale):
    grad_unit = grad * gain
    first = jnp.sum(grad_unit, -1, keepdims=True) * (1.0 / D)
    second = jnp.sum(grad_unit * unit, -1, keepdims=True) * (1.0 / D)
    return scale * (grad_unit - first - unit * second)


def gelu_parts(pre):
    cdf = 0.5 * (1.0 + lax.erf(pre * math.sqrt(0.5)))
    slope = cdf + pre * (jnp.exp(-0.5 * pre * pre) * (1.0 / math.sqrt(2.0 * math.pi)))
    return pre * cdf, slope


def column_sums(value):
    return jnp.sum(value.astype(f32), 0, keepdims=True)


def strided(ref, start, count, stride):
    if count == 1 or stride == 1:
        return ref[pl.ds(start, count), :]
    return ref[pl.ds(start, count, stride=stride), :]


class Flat:
    def __init__(self, even, odd, mix, rows):
        self.even, self.odd, self.mix, self.rows = even, odd, mix, rows

    def shift(self):
        step = 192
        for at in range(0, self.rows, step):
            here = self.even[at : at + step, :]
            after = self.even[at + 1 : at + 1 + step, :]
            self.odd[at : at + step, :] = swap_halves(jnp.where(low_lanes(here.shape), after, here))

    def rows_at(self, half, count, stride):
        return strided(self.odd if half % 2 else self.even, half // 2, count, stride)

    def blocks(self, half, width, rows, cols):
        for at in range(0, cols, LANES):
            start = half + at // HALF
            if rows == 1 or width % 2 == 0:
                value = self.rows_at(start, rows, width // 2)
            else:
                pairs = (rows + 1) // 2
                self.mix[pl.ds(0, pairs, stride=2), :] = self.rows_at(start, pairs, width)
                self.mix[pl.ds(1, pairs, stride=2), :] = self.rows_at(start + width, pairs, width)
                value = self.mix[0:rows, :]
            yield at, min(LANES, cols - at), value

    def read(self, dest, half, width, rows, cols):
        for at, wide, value in self.blocks(half, width, rows, cols):
            dest[0:rows, at : at + wide] = value[:, :wide].astype(dest.dtype)

    def read_row(self, dest, row, half, cols):
        for at, wide, value in self.blocks(half, 2, 1, cols):
            dest[row : row + 1, at : at + wide] = value[:, :wide]

    def clear(self):
        self.even[...] = jnp.zeros(self.even.shape, f32)
        self.odd[...] = jnp.zeros(self.odd.shape, f32)

    def put_rows(self, half, count, stride, value):
        ref, start = (self.odd, half // 2 + 8) if half % 2 else (self.even, half // 2)
        if count == 1 or stride == 1:
            ref[pl.ds(start, count), :] = value
        else:
            ref[pl.ds(start, count, stride=stride), :] = value

    def write(self, value, half, width, cols):
        rows = value.shape[0]
        for at in range(0, cols, LANES):
            wide = min(LANES, cols - at)
            part = value[:, at : at + wide]
            if wide < LANES:
                part = jnp.concatenate([part, jnp.zeros((rows, LANES - wide), f32)], 1)
            start = half + at // HALF
            if rows == 1 or width % 2 == 0:
                self.put_rows(start, rows, width // 2, part)
            else:
                pairs = (rows + 1) // 2
                self.mix[0:rows, :] = part
                self.put_rows(start, pairs, width, self.mix[pl.ds(0, pairs, stride=2), :])
                self.put_rows(start + width, pairs, width, self.mix[pl.ds(1, pairs, stride=2), :])

    def merged(self, at, count):
        here = self.odd[at + 8 : at + 8 + count, :]
        before = self.odd[at + 7 : at + 7 + count, :]
        moved_back = swap_halves(jnp.where(low_lanes(here.shape), here, before))
        return self.even[at : at + count, :] + moved_back


def paired(size):
    return size & (size - 1) == 0


class Place:
    def __init__(self, dims, shard_rows):
        self.z, self.y, self.x = dims
        self.count = self.z * self.y * self.x
        self.shard_rows = shard_rows
        self.sent_rows = -(-(shard_rows + 1) // 16) * 16
        self.first_rows = self.sent_rows * 13 // 20 // 16 * 16

        self.half_rows = self.sent_rows // 32 * 16

    def split(self, index):
        plane = self.y * self.x
        return index // plane, lax.rem(index, plane) // self.x, lax.rem(index, self.x)

    def turns(self):
        return [(a, b) for a in range(self.y) for b in range(self.x)]


def load_section(place, pieces, wanted, flat):
    own, other = pieces
    section = lax.axis_index("section")
    zed, why, ex = place.split(lax.axis_index("dp"))
    rows = place.shard_rows

    def copy(refs):
        for turn, (a, b) in enumerate(place.turns()):
            for d in range(place.z):
                shard = lax.rem(zed + (place.z - d), place.z) * (place.y * place.x)
                shard = shard + lax.rem(why + (place.y - a), place.y) * place.x
                shard = shard + lax.rem(ex + (place.x - b), place.x)
                start = shard * rows
                if rows % 8 == 0:
                    start = pl.multiple_of(start, 8)
                cut = place.first_rows
                flat.even[pl.ds(start, cut), :] = refs[turn][d].astype(f32)
                value = refs[len(place.turns()) + d][turn].astype(f32)
                after = start + cut
                if rows % 8 == 0:
                    after = pl.multiple_of(after, 8)
                flat.even[pl.ds(after, rows - cut), :] = value[: rows - cut]

    @pl.when(section == wanted)
    def _():
        copy(own)

    @pl.when(section != wanted)
    def _():
        copy(other)

    flat.shift()


def read_block(flat, weights, vec):
    at = BLOCK_AT
    w_q, w_k, w_v, w_out, w_up, w_down = weights
    for place, dest in enumerate((w_q, w_k, w_v)):
        flat.read(dest, at["w_qkv"] + 3 * place, 9, D, D)
    flat.read(w_out, at["w_out"], 3, D, D)
    flat.read(w_up, at["w_up"], 12, D, FF)
    flat.read(w_down, at["w_down"], 3, FF, D)
    starts = dict(at, b_q=at["b_qkv"], b_v=at["b_qkv"] + 3)
    for row, name in enumerate(VECTORS):
        flat.read_row(vec, row, starts[name], FF if name == "b_up" else D)


def vector(vec, name):
    row = VECTORS.index(name)
    return vec[row : row + 1, 0 : FF if name == "b_up" else D]


def write_vectors(flat, sums):
    at = BLOCK_AT
    starts = dict(at, b_q=at["b_qkv"], b_v=at["b_qkv"] + 3)
    for name, value in sums.items():
        flat.write(value, starts[name], 2, value.shape[1])


def send_out(place, flat, write):
    zed, why, ex = place.split(lax.axis_index("dp"))
    rows, spare = place.shard_rows, place.sent_rows - place.shard_rows
    for shard in range(place.count):
        zk, yk, xk = shard // (place.y * place.x), shard // place.x % place.y, shard % place.x
        there = ((zk, zed, place.z), (yk, why, place.y), (xk, ex, place.x))
        d, a, b = [to ^ at if paired(size) else lax.rem(to + size - at, size) for to, at, size in there]
        value = flat.merged(shard * rows, rows)
        value = jnp.concatenate([value, jnp.zeros((spare, LANES), f32)], 0)
        write((a * place.x + b) * place.z + d, value.astype(bf16))


def shard_kernel(replay, master, out):
    rows = master.shape[0]
    count = sum(replay[i].astype(f32) for i in range(replay.shape[0]))
    tail = jnp.full((out.shape[0] - rows, LANES), count, f32)
    out[...] = jnp.concatenate([master[...], tail], 0).astype(bf16)


def front_kernel(place, per, *refs):
    parts = len(place.turns()) + place.z
    own, other, refs = refs[:parts], refs[parts : 2 * parts], refs[2 * parts :]
    patches, kept, middle_out, weights = refs[0], refs[1:10], refs[10], refs[11:18]
    even, odd, mix, w_patch, added, tokens = refs[18:]
    vec = weights[-1]
    flat = Flat(even, odd, mix, place.count * place.shard_rows)
    load_section(place, (own, other), 0, flat)
    read_block(flat, weights[:-1], vec)
    flat.read(w_patch, W_PATCH, 3, PDIM, D)
    flat.read_row(vec, 9, B_PATCH, D)
    flat.read_row(vec, 10, CLS_TOKEN, D)
    added[...] = jnp.zeros(added.shape, f32)
    tokens[...] = jnp.zeros(tokens.shape, f32)
    for at, wide, value in flat.blocks(POS_EMBED, 3, TOKENS + 1, D):
        added[0:PATCHES, at : at + wide] = value[1:TOKENS, :wide] + vec[9:10, at : at + wide]
        added[CLS : CLS + 1, at : at + wide] = value[0:1, :wide] + vec[10:11, at : at + wide]
    group = group_of(per)
    for step in range(0, per, group):
        cut = slice(step * ROWS, (step + group) * ROWS)
        front_images(step, cut, patches, kept, middle_out, weights, w_patch, added, tokens)


def front_images(step, cut, patches, kept, middle_out, weights, w_patch, added, tokens):
    x_out, q_out, k_out, v_out, probs_out, mixed_out, hidden_out, act_out, slope_out = kept
    w_q, w_k, w_v, w_out, w_up, w_down, vec = weights
    group = (cut.stop - cut.start) // ROWS
    spans = [slice(i * ROWS, (i + 1) * ROWS) for i in range(group)]
    for i, at in enumerate(spans):
        tokens[cut.start + at.start : cut.start + at.start + PATCHES, :] = dot(patches[step + i], w_patch[...])
    x = tokens[cut, :] + jnp.concatenate([added[...]] * group, 0)
    x_out[cut, :] = x
    unit, _ = normalise(x)
    normed = (unit * vector(vec, "gain_one") + vector(vec, "bias_one")).astype(bf16)
    q = (dot(normed, w_q[...]) + vector(vec, "b_q")).astype(bf16)
    k = dot(normed, w_k[...]).astype(bf16)
    v = (dot(normed, w_v[...]) + vector(vec, "b_v")).astype(bf16)
    q_out[cut, :], k_out[cut, :], v_out[cut, :] = q, k, v
    q_scaled = q.astype(f32) * SCALE
    column = lax.broadcasted_iota(jnp.int32, (1, ROWS), 1)
    scores = [dot(by_head(q_scaled[at]).astype(bf16), k[at], 1, 1) for at in spans]
    scores = [jnp.where(column < TOKENS, value, MASKED) for value in scores]
    raised = [jnp.exp(value - jnp.max(value, -1, keepdims=True)) for value in scores]
    probs = [value * (1.0 / jnp.sum(value, -1, keepdims=True)) for value in raised]
    for i, value in enumerate(probs):
        probs_out[(step + i) * HEADS * ROWS : (step + i + 1) * HEADS * ROWS, :] = value
    mixed = [from_heads(dot(value.astype(bf16), v[at])) for value, at in zip(probs, spans)]
    mixed = jnp.concatenate(mixed, 0).astype(bf16)
    mixed_out[cut, :] = mixed
    hidden = x + dot(mixed, w_out[...]) + vector(vec, "b_out")
    hidden_out[cut, :] = hidden
    unit, _ = normalise(hidden)
    normed = (unit * vector(vec, "gain_two") + vector(vec, "bias_two")).astype(bf16)
    pre = dot(normed, w_up[...]) + vector(vec, "b_up")
    act, slope = gelu_parts(pre)
    act = act.astype(bf16)
    act_out[cut, :], slope_out[cut, :] = act, slope
    middle = hidden + dot(act, w_down[...]) + vector(vec, "b_down")
    middle_out[cut, :] = middle.astype(bf16)


def read_head(flat, wide, w_head, b_head):
    first = W_HEAD // 2
    lane = lax.broadcasted_iota(jnp.int32, (16, LANES), 1)
    for phase in range(16):
        start, off = first + CLASSES * phase // LANES, CLASSES * phase % LANES
        got = [strided(flat.even, start + j, 16, 125) for j in range(9 if off else 8)]
        if off:
            got = [pltpu.roll(g, LANES - off, 1) for g in got]
        for j in range(8):
            value = jnp.where(lane < LANES - off, got[j], got[j + 1]) if off else got[j]
            wide[j, pl.ds(phase, 16, stride=16), :] = value
    lane = lax.broadcasted_iota(jnp.int32, (1, LANES), 1)
    for j in range(8):
        keep = lane + j * LANES < CLASSES
        w_head[:, j * LANES : (j + 1) * LANES] = jnp.where(keep, wide[j, 0:D, :], 0.0).astype(bf16)
        value = flat.even[B_HEAD // 2 + j : B_HEAD // 2 + j + 1, :]
        b_head[0:1, j * LANES : (j + 1) * LANES] = jnp.where(keep, value, 0.0)


def write_head(flat, wide, grad_w, grad_b):
    first = W_HEAD // 2
    for j in range(8):
        wide[j, 0:D, :] = grad_w[:, j * LANES : (j + 1) * LANES]
        wide[j, D:, :] = jnp.zeros((wide.shape[1] - D, LANES), f32)
    lane = lax.broadcasted_iota(jnp.int32, (16, LANES), 1)
    for phase in range(16):
        start, off = first + CLASSES * phase // LANES, CLASSES * phase % LANES
        got = [wide[j, pl.ds(phase, 16, stride=16), :] for j in range(8)]
        if off:
            got = [pltpu.roll(g, off, 1) for g in got]
        for j in range(9 if off else 8):
            if not off:
                value = got[j]
            else:
                before = got[j - 1] if j else jnp.zeros((16, LANES), f32)
                value = jnp.where(lane < off, before, got[j] if j < 8 else 0.0)
            flat.even[pl.ds(start + j, 16, stride=125), :] += value
    for j in range(8):
        row = B_HEAD // 2 + j
        flat.even[row : row + 1, :] += grad_b[:, j * LANES : (j + 1) * LANES]


def late_kernel(place, per, image_total, labels, replay, *refs):
    section = lax.axis_index("section")
    parts = len(place.turns()) + place.z
    own, other, refs = refs[:parts], refs[parts : 2 * parts], refs[2 * parts :]
    middle, old_logits, back_out, grad_out, loss_out = refs[:5]
    even, odd, mix, wide, w_q, w_k, w_v, w_out, w_up, w_down, vec, w_head, b_head, few, many = refs[5:]
    flat = Flat(even, odd, mix, place.count * place.shard_rows)
    load_section(place, (own, other), 1, flat)
    read_block(flat, (w_q, w_k, w_v, w_out, w_up, w_down), vec)
    flat.read_row(vec, 9, GAIN_LAST, D)
    flat.read_row(vec, 10, BIAS_LAST, D)
    read_head(flat, wide, w_head, b_head)
    gain_last, bias_last = vec[9:10, 0:D], vec[10:11, 0:D]
    carried = jnp.zeros((1, LANES), f32)
    carrier = place.shard_rows - place.first_rows
    for ref in own[len(place.turns()) :]:
        for turn in range(len(place.turns())):
            carried = carried + ref[turn].astype(f32)[carrier : carrier + 1]
    replay_count = carried[:, 0:1]

    x = middle[...].astype(f32)
    unit, scale = normalise(x)
    normed_f = unit * vector(vec, "gain_one") + vector(vec, "bias_one")
    normed = normed_f.astype(bf16)
    k = dot(normed, w_k[...]).astype(bf16)
    v = (dot(normed, w_v[...]) + vector(vec, "b_v")).astype(bf16)

    def class_rows(value):
        few[...] = jnp.zeros(few.shape, f32)
        for i in range(per):
            few[i : i + 1, :] = value[i * ROWS + CLS : i * ROWS + CLS + 1, :]
        return few[...]

    eight = few.shape[0]
    image = lax.broadcasted_iota(jnp.int32, (eight, 1), 0)
    real = image < per
    x_top = class_rows(x)
    top_normed = class_rows(normed_f).astype(bf16)
    q = (dot(top_normed, w_q[...]) + vector(vec, "b_q")).astype(bf16)
    q_heads = by_head(jnp.where(real, q.astype(f32) * SCALE, 0.0)).astype(bf16)
    scores = dot(q_heads, k, 1, 1)
    column = lax.broadcasted_iota(jnp.int32, scores.shape, 1)
    owner = lax.rem(lax.broadcasted_iota(jnp.int32, scores.shape, 0), eight) * ROWS
    inside = jnp.logical_and(column >= owner, column < owner + TOKENS)
    scores = jnp.where(inside, scores, MASKED)
    raised = jnp.where(inside, jnp.exp(scores - jnp.max(scores, -1, keepdims=True)), 0.0)
    total = jnp.sum(raised, -1, keepdims=True)
    probs = raised * (1.0 / jnp.where(total > 0.0, total, 1.0))
    probs_low = probs.astype(bf16)
    mixed = from_heads(dot(probs_low, v)).astype(bf16)
    hidden = x_top + dot(mixed, w_out[...]) + vector(vec, "b_out")
    unit_two, scale_two = normalise(hidden)
    normed_two = (unit_two * vector(vec, "gain_two") + vector(vec, "bias_two")).astype(bf16)
    act, slope = gelu_parts(dot(normed_two, w_up[...]) + vector(vec, "b_up"))
    act = act.astype(bf16)
    final = hidden + dot(act, w_down[...]) + vector(vec, "b_down")

    unit_last, scale_last = normalise(final)
    top = (unit_last * gain_last + bias_last).astype(bf16)
    classes = lax.broadcasted_iota(jnp.int32, (eight, CPAD), 1)
    logits = dot(top, w_head[...]) + b_head[...]
    logits = jnp.where(classes < CLASSES, logits, MASKED)
    highest = jnp.max(logits, -1, keepdims=True)
    log_total = highest + jnp.log(jnp.sum(jnp.exp(logits - highest), -1, keepdims=True))
    label = jnp.zeros((eight, 1), jnp.int32)
    again = jnp.zeros((eight, 1), f32)
    for i in range(per):
        label = jnp.where(image == i, labels[section * per + i], label)
        again = jnp.where(image == i, replay[section * per + i].astype(f32), again)
    picked = jnp.logical_and(classes == label, real)
    entropy = jnp.where(real, log_total, 0.0) - jnp.sum(jnp.where(picked, logits, 0.0), -1, keepdims=True)
    wanted = jnp.where(section == 0, old_logits[0:per, :], old_logits[per : 2 * per, :])
    if per < eight:
        wanted = jnp.concatenate([wanted, jnp.zeros((eight - per, CLASSES), f32)], 0)
    wanted = jnp.concatenate([wanted, jnp.zeros((eight, CPAD - CLASSES), f32)], 1)
    distance = jnp.where(jnp.logical_and(classes < CLASSES, real), logits - wanted, 0.0)
    squares = again * (jnp.sum(distance * distance, -1, keepdims=True) * (1.0 / CLASSES))
    lane = lax.broadcasted_iota(jnp.int32, (1, LANES), 1)
    entropy_sum = jnp.sum(entropy, 0, keepdims=True)
    replay_sum = jnp.sum(squares, 0, keepdims=True)
    loss_out[...] = jnp.where(lane == 0, entropy_sum, jnp.where(lane == 1, replay_sum, replay_count))

    grad = (jnp.exp(logits - log_total) - jnp.where(picked, 1.0, 0.0)) * (1.0 / image_total)
    grad = grad + again * 2.0 * distance / (CLASSES * replay_count)
    grad = jnp.where(jnp.logical_and(classes < CLASSES, real), grad, 0.0)
    grad_low = grad.astype(bf16)
    flat.clear()
    write_head(flat, wide, dot(top, grad_low, 0, 0), column_sums(grad_low))
    sums = {}
    grad = dot(grad_low, w_head[...], 1, 1)
    flat.write(column_sums(grad * unit_last), GAIN_LAST, 2, D)
    flat.write(column_sums(grad), BIAS_LAST, 2, D)
    grad = normalise_back(grad, gain_last, unit_last, scale_last)

    at = BLOCK_AT
    grad_down = grad.astype(bf16)
    flat.write(dot(act, grad_down, 0, 0), at["w_down"], 3, D)
    sums["b_down"] = column_sums(grad_down)
    grad_up = (dot(grad_down, w_down[...], 1, 1) * slope).astype(bf16)
    flat.write(dot(normed_two, grad_up, 0, 0), at["w_up"], 12, FF)
    sums["b_up"] = column_sums(grad_up)
    grad_two = dot(grad_up, w_up[...], 1, 1)
    sums["gain_two"], sums["bias_two"] = column_sums(grad_two * unit_two), column_sums(grad_two)
    grad_hidden = grad + normalise_back(grad_two, vector(vec, "gain_two"), unit_two, scale_two)
    branch = grad_hidden.astype(bf16)
    flat.write(dot(mixed, branch, 0, 0), at["w_out"], 3, D)
    sums["b_out"] = column_sums(branch)
    mixed_heads = by_head(dot(branch, w_out[...], 1, 1).astype(bf16).astype(f32)).astype(bf16)
    grad_probs = dot(mixed_heads, v, 1, 1)
    grad_v = dot(probs_low, mixed_heads, 0, 0).astype(bf16)
    inner = jnp.sum(grad_probs * probs, -1, keepdims=True)
    grad_scores = (probs * (grad_probs - inner)).astype(bf16)
    grad_q = (from_heads(dot(grad_scores, k)) * SCALE).astype(bf16)
    grad_k = dot(grad_scores, q_heads, 0, 0).astype(bf16)
    flat.write(dot(top_normed, grad_q, 0, 0), at["w_qkv"], 9, D)
    flat.write(dot(normed, grad_k, 0, 0), at["w_qkv"] + 3, 9, D)
    flat.write(dot(normed, grad_v, 0, 0), at["w_qkv"] + 6, 9, D)
    sums["b_q"], sums["b_v"] = column_sums(grad_q), column_sums(grad_v)
    many[...] = dot(grad_k, w_k[...], 1, 1) + dot(grad_v, w_v[...], 1, 1)
    top_back = dot(grad_q, w_q[...], 1, 1)
    for i in range(per):
        many[i * ROWS + CLS : i * ROWS + CLS + 1, :] += top_back[i : i + 1, :]
    grad_one = many[...]
    sums["gain_one"], sums["bias_one"] = column_sums(grad_one * unit), column_sums(grad_one)
    many[...] = normalise_back(grad_one, vector(vec, "gain_one"), unit, scale)
    for i in range(per):
        many[i * ROWS + CLS : i * ROWS + CLS + 1, :] += grad_hidden[i : i + 1, :]
    back_out[...] = many[...].astype(bf16)
    write_vectors(flat, sums)

    def store(at, value):
        grad_out[at] = value

    send_out(place, flat, store)


def back_kernel(place, per, *refs):
    grad_in, kept, patches, weights = refs[0], refs[1:10], refs[10], refs[11:18]
    late_grad, keep_out, give_out = refs[18:21]
    even, odd, mix, *operands = refs[21:]
    s_normed, s_q, s_k, s_v, s_branch, s_two, s_up = operands
    vec = weights[-1]
    group = group_of(per)
    sums = {}
    embedded = []
    positions = jnp.zeros((ROWS, D), f32)
    for step in range(0, per, group):
        cut = slice(step * ROWS, (step + group) * ROWS)
        vectors, grad_x = back_images(step, cut, grad_in, kept, weights, operands)
        sums = {name: sums[name] + value if sums else value for name, value in vectors.items()}
        for i in range(group):
            embedded.append(grad_x[i * ROWS : i * ROWS + PATCHES].astype(bf16))
            positions = positions + grad_x[i * ROWS : (i + 1) * ROWS]

    at = BLOCK_AT
    flat = Flat(even, odd, mix, place.count * place.shard_rows)
    flat.clear()
    normed = s_normed[...]
    for part, ref in enumerate((s_q, s_k, s_v)):
        flat.write(dot(normed, ref[...], 0, 0), at["w_qkv"] + 3 * part, 9, D)
    flat.write(dot(kept[5][...], s_branch[...], 0, 0), at["w_out"], 3, D)
    flat.write(dot(s_two[...], s_up[...], 0, 0), at["w_up"], 12, FF)
    flat.write(dot(kept[7][...], grad_in[...], 0, 0), at["w_down"], 3, D)
    grad_patch = sum(dot(patches[i], value, 0, 0) for i, value in enumerate(embedded))
    flat.write(grad_patch, W_PATCH, 3, D)
    sums["b_q"], sums["b_v"] = column_sums(s_q[...]), column_sums(s_v[...])
    sums["b_out"], sums["b_up"] = column_sums(s_branch[...]), column_sums(s_up[...])
    sums["b_down"] = column_sums(grad_in[...])
    write_vectors(flat, sums)
    flat.write(sum(column_sums(value) for value in embedded), B_PATCH, 2, D)
    token = positions[CLS : CLS + 1, :]
    flat.write(token, CLS_TOKEN, 2, D)
    natural = jnp.concatenate([token, positions[0:PATCHES, :], jnp.zeros((1, D), f32)], 0)
    flat.write(natural, POS_EMBED, 3, D)

    section = lax.axis_index("section")

    @pl.when(section == 0)
    def _():
        def store(at, value):
            keep_out[at] = value
            give_out[at] = late_grad[at]

        send_out(place, flat, store)

    @pl.when(section != 0)
    def _():
        def store(at, value):
            give_out[at] = value
            keep_out[at] = late_grad[at]

        send_out(place, flat, store)


def back_images(step, cut, grad_in, kept, weights, operands):
    x_in, q_in, k_in, v_in, probs_in, mixed_in, hidden_in, act_in, slope_in = kept
    w_q, w_k, w_v, w_out, w_up, w_down, vec = weights
    s_normed, s_q, s_k, s_v, s_branch, s_two, s_up = operands
    group = (cut.stop - cut.start) // ROWS
    spans = [slice(i * ROWS, (i + 1) * ROWS) for i in range(group)]
    sums = {}
    grad_low = grad_in[cut, :]
    grad_up = (dot(grad_low, w_down[...], 1, 1) * slope_in[cut, :]).astype(bf16)
    s_up[cut, :] = grad_up
    unit, scale = normalise(hidden_in[cut, :])
    s_two[cut, :] = (unit * vector(vec, "gain_two") + vector(vec, "bias_two")).astype(bf16)
    grad_two = dot(grad_up, w_up[...], 1, 1)
    sums["gain_two"], sums["bias_two"] = column_sums(grad_two * unit), column_sums(grad_two)
    grad_hidden = grad_low.astype(f32) + normalise_back(grad_two, vector(vec, "gain_two"), unit, scale)
    branch = grad_hidden.astype(bf16)
    s_branch[cut, :] = branch
    grad_mixed = dot(branch, w_out[...], 1, 1).astype(bf16).astype(f32)
    mixed_heads = [by_head(grad_mixed[at]).astype(bf16) for at in spans]
    q_scaled = q_in[cut, :].astype(f32) * SCALE
    q_heads = [by_head(q_scaled[at]).astype(bf16) for at in spans]
    k, v = k_in[cut, :], v_in[cut, :]
    probs = [
        probs_in[(step + i) * HEADS * ROWS : (step + i + 1) * HEADS * ROWS, :] for i in range(group)
    ]
    grad_probs = [dot(value, v[at], 1, 1) for value, at in zip(mixed_heads, spans)]
    grad_v = [dot(value.astype(bf16), right, 0, 0) for value, right in zip(probs, mixed_heads)]
    inner = [jnp.sum(one * two, -1, keepdims=True) for one, two in zip(grad_probs, probs)]
    grad_scores = [(two * (one - less)).astype(bf16) for one, two, less in zip(grad_probs, probs, inner)]
    grad_q = [from_heads(dot(value, k[at])) * SCALE for value, at in zip(grad_scores, spans)]
    grad_k = [dot(value, right, 0, 0) for value, right in zip(grad_scores, q_heads)]
    grad_q, grad_k, grad_v = [jnp.concatenate(value, 0).astype(bf16) for value in (grad_q, grad_k, grad_v)]
    s_q[cut, :], s_k[cut, :], s_v[cut, :] = grad_q, grad_k, grad_v
    unit, scale = normalise(x_in[cut, :])
    s_normed[cut, :] = (unit * vector(vec, "gain_one") + vector(vec, "bias_one")).astype(bf16)
    grad_one = dot(grad_q, w_q[...], 1, 1) + dot(grad_k, w_k[...], 1, 1) + dot(grad_v, w_v[...], 1, 1)
    sums["gain_one"], sums["bias_one"] = column_sums(grad_one * unit), column_sums(grad_one)
    return sums, grad_hidden + normalise_back(grad_one, vector(vec, "gain_one"), unit, scale)


def fetch_kernel(first, last, _, basis, kept, sem):
    copy = pltpu.make_async_copy(basis.at[pl.ds(first, last - first)], kept, sem)
    copy.start()
    copy.wait()


def add_kernel(left, right, _, __, total):
    total[...] = left[...] + right[...]


def split_kernel(place, keep, given, *outs):
    cut = place.half_rows
    for place_y in range(place.y):
        for place_x in range(place.x):
            for d in range(place.z):
                at = (place_y * place.x + place_x) * place.z + d
                total = keep[at].astype(f32) + given[at].astype(f32)
                one, two = outs[place_y], outs[place.y + place_x]
                one[place_x, d] = total[:cut].astype(one.dtype)
                two[place_y, d] = total[cut:].astype(two.dtype)


def turn_kernel(place, one, two, _, *refs):
    count = place.y + place.x
    arrived, outs = refs[: count - 2], refs[count - 2 :]
    for own, came, parts in (
        (one, arrived[: place.y - 1], outs[: place.x]),
        (two, arrived[place.y - 1 :], outs[place.x :]),
    ):
        for step, out in enumerate(parts):
            for d in range(place.z):
                total = own[step, d]
                for ref in came:
                    total = total + ref[step, d].astype(f32)
                out[d] = total.astype(out.dtype)


def plane_kernel(place, one, two, _, *refs):
    arrived, (whole_out, *outs) = refs[: -place.z], refs[-place.z :]
    for d in range(place.z):
        upper, lower = one[d], two[d]
        for ref in arrived[: place.x - 1]:
            upper = upper + ref[d].astype(f32)
        for ref in arrived[place.x - 1 :]:
            lower = lower + ref[d].astype(f32)
        out = outs[d - 1] if d else whole_out
        out[0 : place.half_rows, :] = upper.astype(out.dtype)
        out[place.half_rows :, :] = lower.astype(out.dtype)


def inner_kernel(blocks, *refs):
    first, pieces, (upper, lower, loss, grad_out, sums_out, total) = refs[0], refs[1:-6], refs[-6:]
    shard_rows = grad_out.shape[0]
    value = first[...]
    for ref in pieces:
        value = value + ref[...].astype(f32)
    grad_out[...] = value[:shard_rows]
    total[...] = jnp.zeros(total.shape, f32)

    def step(i, carry):
        base = i * blocks
        rows = [jnp.broadcast_to(grad_out[pl.ds(base + j, 1), :], (8, LANES)) for j in range(blocks)]
        start = pl.multiple_of(base * LANES, LANES)
        for at in range(0, KB, 16):
            basis, row = (upper, at) if at < UPPER else (lower, at - UPPER)
            part = basis[row : row + 16, pl.ds(start, blocks * LANES)].astype(f32)
            for half in range(0, 16, 8):
                acc = total[at + half : at + half + 8, :]
                for j in range(blocks):
                    acc = acc + part[half : half + 8, j * LANES : (j + 1) * LANES] * rows[j]
                total[at + half : at + half + 8, :] = acc
        return carry

    lax.fori_loop(0, shard_rows // blocks, step, 0)
    coefs = jnp.sum(total[...].T, 0, keepdims=True)
    grad = grad_out[...]
    squares = jnp.sum(jnp.sum(grad * grad, 0, keepdims=True), 1, keepdims=True)
    lane = lax.broadcasted_iota(jnp.int32, (1, SUMS - KB), 1)
    rest = jnp.where(lane == 0, squares, 0.0)
    rest = rest + jnp.where(lane == 1, loss[0:1, 0:1], 0.0) + jnp.where(lane == 2, loss[0:1, 1:2], 0.0)
    sums_out[:, 0:KB] = coefs
    sums_out[:, KB:SUMS] = rest


def update_kernel(blocks, whole_len, counts, sums, upper, lower, grad, loss, master, first, second, *refs):
    loss_out, norm_out, coef_out, master_out, first_out, second_out, removed = refs
    norm = jnp.sqrt(sums[0:1, KB : KB + 1])
    factor = jnp.minimum(1.0, CLIP_NORM / (norm + 1e-06))
    lane = lax.broadcasted_iota(jnp.int32, (1, KB), 1)
    limit = jnp.where(lane < KMAX, counts[0], counts[1] + KMAX)
    row = jnp.where(lane < limit, sums[:, 0:KB] * factor, 0.0)
    coef_out[0:1, :] = row[:, 0:KMAX]
    coef_out[1:2, :] = row[:, KMAX:KB]
    norm_out[0] = jnp.sum(norm)
    loss_out[0] = jnp.sum(sums[0:1, KB + 1 : KB + 2])
    loss_out[1] = jnp.sum(sums[0:1, KB + 2 : KB + 3])
    loss_out[2] = jnp.sum(loss[0:1, 2:3])
    high = row.astype(bf16).astype(f32)
    mid = (row - high).astype(bf16).astype(f32)
    low = row - high - mid
    place = lax.broadcasted_iota(jnp.int32, (16, KB), 0)
    split = jnp.where(place == 0, high, jnp.where(place == 1, mid, jnp.where(place == 2, low, 0.0)))
    split = split.astype(bf16)
    rows = grad.shape[0]

    def step(i, carry):
        base = i * blocks
        start = pl.multiple_of(base * LANES, LANES)
        part = dot(split[:, :UPPER], upper[:, pl.ds(start, blocks * LANES)])
        part = part + dot(split[:, UPPER:], lower[:, pl.ds(start, blocks * LANES)])
        part = jnp.sum(part, 0, keepdims=True)
        for j in range(blocks):
            removed[pl.ds(base + j, 1), :] = part[:, j * LANES : (j + 1) * LANES]
        return carry

    lax.fori_loop(0, rows // blocks, step, 0)
    projected = grad[...] * factor - removed[0:rows, :] * (1.0 / whole_len)
    new_first = BETA_ONE * first[...] + (1.0 - BETA_ONE) * projected
    new_second = BETA_TWO * second[...] + (1.0 - BETA_TWO) * projected * projected
    ratio = (
        new_first
        / (1.0 - BETA_ONE**STEP)
        / (jnp.sqrt(new_second / (1.0 - BETA_TWO**STEP)) + ADAM_EPS)
    )
    old = master[...]
    master_out[...] = old - LEARN_RATE * (ratio + WEIGHT_DECAY * old)
    first_out[...] = new_first
    second_out[...] = new_second


def dp_dims(count):
    zed = 4 if count % 4 == 0 else 1
    plane = count // zed
    ex = max(side for side in range(1, math.isqrt(plane) + 1) if plane % side == 0)
    return zed, plane // ex, ex


def moved(value, place, turn=(0, 0, 0), core=0, pairs_too=False):
    def step(index, by, size):
        return index ^ by if pairs_too and paired(size) else (index + by) % size

    pairs = []
    for section in range(2):
        for zed in range(place.z):
            for why in range(place.y):
                for ex in range(place.x):
                    source = (section * place.z + zed) * place.y * place.x + why * place.x + ex
                    there = ((section + core) % 2) * place.z + step(zed, turn[0], place.z)
                    target = (there * place.y + step(why, turn[1], place.y)) * place.x
                    pairs.append((source, target + step(ex, turn[2], place.x)))
    return lax.ppermute(value, ("section", "dp"), pairs)


def add(left, right, resident):
    vmem = pl.BlockSpec(memory_space=pltpu.VMEM)
    return pl.pallas_call(
        add_kernel,
        in_specs=[vmem, vmem] + [pl.BlockSpec(memory_space=pl.ANY)] * 2,
        out_specs=vmem,
        out_shape=jax.ShapeDtypeStruct(left.shape, left.dtype),
        compiler_params=pltpu.CompilerParams(vmem_limit_bytes=2 * 1024 * 1024),
        name="add",
    )(left, right, *resident)


def butterfly(value, place, resident):
    value = add(value, moved(value, place, core=1), resident)
    for axis, size in ((2, place.x), (1, place.y), (0, place.z)):
        span = 1
        while span < size:
            pairs = []
            for index in range(2 * place.count):
                section, rest = divmod(index, place.count)
                at = [rest // (place.y * place.x), rest // place.x % place.y, rest % place.x]
                at[axis] ^= span
                pairs.append((index, section * place.count + (at[0] * place.y + at[1]) * place.x + at[2]))
            value = add(value, lax.ppermute(value, ("section", "dp"), pairs), resident)
            span *= 2
    return value


def whole(shape):
    return pl.BlockSpec(shape, lambda *_: (0,) * len(shape))


def params(megabytes):
    return pltpu.CompilerParams(
        vmem_limit_bytes=megabytes * 1024 * 1024, dimension_semantics=("arbitrary",)
    )


BLOCK_SHAPES = [(D, D)] * 4 + [(D, FF), (FF, D)]
SAVED = [
    ((ROWS, D), f32),
    ((ROWS, D), bf16),
    ((ROWS, D), bf16),
    ((ROWS, D), bf16),
    ((HEADS * ROWS, ROWS), f32),
    ((ROWS, D), bf16),
    ((ROWS, D), f32),
    ((ROWS, FF), bf16),
    ((ROWS, FF), f32),
]
MIDDLE = ((ROWS, D), bf16)
WORK = pl.CostEstimate(flops=3_000_000_000, bytes_accessed=30_000_000, transcendentals=1_000_000)
VMEM = pl.BlockSpec(memory_space=pltpu.VMEM)
SMEM = pl.BlockSpec(memory_space=pltpu.SMEM)
ANY = pl.BlockSpec(memory_space=pl.ANY)


def group_of(per):
    return GROUP if per % GROUP == 0 else 1


def flat_scratch(place):
    flat_rows = place.count * place.shard_rows + SPARE
    return [
        pltpu.VMEM((flat_rows, LANES), f32),
        pltpu.VMEM((flat_rows, LANES), f32),
        pltpu.VMEM((FF + 32, LANES), f32),
    ]


def front(place, per, own, other, patches):
    outs = pl.pallas_call(
        functools.partial(front_kernel, place, per),
        in_specs=[VMEM] * (len(own) + len(other) + 1),
        out_specs=[VMEM] * (len(SAVED) + 1 + len(BLOCK_SHAPES) + 1),
        out_shape=[
            jax.ShapeDtypeStruct((per * shape[0], shape[1]), kind) for shape, kind in SAVED + [MIDDLE]
        ]
        + [jax.ShapeDtypeStruct(shape, bf16) for shape in BLOCK_SHAPES]
        + [jax.ShapeDtypeStruct((VEC_ROWS, FF), f32)],
        scratch_shapes=flat_scratch(place)
        + [pltpu.VMEM((PDIM, D), bf16), pltpu.VMEM((ROWS, D), f32), pltpu.VMEM((per * ROWS, D), f32)],
        compiler_params=pltpu.CompilerParams(vmem_limit_bytes=20 * 1024 * 1024),
        cost_estimate=WORK,
        name="front",
    )(*own, *other, patches)
    return outs[:9], outs[9], outs[10:]


def grad_kind(place):
    return jax.ShapeDtypeStruct((place.count, place.sent_rows, LANES), bf16)


def late(place, per, image_total, labels, replay, own, other, middle, old_logits):
    eight = -(-per // 8) * 8
    return pl.pallas_call(
        functools.partial(late_kernel, place, per, image_total),
        in_specs=[SMEM] * 2 + [VMEM] * (len(own) + len(other) + 2),
        out_specs=[VMEM] * 3,
        out_shape=[
            jax.ShapeDtypeStruct((per * ROWS, D), bf16),
            grad_kind(place),
            jax.ShapeDtypeStruct((1, LANES), f32),
        ],
        scratch_shapes=flat_scratch(place)
        + [pltpu.VMEM((8, 256, LANES), f32)]
        + [pltpu.VMEM(shape, bf16) for shape in BLOCK_SHAPES]
        + [
            pltpu.VMEM((VEC_ROWS, FF), f32),
            pltpu.VMEM((D, CPAD), bf16),
            pltpu.VMEM((1, CPAD), f32),
            pltpu.VMEM((eight, D), f32),
            pltpu.VMEM((per * ROWS, D), f32),
        ],
        compiler_params=pltpu.CompilerParams(vmem_limit_bytes=16 * 1024 * 1024),
        cost_estimate=WORK,
        name="late",
    )(labels, replay, *own, *other, middle, old_logits)


def back(place, per, grad_middle, kept, patches, weights, late_grad):
    return pl.pallas_call(
        functools.partial(back_kernel, place, per),
        in_specs=[VMEM] * (1 + len(kept) + 1 + len(weights) + 1),
        out_specs=[VMEM] * 2,
        out_shape=[grad_kind(place)] * 2,
        scratch_shapes=flat_scratch(place)
        + [pltpu.VMEM((per * ROWS, D), bf16)] * 6
        + [pltpu.VMEM((per * ROWS, FF), bf16)],
        compiler_params=pltpu.CompilerParams(vmem_limit_bytes=20 * 1024 * 1024),
        cost_estimate=WORK,
        name="back",
    )(grad_middle, *kept, patches, *weights, late_grad)


def body(
    patches, labels, replay, old_logits, basis_count, master, first_moment, second_moment, basis
):
    chips = lax.axis_size("dp")
    shard_len = master.shape[1]
    shard_rows = shard_len // LANES
    place = Place(dp_dims(chips), shard_rows)
    images = patches.shape[0]
    per = images // 2
    section = lax.axis_index("section")
    turns = place.turns()

    shard = pl.pallas_call(
        shard_kernel,
        grid=(1,),
        in_specs=[SMEM, whole((shard_rows, LANES))],
        out_specs=whole((place.sent_rows, LANES)),
        out_shape=jax.ShapeDtypeStruct((place.sent_rows, LANES), bf16),
        compiler_params=pltpu.CompilerParams(vmem_limit_bytes=2 * 1024 * 1024),
        name="shard",
    )(
        pltpu.with_memory_space_constraint(replay, pltpu.HBM),
        pltpu.with_memory_space_constraint(master.reshape(shard_rows, LANES), pltpu.HBM),
    )
    mine = lax.dynamic_slice_in_dim(patches, section * per, per, 0)
    early, late_part = shard[: place.first_rows], shard[place.first_rows :]
    column = [early] + [moved(early, place, (d, 0, 0)) for d in range(1, place.z)]
    plane = [moved(late_part, place, (0, a, b)) if a + b else late_part for a, b in turns]
    column[-1], mine = lax.optimization_barrier((column[-1], mine))
    column, plane = jnp.stack(column), jnp.stack(plane)
    own = [moved(column, place, (0, a, b)) if a + b else column for a, b in turns]
    own += [moved(plane, place, (d, 0, 0)) if d else plane for d in range(place.z)]
    other = [moved(piece, place, core=1) for piece in own]

    kept, middle, weights = front(place, per, own, other, mine)
    grad_middle, late_grad, loss = late(
        place, per, float(images * chips), labels, replay, own, other, middle, old_logits
    )
    keep, give = back(place, per, grad_middle, kept, mine, weights, late_grad)

    given = moved(give, place, core=1)

    def kinds(lead, rows, count):
        shape = (*lead, place.z, rows, LANES)
        return [jax.ShapeDtypeStruct(shape, bf16 if i else f32) for i in range(count)]

    one_rows, two_rows = place.half_rows, place.sent_rows - place.half_rows
    parts = pl.pallas_call(
        functools.partial(split_kernel, place),
        in_specs=[VMEM] * 2,
        out_specs=[VMEM] * (place.y + place.x),
        out_shape=kinds((place.x,), one_rows, place.y) + kinds((place.y,), two_rows, place.x),
        compiler_params=pltpu.CompilerParams(vmem_limit_bytes=12 * 1024 * 1024),
        name="split",
    )(keep, given)
    ones, twos = parts[: place.y], parts[place.y :]
    rows_basis = pltpu.with_memory_space_constraint(basis.reshape(KB, shard_len), pltpu.HBM)

    def fetch(first, last, after):
        return pl.pallas_call(
            functools.partial(fetch_kernel, first, last),
            in_specs=[ANY, ANY],
            out_specs=ANY,
            out_shape=pltpu.VMEM((last - first, shard_len), bf16),
            scratch_shapes=[pltpu.SemaphoreType.DMA],
            compiler_params=pltpu.CompilerParams(vmem_limit_bytes=2 * 1024 * 1024),
            cost_estimate=pl.CostEstimate(
                flops=0, bytes_accessed=4 * (last - first) * shard_len, transcendentals=0
            ),
            name="fetch",
        )(after, rows_basis)

    upper = fetch(0, UPPER, ones[-1])

    def along_y(values):
        return [moved(values[i], place, (0, i, 0), pairs_too=True) for i in range(1, place.y)]

    def along_x(values):
        return [moved(values[i], place, (0, 0, i), pairs_too=True) for i in range(1, place.x)]

    arrived = along_y(ones) + along_x(twos)
    parts = pl.pallas_call(
        functools.partial(turn_kernel, place),
        in_specs=[VMEM, VMEM, ANY] + [VMEM] * len(arrived),
        out_specs=[VMEM] * (place.y + place.x),
        out_shape=kinds((), one_rows, place.x) + kinds((), two_rows, place.y),
        compiler_params=pltpu.CompilerParams(vmem_limit_bytes=2 * 1024 * 1024),
        name="turn",
    )(ones[0], twos[0], upper, *arrived)
    ones, twos = parts[: place.x], parts[place.x :]
    arrived = along_x(ones) + along_y(twos)
    piece_shape = (place.sent_rows, LANES)
    first, *rest = pl.pallas_call(
        functools.partial(plane_kernel, place),
        in_specs=[VMEM, VMEM, ANY] + [VMEM] * len(arrived),
        out_specs=[VMEM] * place.z,
        out_shape=[jax.ShapeDtypeStruct(piece_shape, bf16 if d else f32) for d in range(place.z)],
        compiler_params=pltpu.CompilerParams(vmem_limit_bytes=2 * 1024 * 1024),
        name="plane",
    )(ones[0], twos[0], upper, *arrived)
    resident = (upper, fetch(UPPER, KB, rest[0]))
    pieces = [moved(rest[d - 1], place, (d, 0, 0), pairs_too=True) for d in range(1, place.z)]

    def divisor(most):
        return max(n for n in range(1, most + 1) if shard_rows % n == 0)

    flat_kind = jax.ShapeDtypeStruct((shard_rows, LANES), f32)
    grad, sums = pl.pallas_call(
        functools.partial(inner_kernel, divisor(26)),
        in_specs=[VMEM] * (place.z + 3),
        out_specs=[VMEM] * 2,
        out_shape=[flat_kind, jax.ShapeDtypeStruct((1, SUMS), f32)],
        scratch_shapes=[pltpu.VMEM((KB, LANES), f32)],
        compiler_params=pltpu.CompilerParams(vmem_limit_bytes=2 * 1024 * 1024),
        name="inner",
    )(first, *pieces, *resident, loss)
    sums = butterfly(sums, place, resident)
    padded_rows = -(-shard_rows // 8) * 8
    loss_parts, norm, coefficients, new_master, new_first, new_second = pl.pallas_call(
        functools.partial(update_kernel, divisor(78), float(2 * shard_len * chips)),
        in_specs=[SMEM] + [VMEM] * 8,
        out_specs=[SMEM, SMEM] + [VMEM] * 4,
        out_shape=[
            jax.ShapeDtypeStruct((3,), f32),
            jax.ShapeDtypeStruct((1,), f32),
            jax.ShapeDtypeStruct((TASKS, KMAX), f32),
        ]
        + [flat_kind] * 3,
        scratch_shapes=[pltpu.VMEM((padded_rows, LANES), f32)],
        compiler_params=pltpu.CompilerParams(vmem_limit_bytes=2 * 1024 * 1024),
        name="update",
    )(
        basis_count,
        sums,
        *resident,
        grad,
        loss,
        master.reshape(shard_rows, LANES),
        first_moment.reshape(shard_rows, LANES),
        second_moment.reshape(shard_rows, LANES),
    )
    return (
        loss_parts,
        norm[0],
        coefficients,
        new_master.reshape(1, shard_len),
        new_first.reshape(1, shard_len),
        new_second.reshape(1, shard_len),
    )


def solution(mesh):
    in_specs = (
        P("dp", None, None),
        P("dp"),
        P("dp"),
        P("dp", None),
        P(),
        P("section", "dp"),
        P("section", "dp"),
        P("section", "dp"),
        P(None, "section", "dp"),
    )
    out_specs = (P(), P(), P(), P("section", "dp"), P("section", "dp"), P("section", "dp"))
    return jax.shard_map(body, mesh=mesh, in_specs=in_specs, out_specs=out_specs, check_vma=False)
```

```python
import functools
import math

import jax
import jax.numpy as jnp
from jax import lax
from jax.experimental import pallas as pl
from jax.experimental.pallas import tpu as pltpu
from jax.sharding import PartitionSpec as P

HEADS = 3
HD = 64
D = 192
FF = 768
PDIM = 768
PATCHES = 196
TOKENS = PATCHES + 1
ROWS = 208
CLS = PATCHES
GROUP = 4
CLASSES = 1000
CPAD = 1024
TASKS = 2
KMAX = 200
KB = TASKS * KMAX
UPPER = 256
STEP = 10
LANES = 128
HALF = 64
SPARE = 512
SUMS = 512

NORM_EPS = 1e-06
CLIP_NORM = 0.02
LEARN_RATE = 0.05
BETA_ONE = 0.9
BETA_TWO = 0.999
ADAM_EPS = 1e-08
WEIGHT_DECAY = 0.05
SCALE = HD ** (-0.5)
MASKED = -1e30

BLOCK_AT = dict(
    gain_one=0,
    bias_one=3,
    w_qkv=6,
    b_qkv=1734,
    w_out=1740,
    b_out=2316,
    gain_two=2319,
    bias_two=2322,
    w_up=2325,
    b_up=4629,
    w_down=4641,
    b_down=6945,
)
W_PATCH, B_PATCH, CLS_TOKEN, POS_EMBED = 6948, 9252, 9255, 9258
GAIN_LAST, BIAS_LAST, W_HEAD, B_HEAD = 6948, 6951, 6954, 9954
VECTORS = ("gain_one", "bias_one", "b_q", "b_v", "b_out", "gain_two", "bias_two", "b_up", "b_down")
VEC_ROWS = 16

f32 = jnp.float32
bf16 = jnp.bfloat16


def dot(left, right, left_dim=1, right_dim=0):
    return lax.dot_general(
        left, right, (((left_dim,), (right_dim,)), ((), ())), preferred_element_type=f32
    )


def low_lanes(shape):
    return lax.broadcasted_iota(jnp.int32, shape, 1) < HALF


def swap_halves(value):
    return pltpu.roll(value, HALF, 1)


def head_masks():
    lane = lax.broadcasted_iota(jnp.int32, (1, D), 1)
    return [jnp.logical_and(lane >= h * HD, lane < (h + 1) * HD) for h in range(HEADS)]


def by_head(value):
    return jnp.concatenate([jnp.where(m, value, 0.0) for m in head_masks()], 0)


def from_heads(value):
    rows = value.shape[0] // HEADS
    parts = [value[h * rows : (h + 1) * rows] for h in range(HEADS)]
    masks = head_masks()
    return jnp.where(masks[0], parts[0], jnp.where(masks[1], parts[1], parts[2]))


def normalise(rows_in):
    mean = jnp.sum(rows_in, -1, keepdims=True) * (1.0 / D)
    centred = rows_in - mean
    variance = jnp.sum(centred * centred, -1, keepdims=True) * (1.0 / D)
    scale = lax.rsqrt(variance + NORM_EPS)
    return centred * scale, scale


def normalise_back(grad, gain, unit, scale):
    grad_unit = grad * gain
    first = jnp.sum(grad_unit, -1, keepdims=True) * (1.0 / D)
    second = jnp.sum(grad_unit * unit, -1, keepdims=True) * (1.0 / D)
    return scale * (grad_unit - first - unit * second)


def gelu_parts(pre):
    cdf = 0.5 * (1.0 + lax.erf(pre * math.sqrt(0.5)))
    slope = cdf + pre * (jnp.exp(-0.5 * pre * pre) * (1.0 / math.sqrt(2.0 * math.pi)))
    return pre * cdf, slope


def column_sums(value):
    return jnp.sum(value.astype(f32), 0, keepdims=True)


def strided(ref, start, count, stride):
    if count == 1 or stride == 1:
        return ref[pl.ds(start, count), :]
    return ref[pl.ds(start, count, stride=stride), :]


class Flat:
    def __init__(self, even, odd, mix, rows):
        self.even, self.odd, self.mix, self.rows = even, odd, mix, rows

    def shift(self):
        step = 192
        for at in range(0, self.rows, step):
            here = self.even[at : at + step, :]
            after = self.even[at + 1 : at + 1 + step, :]
            self.odd[at : at + step, :] = swap_halves(jnp.where(low_lanes(here.shape), after, here))

    def rows_at(self, half, count, stride):
        return strided(self.odd if half % 2 else self.even, half // 2, count, stride)

    def blocks(self, half, width, rows, cols):
        for at in range(0, cols, LANES):
            start = half + at // HALF
            if rows == 1 or width % 2 == 0:
                value = self.rows_at(start, rows, width // 2)
            else:
                pairs = (rows + 1) // 2
                self.mix[pl.ds(0, pairs, stride=2), :] = self.rows_at(start, pairs, width)
                self.mix[pl.ds(1, pairs, stride=2), :] = self.rows_at(start + width, pairs, width)
                value = self.mix[0:rows, :]
            yield at, min(LANES, cols - at), value

    def read(self, dest, half, width, rows, cols):
        for at, wide, value in self.blocks(half, width, rows, cols):
            dest[0:rows, at : at + wide] = value[:, :wide].astype(dest.dtype)

    def read_row(self, dest, row, half, cols):
        for at, wide, value in self.blocks(half, 2, 1, cols):
            dest[row : row + 1, at : at + wide] = value[:, :wide]

    def clear(self):
        self.even[...] = jnp.zeros(self.even.shape, f32)
        self.odd[...] = jnp.zeros(self.odd.shape, f32)

    def put_rows(self, half, count, stride, value):
        ref, start = (self.odd, half // 2 + 8) if half % 2 else (self.even, half // 2)
        if count == 1 or stride == 1:
            ref[pl.ds(start, count), :] = value
        else:
            ref[pl.ds(start, count, stride=stride), :] = value

    def write(self, value, half, width, cols):
        rows = value.shape[0]
        for at in range(0, cols, LANES):
            wide = min(LANES, cols - at)
            part = value[:, at : at + wide]
            if wide < LANES:
                part = jnp.concatenate([part, jnp.zeros((rows, LANES - wide), f32)], 1)
            start = half + at // HALF
            if rows == 1 or width % 2 == 0:
                self.put_rows(start, rows, width // 2, part)
            else:
                pairs = (rows + 1) // 2
                self.mix[0:rows, :] = part
                self.put_rows(start, pairs, width, self.mix[pl.ds(0, pairs, stride=2), :])
                self.put_rows(start + width, pairs, width, self.mix[pl.ds(1, pairs, stride=2), :])

    def merged(self, at, count):
        here = self.odd[at + 8 : at + 8 + count, :]
        before = self.odd[at + 7 : at + 7 + count, :]
        moved_back = swap_halves(jnp.where(low_lanes(here.shape), here, before))
        return self.even[at : at + count, :] + moved_back


def paired(size):
    return size & (size - 1) == 0


class Place:
    def __init__(self, dims, shard_rows):
        self.z, self.y, self.x = dims
        self.count = self.z * self.y * self.x
        self.shard_rows = shard_rows
        self.sent_rows = -(-(shard_rows + 1) // 16) * 16
        self.first_rows = self.sent_rows * 13 // 20 // 16 * 16

        self.half_rows = self.sent_rows // 32 * 16

    def split(self, index):
        plane = self.y * self.x
        return index // plane, lax.rem(index, plane) // self.x, lax.rem(index, self.x)

    def turns(self):
        return [(a, b) for a in range(self.y) for b in range(self.x)]


def load_section(place, pieces, wanted, flat):
    own, other = pieces
    section = lax.axis_index("section")
    zed, why, ex = place.split(lax.axis_index("dp"))
    rows = place.shard_rows

    def copy(refs):
        for turn, (a, b) in enumerate(place.turns()):
            for d in range(place.z):
                shard = lax.rem(zed + (place.z - d), place.z) * (place.y * place.x)
                shard = shard + lax.rem(why + (place.y - a), place.y) * place.x
                shard = shard + lax.rem(ex + (place.x - b), place.x)
                start = shard * rows
                if rows % 8 == 0:
                    start = pl.multiple_of(start, 8)
                cut = place.first_rows
                flat.even[pl.ds(start, cut), :] = refs[turn][d].astype(f32)
                value = refs[len(place.turns()) + d][turn].astype(f32)
                after = start + cut
                if rows % 8 == 0:
                    after = pl.multiple_of(after, 8)
                flat.even[pl.ds(after, rows - cut), :] = value[: rows - cut]

    @pl.when(section == wanted)
    def _():
        copy(own)

    @pl.when(section != wanted)
    def _():
        copy(other)

    flat.shift()


def read_block(flat, weights, vec):
    at = BLOCK_AT
    w_q, w_k, w_v, w_out, w_up, w_down = weights
    for place, dest in enumerate((w_q, w_k, w_v)):
        flat.read(dest, at["w_qkv"] + 3 * place, 9, D, D)
    flat.read(w_out, at["w_out"], 3, D, D)
    flat.read(w_up, at["w_up"], 12, D, FF)
    flat.read(w_down, at["w_down"], 3, FF, D)
    starts = dict(at, b_q=at["b_qkv"], b_v=at["b_qkv"] + 3)
    for row, name in enumerate(VECTORS):
        flat.read_row(vec, row, starts[name], FF if name == "b_up" else D)


def vector(vec, name):
    row = VECTORS.index(name)
    return vec[row : row + 1, 0 : FF if name == "b_up" else D]


def write_vectors(flat, sums):
    at = BLOCK_AT
    starts = dict(at, b_q=at["b_qkv"], b_v=at["b_qkv"] + 3)
    for name, value in sums.items():
        flat.write(value, starts[name], 2, value.shape[1])


def send_out(place, flat, write):
    zed, why, ex = place.split(lax.axis_index("dp"))
    rows, spare = place.shard_rows, place.sent_rows - place.shard_rows
    for shard in range(place.count):
        zk, yk, xk = shard // (place.y * place.x), shard // place.x % place.y, shard % place.x
        there = ((zk, zed, place.z), (yk, why, place.y), (xk, ex, place.x))
        d, a, b = [to ^ at if paired(size) else lax.rem(to + size - at, size) for to, at, size in there]
        value = flat.merged(shard * rows, rows)
        value = jnp.concatenate([value, jnp.zeros((spare, LANES), f32)], 0)
        write((a * place.x + b) * place.z + d, value.astype(bf16))


def shard_kernel(replay, master, out):
    rows = master.shape[0]
    count = sum(replay[i].astype(f32) for i in range(replay.shape[0]))
    tail = jnp.full((out.shape[0] - rows, LANES), count, f32)
    out[...] = jnp.concatenate([master[...], tail], 0).astype(bf16)


def front_kernel(place, per, *refs):
    parts = len(place.turns()) + place.z
    own, other, refs = refs[:parts], refs[parts : 2 * parts], refs[2 * parts :]
    patches, kept, middle_out, weights = refs[0], refs[1:10], refs[10], refs[11:18]
    even, odd, mix, w_patch, added, tokens = refs[18:]
    vec = weights[-1]
    flat = Flat(even, odd, mix, place.count * place.shard_rows)
    load_section(place, (own, other), 0, flat)
    read_block(flat, weights[:-1], vec)
    flat.read(w_patch, W_PATCH, 3, PDIM, D)
    flat.read_row(vec, 9, B_PATCH, D)
    flat.read_row(vec, 10, CLS_TOKEN, D)
    added[...] = jnp.zeros(added.shape, f32)
    tokens[...] = jnp.zeros(tokens.shape, f32)
    for at, wide, value in flat.blocks(POS_EMBED, 3, TOKENS + 1, D):
        added[0:PATCHES, at : at + wide] = value[1:TOKENS, :wide] + vec[9:10, at : at + wide]
        added[CLS : CLS + 1, at : at + wide] = value[0:1, :wide] + vec[10:11, at : at + wide]
    group = group_of(per)
    for step in range(0, per, group):
        cut = slice(step * ROWS, (step + group) * ROWS)
        front_images(step, cut, patches, kept, middle_out, weights, w_patch, added, tokens)


def front_images(step, cut, patches, kept, middle_out, weights, w_patch, added, tokens):
    x_out, q_out, k_out, v_out, probs_out, mixed_out, hidden_out, act_out, slope_out = kept
    w_q, w_k, w_v, w_out, w_up, w_down, vec = weights
    group = (cut.stop - cut.start) // ROWS
    spans = [slice(i * ROWS, (i + 1) * ROWS) for i in range(group)]
    for i, at in enumerate(spans):
        tokens[cut.start + at.start : cut.start + at.start + PATCHES, :] = dot(patches[step + i], w_patch[...])
    x = tokens[cut, :] + jnp.concatenate([added[...]] * group, 0)
    x_out[cut, :] = x
    unit, _ = normalise(x)
    normed = (unit * vector(vec, "gain_one") + vector(vec, "bias_one")).astype(bf16)
    q = (dot(normed, w_q[...]) + vector(vec, "b_q")).astype(bf16)
    k = dot(normed, w_k[...]).astype(bf16)
    v = (dot(normed, w_v[...]) + vector(vec, "b_v")).astype(bf16)
    q_out[cut, :], k_out[cut, :], v_out[cut, :] = q, k, v
    q_scaled = q.astype(f32) * SCALE
    column = lax.broadcasted_iota(jnp.int32, (1, ROWS), 1)
    scores = [dot(by_head(q_scaled[at]).astype(bf16), k[at], 1, 1) for at in spans]
    scores = [jnp.where(column < TOKENS, value, MASKED) for value in scores]
    raised = [jnp.exp(value - jnp.max(value, -1, keepdims=True)) for value in scores]
    probs = [value * (1.0 / jnp.sum(value, -1, keepdims=True)) for value in raised]
    for i, value in enumerate(probs):
        probs_out[(step + i) * HEADS * ROWS : (step + i + 1) * HEADS * ROWS, :] = value
    mixed = [from_heads(dot(value.astype(bf16), v[at])) for value, at in zip(probs, spans)]
    mixed = jnp.concatenate(mixed, 0).astype(bf16)
    mixed_out[cut, :] = mixed
    hidden = x + dot(mixed, w_out[...]) + vector(vec, "b_out")
    hidden_out[cut, :] = hidden
    unit, _ = normalise(hidden)
    normed = (unit * vector(vec, "gain_two") + vector(vec, "bias_two")).astype(bf16)
    pre = dot(normed, w_up[...]) + vector(vec, "b_up")
    act, slope = gelu_parts(pre)
    act = act.astype(bf16)
    act_out[cut, :], slope_out[cut, :] = act, slope
    middle = hidden + dot(act, w_down[...]) + vector(vec, "b_down")
    middle_out[cut, :] = middle.astype(bf16)


def read_head(flat, wide, w_head, b_head):
    first = W_HEAD // 2
    lane = lax.broadcasted_iota(jnp.int32, (16, LANES), 1)
    for phase in range(16):
        start, off = first + CLASSES * phase // LANES, CLASSES * phase % LANES
        got = [strided(flat.even, start + j, 16, 125) for j in range(9 if off else 8)]
        if off:
            got = [pltpu.roll(g, LANES - off, 1) for g in got]
        for j in range(8):
            value = jnp.where(lane < LANES - off, got[j], got[j + 1]) if off else got[j]
            wide[j, pl.ds(phase, 16, stride=16), :] = value
    lane = lax.broadcasted_iota(jnp.int32, (1, LANES), 1)
    for j in range(8):
        keep = lane + j * LANES < CLASSES
        w_head[:, j * LANES : (j + 1) * LANES] = jnp.where(keep, wide[j, 0:D, :], 0.0).astype(bf16)
        value = flat.even[B_HEAD // 2 + j : B_HEAD // 2 + j + 1, :]
        b_head[0:1, j * LANES : (j + 1) * LANES] = jnp.where(keep, value, 0.0)


def write_head(flat, wide, grad_w, grad_b):
    first = W_HEAD // 2
    for j in range(8):
        wide[j, 0:D, :] = grad_w[:, j * LANES : (j + 1) * LANES]
        wide[j, D:, :] = jnp.zeros((wide.shape[1] - D, LANES), f32)
    lane = lax.broadcasted_iota(jnp.int32, (16, LANES), 1)
    for phase in range(16):
        start, off = first + CLASSES * phase // LANES, CLASSES * phase % LANES
        got = [wide[j, pl.ds(phase, 16, stride=16), :] for j in range(8)]
        if off:
            got = [pltpu.roll(g, off, 1) for g in got]
        for j in range(9 if off else 8):
            if not off:
                value = got[j]
            else:
                before = got[j - 1] if j else jnp.zeros((16, LANES), f32)
                value = jnp.where(lane < off, before, got[j] if j < 8 else 0.0)
            flat.even[pl.ds(start + j, 16, stride=125), :] += value
    for j in range(8):
        row = B_HEAD // 2 + j
        flat.even[row : row + 1, :] += grad_b[:, j * LANES : (j + 1) * LANES]


def late_kernel(place, per, image_total, labels, replay, *refs):
    section = lax.axis_index("section")
    parts = len(place.turns()) + place.z
    own, other, refs = refs[:parts], refs[parts : 2 * parts], refs[2 * parts :]
    middle, old_logits, back_out, grad_out, loss_out = refs[:5]
    even, odd, mix, wide, w_q, w_k, w_v, w_out, w_up, w_down, vec, w_head, b_head, few, many = refs[5:]
    flat = Flat(even, odd, mix, place.count * place.shard_rows)
    load_section(place, (own, other), 1, flat)
    read_block(flat, (w_q, w_k, w_v, w_out, w_up, w_down), vec)
    flat.read_row(vec, 9, GAIN_LAST, D)
    flat.read_row(vec, 10, BIAS_LAST, D)
    read_head(flat, wide, w_head, b_head)
    gain_last, bias_last = vec[9:10, 0:D], vec[10:11, 0:D]
    carried = jnp.zeros((1, LANES), f32)
    carrier = place.shard_rows - place.first_rows
    for ref in own[len(place.turns()) :]:
        for turn in range(len(place.turns())):
            carried = carried + ref[turn].astype(f32)[carrier : carrier + 1]
    replay_count = carried[:, 0:1]

    x = middle[...].astype(f32)
    unit, scale = normalise(x)
    normed_f = unit * vector(vec, "gain_one") + vector(vec, "bias_one")
    normed = normed_f.astype(bf16)
    k = dot(normed, w_k[...]).astype(bf16)
    v = (dot(normed, w_v[...]) + vector(vec, "b_v")).astype(bf16)

    def class_rows(value):
        few[...] = jnp.zeros(few.shape, f32)
        for i in range(per):
            few[i : i + 1, :] = value[i * ROWS + CLS : i * ROWS + CLS + 1, :]
        return few[...]

    eight = few.shape[0]
    image = lax.broadcasted_iota(jnp.int32, (eight, 1), 0)
    real = image < per
    x_top = class_rows(x)
    top_normed = class_rows(normed_f).astype(bf16)
    q = (dot(top_normed, w_q[...]) + vector(vec, "b_q")).astype(bf16)
    q_heads = by_head(jnp.where(real, q.astype(f32) * SCALE, 0.0)).astype(bf16)
    scores = dot(q_heads, k, 1, 1)
    column = lax.broadcasted_iota(jnp.int32, scores.shape, 1)
    owner = lax.rem(lax.broadcasted_iota(jnp.int32, scores.shape, 0), eight) * ROWS
    inside = jnp.logical_and(column >= owner, column < owner + TOKENS)
    scores = jnp.where(inside, scores, MASKED)
    raised = jnp.where(inside, jnp.exp(scores - jnp.max(scores, -1, keepdims=True)), 0.0)
    total = jnp.sum(raised, -1, keepdims=True)
    probs = raised * (1.0 / jnp.where(total > 0.0, total, 1.0))
    probs_low = probs.astype(bf16)
    mixed = from_heads(dot(probs_low, v)).astype(bf16)
    hidden = x_top + dot(mixed, w_out[...]) + vector(vec, "b_out")
    unit_two, scale_two = normalise(hidden)
    normed_two = (unit_two * vector(vec, "gain_two") + vector(vec, "bias_two")).astype(bf16)
    act, slope = gelu_parts(dot(normed_two, w_up[...]) + vector(vec, "b_up"))
    act = act.astype(bf16)
    final = hidden + dot(act, w_down[...]) + vector(vec, "b_down")

    unit_last, scale_last = normalise(final)
    top = (unit_last * gain_last + bias_last).astype(bf16)
    classes = lax.broadcasted_iota(jnp.int32, (eight, CPAD), 1)
    logits = dot(top, w_head[...]) + b_head[...]
    logits = jnp.where(classes < CLASSES, logits, MASKED)
    highest = jnp.max(logits, -1, keepdims=True)
    log_total = highest + jnp.log(jnp.sum(jnp.exp(logits - highest), -1, keepdims=True))
    label = jnp.zeros((eight, 1), jnp.int32)
    again = jnp.zeros((eight, 1), f32)
    for i in range(per):
        label = jnp.where(image == i, labels[section * per + i], label)
        again = jnp.where(image == i, replay[section * per + i].astype(f32), again)
    picked = jnp.logical_and(classes == label, real)
    entropy = jnp.where(real, log_total, 0.0) - jnp.sum(jnp.where(picked, logits, 0.0), -1, keepdims=True)
    wanted = jnp.where(section == 0, old_logits[0:per, :], old_logits[per : 2 * per, :])
    if per < eight:
        wanted = jnp.concatenate([wanted, jnp.zeros((eight - per, CLASSES), f32)], 0)
    wanted = jnp.concatenate([wanted, jnp.zeros((eight, CPAD - CLASSES), f32)], 1)
    distance = jnp.where(jnp.logical_and(classes < CLASSES, real), logits - wanted, 0.0)
    squares = again * (jnp.sum(distance * distance, -1, keepdims=True) * (1.0 / CLASSES))
    lane = lax.broadcasted_iota(jnp.int32, (1, LANES), 1)
    entropy_sum = jnp.sum(entropy, 0, keepdims=True)
    replay_sum = jnp.sum(squares, 0, keepdims=True)
    loss_out[...] = jnp.where(lane == 0, entropy_sum, jnp.where(lane == 1, replay_sum, replay_count))

    grad = (jnp.exp(logits - log_total) - jnp.where(picked, 1.0, 0.0)) * (1.0 / image_total)
    grad = grad + again * 2.0 * distance / (CLASSES * replay_count)
    grad = jnp.where(jnp.logical_and(classes < CLASSES, real), grad, 0.0)
    grad_low = grad.astype(bf16)
    flat.clear()
    write_head(flat, wide, dot(top, grad_low, 0, 0), column_sums(grad_low))
    sums = {}
    grad = dot(grad_low, w_head[...], 1, 1)
    flat.write(column_sums(grad * unit_last), GAIN_LAST, 2, D)
    flat.write(column_sums(grad), BIAS_LAST, 2, D)
    grad = normalise_back(grad, gain_last, unit_last, scale_last)

    at = BLOCK_AT
    grad_down = grad.astype(bf16)
    flat.write(dot(act, grad_down, 0, 0), at["w_down"], 3, D)
    sums["b_down"] = column_sums(grad_down)
    grad_up = (dot(grad_down, w_down[...], 1, 1) * slope).astype(bf16)
    flat.write(dot(normed_two, grad_up, 0, 0), at["w_up"], 12, FF)
    sums["b_up"] = column_sums(grad_up)
    grad_two = dot(grad_up, w_up[...], 1, 1)
    sums["gain_two"], sums["bias_two"] = column_sums(grad_two * unit_two), column_sums(grad_two)
    grad_hidden = grad + normalise_back(grad_two, vector(vec, "gain_two"), unit_two, scale_two)
    branch = grad_hidden.astype(bf16)
    flat.write(dot(mixed, branch, 0, 0), at["w_out"], 3, D)
    sums["b_out"] = column_sums(branch)
    mixed_heads = by_head(dot(branch, w_out[...], 1, 1).astype(bf16).astype(f32)).astype(bf16)
    grad_probs = dot(mixed_heads, v, 1, 1)
    grad_v = dot(probs_low, mixed_heads, 0, 0).astype(bf16)
    inner = jnp.sum(grad_probs * probs, -1, keepdims=True)
    grad_scores = (probs * (grad_probs - inner)).astype(bf16)
    grad_q = (from_heads(dot(grad_scores, k)) * SCALE).astype(bf16)
    grad_k = dot(grad_scores, q_heads, 0, 0).astype(bf16)
    flat.write(dot(top_normed, grad_q, 0, 0), at["w_qkv"], 9, D)
    flat.write(dot(normed, grad_k, 0, 0), at["w_qkv"] + 3, 9, D)
    flat.write(dot(normed, grad_v, 0, 0), at["w_qkv"] + 6, 9, D)
    sums["b_q"], sums["b_v"] = column_sums(grad_q), column_sums(grad_v)
    many[...] = dot(grad_k, w_k[...], 1, 1) + dot(grad_v, w_v[...], 1, 1)
    top_back = dot(grad_q, w_q[...], 1, 1)
    for i in range(per):
        many[i * ROWS + CLS : i * ROWS + CLS + 1, :] += top_back[i : i + 1, :]
    grad_one = many[...]
    sums["gain_one"], sums["bias_one"] = column_sums(grad_one * unit), column_sums(grad_one)
    many[...] = normalise_back(grad_one, vector(vec, "gain_one"), unit, scale)
    for i in range(per):
        many[i * ROWS + CLS : i * ROWS + CLS + 1, :] += grad_hidden[i : i + 1, :]
    back_out[...] = many[...].astype(bf16)
    write_vectors(flat, sums)

    def store(at, value):
        grad_out[at] = value

    send_out(place, flat, store)


def back_kernel(place, per, *refs):
    grad_in, kept, patches, weights = refs[0], refs[1:10], refs[10], refs[11:18]
    late_grad, keep_out, give_out = refs[18:21]
    even, odd, mix, *operands = refs[21:]
    s_normed, s_q, s_k, s_v, s_branch, s_two, s_up = operands
    vec = weights[-1]
    group = group_of(per)
    sums = {}
    embedded = []
    positions = jnp.zeros((ROWS, D), f32)
    for step in range(0, per, group):
        cut = slice(step * ROWS, (step + group) * ROWS)
        vectors, grad_x = back_images(step, cut, grad_in, kept, weights, operands)
        sums = {name: sums[name] + value if sums else value for name, value in vectors.items()}
        for i in range(group):
            embedded.append(grad_x[i * ROWS : i * ROWS + PATCHES].astype(bf16))
            positions = positions + grad_x[i * ROWS : (i + 1) * ROWS]

    at = BLOCK_AT
    flat = Flat(even, odd, mix, place.count * place.shard_rows)
    flat.clear()
    normed = s_normed[...]
    for part, ref in enumerate((s_q, s_k, s_v)):
        flat.write(dot(normed, ref[...], 0, 0), at["w_qkv"] + 3 * part, 9, D)
    flat.write(dot(kept[5][...], s_branch[...], 0, 0), at["w_out"], 3, D)
    flat.write(dot(s_two[...], s_up[...], 0, 0), at["w_up"], 12, FF)
    flat.write(dot(kept[7][...], grad_in[...], 0, 0), at["w_down"], 3, D)
    grad_patch = sum(dot(patches[i], value, 0, 0) for i, value in enumerate(embedded))
    flat.write(grad_patch, W_PATCH, 3, D)
    sums["b_q"], sums["b_v"] = column_sums(s_q[...]), column_sums(s_v[...])
    sums["b_out"], sums["b_up"] = column_sums(s_branch[...]), column_sums(s_up[...])
    sums["b_down"] = column_sums(grad_in[...])
    write_vectors(flat, sums)
    flat.write(sum(column_sums(value) for value in embedded), B_PATCH, 2, D)
    token = positions[CLS : CLS + 1, :]
    flat.write(token, CLS_TOKEN, 2, D)
    natural = jnp.concatenate([token, positions[0:PATCHES, :], jnp.zeros((1, D), f32)], 0)
    flat.write(natural, POS_EMBED, 3, D)

    section = lax.axis_index("section")

    @pl.when(section == 0)
    def _():
        def store(at, value):
            keep_out[at] = value
            give_out[at] = late_grad[at]

        send_out(place, flat, store)

    @pl.when(section != 0)
    def _():
        def store(at, value):
            give_out[at] = value
            keep_out[at] = late_grad[at]

        send_out(place, flat, store)


def back_images(step, cut, grad_in, kept, weights, operands):
    x_in, q_in, k_in, v_in, probs_in, mixed_in, hidden_in, act_in, slope_in = kept
    w_q, w_k, w_v, w_out, w_up, w_down, vec = weights
    s_normed, s_q, s_k, s_v, s_branch, s_two, s_up = operands
    group = (cut.stop - cut.start) // ROWS
    spans = [slice(i * ROWS, (i + 1) * ROWS) for i in range(group)]
    sums = {}
    grad_low = grad_in[cut, :]
    grad_up = (dot(grad_low, w_down[...], 1, 1) * slope_in[cut, :]).astype(bf16)
    s_up[cut, :] = grad_up
    unit, scale = normalise(hidden_in[cut, :])
    s_two[cut, :] = (unit * vector(vec, "gain_two") + vector(vec, "bias_two")).astype(bf16)
    grad_two = dot(grad_up, w_up[...], 1, 1)
    sums["gain_two"], sums["bias_two"] = column_sums(grad_two * unit), column_sums(grad_two)
    grad_hidden = grad_low.astype(f32) + normalise_back(grad_two, vector(vec, "gain_two"), unit, scale)
    branch = grad_hidden.astype(bf16)
    s_branch[cut, :] = branch
    grad_mixed = dot(branch, w_out[...], 1, 1).astype(bf16).astype(f32)
    mixed_heads = [by_head(grad_mixed[at]).astype(bf16) for at in spans]
    q_scaled = q_in[cut, :].astype(f32) * SCALE
    q_heads = [by_head(q_scaled[at]).astype(bf16) for at in spans]
    k, v = k_in[cut, :], v_in[cut, :]
    probs = [
        probs_in[(step + i) * HEADS * ROWS : (step + i + 1) * HEADS * ROWS, :] for i in range(group)
    ]
    grad_probs = [dot(value, v[at], 1, 1) for value, at in zip(mixed_heads, spans)]
    grad_v = [dot(value.astype(bf16), right, 0, 0) for value, right in zip(probs, mixed_heads)]
    inner = [jnp.sum(one * two, -1, keepdims=True) for one, two in zip(grad_probs, probs)]
    grad_scores = [(two * (one - less)).astype(bf16) for one, two, less in zip(grad_probs, probs, inner)]
    grad_q = [from_heads(dot(value, k[at])) * SCALE for value, at in zip(grad_scores, spans)]
    grad_k = [dot(value, right, 0, 0) for value, right in zip(grad_scores, q_heads)]
    grad_q, grad_k, grad_v = [jnp.concatenate(value, 0).astype(bf16) for value in (grad_q, grad_k, grad_v)]
    s_q[cut, :], s_k[cut, :], s_v[cut, :] = grad_q, grad_k, grad_v
    unit, scale = normalise(x_in[cut, :])
    s_normed[cut, :] = (unit * vector(vec, "gain_one") + vector(vec, "bias_one")).astype(bf16)
    grad_one = dot(grad_q, w_q[...], 1, 1) + dot(grad_k, w_k[...], 1, 1) + dot(grad_v, w_v[...], 1, 1)
    sums["gain_one"], sums["bias_one"] = column_sums(grad_one * unit), column_sums(grad_one)
    return sums, grad_hidden + normalise_back(grad_one, vector(vec, "gain_one"), unit, scale)


def fetch_kernel(first, last, _, basis, kept, sem):
    copy = pltpu.make_async_copy(basis.at[pl.ds(first, last - first)], kept, sem)
    copy.start()
    copy.wait()


def add_kernel(left, right, _, __, total):
    total[...] = left[...] + right[...]


def split_kernel(place, keep, given, *outs):
    cut = place.half_rows
    for place_y in range(place.y):
        for place_x in range(place.x):
            for d in range(place.z):
                at = (place_y * place.x + place_x) * place.z + d
                total = keep[at].astype(f32) + given[at].astype(f32)
                one, two = outs[place_y], outs[place.y + place_x]
                one[place_x, d] = total[:cut].astype(one.dtype)
                two[place_y, d] = total[cut:].astype(two.dtype)


def turn_kernel(place, one, two, _, *refs):
    count = place.y + place.x
    arrived, outs = refs[: count - 2], refs[count - 2 :]
    for own, came, parts in (
        (one, arrived[: place.y - 1], outs[: place.x]),
        (two, arrived[place.y - 1 :], outs[place.x :]),
    ):
        for step, out in enumerate(parts):
            for d in range(place.z):
                total = own[step, d]
                for ref in came:
                    total = total + ref[step, d].astype(f32)
                out[d] = total.astype(out.dtype)


def plane_kernel(place, one, two, _, *refs):
    arrived, (whole_out, *outs) = refs[: -place.z], refs[-place.z :]
    for d in range(place.z):
        upper, lower = one[d], two[d]
        for ref in arrived[: place.x - 1]:
            upper = upper + ref[d].astype(f32)
        for ref in arrived[place.x - 1 :]:
            lower = lower + ref[d].astype(f32)
        out = outs[d - 1] if d else whole_out
        out[0 : place.half_rows, :] = upper.astype(out.dtype)
        out[place.half_rows :, :] = lower.astype(out.dtype)


def inner_kernel(blocks, *refs):
    first, pieces, (upper, lower, loss, grad_out, sums_out, total) = refs[0], refs[1:-6], refs[-6:]
    shard_rows = grad_out.shape[0]
    value = first[...]
    for ref in pieces:
        value = value + ref[...].astype(f32)
    grad_out[...] = value[:shard_rows]
    total[...] = jnp.zeros(total.shape, f32)

    def step(i, carry):
        base = i * blocks
        rows = [jnp.broadcast_to(grad_out[pl.ds(base + j, 1), :], (8, LANES)) for j in range(blocks)]
        start = pl.multiple_of(base * LANES, LANES)
        for at in range(0, KB, 16):
            basis, row = (upper, at) if at < UPPER else (lower, at - UPPER)
            part = basis[row : row + 16, pl.ds(start, blocks * LANES)].astype(f32)
            for half in range(0, 16, 8):
                acc = total[at + half : at + half + 8, :]
                for j in range(blocks):
                    acc = acc + part[half : half + 8, j * LANES : (j + 1) * LANES] * rows[j]
                total[at + half : at + half + 8, :] = acc
        return carry

    lax.fori_loop(0, shard_rows // blocks, step, 0)
    coefs = jnp.sum(total[...].T, 0, keepdims=True)
    grad = grad_out[...]
    squares = jnp.sum(jnp.sum(grad * grad, 0, keepdims=True), 1, keepdims=True)
    lane = lax.broadcasted_iota(jnp.int32, (1, SUMS - KB), 1)
    rest = jnp.where(lane == 0, squares, 0.0)
    rest = rest + jnp.where(lane == 1, loss[0:1, 0:1], 0.0) + jnp.where(lane == 2, loss[0:1, 1:2], 0.0)
    sums_out[:, 0:KB] = coefs
    sums_out[:, KB:SUMS] = rest


def update_kernel(blocks, whole_len, counts, sums, upper, lower, grad, loss, master, first, second, *refs):
    loss_out, norm_out, coef_out, master_out, first_out, second_out, removed = refs
    norm = jnp.sqrt(sums[0:1, KB : KB + 1])
    factor = jnp.minimum(1.0, CLIP_NORM / (norm + 1e-06))
    lane = lax.broadcasted_iota(jnp.int32, (1, KB), 1)
    limit = jnp.where(lane < KMAX, counts[0], counts[1] + KMAX)
    row = jnp.where(lane < limit, sums[:, 0:KB] * factor, 0.0)
    coef_out[0:1, :] = row[:, 0:KMAX]
    coef_out[1:2, :] = row[:, KMAX:KB]
    norm_out[0] = jnp.sum(norm)
    loss_out[0] = jnp.sum(sums[0:1, KB + 1 : KB + 2])
    loss_out[1] = jnp.sum(sums[0:1, KB + 2 : KB + 3])
    loss_out[2] = jnp.sum(loss[0:1, 2:3])
    high = row.astype(bf16).astype(f32)
    mid = (row - high).astype(bf16).astype(f32)
    low = row - high - mid
    place = lax.broadcasted_iota(jnp.int32, (16, KB), 0)
    split = jnp.where(place == 0, high, jnp.where(place == 1, mid, jnp.where(place == 2, low, 0.0)))
    split = split.astype(bf16)
    rows = grad.shape[0]

    def step(i, carry):
        base = i * blocks
        start = pl.multiple_of(base * LANES, LANES)
        part = dot(split[:, :UPPER], upper[:, pl.ds(start, blocks * LANES)])
        part = part + dot(split[:, UPPER:], lower[:, pl.ds(start, blocks * LANES)])
        part = jnp.sum(part, 0, keepdims=True)
        for j in range(blocks):
            removed[pl.ds(base + j, 1), :] = part[:, j * LANES : (j + 1) * LANES]
        return carry

    lax.fori_loop(0, rows // blocks, step, 0)
    projected = grad[...] * factor - removed[0:rows, :] * (1.0 / whole_len)
    new_first = BETA_ONE * first[...] + (1.0 - BETA_ONE) * projected
    new_second = BETA_TWO * second[...] + (1.0 - BETA_TWO) * projected * projected
    ratio = (
        new_first
        / (1.0 - BETA_ONE**STEP)
        / (jnp.sqrt(new_second / (1.0 - BETA_TWO**STEP)) + ADAM_EPS)
    )
    old = master[...]
    master_out[...] = old - LEARN_RATE * (ratio + WEIGHT_DECAY * old)
    first_out[...] = new_first
    second_out[...] = new_second


def dp_dims(count):
    zed = 4 if count % 4 == 0 else 1
    plane = count // zed
    ex = max(side for side in range(1, math.isqrt(plane) + 1) if plane % side == 0)
    return zed, plane // ex, ex


def moved(value, place, turn=(0, 0, 0), core=0, pairs_too=False):
    def step(index, by, size):
        return index ^ by if pairs_too and paired(size) else (index + by) % size

    pairs = []
    for section in range(2):
        for zed in range(place.z):
            for why in range(place.y):
                for ex in range(place.x):
                    source = (section * place.z + zed) * place.y * place.x + why * place.x + ex
                    there = ((section + core) % 2) * place.z + step(zed, turn[0], place.z)
                    target = (there * place.y + step(why, turn[1], place.y)) * place.x
                    pairs.append((source, target + step(ex, turn[2], place.x)))
    return lax.ppermute(value, ("section", "dp"), pairs)


def add(left, right, resident):
    vmem = pl.BlockSpec(memory_space=pltpu.VMEM)
    return pl.pallas_call(
        add_kernel,
        in_specs=[vmem, vmem] + [pl.BlockSpec(memory_space=pl.ANY)] * 2,
        out_specs=vmem,
        out_shape=jax.ShapeDtypeStruct(left.shape, left.dtype),
        compiler_params=pltpu.CompilerParams(vmem_limit_bytes=2 * 1024 * 1024),
        name="add",
    )(left, right, *resident)


def butterfly(value, place, resident):
    value = add(value, moved(value, place, core=1), resident)
    for axis, size in ((2, place.x), (1, place.y), (0, place.z)):
        span = 1
        while span < size:
            pairs = []
            for index in range(2 * place.count):
                section, rest = divmod(index, place.count)
                at = [rest // (place.y * place.x), rest // place.x % place.y, rest % place.x]
                at[axis] ^= span
                pairs.append((index, section * place.count + (at[0] * place.y + at[1]) * place.x + at[2]))
            value = add(value, lax.ppermute(value, ("section", "dp"), pairs), resident)
            span *= 2
    return value


def whole(shape):
    return pl.BlockSpec(shape, lambda *_: (0,) * len(shape))


def params(megabytes):
    return pltpu.CompilerParams(
        vmem_limit_bytes=megabytes * 1024 * 1024, dimension_semantics=("arbitrary",)
    )


BLOCK_SHAPES = [(D, D)] * 4 + [(D, FF), (FF, D)]
SAVED = [
    ((ROWS, D), f32),
    ((ROWS, D), bf16),
    ((ROWS, D), bf16),
    ((ROWS, D), bf16),
    ((HEADS * ROWS, ROWS), f32),
    ((ROWS, D), bf16),
    ((ROWS, D), f32),
    ((ROWS, FF), bf16),
    ((ROWS, FF), f32),
]
MIDDLE = ((ROWS, D), bf16)
WORK = pl.CostEstimate(flops=3_000_000_000, bytes_accessed=30_000_000, transcendentals=1_000_000)
VMEM = pl.BlockSpec(memory_space=pltpu.VMEM)
SMEM = pl.BlockSpec(memory_space=pltpu.SMEM)
ANY = pl.BlockSpec(memory_space=pl.ANY)


def group_of(per):
    return GROUP if per % GROUP == 0 else 1


def flat_scratch(place):
    flat_rows = place.count * place.shard_rows + SPARE
    return [
        pltpu.VMEM((flat_rows, LANES), f32),
        pltpu.VMEM((flat_rows, LANES), f32),
        pltpu.VMEM((FF + 32, LANES), f32),
    ]


def front(place, per, own, other, patches):
    outs = pl.pallas_call(
        functools.partial(front_kernel, place, per),
        in_specs=[VMEM] * (len(own) + len(other) + 1),
        out_specs=[VMEM] * (len(SAVED) + 1 + len(BLOCK_SHAPES) + 1),
        out_shape=[
            jax.ShapeDtypeStruct((per * shape[0], shape[1]), kind) for shape, kind in SAVED + [MIDDLE]
        ]
        + [jax.ShapeDtypeStruct(shape, bf16) for shape in BLOCK_SHAPES]
        + [jax.ShapeDtypeStruct((VEC_ROWS, FF), f32)],
        scratch_shapes=flat_scratch(place)
        + [pltpu.VMEM((PDIM, D), bf16), pltpu.VMEM((ROWS, D), f32), pltpu.VMEM((per * ROWS, D), f32)],
        compiler_params=pltpu.CompilerParams(vmem_limit_bytes=20 * 1024 * 1024),
        cost_estimate=WORK,
        name="front",
    )(*own, *other, patches)
    return outs[:9], outs[9], outs[10:]


def grad_kind(place):
    return jax.ShapeDtypeStruct((place.count, place.sent_rows, LANES), bf16)


def late(place, per, image_total, labels, replay, own, other, middle, old_logits):
    eight = -(-per // 8) * 8
    return pl.pallas_call(
        functools.partial(late_kernel, place, per, image_total),
        in_specs=[SMEM] * 2 + [VMEM] * (len(own) + len(other) + 2),
        out_specs=[VMEM] * 3,
        out_shape=[
            jax.ShapeDtypeStruct((per * ROWS, D), bf16),
            grad_kind(place),
            jax.ShapeDtypeStruct((1, LANES), f32),
        ],
        scratch_shapes=flat_scratch(place)
        + [pltpu.VMEM((8, 256, LANES), f32)]
        + [pltpu.VMEM(shape, bf16) for shape in BLOCK_SHAPES]
        + [
            pltpu.VMEM((VEC_ROWS, FF), f32),
            pltpu.VMEM((D, CPAD), bf16),
            pltpu.VMEM((1, CPAD), f32),
            pltpu.VMEM((eight, D), f32),
            pltpu.VMEM((per * ROWS, D), f32),
        ],
        compiler_params=pltpu.CompilerParams(vmem_limit_bytes=16 * 1024 * 1024),
        cost_estimate=WORK,
        name="late",
    )(labels, replay, *own, *other, middle, old_logits)


def back(place, per, grad_middle, kept, patches, weights, late_grad):
    return pl.pallas_call(
        functools.partial(back_kernel, place, per),
        in_specs=[VMEM] * (1 + len(kept) + 1 + len(weights) + 1),
        out_specs=[VMEM] * 2,
        out_shape=[grad_kind(place)] * 2,
        scratch_shapes=flat_scratch(place)
        + [pltpu.VMEM((per * ROWS, D), bf16)] * 6
        + [pltpu.VMEM((per * ROWS, FF), bf16)],
        compiler_params=pltpu.CompilerParams(vmem_limit_bytes=20 * 1024 * 1024),
        cost_estimate=WORK,
        name="back",
    )(grad_middle, *kept, patches, *weights, late_grad)


def body(
    patches, labels, replay, old_logits, basis_count, master, first_moment, second_moment, basis
):
    chips = lax.axis_size("dp")
    shard_len = master.shape[1]
    shard_rows = shard_len // LANES
    place = Place(dp_dims(chips), shard_rows)
    images = patches.shape[0]
    per = images // 2
    section = lax.axis_index("section")
    turns = place.turns()

    shard = pl.pallas_call(
        shard_kernel,
        grid=(1,),
        in_specs=[SMEM, whole((shard_rows, LANES))],
        out_specs=whole((place.sent_rows, LANES)),
        out_shape=jax.ShapeDtypeStruct((place.sent_rows, LANES), bf16),
        compiler_params=pltpu.CompilerParams(vmem_limit_bytes=2 * 1024 * 1024),
        name="shard",
    )(
        pltpu.with_memory_space_constraint(replay, pltpu.HBM),
        pltpu.with_memory_space_constraint(master.reshape(shard_rows, LANES), pltpu.HBM),
    )
    mine = lax.dynamic_slice_in_dim(patches, section * per, per, 0)
    early, late_part = shard[: place.first_rows], shard[place.first_rows :]
    column = [early] + [moved(early, place, (d, 0, 0)) for d in range(1, place.z)]
    plane = [moved(late_part, place, (0, a, b)) if a + b else late_part for a, b in turns]
    column[-1], mine = lax.optimization_barrier((column[-1], mine))
    column, plane = jnp.stack(column), jnp.stack(plane)
    own = [moved(column, place, (0, a, b)) if a + b else column for a, b in turns]
    own += [moved(plane, place, (d, 0, 0)) if d else plane for d in range(place.z)]
    other = [moved(piece, place, core=1) for piece in own]

    kept, middle, weights = front(place, per, own, other, mine)
    grad_middle, late_grad, loss = late(
        place, per, float(images * chips), labels, replay, own, other, middle, old_logits
    )
    keep, give = back(place, per, grad_middle, kept, mine, weights, late_grad)

    given = moved(give, place, core=1)

    def kinds(lead, rows, count):
        shape = (*lead, place.z, rows, LANES)
        return [jax.ShapeDtypeStruct(shape, bf16 if i else f32) for i in range(count)]

    one_rows, two_rows = place.half_rows, place.sent_rows - place.half_rows
    parts = pl.pallas_call(
        functools.partial(split_kernel, place),
        in_specs=[VMEM] * 2,
        out_specs=[VMEM] * (place.y + place.x),
        out_shape=kinds((place.x,), one_rows, place.y) + kinds((place.y,), two_rows, place.x),
        compiler_params=pltpu.CompilerParams(vmem_limit_bytes=12 * 1024 * 1024),
        name="split",
    )(keep, given)
    ones, twos = parts[: place.y], parts[place.y :]
    rows_basis = pltpu.with_memory_space_constraint(basis.reshape(KB, shard_len), pltpu.HBM)

    def fetch(first, last, after):
        return pl.pallas_call(
            functools.partial(fetch_kernel, first, last),
            in_specs=[ANY, ANY],
            out_specs=ANY,
            out_shape=pltpu.VMEM((last - first, shard_len), bf16),
            scratch_shapes=[pltpu.SemaphoreType.DMA],
            compiler_params=pltpu.CompilerParams(vmem_limit_bytes=2 * 1024 * 1024),
            cost_estimate=pl.CostEstimate(
                flops=0, bytes_accessed=4 * (last - first) * shard_len, transcendentals=0
            ),
            name="fetch",
        )(after, rows_basis)

    upper = fetch(0, UPPER, ones[-1])

    def along_y(values):
        return [moved(values[i], place, (0, i, 0), pairs_too=True) for i in range(1, place.y)]

    def along_x(values):
        return [moved(values[i], place, (0, 0, i), pairs_too=True) for i in range(1, place.x)]

    arrived = along_y(ones) + along_x(twos)
    parts = pl.pallas_call(
        functools.partial(turn_kernel, place),
        in_specs=[VMEM, VMEM, ANY] + [VMEM] * len(arrived),
        out_specs=[VMEM] * (place.y + place.x),
        out_shape=kinds((), one_rows, place.x) + kinds((), two_rows, place.y),
        compiler_params=pltpu.CompilerParams(vmem_limit_bytes=2 * 1024 * 1024),
        name="turn",
    )(ones[0], twos[0], upper, *arrived)
    ones, twos = parts[: place.x], parts[place.x :]
    arrived = along_x(ones) + along_y(twos)
    piece_shape = (place.sent_rows, LANES)
    first, *rest = pl.pallas_call(
        functools.partial(plane_kernel, place),
        in_specs=[VMEM, VMEM, ANY] + [VMEM] * len(arrived),
        out_specs=[VMEM] * place.z,
        out_shape=[jax.ShapeDtypeStruct(piece_shape, bf16 if d else f32) for d in range(place.z)],
        compiler_params=pltpu.CompilerParams(vmem_limit_bytes=2 * 1024 * 1024),
        name="plane",
    )(ones[0], twos[0], upper, *arrived)
    resident = (upper, fetch(UPPER, KB, rest[0]))
    pieces = [moved(rest[d - 1], place, (d, 0, 0), pairs_too=True) for d in range(1, place.z)]

    def divisor(most):
        return max(n for n in range(1, most + 1) if shard_rows % n == 0)

    flat_kind = jax.ShapeDtypeStruct((shard_rows, LANES), f32)
    grad, sums = pl.pallas_call(
        functools.partial(inner_kernel, divisor(26)),
        in_specs=[VMEM] * (place.z + 3),
        out_specs=[VMEM] * 2,
        out_shape=[flat_kind, jax.ShapeDtypeStruct((1, SUMS), f32)],
        scratch_shapes=[pltpu.VMEM((KB, LANES), f32)],
        compiler_params=pltpu.CompilerParams(vmem_limit_bytes=2 * 1024 * 1024),
        name="inner",
    )(first, *pieces, *resident, loss)
    sums = butterfly(sums, place, resident)
    padded_rows = -(-shard_rows // 8) * 8
    loss_parts, norm, coefficients, new_master, new_first, new_second = pl.pallas_call(
        functools.partial(update_kernel, divisor(156), float(2 * shard_len * chips)),
        in_specs=[SMEM] + [VMEM] * 8,
        out_specs=[SMEM, SMEM] + [VMEM] * 4,
        out_shape=[
            jax.ShapeDtypeStruct((3,), f32),
            jax.ShapeDtypeStruct((1,), f32),
            jax.ShapeDtypeStruct((TASKS, KMAX), f32),
        ]
        + [flat_kind] * 3,
        scratch_shapes=[pltpu.VMEM((padded_rows, LANES), f32)],
        compiler_params=pltpu.CompilerParams(vmem_limit_bytes=2 * 1024 * 1024),
        name="update",
    )(
        basis_count,
        sums,
        *resident,
        grad,
        loss,
        master.reshape(shard_rows, LANES),
        first_moment.reshape(shard_rows, LANES),
        second_moment.reshape(shard_rows, LANES),
    )
    return (
        loss_parts,
        norm[0],
        coefficients,
        new_master.reshape(1, shard_len),
        new_first.reshape(1, shard_len),
        new_second.reshape(1, shard_len),
    )


def solution(mesh):
    in_specs = (
        P("dp", None, None),
        P("dp"),
        P("dp"),
        P("dp", None),
        P(),
        P("section", "dp"),
        P("section", "dp"),
        P("section", "dp"),
        P(None, "section", "dp"),
    )
    out_specs = (P(), P(), P(), P("section", "dp"), P("section", "dp"), P("section", "dp"))
    return jax.shard_map(body, mesh=mesh, in_specs=in_specs, out_specs=out_specs, check_vma=False)
```

```python
import functools
import math

import jax
import jax.numpy as jnp
from jax import lax
from jax.experimental import pallas as pl
from jax.experimental.pallas import tpu as pltpu
from jax.sharding import PartitionSpec as P

HEADS = 3
HD = 64
D = 192
FF = 768
PDIM = 768
PATCHES = 196
TOKENS = PATCHES + 1
ROWS = 208
CLS = PATCHES
GROUP = 4
CLASSES = 1000
CPAD = 1024
TASKS = 2
KMAX = 200
KB = TASKS * KMAX
UPPER = 256
STEP = 10
LANES = 128
HALF = 64
SPARE = 512
SUMS = 512

NORM_EPS = 1e-06
CLIP_NORM = 0.02
LEARN_RATE = 0.05
BETA_ONE = 0.9
BETA_TWO = 0.999
ADAM_EPS = 1e-08
WEIGHT_DECAY = 0.05
SCALE = HD ** (-0.5)
MASKED = -1e30

BLOCK_AT = dict(
    gain_one=0,
    bias_one=3,
    w_qkv=6,
    b_qkv=1734,
    w_out=1740,
    b_out=2316,
    gain_two=2319,
    bias_two=2322,
    w_up=2325,
    b_up=4629,
    w_down=4641,
    b_down=6945,
)
W_PATCH, B_PATCH, CLS_TOKEN, POS_EMBED = 6948, 9252, 9255, 9258
GAIN_LAST, BIAS_LAST, W_HEAD, B_HEAD = 6948, 6951, 6954, 9954
VECTORS = ("gain_one", "bias_one", "b_q", "b_v", "b_out", "gain_two", "bias_two", "b_up", "b_down")
VEC_ROWS = 16

f32 = jnp.float32
bf16 = jnp.bfloat16


def dot(left, right, left_dim=1, right_dim=0):
    return lax.dot_general(
        left, right, (((left_dim,), (right_dim,)), ((), ())), preferred_element_type=f32
    )


def low_lanes(shape):
    return lax.broadcasted_iota(jnp.int32, shape, 1) < HALF


def swap_halves(value):
    return pltpu.roll(value, HALF, 1)


def head_masks():
    lane = lax.broadcasted_iota(jnp.int32, (1, D), 1)
    return [jnp.logical_and(lane >= h * HD, lane < (h + 1) * HD) for h in range(HEADS)]


def by_head(value):
    return jnp.concatenate([jnp.where(m, value, 0.0) for m in head_masks()], 0)


def from_heads(value):
    rows = value.shape[0] // HEADS
    parts = [value[h * rows : (h + 1) * rows] for h in range(HEADS)]
    masks = head_masks()
    return jnp.where(masks[0], parts[0], jnp.where(masks[1], parts[1], parts[2]))


def normalise(rows_in):
    mean = jnp.sum(rows_in, -1, keepdims=True) * (1.0 / D)
    centred = rows_in - mean
    variance = jnp.sum(centred * centred, -1, keepdims=True) * (1.0 / D)
    scale = lax.rsqrt(variance + NORM_EPS)
    return centred * scale, scale


def normalise_back(grad, gain, unit, scale):
    grad_unit = grad * gain
    first = jnp.sum(grad_unit, -1, keepdims=True) * (1.0 / D)
    second = jnp.sum(grad_unit * unit, -1, keepdims=True) * (1.0 / D)
    return scale * (grad_unit - first - unit * second)


def gelu_parts(pre):
    cdf = 0.5 * (1.0 + lax.erf(pre * math.sqrt(0.5)))
    slope = cdf + pre * (jnp.exp(-0.5 * pre * pre) * (1.0 / math.sqrt(2.0 * math.pi)))
    return pre * cdf, slope


def column_sums(value):
    return jnp.sum(value.astype(f32), 0, keepdims=True)


def strided(ref, start, count, stride):
    if count == 1 or stride == 1:
        return ref[pl.ds(start, count), :]
    return ref[pl.ds(start, count, stride=stride), :]


class Flat:
    def __init__(self, even, odd, mix, odd_rows):
        self.even, self.odd, self.mix, self.odd_rows = even, odd, mix, odd_rows

    def shift(self):
        step = 192
        for at in range(0, self.odd_rows, step):
            here = self.even[at : at + step, :]
            after = self.even[at + 1 : at + 1 + step, :]
            self.odd[at : at + step, :] = swap_halves(jnp.where(low_lanes(here.shape), after, here))

    def rows_at(self, half, count, stride):
        return strided(self.odd if half % 2 else self.even, half // 2, count, stride)

    def blocks(self, half, width, rows, cols):
        for at in range(0, cols, LANES):
            start = half + at // HALF
            if rows == 1 or width % 2 == 0:
                value = self.rows_at(start, rows, width // 2)
            else:
                pairs = (rows + 1) // 2
                self.mix[pl.ds(0, pairs, stride=2), :] = self.rows_at(start, pairs, width)
                self.mix[pl.ds(1, pairs, stride=2), :] = self.rows_at(start + width, pairs, width)
                value = self.mix[0:rows, :]
            yield at, min(LANES, cols - at), value

    def read(self, dest, half, width, rows, cols):
        for at, wide, value in self.blocks(half, width, rows, cols):
            dest[0:rows, at : at + wide] = value[:, :wide].astype(dest.dtype)

    def read_row(self, dest, row, half, cols):
        for at, wide, value in self.blocks(half, 2, 1, cols):
            dest[row : row + 1, at : at + wide] = value[:, :wide]

    def clear(self):
        rows = self.odd_rows + 16
        self.even[...] = jnp.zeros(self.even.shape, f32)
        self.odd[0:rows, :] = jnp.zeros((rows, LANES), f32)

    def put_rows(self, half, count, stride, value):
        ref, start = (self.odd, half // 2 + 8) if half % 2 else (self.even, half // 2)
        if count == 1 or stride == 1:
            ref[pl.ds(start, count), :] = value
        else:
            ref[pl.ds(start, count, stride=stride), :] = value

    def write(self, value, half, width, cols):
        rows = value.shape[0]
        for at in range(0, cols, LANES):
            wide = min(LANES, cols - at)
            part = value[:, at : at + wide]
            if wide < LANES:
                part = jnp.concatenate([part, jnp.zeros((rows, LANES - wide), f32)], 1)
            start = half + at // HALF
            if rows == 1 or width % 2 == 0:
                self.put_rows(start, rows, width // 2, part)
            else:
                pairs = (rows + 1) // 2
                self.mix[0:rows, :] = part
                self.put_rows(start, pairs, width, self.mix[pl.ds(0, pairs, stride=2), :])
                self.put_rows(start + width, pairs, width, self.mix[pl.ds(1, pairs, stride=2), :])

    def merged(self, at, count):
        if at >= self.odd_rows:
            return self.even[at : at + count, :]
        here = self.odd[at + 8 : at + 8 + count, :]
        before = self.odd[at + 7 : at + 7 + count, :]
        moved_back = swap_halves(jnp.where(low_lanes(here.shape), here, before))
        return self.even[at : at + count, :] + moved_back


def paired(size):
    return size & (size - 1) == 0


class Place:
    def __init__(self, dims, shard_rows):
        self.z, self.y, self.x = dims
        self.count = self.z * self.y * self.x
        self.shard_rows = shard_rows
        self.sent_rows = -(-(shard_rows + 1) // 16) * 16
        self.first_rows = self.sent_rows * 13 // 20 // 16 * 16

        self.half_rows = self.sent_rows // 32 * 16

    def split(self, index):
        plane = self.y * self.x
        return index // plane, lax.rem(index, plane) // self.x, lax.rem(index, self.x)

    def turns(self):
        return [(a, b) for a in range(self.y) for b in range(self.x)]


def load_section(place, pieces, wanted, flat):
    own, other = pieces
    section = lax.axis_index("section")
    zed, why, ex = place.split(lax.axis_index("dp"))
    rows = place.shard_rows

    def copy(refs):
        for turn, (a, b) in enumerate(place.turns()):
            for d in range(place.z):
                shard = lax.rem(zed + (place.z - d), place.z) * (place.y * place.x)
                shard = shard + lax.rem(why + (place.y - a), place.y) * place.x
                shard = shard + lax.rem(ex + (place.x - b), place.x)
                start = shard * rows
                if rows % 8 == 0:
                    start = pl.multiple_of(start, 8)
                cut = place.first_rows
                flat.even[pl.ds(start, cut), :] = refs[turn][d].astype(f32)
                value = refs[len(place.turns()) + d][turn].astype(f32)
                after = start + cut
                if rows % 8 == 0:
                    after = pl.multiple_of(after, 8)
                flat.even[pl.ds(after, rows - cut), :] = value[: rows - cut]

    @pl.when(section == wanted)
    def _():
        copy(own)

    @pl.when(section != wanted)
    def _():
        copy(other)

    flat.shift()


def read_block(flat, weights, vec):
    at = BLOCK_AT
    w_q, w_k, w_v, w_out, w_up, w_down = weights
    for place, dest in enumerate((w_q, w_k, w_v)):
        flat.read(dest, at["w_qkv"] + 3 * place, 9, D, D)
    flat.read(w_out, at["w_out"], 3, D, D)
    flat.read(w_up, at["w_up"], 12, D, FF)
    flat.read(w_down, at["w_down"], 3, FF, D)
    starts = dict(at, b_q=at["b_qkv"], b_v=at["b_qkv"] + 3)
    for row, name in enumerate(VECTORS):
        flat.read_row(vec, row, starts[name], FF if name == "b_up" else D)


def vector(vec, name):
    row = VECTORS.index(name)
    return vec[row : row + 1, 0 : FF if name == "b_up" else D]


def write_vectors(flat, sums):
    at = BLOCK_AT
    starts = dict(at, b_q=at["b_qkv"], b_v=at["b_qkv"] + 3)
    for name, value in sums.items():
        flat.write(value, starts[name], 2, value.shape[1])


def send_out(place, flat, write):
    zed, why, ex = place.split(lax.axis_index("dp"))
    rows, spare = place.shard_rows, place.sent_rows - place.shard_rows
    for shard in range(place.count):
        zk, yk, xk = shard // (place.y * place.x), shard // place.x % place.y, shard % place.x
        there = ((zk, zed, place.z), (yk, why, place.y), (xk, ex, place.x))
        d, a, b = [to ^ at if paired(size) else lax.rem(to + size - at, size) for to, at, size in there]
        value = flat.merged(shard * rows, rows)
        value = jnp.concatenate([value, jnp.zeros((spare, LANES), f32)], 0)
        write((a * place.x + b) * place.z + d, value.astype(bf16))


def shard_kernel(replay, master, out):
    rows = master.shape[0]
    count = sum(replay[i].astype(f32) for i in range(replay.shape[0]))
    tail = jnp.full((out.shape[0] - rows, LANES), count, f32)
    out[...] = jnp.concatenate([master[...], tail], 0).astype(bf16)


def front_kernel(place, per, *refs):
    parts = len(place.turns()) + place.z
    own, other, refs = refs[:parts], refs[parts : 2 * parts], refs[2 * parts :]
    patches, kept, middle_out, weights = refs[0], refs[1:10], refs[10], refs[11:18]
    even, odd, mix, w_patch, added, tokens = refs[18:]
    vec = weights[-1]
    flat = Flat(even, odd, mix, place.count * place.shard_rows)
    load_section(place, (own, other), 0, flat)
    read_block(flat, weights[:-1], vec)
    flat.read(w_patch, W_PATCH, 3, PDIM, D)
    flat.read_row(vec, 9, B_PATCH, D)
    flat.read_row(vec, 10, CLS_TOKEN, D)
    added[...] = jnp.zeros(added.shape, f32)
    tokens[...] = jnp.zeros(tokens.shape, f32)
    for at, wide, value in flat.blocks(POS_EMBED, 3, TOKENS + 1, D):
        added[0:PATCHES, at : at + wide] = value[1:TOKENS, :wide] + vec[9:10, at : at + wide]
        added[CLS : CLS + 1, at : at + wide] = value[0:1, :wide] + vec[10:11, at : at + wide]
    group = group_of(per)
    for step in range(0, per, group):
        cut = slice(step * ROWS, (step + group) * ROWS)
        front_images(step, cut, patches, kept, middle_out, weights, w_patch, added, tokens)


def front_images(step, cut, patches, kept, middle_out, weights, w_patch, added, tokens):
    x_out, q_out, k_out, v_out, probs_out, mixed_out, hidden_out, act_out, slope_out = kept
    w_q, w_k, w_v, w_out, w_up, w_down, vec = weights
    group = (cut.stop - cut.start) // ROWS
    spans = [slice(i * ROWS, (i + 1) * ROWS) for i in range(group)]
    for i, at in enumerate(spans):
        tokens[cut.start + at.start : cut.start + at.start + PATCHES, :] = dot(patches[step + i], w_patch[...])
    x = tokens[cut, :] + jnp.concatenate([added[...]] * group, 0)
    x_out[cut, :] = x
    unit, _ = normalise(x)
    normed = (unit * vector(vec, "gain_one") + vector(vec, "bias_one")).astype(bf16)
    q = (dot(normed, w_q[...]) + vector(vec, "b_q")).astype(bf16)
    k = dot(normed, w_k[...]).astype(bf16)
    v = (dot(normed, w_v[...]) + vector(vec, "b_v")).astype(bf16)
    q_out[cut, :], k_out[cut, :], v_out[cut, :] = q, k, v
    q_scaled = q.astype(f32) * SCALE
    column = lax.broadcasted_iota(jnp.int32, (1, ROWS), 1)
    scores = [dot(by_head(q_scaled[at]).astype(bf16), k[at], 1, 1) for at in spans]
    scores = [jnp.where(column < TOKENS, value, MASKED) for value in scores]
    raised = [jnp.exp(value - jnp.max(value, -1, keepdims=True)) for value in scores]
    probs = [value * (1.0 / jnp.sum(value, -1, keepdims=True)) for value in raised]
    for i, value in enumerate(probs):
        probs_out[(step + i) * HEADS * ROWS : (step + i + 1) * HEADS * ROWS, :] = value
    mixed = [from_heads(dot(value.astype(bf16), v[at])) for value, at in zip(probs, spans)]
    mixed = jnp.concatenate(mixed, 0).astype(bf16)
    mixed_out[cut, :] = mixed
    hidden = x + dot(mixed, w_out[...]) + vector(vec, "b_out")
    hidden_out[cut, :] = hidden
    unit, _ = normalise(hidden)
    normed = (unit * vector(vec, "gain_two") + vector(vec, "bias_two")).astype(bf16)
    pre = dot(normed, w_up[...]) + vector(vec, "b_up")
    act, slope = gelu_parts(pre)
    act = act.astype(bf16)
    act_out[cut, :], slope_out[cut, :] = act, slope
    middle = hidden + dot(act, w_down[...]) + vector(vec, "b_down")
    middle_out[cut, :] = middle.astype(bf16)


def read_head(flat, wide, w_head, b_head):
    first = W_HEAD // 2
    lane = lax.broadcasted_iota(jnp.int32, (16, LANES), 1)
    for phase in range(16):
        start, off = first + CLASSES * phase // LANES, CLASSES * phase % LANES
        got = [strided(flat.even, start + j, 16, 125) for j in range(9 if off else 8)]
        if off:
            got = [pltpu.roll(g, LANES - off, 1) for g in got]
        for j in range(8):
            value = jnp.where(lane < LANES - off, got[j], got[j + 1]) if off else got[j]
            wide[j, pl.ds(phase, 16, stride=16), :] = value
    lane = lax.broadcasted_iota(jnp.int32, (1, LANES), 1)
    for j in range(8):
        keep = lane + j * LANES < CLASSES
        w_head[:, j * LANES : (j + 1) * LANES] = jnp.where(keep, wide[j, 0:D, :], 0.0).astype(bf16)
        value = flat.even[B_HEAD // 2 + j : B_HEAD // 2 + j + 1, :]
        b_head[0:1, j * LANES : (j + 1) * LANES] = jnp.where(keep, value, 0.0)


def write_head(flat, wide, grad_w, grad_b):
    first = W_HEAD // 2
    for j in range(8):
        wide[j, 0:D, :] = grad_w[:, j * LANES : (j + 1) * LANES]
        wide[j, D:, :] = jnp.zeros((wide.shape[1] - D, LANES), f32)
    lane = lax.broadcasted_iota(jnp.int32, (16, LANES), 1)
    for phase in range(16):
        start, off = first + CLASSES * phase // LANES, CLASSES * phase % LANES
        got = [wide[j, pl.ds(phase, 16, stride=16), :] for j in range(8)]
        if off:
            got = [pltpu.roll(g, off, 1) for g in got]
        for j in range(9 if off else 8):
            if not off:
                value = got[j]
            else:
                before = got[j - 1] if j else jnp.zeros((16, LANES), f32)
                value = jnp.where(lane < off, before, got[j] if j < 8 else 0.0)
            flat.even[pl.ds(start + j, 16, stride=125), :] += value
    for j in range(8):
        row = B_HEAD // 2 + j
        flat.even[row : row + 1, :] += grad_b[:, j * LANES : (j + 1) * LANES]


def late_kernel(place, per, image_total, labels, replay, *refs):
    section = lax.axis_index("section")
    parts = len(place.turns()) + place.z
    odd_rows = -(-(W_HEAD // 2 + 1) // place.shard_rows) * place.shard_rows
    own, other, refs = refs[:parts], refs[parts : 2 * parts], refs[2 * parts :]
    middle, old_logits, back_out, grad_out, loss_out = refs[:5]
    even, odd, mix, wide, w_q, w_k, w_v, w_out, w_up, w_down, vec, w_head, b_head, few, many = refs[5:]
    flat = Flat(even, odd, mix, odd_rows)
    load_section(place, (own, other), 1, flat)
    read_block(flat, (w_q, w_k, w_v, w_out, w_up, w_down), vec)
    flat.read_row(vec, 9, GAIN_LAST, D)
    flat.read_row(vec, 10, BIAS_LAST, D)
    read_head(flat, wide, w_head, b_head)
    gain_last, bias_last = vec[9:10, 0:D], vec[10:11, 0:D]
    carried = jnp.zeros((1, LANES), f32)
    carrier = place.shard_rows - place.first_rows
    for ref in own[len(place.turns()) :]:
        for turn in range(len(place.turns())):
            carried = carried + ref[turn].astype(f32)[carrier : carrier + 1]
    replay_count = carried[:, 0:1]

    x = middle[...].astype(f32)
    unit, scale = normalise(x)
    normed_f = unit * vector(vec, "gain_one") + vector(vec, "bias_one")
    normed = normed_f.astype(bf16)
    k = dot(normed, w_k[...]).astype(bf16)
    v = (dot(normed, w_v[...]) + vector(vec, "b_v")).astype(bf16)

    def class_rows(value):
        few[...] = jnp.zeros(few.shape, f32)
        for i in range(per):
            few[i : i + 1, :] = value[i * ROWS + CLS : i * ROWS + CLS + 1, :]
        return few[...]

    eight = few.shape[0]
    image = lax.broadcasted_iota(jnp.int32, (eight, 1), 0)
    real = image < per
    x_top = class_rows(x)
    top_normed = class_rows(normed_f).astype(bf16)
    q = (dot(top_normed, w_q[...]) + vector(vec, "b_q")).astype(bf16)
    q_heads = by_head(jnp.where(real, q.astype(f32) * SCALE, 0.0)).astype(bf16)
    scores = dot(q_heads, k, 1, 1)
    column = lax.broadcasted_iota(jnp.int32, scores.shape, 1)
    owner = lax.rem(lax.broadcasted_iota(jnp.int32, scores.shape, 0), eight) * ROWS
    inside = jnp.logical_and(column >= owner, column < owner + TOKENS)
    scores = jnp.where(inside, scores, MASKED)
    raised = jnp.where(inside, jnp.exp(scores - jnp.max(scores, -1, keepdims=True)), 0.0)
    total = jnp.sum(raised, -1, keepdims=True)
    probs = raised * (1.0 / jnp.where(total > 0.0, total, 1.0))
    probs_low = probs.astype(bf16)
    mixed = from_heads(dot(probs_low, v)).astype(bf16)
    hidden = x_top + dot(mixed, w_out[...]) + vector(vec, "b_out")
    unit_two, scale_two = normalise(hidden)
    normed_two = (unit_two * vector(vec, "gain_two") + vector(vec, "bias_two")).astype(bf16)
    act, slope = gelu_parts(dot(normed_two, w_up[...]) + vector(vec, "b_up"))
    act = act.astype(bf16)
    final = hidden + dot(act, w_down[...]) + vector(vec, "b_down")

    unit_last, scale_last = normalise(final)
    top = (unit_last * gain_last + bias_last).astype(bf16)
    classes = lax.broadcasted_iota(jnp.int32, (eight, CPAD), 1)
    logits = dot(top, w_head[...]) + b_head[...]
    logits = jnp.where(classes < CLASSES, logits, MASKED)
    highest = jnp.max(logits, -1, keepdims=True)
    log_total = highest + jnp.log(jnp.sum(jnp.exp(logits - highest), -1, keepdims=True))
    label = jnp.zeros((eight, 1), jnp.int32)
    again = jnp.zeros((eight, 1), f32)
    for i in range(per):
        label = jnp.where(image == i, labels[section * per + i], label)
        again = jnp.where(image == i, replay[section * per + i].astype(f32), again)
    picked = jnp.logical_and(classes == label, real)
    entropy = jnp.where(real, log_total, 0.0) - jnp.sum(jnp.where(picked, logits, 0.0), -1, keepdims=True)
    wanted = jnp.where(section == 0, old_logits[0:per, :], old_logits[per : 2 * per, :])
    if per < eight:
        wanted = jnp.concatenate([wanted, jnp.zeros((eight - per, CLASSES), f32)], 0)
    wanted = jnp.concatenate([wanted, jnp.zeros((eight, CPAD - CLASSES), f32)], 1)
    distance = jnp.where(jnp.logical_and(classes < CLASSES, real), logits - wanted, 0.0)
    squares = again * (jnp.sum(distance * distance, -1, keepdims=True) * (1.0 / CLASSES))
    lane = lax.broadcasted_iota(jnp.int32, (1, LANES), 1)
    entropy_sum = jnp.sum(entropy, 0, keepdims=True)
    replay_sum = jnp.sum(squares, 0, keepdims=True)
    loss_out[...] = jnp.where(lane == 0, entropy_sum, jnp.where(lane == 1, replay_sum, replay_count))

    grad = (jnp.exp(logits - log_total) - jnp.where(picked, 1.0, 0.0)) * (1.0 / image_total)
    grad = grad + again * 2.0 * distance / (CLASSES * replay_count)
    grad = jnp.where(jnp.logical_and(classes < CLASSES, real), grad, 0.0)
    grad_low = grad.astype(bf16)
    flat.clear()
    write_head(flat, wide, dot(top, grad_low, 0, 0), column_sums(grad_low))
    sums = {}
    grad = dot(grad_low, w_head[...], 1, 1)
    flat.write(column_sums(grad * unit_last), GAIN_LAST, 2, D)
    flat.write(column_sums(grad), BIAS_LAST, 2, D)
    grad = normalise_back(grad, gain_last, unit_last, scale_last)

    at = BLOCK_AT
    grad_down = grad.astype(bf16)
    flat.write(dot(act, grad_down, 0, 0), at["w_down"], 3, D)
    sums["b_down"] = column_sums(grad_down)
    grad_up = (dot(grad_down, w_down[...], 1, 1) * slope).astype(bf16)
    flat.write(dot(normed_two, grad_up, 0, 0), at["w_up"], 12, FF)
    sums["b_up"] = column_sums(grad_up)
    grad_two = dot(grad_up, w_up[...], 1, 1)
    sums["gain_two"], sums["bias_two"] = column_sums(grad_two * unit_two), column_sums(grad_two)
    grad_hidden = grad + normalise_back(grad_two, vector(vec, "gain_two"), unit_two, scale_two)
    branch = grad_hidden.astype(bf16)
    flat.write(dot(mixed, branch, 0, 0), at["w_out"], 3, D)
    sums["b_out"] = column_sums(branch)
    mixed_heads = by_head(dot(branch, w_out[...], 1, 1).astype(bf16).astype(f32)).astype(bf16)
    grad_probs = dot(mixed_heads, v, 1, 1)
    grad_v = dot(probs_low, mixed_heads, 0, 0).astype(bf16)
    inner = jnp.sum(grad_probs * probs, -1, keepdims=True)
    grad_scores = (probs * (grad_probs - inner)).astype(bf16)
    grad_q = (from_heads(dot(grad_scores, k)) * SCALE).astype(bf16)
    grad_k = dot(grad_scores, q_heads, 0, 0).astype(bf16)
    flat.write(dot(top_normed, grad_q, 0, 0), at["w_qkv"], 9, D)
    flat.write(dot(normed, grad_k, 0, 0), at["w_qkv"] + 3, 9, D)
    flat.write(dot(normed, grad_v, 0, 0), at["w_qkv"] + 6, 9, D)
    sums["b_q"], sums["b_v"] = column_sums(grad_q), column_sums(grad_v)
    many[...] = dot(grad_k, w_k[...], 1, 1) + dot(grad_v, w_v[...], 1, 1)
    top_back = dot(grad_q, w_q[...], 1, 1)
    for i in range(per):
        many[i * ROWS + CLS : i * ROWS + CLS + 1, :] += top_back[i : i + 1, :]
    grad_one = many[...]
    sums["gain_one"], sums["bias_one"] = column_sums(grad_one * unit), column_sums(grad_one)
    many[...] = normalise_back(grad_one, vector(vec, "gain_one"), unit, scale)
    for i in range(per):
        many[i * ROWS + CLS : i * ROWS + CLS + 1, :] += grad_hidden[i : i + 1, :]
    back_out[...] = many[...].astype(bf16)
    write_vectors(flat, sums)

    def store(at, value):
        grad_out[at] = value

    send_out(place, flat, store)


def back_kernel(place, per, *refs):
    grad_in, kept, patches, weights = refs[0], refs[1:10], refs[10], refs[11:18]
    late_grad, keep_out, give_out = refs[18:21]
    even, odd, mix, *operands = refs[21:]
    s_normed, s_q, s_k, s_v, s_branch, s_two, s_up = operands
    vec = weights[-1]
    group = group_of(per)
    sums = {}
    embedded = []
    positions = jnp.zeros((ROWS, D), f32)
    for step in range(0, per, group):
        cut = slice(step * ROWS, (step + group) * ROWS)
        vectors, grad_x = back_images(step, cut, grad_in, kept, weights, operands)
        sums = {name: sums[name] + value if sums else value for name, value in vectors.items()}
        for i in range(group):
            embedded.append(grad_x[i * ROWS : i * ROWS + PATCHES].astype(bf16))
            positions = positions + grad_x[i * ROWS : (i + 1) * ROWS]

    at = BLOCK_AT
    flat = Flat(even, odd, mix, place.count * place.shard_rows)
    flat.clear()
    normed = s_normed[...]
    for part, ref in enumerate((s_q, s_k, s_v)):
        flat.write(dot(normed, ref[...], 0, 0), at["w_qkv"] + 3 * part, 9, D)
    flat.write(dot(kept[5][...], s_branch[...], 0, 0), at["w_out"], 3, D)
    flat.write(dot(s_two[...], s_up[...], 0, 0), at["w_up"], 12, FF)
    flat.write(dot(kept[7][...], grad_in[...], 0, 0), at["w_down"], 3, D)
    grad_patch = sum(dot(patches[i], value, 0, 0) for i, value in enumerate(embedded))
    flat.write(grad_patch, W_PATCH, 3, D)
    sums["b_q"], sums["b_v"] = column_sums(s_q[...]), column_sums(s_v[...])
    sums["b_out"], sums["b_up"] = column_sums(s_branch[...]), column_sums(s_up[...])
    sums["b_down"] = column_sums(grad_in[...])
    write_vectors(flat, sums)
    flat.write(sum(column_sums(value) for value in embedded), B_PATCH, 2, D)
    token = positions[CLS : CLS + 1, :]
    flat.write(token, CLS_TOKEN, 2, D)
    natural = jnp.concatenate([token, positions[0:PATCHES, :], jnp.zeros((1, D), f32)], 0)
    flat.write(natural, POS_EMBED, 3, D)

    section = lax.axis_index("section")

    @pl.when(section == 0)
    def _():
        def store(at, value):
            keep_out[at] = value
            give_out[at] = late_grad[at]

        send_out(place, flat, store)

    @pl.when(section != 0)
    def _():
        def store(at, value):
            give_out[at] = value
            keep_out[at] = late_grad[at]

        send_out(place, flat, store)


def back_images(step, cut, grad_in, kept, weights, operands):
    x_in, q_in, k_in, v_in, probs_in, mixed_in, hidden_in, act_in, slope_in = kept
    w_q, w_k, w_v, w_out, w_up, w_down, vec = weights
    s_normed, s_q, s_k, s_v, s_branch, s_two, s_up = operands
    group = (cut.stop - cut.start) // ROWS
    spans = [slice(i * ROWS, (i + 1) * ROWS) for i in range(group)]
    sums = {}
    grad_low = grad_in[cut, :]
    grad_up = (dot(grad_low, w_down[...], 1, 1) * slope_in[cut, :]).astype(bf16)
    s_up[cut, :] = grad_up
    unit, scale = normalise(hidden_in[cut, :])
    s_two[cut, :] = (unit * vector(vec, "gain_two") + vector(vec, "bias_two")).astype(bf16)
    grad_two = dot(grad_up, w_up[...], 1, 1)
    sums["gain_two"], sums["bias_two"] = column_sums(grad_two * unit), column_sums(grad_two)
    grad_hidden = grad_low.astype(f32) + normalise_back(grad_two, vector(vec, "gain_two"), unit, scale)
    branch = grad_hidden.astype(bf16)
    s_branch[cut, :] = branch
    grad_mixed = dot(branch, w_out[...], 1, 1).astype(bf16).astype(f32)
    mixed_heads = [by_head(grad_mixed[at]).astype(bf16) for at in spans]
    q_scaled = q_in[cut, :].astype(f32) * SCALE
    q_heads = [by_head(q_scaled[at]).astype(bf16) for at in spans]
    k, v = k_in[cut, :], v_in[cut, :]
    probs = [
        probs_in[(step + i) * HEADS * ROWS : (step + i + 1) * HEADS * ROWS, :] for i in range(group)
    ]
    grad_probs = [dot(value, v[at], 1, 1) for value, at in zip(mixed_heads, spans)]
    grad_v = [dot(value.astype(bf16), right, 0, 0) for value, right in zip(probs, mixed_heads)]
    inner = [jnp.sum(one * two, -1, keepdims=True) for one, two in zip(grad_probs, probs)]
    grad_scores = [(two * (one - less)).astype(bf16) for one, two, less in zip(grad_probs, probs, inner)]
    grad_q = [from_heads(dot(value, k[at])) * SCALE for value, at in zip(grad_scores, spans)]
    grad_k = [dot(value, right, 0, 0) for value, right in zip(grad_scores, q_heads)]
    grad_q, grad_k, grad_v = [jnp.concatenate(value, 0).astype(bf16) for value in (grad_q, grad_k, grad_v)]
    s_q[cut, :], s_k[cut, :], s_v[cut, :] = grad_q, grad_k, grad_v
    unit, scale = normalise(x_in[cut, :])
    s_normed[cut, :] = (unit * vector(vec, "gain_one") + vector(vec, "bias_one")).astype(bf16)
    grad_one = dot(grad_q, w_q[...], 1, 1) + dot(grad_k, w_k[...], 1, 1) + dot(grad_v, w_v[...], 1, 1)
    sums["gain_one"], sums["bias_one"] = column_sums(grad_one * unit), column_sums(grad_one)
    return sums, grad_hidden + normalise_back(grad_one, vector(vec, "gain_one"), unit, scale)


def fetch_kernel(first, last, _, basis, kept, sem):
    copy = pltpu.make_async_copy(basis.at[pl.ds(first, last - first)], kept, sem)
    copy.start()
    copy.wait()


def add_kernel(left, right, _, __, total):
    total[...] = left[...] + right[...]


def split_kernel(place, keep, given, *outs):
    cut = place.half_rows
    for place_y in range(place.y):
        for place_x in range(place.x):
            for d in range(place.z):
                at = (place_y * place.x + place_x) * place.z + d
                total = keep[at].astype(f32) + given[at].astype(f32)
                one, two = outs[place_y], outs[place.y + place_x]
                one[place_x, d] = total[:cut].astype(one.dtype)
                two[place_y, d] = total[cut:].astype(two.dtype)


def turn_kernel(place, one, two, _, *refs):
    count = place.y + place.x
    arrived, outs = refs[: count - 2], refs[count - 2 :]
    for own, came, parts in (
        (one, arrived[: place.y - 1], outs[: place.x]),
        (two, arrived[place.y - 1 :], outs[place.x :]),
    ):
        for step, out in enumerate(parts):
            for d in range(place.z):
                total = own[step, d]
                for ref in came:
                    total = total + ref[step, d].astype(f32)
                out[d] = total.astype(out.dtype)


def plane_kernel(place, one, two, _, *refs):
    arrived, (whole_out, *outs) = refs[: -place.z], refs[-place.z :]
    for d in range(place.z):
        upper, lower = one[d], two[d]
        for ref in arrived[: place.x - 1]:
            upper = upper + ref[d].astype(f32)
        for ref in arrived[place.x - 1 :]:
            lower = lower + ref[d].astype(f32)
        out = outs[d - 1] if d else whole_out
        out[0 : place.half_rows, :] = upper.astype(out.dtype)
        out[place.half_rows :, :] = lower.astype(out.dtype)


def inner_kernel(blocks, *refs):
    first, pieces, (upper, lower, loss, grad_out, sums_out, total) = refs[0], refs[1:-6], refs[-6:]
    shard_rows = grad_out.shape[0]
    value = first[...]
    for ref in pieces:
        value = value + ref[...].astype(f32)
    grad_out[...] = value[:shard_rows]
    total[...] = jnp.zeros(total.shape, f32)

    def step(i, carry):
        base = i * blocks
        rows = [jnp.broadcast_to(grad_out[pl.ds(base + j, 1), :], (8, LANES)) for j in range(blocks)]
        start = pl.multiple_of(base * LANES, LANES)
        for at in range(0, KB, 16):
            basis, row = (upper, at) if at < UPPER else (lower, at - UPPER)
            part = basis[row : row + 16, pl.ds(start, blocks * LANES)].astype(f32)
            for half in range(0, 16, 8):
                acc = total[at + half : at + half + 8, :]
                for j in range(blocks):
                    acc = acc + part[half : half + 8, j * LANES : (j + 1) * LANES] * rows[j]
                total[at + half : at + half + 8, :] = acc
        return carry

    lax.fori_loop(0, shard_rows // blocks, step, 0)
    coefs = jnp.sum(total[...].T, 0, keepdims=True)
    grad = grad_out[...]
    squares = jnp.sum(jnp.sum(grad * grad, 0, keepdims=True), 1, keepdims=True)
    lane = lax.broadcasted_iota(jnp.int32, (1, SUMS - KB), 1)
    rest = jnp.where(lane == 0, squares, 0.0)
    rest = rest + jnp.where(lane == 1, loss[0:1, 0:1], 0.0) + jnp.where(lane == 2, loss[0:1, 1:2], 0.0)
    sums_out[:, 0:KB] = coefs
    sums_out[:, KB:SUMS] = rest


def update_kernel(blocks, whole_len, counts, sums, upper, lower, grad, loss, master, first, second, *refs):
    loss_out, norm_out, coef_out, master_out, first_out, second_out, removed = refs
    norm = jnp.sqrt(sums[0:1, KB : KB + 1])
    factor = jnp.minimum(1.0, CLIP_NORM / (norm + 1e-06))
    lane = lax.broadcasted_iota(jnp.int32, (1, KB), 1)
    limit = jnp.where(lane < KMAX, counts[0], counts[1] + KMAX)
    row = jnp.where(lane < limit, sums[:, 0:KB] * factor, 0.0)
    coef_out[0:1, :] = row[:, 0:KMAX]
    coef_out[1:2, :] = row[:, KMAX:KB]
    norm_out[0] = jnp.sum(norm)
    loss_out[0] = jnp.sum(sums[0:1, KB + 1 : KB + 2])
    loss_out[1] = jnp.sum(sums[0:1, KB + 2 : KB + 3])
    loss_out[2] = jnp.sum(loss[0:1, 2:3])
    high = row.astype(bf16).astype(f32)
    mid = (row - high).astype(bf16).astype(f32)
    low = row - high - mid
    place = lax.broadcasted_iota(jnp.int32, (16, KB), 0)
    split = jnp.where(place == 0, high, jnp.where(place == 1, mid, jnp.where(place == 2, low, 0.0)))
    split = split.astype(bf16)
    rows = grad.shape[0]

    def step(i, carry):
        base = i * blocks
        start = pl.multiple_of(base * LANES, LANES)
        part = dot(split[:, :UPPER], upper[:, pl.ds(start, blocks * LANES)])
        part = part + dot(split[:, UPPER:], lower[:, pl.ds(start, blocks * LANES)])
        part = jnp.sum(part, 0, keepdims=True)
        for j in range(blocks):
            removed[pl.ds(base + j, 1), :] = part[:, j * LANES : (j + 1) * LANES]
        return carry

    lax.fori_loop(0, rows // blocks, step, 0)
    projected = grad[...] * factor - removed[0:rows, :] * (1.0 / whole_len)
    new_first = BETA_ONE * first[...] + (1.0 - BETA_ONE) * projected
    new_second = BETA_TWO * second[...] + (1.0 - BETA_TWO) * projected * projected
    ratio = (
        new_first
        / (1.0 - BETA_ONE**STEP)
        / (jnp.sqrt(new_second / (1.0 - BETA_TWO**STEP)) + ADAM_EPS)
    )
    old = master[...]
    master_out[...] = old - LEARN_RATE * (ratio + WEIGHT_DECAY * old)
    first_out[...] = new_first
    second_out[...] = new_second


def dp_dims(count):
    zed = 4 if count % 4 == 0 else 1
    plane = count // zed
    ex = max(side for side in range(1, math.isqrt(plane) + 1) if plane % side == 0)
    return zed, plane // ex, ex


def moved(value, place, turn=(0, 0, 0), core=0, pairs_too=False):
    def step(index, by, size):
        return index ^ by if pairs_too and paired(size) else (index + by) % size

    pairs = []
    for section in range(2):
        for zed in range(place.z):
            for why in range(place.y):
                for ex in range(place.x):
                    source = (section * place.z + zed) * place.y * place.x + why * place.x + ex
                    there = ((section + core) % 2) * place.z + step(zed, turn[0], place.z)
                    target = (there * place.y + step(why, turn[1], place.y)) * place.x
                    pairs.append((source, target + step(ex, turn[2], place.x)))
    return lax.ppermute(value, ("section", "dp"), pairs)


def add(left, right, resident):
    vmem = pl.BlockSpec(memory_space=pltpu.VMEM)
    return pl.pallas_call(
        add_kernel,
        in_specs=[vmem, vmem] + [pl.BlockSpec(memory_space=pl.ANY)] * 2,
        out_specs=vmem,
        out_shape=jax.ShapeDtypeStruct(left.shape, left.dtype),
        compiler_params=pltpu.CompilerParams(vmem_limit_bytes=2 * 1024 * 1024),
        name="add",
    )(left, right, *resident)


def butterfly(value, place, resident):
    value = add(value, moved(value, place, core=1), resident)
    for axis, size in ((2, place.x), (1, place.y), (0, place.z)):
        span = 1
        while span < size:
            pairs = []
            for index in range(2 * place.count):
                section, rest = divmod(index, place.count)
                at = [rest // (place.y * place.x), rest // place.x % place.y, rest % place.x]
                at[axis] ^= span
                pairs.append((index, section * place.count + (at[0] * place.y + at[1]) * place.x + at[2]))
            value = add(value, lax.ppermute(value, ("section", "dp"), pairs), resident)
            span *= 2
    return value


def whole(shape):
    return pl.BlockSpec(shape, lambda *_: (0,) * len(shape))


def params(megabytes):
    return pltpu.CompilerParams(
        vmem_limit_bytes=megabytes * 1024 * 1024, dimension_semantics=("arbitrary",)
    )


BLOCK_SHAPES = [(D, D)] * 4 + [(D, FF), (FF, D)]
SAVED = [
    ((ROWS, D), f32),
    ((ROWS, D), bf16),
    ((ROWS, D), bf16),
    ((ROWS, D), bf16),
    ((HEADS * ROWS, ROWS), f32),
    ((ROWS, D), bf16),
    ((ROWS, D), f32),
    ((ROWS, FF), bf16),
    ((ROWS, FF), f32),
]
MIDDLE = ((ROWS, D), bf16)
WORK = pl.CostEstimate(flops=3_000_000_000, bytes_accessed=30_000_000, transcendentals=1_000_000)
VMEM = pl.BlockSpec(memory_space=pltpu.VMEM)
SMEM = pl.BlockSpec(memory_space=pltpu.SMEM)
ANY = pl.BlockSpec(memory_space=pl.ANY)


def group_of(per):
    return GROUP if per % GROUP == 0 else 1


def flat_scratch(place):
    flat_rows = place.count * place.shard_rows + SPARE
    return [
        pltpu.VMEM((flat_rows, LANES), f32),
        pltpu.VMEM((flat_rows, LANES), f32),
        pltpu.VMEM((FF + 32, LANES), f32),
    ]


def front(place, per, own, other, patches):
    outs = pl.pallas_call(
        functools.partial(front_kernel, place, per),
        in_specs=[VMEM] * (len(own) + len(other) + 1),
        out_specs=[VMEM] * (len(SAVED) + 1 + len(BLOCK_SHAPES) + 1),
        out_shape=[
            jax.ShapeDtypeStruct((per * shape[0], shape[1]), kind) for shape, kind in SAVED + [MIDDLE]
        ]
        + [jax.ShapeDtypeStruct(shape, bf16) for shape in BLOCK_SHAPES]
        + [jax.ShapeDtypeStruct((VEC_ROWS, FF), f32)],
        scratch_shapes=flat_scratch(place)
        + [pltpu.VMEM((PDIM, D), bf16), pltpu.VMEM((ROWS, D), f32), pltpu.VMEM((per * ROWS, D), f32)],
        compiler_params=pltpu.CompilerParams(vmem_limit_bytes=20 * 1024 * 1024),
        cost_estimate=WORK,
        name="front",
    )(*own, *other, patches)
    return outs[:9], outs[9], outs[10:]


def grad_kind(place):
    return jax.ShapeDtypeStruct((place.count, place.sent_rows, LANES), bf16)


def late(place, per, image_total, labels, replay, own, other, middle, old_logits):
    eight = -(-per // 8) * 8
    return pl.pallas_call(
        functools.partial(late_kernel, place, per, image_total),
        in_specs=[SMEM] * 2 + [VMEM] * (len(own) + len(other) + 2),
        out_specs=[VMEM] * 3,
        out_shape=[
            jax.ShapeDtypeStruct((per * ROWS, D), bf16),
            grad_kind(place),
            jax.ShapeDtypeStruct((1, LANES), f32),
        ],
        scratch_shapes=flat_scratch(place)
        + [pltpu.VMEM((8, 256, LANES), f32)]
        + [pltpu.VMEM(shape, bf16) for shape in BLOCK_SHAPES]
        + [
            pltpu.VMEM((VEC_ROWS, FF), f32),
            pltpu.VMEM((D, CPAD), bf16),
            pltpu.VMEM((1, CPAD), f32),
            pltpu.VMEM((eight, D), f32),
            pltpu.VMEM((per * ROWS, D), f32),
        ],
        compiler_params=pltpu.CompilerParams(vmem_limit_bytes=16 * 1024 * 1024),
        cost_estimate=WORK,
        name="late",
    )(labels, replay, *own, *other, middle, old_logits)


def back(place, per, grad_middle, kept, patches, weights, late_grad):
    return pl.pallas_call(
        functools.partial(back_kernel, place, per),
        in_specs=[VMEM] * (1 + len(kept) + 1 + len(weights) + 1),
        out_specs=[VMEM] * 2,
        out_shape=[grad_kind(place)] * 2,
        scratch_shapes=flat_scratch(place)
        + [pltpu.VMEM((per * ROWS, D), bf16)] * 6
        + [pltpu.VMEM((per * ROWS, FF), bf16)],
        compiler_params=pltpu.CompilerParams(vmem_limit_bytes=20 * 1024 * 1024),
        cost_estimate=WORK,
        name="back",
    )(grad_middle, *kept, patches, *weights, late_grad)


def body(
    patches, labels, replay, old_logits, basis_count, master, first_moment, second_moment, basis
):
    chips = lax.axis_size("dp")
    shard_len = master.shape[1]
    shard_rows = shard_len // LANES
    place = Place(dp_dims(chips), shard_rows)
    images = patches.shape[0]
    per = images // 2
    section = lax.axis_index("section")
    turns = place.turns()

    shard = pl.pallas_call(
        shard_kernel,
        grid=(1,),
        in_specs=[SMEM, whole((shard_rows, LANES))],
        out_specs=whole((place.sent_rows, LANES)),
        out_shape=jax.ShapeDtypeStruct((place.sent_rows, LANES), bf16),
        compiler_params=pltpu.CompilerParams(vmem_limit_bytes=2 * 1024 * 1024),
        name="shard",
    )(
        pltpu.with_memory_space_constraint(replay, pltpu.HBM),
        pltpu.with_memory_space_constraint(master.reshape(shard_rows, LANES), pltpu.HBM),
    )
    mine = lax.dynamic_slice_in_dim(patches, section * per, per, 0)
    early, late_part = shard[: place.first_rows], shard[place.first_rows :]
    column = [early] + [moved(early, place, (d, 0, 0)) for d in range(1, place.z)]
    plane = [moved(late_part, place, (0, a, b)) if a + b else late_part for a, b in turns]
    column[-1], mine = lax.optimization_barrier((column[-1], mine))
    column, plane = jnp.stack(column), jnp.stack(plane)
    own = [moved(column, place, (0, a, b)) if a + b else column for a, b in turns]
    own += [moved(plane, place, (d, 0, 0)) if d else plane for d in range(place.z)]
    other = [moved(piece, place, core=1) for piece in own]

    kept, middle, weights = front(place, per, own, other, mine)
    grad_middle, late_grad, loss = late(
        place, per, float(images * chips), labels, replay, own, other, middle, old_logits
    )
    keep, give = back(place, per, grad_middle, kept, mine, weights, late_grad)

    given = moved(give, place, core=1)

    def kinds(lead, rows, count):
        shape = (*lead, place.z, rows, LANES)
        return [jax.ShapeDtypeStruct(shape, bf16 if i else f32) for i in range(count)]

    one_rows, two_rows = place.half_rows, place.sent_rows - place.half_rows
    parts = pl.pallas_call(
        functools.partial(split_kernel, place),
        in_specs=[VMEM] * 2,
        out_specs=[VMEM] * (place.y + place.x),
        out_shape=kinds((place.x,), one_rows, place.y) + kinds((place.y,), two_rows, place.x),
        compiler_params=pltpu.CompilerParams(vmem_limit_bytes=12 * 1024 * 1024),
        name="split",
    )(keep, given)
    ones, twos = parts[: place.y], parts[place.y :]
    rows_basis = pltpu.with_memory_space_constraint(basis.reshape(KB, shard_len), pltpu.HBM)

    def fetch(first, last, after):
        return pl.pallas_call(
            functools.partial(fetch_kernel, first, last),
            in_specs=[ANY, ANY],
            out_specs=ANY,
            out_shape=pltpu.VMEM((last - first, shard_len), bf16),
            scratch_shapes=[pltpu.SemaphoreType.DMA],
            compiler_params=pltpu.CompilerParams(vmem_limit_bytes=2 * 1024 * 1024),
            cost_estimate=pl.CostEstimate(
                flops=0, bytes_accessed=4 * (last - first) * shard_len, transcendentals=0
            ),
            name="fetch",
        )(after, rows_basis)

    upper = fetch(0, UPPER, ones[-1])

    def along_y(values):
        return [moved(values[i], place, (0, i, 0), pairs_too=True) for i in range(1, place.y)]

    def along_x(values):
        return [moved(values[i], place, (0, 0, i), pairs_too=True) for i in range(1, place.x)]

    arrived = along_y(ones) + along_x(twos)
    parts = pl.pallas_call(
        functools.partial(turn_kernel, place),
        in_specs=[VMEM, VMEM, ANY] + [VMEM] * len(arrived),
        out_specs=[VMEM] * (place.y + place.x),
        out_shape=kinds((), one_rows, place.x) + kinds((), two_rows, place.y),
        compiler_params=pltpu.CompilerParams(vmem_limit_bytes=2 * 1024 * 1024),
        name="turn",
    )(ones[0], twos[0], upper, *arrived)
    ones, twos = parts[: place.x], parts[place.x :]
    arrived = along_x(ones) + along_y(twos)
    piece_shape = (place.sent_rows, LANES)
    first, *rest = pl.pallas_call(
        functools.partial(plane_kernel, place),
        in_specs=[VMEM, VMEM, ANY] + [VMEM] * len(arrived),
        out_specs=[VMEM] * place.z,
        out_shape=[jax.ShapeDtypeStruct(piece_shape, bf16 if d else f32) for d in range(place.z)],
        compiler_params=pltpu.CompilerParams(vmem_limit_bytes=2 * 1024 * 1024),
        name="plane",
    )(ones[0], twos[0], upper, *arrived)
    resident = (upper, fetch(UPPER, KB, rest[0]))
    pieces = [moved(rest[d - 1], place, (d, 0, 0), pairs_too=True) for d in range(1, place.z)]

    def divisor(most):
        return max(n for n in range(1, most + 1) if shard_rows % n == 0)

    flat_kind = jax.ShapeDtypeStruct((shard_rows, LANES), f32)
    grad, sums = pl.pallas_call(
        functools.partial(inner_kernel, divisor(26)),
        in_specs=[VMEM] * (place.z + 3),
        out_specs=[VMEM] * 2,
        out_shape=[flat_kind, jax.ShapeDtypeStruct((1, SUMS), f32)],
        scratch_shapes=[pltpu.VMEM((KB, LANES), f32)],
        compiler_params=pltpu.CompilerParams(vmem_limit_bytes=2 * 1024 * 1024),
        name="inner",
    )(first, *pieces, *resident, loss)
    sums = butterfly(sums, place, resident)
    padded_rows = -(-shard_rows // 8) * 8
    loss_parts, norm, coefficients, new_master, new_first, new_second = pl.pallas_call(
        functools.partial(update_kernel, divisor(312), float(2 * shard_len * chips)),
        in_specs=[SMEM] + [VMEM] * 8,
        out_specs=[SMEM, SMEM] + [VMEM] * 4,
        out_shape=[
            jax.ShapeDtypeStruct((3,), f32),
            jax.ShapeDtypeStruct((1,), f32),
            jax.ShapeDtypeStruct((TASKS, KMAX), f32),
        ]
        + [flat_kind] * 3,
        scratch_shapes=[pltpu.VMEM((padded_rows, LANES), f32)],
        compiler_params=pltpu.CompilerParams(vmem_limit_bytes=2 * 1024 * 1024),
        name="update",
    )(
        basis_count,
        sums,
        *resident,
        grad,
        loss,
        master.reshape(shard_rows, LANES),
        first_moment.reshape(shard_rows, LANES),
        second_moment.reshape(shard_rows, LANES),
    )
    return (
        loss_parts,
        norm[0],
        coefficients,
        new_master.reshape(1, shard_len),
        new_first.reshape(1, shard_len),
        new_second.reshape(1, shard_len),
    )


def solution(mesh):
    in_specs = (
        P("dp", None, None),
        P("dp"),
        P("dp"),
        P("dp", None),
        P(),
        P("section", "dp"),
        P("section", "dp"),
        P("section", "dp"),
        P(None, "section", "dp"),
    )
    out_specs = (P(), P(), P(), P("section", "dp"), P("section", "dp"), P("section", "dp"))
    return jax.shard_map(body, mesh=mesh, in_specs=in_specs, out_specs=out_specs, check_vma=False)
```

```python
import functools
import math

import jax
import jax.numpy as jnp
from jax import lax
from jax.experimental import pallas as pl
from jax.experimental.pallas import tpu as pltpu
from jax.sharding import PartitionSpec as P

HEADS = 3
HD = 64
D = 192
FF = 768
PDIM = 768
PATCHES = 196
TOKENS = PATCHES + 1
ROWS = 208
CLS = PATCHES
GROUP = 4
CLASSES = 1000
CPAD = 1024
TASKS = 2
KMAX = 200
KB = TASKS * KMAX
UPPER = 256
STEP = 10
LANES = 128
HALF = 64
SPARE = 512
SUMS = 512

NORM_EPS = 1e-06
CLIP_NORM = 0.02
LEARN_RATE = 0.05
BETA_ONE = 0.9
BETA_TWO = 0.999
ADAM_EPS = 1e-08
WEIGHT_DECAY = 0.05
SCALE = HD ** (-0.5)
MASKED = -1e30

BLOCK_AT = dict(
    gain_one=0,
    bias_one=3,
    w_qkv=6,
    b_qkv=1734,
    w_out=1740,
    b_out=2316,
    gain_two=2319,
    bias_two=2322,
    w_up=2325,
    b_up=4629,
    w_down=4641,
    b_down=6945,
)
W_PATCH, B_PATCH, CLS_TOKEN, POS_EMBED = 6948, 9252, 9255, 9258
GAIN_LAST, BIAS_LAST, W_HEAD, B_HEAD = 6948, 6951, 6954, 9954
VECTORS = ("gain_one", "bias_one", "b_q", "b_v", "b_out", "gain_two", "bias_two", "b_up", "b_down")
VEC_ROWS = 16

f32 = jnp.float32
bf16 = jnp.bfloat16


def dot(left, right, left_dim=1, right_dim=0):
    return lax.dot_general(
        left, right, (((left_dim,), (right_dim,)), ((), ())), preferred_element_type=f32
    )


def low_lanes(shape):
    return lax.broadcasted_iota(jnp.int32, shape, 1) < HALF


def swap_halves(value):
    return pltpu.roll(value, HALF, 1)


def head_masks():
    lane = lax.broadcasted_iota(jnp.int32, (1, D), 1)
    return [jnp.logical_and(lane >= h * HD, lane < (h + 1) * HD) for h in range(HEADS)]


def by_head(value):
    return jnp.concatenate([jnp.where(m, value, 0.0) for m in head_masks()], 0)


def from_heads(value):
    rows = value.shape[0] // HEADS
    parts = [value[h * rows : (h + 1) * rows] for h in range(HEADS)]
    masks = head_masks()
    return jnp.where(masks[0], parts[0], jnp.where(masks[1], parts[1], parts[2]))


def normalise(rows_in):
    mean = jnp.sum(rows_in, -1, keepdims=True) * (1.0 / D)
    centred = rows_in - mean
    variance = jnp.sum(centred * centred, -1, keepdims=True) * (1.0 / D)
    scale = lax.rsqrt(variance + NORM_EPS)
    return centred * scale, scale


def normalise_back(grad, gain, unit, scale):
    grad_unit = grad * gain
    first = jnp.sum(grad_unit, -1, keepdims=True) * (1.0 / D)
    second = jnp.sum(grad_unit * unit, -1, keepdims=True) * (1.0 / D)
    return scale * (grad_unit - first - unit * second)


def gelu_parts(pre):
    cdf = 0.5 * (1.0 + lax.erf(pre * math.sqrt(0.5)))
    slope = cdf + pre * (jnp.exp(-0.5 * pre * pre) * (1.0 / math.sqrt(2.0 * math.pi)))
    return pre * cdf, slope


def column_sums(value):
    return jnp.sum(value.astype(f32), 0, keepdims=True)


def strided(ref, start, count, stride):
    if count == 1 or stride == 1:
        return ref[pl.ds(start, count), :]
    return ref[pl.ds(start, count, stride=stride), :]


class Flat:
    def __init__(self, even, odd, mix, odd_rows):
        self.even, self.odd, self.mix, self.odd_rows = even, odd, mix, odd_rows

    def shift(self):
        step = 192
        for at in range(0, self.odd_rows, step):
            here = self.even[at : at + step, :]
            after = self.even[at + 1 : at + 1 + step, :]
            self.odd[at : at + step, :] = swap_halves(jnp.where(low_lanes(here.shape), after, here))

    def rows_at(self, half, count, stride):
        return strided(self.odd if half % 2 else self.even, half // 2, count, stride)

    def blocks(self, half, width, rows, cols):
        for at in range(0, cols, LANES):
            start = half + at // HALF
            if rows == 1 or width % 2 == 0:
                value = self.rows_at(start, rows, width // 2)
            else:
                pairs = (rows + 1) // 2
                self.mix[pl.ds(0, pairs, stride=2), :] = self.rows_at(start, pairs, width)
                self.mix[pl.ds(1, pairs, stride=2), :] = self.rows_at(start + width, pairs, width)
                value = self.mix[0:rows, :]
            yield at, min(LANES, cols - at), value

    def read(self, dest, half, width, rows, cols):
        for at, wide, value in self.blocks(half, width, rows, cols):
            dest[0:rows, at : at + wide] = value[:, :wide].astype(dest.dtype)

    def read_row(self, dest, row, half, cols):
        for at, wide, value in self.blocks(half, 2, 1, cols):
            dest[row : row + 1, at : at + wide] = value[:, :wide]

    def clear(self):
        rows = self.odd_rows + 16
        self.even[...] = jnp.zeros(self.even.shape, f32)
        self.odd[0:rows, :] = jnp.zeros((rows, LANES), f32)

    def put_rows(self, half, count, stride, value):
        ref, start = (self.odd, half // 2 + 8) if half % 2 else (self.even, half // 2)
        if count == 1 or stride == 1:
            ref[pl.ds(start, count), :] = value
        else:
            ref[pl.ds(start, count, stride=stride), :] = value

    def write(self, value, half, width, cols):
        rows = value.shape[0]
        for at in range(0, cols, LANES):
            wide = min(LANES, cols - at)
            part = value[:, at : at + wide]
            if wide < LANES:
                part = jnp.concatenate([part, jnp.zeros((rows, LANES - wide), f32)], 1)
            start = half + at // HALF
            if rows == 1 or width % 2 == 0:
                self.put_rows(start, rows, width // 2, part)
            else:
                pairs = (rows + 1) // 2
                self.mix[0:rows, :] = part
                self.put_rows(start, pairs, width, self.mix[pl.ds(0, pairs, stride=2), :])
                self.put_rows(start + width, pairs, width, self.mix[pl.ds(1, pairs, stride=2), :])

    def merged(self, at, count):
        if at >= self.odd_rows:
            return self.even[at : at + count, :]
        here = self.odd[at + 8 : at + 8 + count, :]
        before = self.odd[at + 7 : at + 7 + count, :]
        moved_back = swap_halves(jnp.where(low_lanes(here.shape), here, before))
        return self.even[at : at + count, :] + moved_back


def paired(size):
    return size & (size - 1) == 0


class Place:
    def __init__(self, dims, shard_rows):
        self.z, self.y, self.x = dims
        self.count = self.z * self.y * self.x
        self.shard_rows = shard_rows
        self.sent_rows = -(-(shard_rows + 1) // 16) * 16
        self.first_rows = self.sent_rows * 13 // 20 // 16 * 16

        self.half_rows = self.sent_rows // 32 * 16

    def split(self, index):
        plane = self.y * self.x
        return index // plane, lax.rem(index, plane) // self.x, lax.rem(index, self.x)

    def turns(self):
        return [(a, b) for a in range(self.y) for b in range(self.x)]


def load_section(place, pieces, wanted, flat):
    own, other = pieces
    section = lax.axis_index("section")
    zed, why, ex = place.split(lax.axis_index("dp"))
    rows = place.shard_rows

    def copy(refs):
        for turn, (a, b) in enumerate(place.turns()):
            for d in range(place.z):
                shard = lax.rem(zed + (place.z - d), place.z) * (place.y * place.x)
                shard = shard + lax.rem(why + (place.y - a), place.y) * place.x
                shard = shard + lax.rem(ex + (place.x - b), place.x)
                start = shard * rows
                if rows % 8 == 0:
                    start = pl.multiple_of(start, 8)
                cut = place.first_rows
                flat.even[pl.ds(start, cut), :] = refs[turn][d].astype(f32)
                value = refs[len(place.turns()) + d][turn].astype(f32)
                after = start + cut
                if rows % 8 == 0:
                    after = pl.multiple_of(after, 8)
                flat.even[pl.ds(after, rows - cut), :] = value[: rows - cut]

    @pl.when(section == wanted)
    def _():
        copy(own)

    @pl.when(section != wanted)
    def _():
        copy(other)

    flat.shift()


def read_block(flat, weights, vec):
    at = BLOCK_AT
    w_q, w_k, w_v, w_out, w_up, w_down = weights
    for place, dest in enumerate((w_q, w_k, w_v)):
        flat.read(dest, at["w_qkv"] + 3 * place, 9, D, D)
    flat.read(w_out, at["w_out"], 3, D, D)
    flat.read(w_up, at["w_up"], 12, D, FF)
    flat.read(w_down, at["w_down"], 3, FF, D)
    starts = dict(at, b_q=at["b_qkv"], b_v=at["b_qkv"] + 3)
    for row, name in enumerate(VECTORS):
        flat.read_row(vec, row, starts[name], FF if name == "b_up" else D)


def vector(vec, name):
    row = VECTORS.index(name)
    return vec[row : row + 1, 0 : FF if name == "b_up" else D]


def write_vectors(flat, sums):
    at = BLOCK_AT
    starts = dict(at, b_q=at["b_qkv"], b_v=at["b_qkv"] + 3)
    for name, value in sums.items():
        flat.write(value, starts[name], 2, value.shape[1])


def send_out(place, flat, write):
    zed, why, ex = place.split(lax.axis_index("dp"))
    rows, spare = place.shard_rows, place.sent_rows - place.shard_rows
    for shard in range(place.count):
        zk, yk, xk = shard // (place.y * place.x), shard // place.x % place.y, shard % place.x
        there = ((zk, zed, place.z), (yk, why, place.y), (xk, ex, place.x))
        d, a, b = [to ^ at if paired(size) else lax.rem(to + size - at, size) for to, at, size in there]
        value = flat.merged(shard * rows, rows)
        value = jnp.concatenate([value, jnp.zeros((spare, LANES), f32)], 0)
        write((a * place.x + b) * place.z + d, value.astype(bf16))


def shard_kernel(replay, master, out):
    rows = master.shape[0]
    count = sum(replay[i].astype(f32) for i in range(replay.shape[0]))
    tail = jnp.full((out.shape[0] - rows, LANES), count, f32)
    out[...] = jnp.concatenate([master[...], tail], 0).astype(bf16)


def front_kernel(place, per, *refs):
    parts = len(place.turns()) + place.z
    own, other, refs = refs[:parts], refs[parts : 2 * parts], refs[2 * parts :]
    patches, kept, middle_out, weights = refs[0], refs[1:10], refs[10], refs[11:18]
    even, odd, mix, w_patch, added, tokens = refs[18:]
    vec = weights[-1]
    flat = Flat(even, odd, mix, place.count * place.shard_rows)
    load_section(place, (own, other), 0, flat)
    read_block(flat, weights[:-1], vec)
    flat.read(w_patch, W_PATCH, 3, PDIM, D)
    flat.read_row(vec, 9, B_PATCH, D)
    flat.read_row(vec, 10, CLS_TOKEN, D)
    added[...] = jnp.zeros(added.shape, f32)
    tokens[...] = jnp.zeros(tokens.shape, f32)
    for at, wide, value in flat.blocks(POS_EMBED, 3, TOKENS + 1, D):
        added[0:PATCHES, at : at + wide] = value[1:TOKENS, :wide] + vec[9:10, at : at + wide]
        added[CLS : CLS + 1, at : at + wide] = value[0:1, :wide] + vec[10:11, at : at + wide]
    group = group_of(per)
    for step in range(0, per, group):
        cut = slice(step * ROWS, (step + group) * ROWS)
        front_images(step, cut, patches, kept, middle_out, weights, w_patch, added, tokens)


def front_images(step, cut, patches, kept, middle_out, weights, w_patch, added, tokens):
    x_out, q_out, k_out, v_out, probs_out, mixed_out, hidden_out, act_out, slope_out = kept
    w_q, w_k, w_v, w_out, w_up, w_down, vec = weights
    group = (cut.stop - cut.start) // ROWS
    spans = [slice(i * ROWS, (i + 1) * ROWS) for i in range(group)]
    for i, at in enumerate(spans):
        tokens[cut.start + at.start : cut.start + at.start + PATCHES, :] = dot(patches[step + i], w_patch[...])
    x = tokens[cut, :] + jnp.concatenate([added[...]] * group, 0)
    x_out[cut, :] = x
    unit, _ = normalise(x)
    normed = (unit * vector(vec, "gain_one") + vector(vec, "bias_one")).astype(bf16)
    q = (dot(normed, w_q[...]) + vector(vec, "b_q")).astype(bf16)
    k = dot(normed, w_k[...]).astype(bf16)
    v = (dot(normed, w_v[...]) + vector(vec, "b_v")).astype(bf16)
    q_out[cut, :], k_out[cut, :], v_out[cut, :] = q, k, v
    q_scaled = q.astype(f32) * SCALE
    column = lax.broadcasted_iota(jnp.int32, (1, ROWS), 1)
    scores = [dot(by_head(q_scaled[at]).astype(bf16), k[at], 1, 1) for at in spans]
    scores = [jnp.where(column < TOKENS, value, MASKED) for value in scores]
    raised = [jnp.exp(value - jnp.max(value, -1, keepdims=True)) for value in scores]
    probs = [value * (1.0 / jnp.sum(value, -1, keepdims=True)) for value in raised]
    for i, value in enumerate(probs):
        probs_out[(step + i) * HEADS * ROWS : (step + i + 1) * HEADS * ROWS, :] = value
    mixed = [from_heads(dot(value.astype(bf16), v[at])) for value, at in zip(probs, spans)]
    mixed = jnp.concatenate(mixed, 0).astype(bf16)
    mixed_out[cut, :] = mixed
    hidden = x + dot(mixed, w_out[...]) + vector(vec, "b_out")
    hidden_out[cut, :] = hidden
    unit, _ = normalise(hidden)
    normed = (unit * vector(vec, "gain_two") + vector(vec, "bias_two")).astype(bf16)
    pre = dot(normed, w_up[...]) + vector(vec, "b_up")
    act, slope = gelu_parts(pre)
    act = act.astype(bf16)
    act_out[cut, :], slope_out[cut, :] = act, slope
    middle = hidden + dot(act, w_down[...]) + vector(vec, "b_down")
    middle_out[cut, :] = middle.astype(bf16)


def read_head(flat, wide, w_head, b_head):
    first = W_HEAD // 2
    lane = lax.broadcasted_iota(jnp.int32, (16, LANES), 1)
    for phase in range(16):
        start, off = first + CLASSES * phase // LANES, CLASSES * phase % LANES
        got = [strided(flat.even, start + j, 16, 125) for j in range(9 if off else 8)]
        if off:
            got = [pltpu.roll(g, LANES - off, 1) for g in got]
        for j in range(8):
            value = jnp.where(lane < LANES - off, got[j], got[j + 1]) if off else got[j]
            wide[j, pl.ds(phase, 16, stride=16), :] = value
    lane = lax.broadcasted_iota(jnp.int32, (1, LANES), 1)
    for j in range(8):
        keep = lane + j * LANES < CLASSES
        w_head[:, j * LANES : (j + 1) * LANES] = jnp.where(keep, wide[j, 0:D, :], 0.0).astype(bf16)
        value = flat.even[B_HEAD // 2 + j : B_HEAD // 2 + j + 1, :]
        b_head[0:1, j * LANES : (j + 1) * LANES] = jnp.where(keep, value, 0.0)


def write_head(flat, wide, grad_w, grad_b):
    first = W_HEAD // 2
    for j in range(8):
        wide[j, 0:D, :] = grad_w[:, j * LANES : (j + 1) * LANES]
        wide[j, D:, :] = jnp.zeros((wide.shape[1] - D, LANES), f32)
    lane = lax.broadcasted_iota(jnp.int32, (16, LANES), 1)
    for phase in range(16):
        start, off = first + CLASSES * phase // LANES, CLASSES * phase % LANES
        got = [wide[j, pl.ds(phase, 16, stride=16), :] for j in range(8)]
        if off:
            got = [pltpu.roll(g, off, 1) for g in got]
        for j in range(9 if off else 8):
            if not off:
                value = got[j]
            else:
                before = got[j - 1] if j else jnp.zeros((16, LANES), f32)
                value = jnp.where(lane < off, before, got[j] if j < 8 else 0.0)
            flat.even[pl.ds(start + j, 16, stride=125), :] += value
    for j in range(8):
        row = B_HEAD // 2 + j
        flat.even[row : row + 1, :] += grad_b[:, j * LANES : (j + 1) * LANES]


def late_kernel(place, per, image_total, labels, replay, *refs):
    section = lax.axis_index("section")
    parts = len(place.turns()) + place.z
    odd_rows = -(-(W_HEAD // 2 + 1) // place.shard_rows) * place.shard_rows
    own, other, refs = refs[:parts], refs[parts : 2 * parts], refs[2 * parts :]
    middle, old_logits, back_out, grad_out, loss_out = refs[:5]
    even, odd, mix, wide, w_q, w_k, w_v, w_out, w_up, w_down, vec, w_head, b_head, few, many = refs[5:]
    flat = Flat(even, odd, mix, odd_rows)
    load_section(place, (own, other), 1, flat)
    read_block(flat, (w_q, w_k, w_v, w_out, w_up, w_down), vec)
    flat.read_row(vec, 9, GAIN_LAST, D)
    flat.read_row(vec, 10, BIAS_LAST, D)
    read_head(flat, wide, w_head, b_head)
    gain_last, bias_last = vec[9:10, 0:D], vec[10:11, 0:D]
    carried = jnp.zeros((1, LANES), f32)
    carrier = place.shard_rows - place.first_rows
    for ref in own[len(place.turns()) :]:
        for turn in range(len(place.turns())):
            carried = carried + ref[turn].astype(f32)[carrier : carrier + 1]
    replay_count = carried[:, 0:1]

    x = middle[...].astype(f32)
    unit, scale = normalise(x)
    normed_f = unit * vector(vec, "gain_one") + vector(vec, "bias_one")
    normed = normed_f.astype(bf16)
    k = dot(normed, w_k[...]).astype(bf16)
    v = (dot(normed, w_v[...]) + vector(vec, "b_v")).astype(bf16)

    def class_rows(value):
        few[...] = jnp.zeros(few.shape, f32)
        for i in range(per):
            few[i : i + 1, :] = value[i * ROWS + CLS : i * ROWS + CLS + 1, :]
        return few[...]

    eight = few.shape[0]
    image = lax.broadcasted_iota(jnp.int32, (eight, 1), 0)
    real = image < per
    x_top = class_rows(x)
    top_normed = class_rows(normed_f).astype(bf16)
    q = (dot(top_normed, w_q[...]) + vector(vec, "b_q")).astype(bf16)
    q_heads = by_head(jnp.where(real, q.astype(f32) * SCALE, 0.0)).astype(bf16)
    scores = dot(q_heads, k, 1, 1)
    column = lax.broadcasted_iota(jnp.int32, scores.shape, 1)
    owner = lax.rem(lax.broadcasted_iota(jnp.int32, scores.shape, 0), eight) * ROWS
    inside = jnp.logical_and(column >= owner, column < owner + TOKENS)
    scores = jnp.where(inside, scores, MASKED)
    raised = jnp.where(inside, jnp.exp(scores - jnp.max(scores, -1, keepdims=True)), 0.0)
    total = jnp.sum(raised, -1, keepdims=True)
    probs = raised * (1.0 / jnp.where(total > 0.0, total, 1.0))
    probs_low = probs.astype(bf16)
    mixed = from_heads(dot(probs_low, v)).astype(bf16)
    hidden = x_top + dot(mixed, w_out[...]) + vector(vec, "b_out")
    unit_two, scale_two = normalise(hidden)
    normed_two = (unit_two * vector(vec, "gain_two") + vector(vec, "bias_two")).astype(bf16)
    act, slope = gelu_parts(dot(normed_two, w_up[...]) + vector(vec, "b_up"))
    act = act.astype(bf16)
    final = hidden + dot(act, w_down[...]) + vector(vec, "b_down")

    unit_last, scale_last = normalise(final)
    top = (unit_last * gain_last + bias_last).astype(bf16)
    classes = lax.broadcasted_iota(jnp.int32, (eight, CPAD), 1)
    logits = dot(top, w_head[...]) + b_head[...]
    logits = jnp.where(classes < CLASSES, logits, MASKED)
    highest = jnp.max(logits, -1, keepdims=True)
    log_total = highest + jnp.log(jnp.sum(jnp.exp(logits - highest), -1, keepdims=True))
    label = jnp.zeros((eight, 1), jnp.int32)
    again = jnp.zeros((eight, 1), f32)
    for i in range(per):
        label = jnp.where(image == i, labels[section * per + i], label)
        again = jnp.where(image == i, replay[section * per + i].astype(f32), again)
    picked = jnp.logical_and(classes == label, real)
    entropy = jnp.where(real, log_total, 0.0) - jnp.sum(jnp.where(picked, logits, 0.0), -1, keepdims=True)
    wanted = jnp.where(section == 0, old_logits[0:per, :], old_logits[per : 2 * per, :])
    if per < eight:
        wanted = jnp.concatenate([wanted, jnp.zeros((eight - per, CLASSES), f32)], 0)
    wanted = jnp.concatenate([wanted, jnp.zeros((eight, CPAD - CLASSES), f32)], 1)
    distance = jnp.where(jnp.logical_and(classes < CLASSES, real), logits - wanted, 0.0)
    squares = again * (jnp.sum(distance * distance, -1, keepdims=True) * (1.0 / CLASSES))
    lane = lax.broadcasted_iota(jnp.int32, (1, LANES), 1)
    entropy_sum = jnp.sum(entropy, 0, keepdims=True)
    replay_sum = jnp.sum(squares, 0, keepdims=True)
    loss_out[...] = jnp.where(lane == 0, entropy_sum, jnp.where(lane == 1, replay_sum, replay_count))

    grad = (jnp.exp(logits - log_total) - jnp.where(picked, 1.0, 0.0)) * (1.0 / image_total)
    grad = grad + again * 2.0 * distance / (CLASSES * replay_count)
    grad = jnp.where(jnp.logical_and(classes < CLASSES, real), grad, 0.0)
    grad_low = grad.astype(bf16)
    flat.clear()
    write_head(flat, wide, dot(top, grad_low, 0, 0), column_sums(grad_low))
    sums = {}
    grad = dot(grad_low, w_head[...], 1, 1)
    flat.write(column_sums(grad * unit_last), GAIN_LAST, 2, D)
    flat.write(column_sums(grad), BIAS_LAST, 2, D)
    grad = normalise_back(grad, gain_last, unit_last, scale_last)

    at = BLOCK_AT
    grad_down = grad.astype(bf16)
    flat.write(dot(act, grad_down, 0, 0), at["w_down"], 3, D)
    sums["b_down"] = column_sums(grad_down)
    grad_up = (dot(grad_down, w_down[...], 1, 1) * slope).astype(bf16)
    flat.write(dot(normed_two, grad_up, 0, 0), at["w_up"], 12, FF)
    sums["b_up"] = column_sums(grad_up)
    grad_two = dot(grad_up, w_up[...], 1, 1)
    sums["gain_two"], sums["bias_two"] = column_sums(grad_two * unit_two), column_sums(grad_two)
    grad_hidden = grad + normalise_back(grad_two, vector(vec, "gain_two"), unit_two, scale_two)
    branch = grad_hidden.astype(bf16)
    flat.write(dot(mixed, branch, 0, 0), at["w_out"], 3, D)
    sums["b_out"] = column_sums(branch)
    mixed_heads = by_head(dot(branch, w_out[...], 1, 1).astype(bf16).astype(f32)).astype(bf16)
    grad_probs = dot(mixed_heads, v, 1, 1)
    grad_v = dot(probs_low, mixed_heads, 0, 0).astype(bf16)
    inner = jnp.sum(grad_probs * probs, -1, keepdims=True)
    grad_scores = (probs * (grad_probs - inner)).astype(bf16)
    grad_q = (from_heads(dot(grad_scores, k)) * SCALE).astype(bf16)
    grad_k = dot(grad_scores, q_heads, 0, 0).astype(bf16)
    flat.write(dot(top_normed, grad_q, 0, 0), at["w_qkv"], 9, D)
    flat.write(dot(normed, grad_k, 0, 0), at["w_qkv"] + 3, 9, D)
    flat.write(dot(normed, grad_v, 0, 0), at["w_qkv"] + 6, 9, D)
    sums["b_q"], sums["b_v"] = column_sums(grad_q), column_sums(grad_v)
    many[...] = dot(grad_k, w_k[...], 1, 1) + dot(grad_v, w_v[...], 1, 1)
    top_back = dot(grad_q, w_q[...], 1, 1)
    for i in range(per):
        many[i * ROWS + CLS : i * ROWS + CLS + 1, :] += top_back[i : i + 1, :]
    grad_one = many[...]
    sums["gain_one"], sums["bias_one"] = column_sums(grad_one * unit), column_sums(grad_one)
    many[...] = normalise_back(grad_one, vector(vec, "gain_one"), unit, scale)
    for i in range(per):
        many[i * ROWS + CLS : i * ROWS + CLS + 1, :] += grad_hidden[i : i + 1, :]
    back_out[...] = many[...].astype(bf16)
    write_vectors(flat, sums)

    def store(at, value):
        grad_out[at] = value

    send_out(place, flat, store)


def back_kernel(place, per, *refs):
    grad_in, kept, patches, weights = refs[0], refs[1:10], refs[10], refs[11:18]
    late_grad, keep_out, give_out = refs[18:21]
    even, odd, mix, *operands = refs[21:]
    s_normed, s_q, s_k, s_v, s_branch, s_two, s_up = operands
    vec = weights[-1]
    group = group_of(per)
    sums = {}
    embedded = []
    positions = jnp.zeros((ROWS, D), f32)
    for step in range(0, per, group):
        cut = slice(step * ROWS, (step + group) * ROWS)
        vectors, grad_x = back_images(step, cut, grad_in, kept, weights, operands)
        sums = {name: sums[name] + value if sums else value for name, value in vectors.items()}
        for i in range(group):
            embedded.append(grad_x[i * ROWS : i * ROWS + PATCHES].astype(bf16))
            positions = positions + grad_x[i * ROWS : (i + 1) * ROWS]

    at = BLOCK_AT
    flat = Flat(even, odd, mix, place.count * place.shard_rows)
    flat.clear()
    normed = s_normed[...]
    for part, ref in enumerate((s_q, s_k, s_v)):
        flat.write(dot(normed, ref[...], 0, 0), at["w_qkv"] + 3 * part, 9, D)
    flat.write(dot(kept[5][...], s_branch[...], 0, 0), at["w_out"], 3, D)
    flat.write(dot(s_two[...], s_up[...], 0, 0), at["w_up"], 12, FF)
    flat.write(dot(kept[7][...], grad_in[...], 0, 0), at["w_down"], 3, D)
    grad_patch = sum(dot(patches[i], value, 0, 0) for i, value in enumerate(embedded))
    flat.write(grad_patch, W_PATCH, 3, D)
    sums["b_q"], sums["b_v"] = column_sums(s_q[...]), column_sums(s_v[...])
    sums["b_out"], sums["b_up"] = column_sums(s_branch[...]), column_sums(s_up[...])
    sums["b_down"] = column_sums(grad_in[...])
    write_vectors(flat, sums)
    flat.write(sum(column_sums(value) for value in embedded), B_PATCH, 2, D)
    token = positions[CLS : CLS + 1, :]
    flat.write(token, CLS_TOKEN, 2, D)
    natural = jnp.concatenate([token, positions[0:PATCHES, :], jnp.zeros((1, D), f32)], 0)
    flat.write(natural, POS_EMBED, 3, D)

    section = lax.axis_index("section")

    @pl.when(section == 0)
    def _():
        def store(at, value):
            keep_out[at] = value
            give_out[at] = late_grad[at]

        send_out(place, flat, store)

    @pl.when(section != 0)
    def _():
        def store(at, value):
            give_out[at] = value
            keep_out[at] = late_grad[at]

        send_out(place, flat, store)


def back_images(step, cut, grad_in, kept, weights, operands):
    x_in, q_in, k_in, v_in, probs_in, mixed_in, hidden_in, act_in, slope_in = kept
    w_q, w_k, w_v, w_out, w_up, w_down, vec = weights
    s_normed, s_q, s_k, s_v, s_branch, s_two, s_up = operands
    group = (cut.stop - cut.start) // ROWS
    spans = [slice(i * ROWS, (i + 1) * ROWS) for i in range(group)]
    sums = {}
    grad_low = grad_in[cut, :]
    grad_up = (dot(grad_low, w_down[...], 1, 1) * slope_in[cut, :]).astype(bf16)
    s_up[cut, :] = grad_up
    unit, scale = normalise(hidden_in[cut, :])
    s_two[cut, :] = (unit * vector(vec, "gain_two") + vector(vec, "bias_two")).astype(bf16)
    grad_two = dot(grad_up, w_up[...], 1, 1)
    sums["gain_two"], sums["bias_two"] = column_sums(grad_two * unit), column_sums(grad_two)
    grad_hidden = grad_low.astype(f32) + normalise_back(grad_two, vector(vec, "gain_two"), unit, scale)
    branch = grad_hidden.astype(bf16)
    s_branch[cut, :] = branch
    grad_mixed = dot(branch, w_out[...], 1, 1).astype(bf16).astype(f32)
    mixed_heads = [by_head(grad_mixed[at]).astype(bf16) for at in spans]
    q_scaled = q_in[cut, :].astype(f32) * SCALE
    q_heads = [by_head(q_scaled[at]).astype(bf16) for at in spans]
    k, v = k_in[cut, :], v_in[cut, :]
    probs = [
        probs_in[(step + i) * HEADS * ROWS : (step + i + 1) * HEADS * ROWS, :] for i in range(group)
    ]
    grad_probs = [dot(value, v[at], 1, 1) for value, at in zip(mixed_heads, spans)]
    grad_v = [dot(value.astype(bf16), right, 0, 0) for value, right in zip(probs, mixed_heads)]
    inner = [jnp.sum(one * two, -1, keepdims=True) for one, two in zip(grad_probs, probs)]
    grad_scores = [(two * (one - less)).astype(bf16) for one, two, less in zip(grad_probs, probs, inner)]
    grad_q = [from_heads(dot(value, k[at])) * SCALE for value, at in zip(grad_scores, spans)]
    grad_k = [dot(value, right, 0, 0) for value, right in zip(grad_scores, q_heads)]
    grad_q, grad_k, grad_v = [jnp.concatenate(value, 0).astype(bf16) for value in (grad_q, grad_k, grad_v)]
    s_q[cut, :], s_k[cut, :], s_v[cut, :] = grad_q, grad_k, grad_v
    unit, scale = normalise(x_in[cut, :])
    s_normed[cut, :] = (unit * vector(vec, "gain_one") + vector(vec, "bias_one")).astype(bf16)
    grad_one = dot(grad_q, w_q[...], 1, 1) + dot(grad_k, w_k[...], 1, 1) + dot(grad_v, w_v[...], 1, 1)
    sums["gain_one"], sums["bias_one"] = column_sums(grad_one * unit), column_sums(grad_one)
    return sums, grad_hidden + normalise_back(grad_one, vector(vec, "gain_one"), unit, scale)


def fetch_kernel(first, last, _, basis, kept, sem):
    copy = pltpu.make_async_copy(basis.at[pl.ds(first, last - first)], kept, sem)
    copy.start()
    copy.wait()


def add_kernel(left, right, _, __, total):
    total[...] = left[...] + right[...]


def split_kernel(place, keep, given, *outs):
    cut = place.half_rows
    for place_y in range(place.y):
        for place_x in range(place.x):
            for d in range(place.z):
                at = (place_y * place.x + place_x) * place.z + d
                total = keep[at].astype(f32) + given[at].astype(f32)
                one, two = outs[place_y], outs[place.y + place_x]
                one[place_x, d] = total[:cut].astype(one.dtype)
                two[place_y, d] = total[cut:].astype(two.dtype)


def turn_kernel(place, one, two, _, *refs):
    count = place.y + place.x
    arrived, outs = refs[: count - 2], refs[count - 2 :]
    for own, came, parts in (
        (one, arrived[: place.y - 1], outs[: place.x]),
        (two, arrived[place.y - 1 :], outs[place.x :]),
    ):
        for step, out in enumerate(parts):
            for d in range(place.z):
                total = own[step, d]
                for ref in came:
                    total = total + ref[step, d].astype(f32)
                out[d] = total.astype(out.dtype)


def plane_kernel(place, one, two, _, *refs):
    arrived, (whole_out, *outs) = refs[: -place.z], refs[-place.z :]
    for d in range(place.z):
        upper, lower = one[d], two[d]
        for ref in arrived[: place.x - 1]:
            upper = upper + ref[d].astype(f32)
        for ref in arrived[place.x - 1 :]:
            lower = lower + ref[d].astype(f32)
        out = outs[d - 1] if d else whole_out
        out[0 : place.half_rows, :] = upper.astype(out.dtype)
        out[place.half_rows :, :] = lower.astype(out.dtype)


def inner_kernel(blocks, *refs):
    first, pieces, (upper, lower, loss, grad_out, sums_out, total) = refs[0], refs[1:-6], refs[-6:]
    shard_rows = grad_out.shape[0]
    value = first[...]
    for ref in pieces:
        value = value + ref[...].astype(f32)
    grad_out[...] = value[:shard_rows]
    total[...] = jnp.zeros(total.shape, f32)

    def step(i, carry):
        base = i * blocks
        rows = [jnp.broadcast_to(grad_out[pl.ds(base + j, 1), :], (8, LANES)) for j in range(blocks)]
        start = pl.multiple_of(base * LANES, LANES)
        for at in range(0, KB, 16):
            basis, row = (upper, at) if at < UPPER else (lower, at - UPPER)
            part = basis[row : row + 16, pl.ds(start, blocks * LANES)].astype(f32)
            for half in range(0, 16, 8):
                acc = total[at + half : at + half + 8, :]
                for j in range(blocks):
                    acc = acc + part[half : half + 8, j * LANES : (j + 1) * LANES] * rows[j]
                total[at + half : at + half + 8, :] = acc
        return carry

    lax.fori_loop(0, shard_rows // blocks, step, 0)
    coefs = jnp.sum(total[...].T, 0, keepdims=True)
    grad = grad_out[...]
    squares = jnp.sum(jnp.sum(grad * grad, 0, keepdims=True), 1, keepdims=True)
    lane = lax.broadcasted_iota(jnp.int32, (1, SUMS - KB), 1)
    rest = jnp.where(lane == 0, squares, 0.0)
    rest = rest + jnp.where(lane == 1, loss[0:1, 0:1], 0.0) + jnp.where(lane == 2, loss[0:1, 1:2], 0.0)
    sums_out[:, 0:KB] = coefs
    sums_out[:, KB:SUMS] = rest


def update_kernel(blocks, whole_len, counts, sums, upper, lower, grad, loss, master, first, second, *refs):
    loss_out, norm_out, coef_out, master_out, first_out, second_out, removed = refs
    norm = jnp.sqrt(sums[0:1, KB : KB + 1])
    factor = jnp.minimum(1.0, CLIP_NORM / (norm + 1e-06))
    lane = lax.broadcasted_iota(jnp.int32, (1, KB), 1)
    limit = jnp.where(lane < KMAX, counts[0], counts[1] + KMAX)
    row = jnp.where(lane < limit, sums[:, 0:KB] * factor, 0.0)
    coef_out[0:1, :] = row[:, 0:KMAX]
    coef_out[1:2, :] = row[:, KMAX:KB]
    norm_out[0] = jnp.sum(norm)
    loss_out[0] = jnp.sum(sums[0:1, KB + 1 : KB + 2])
    loss_out[1] = jnp.sum(sums[0:1, KB + 2 : KB + 3])
    loss_out[2] = jnp.sum(loss[0:1, 2:3])
    high = row.astype(bf16).astype(f32)
    mid = (row - high).astype(bf16).astype(f32)
    low = row - high - mid
    place = lax.broadcasted_iota(jnp.int32, (16, KB), 0)
    split = jnp.where(place == 0, high, jnp.where(place == 1, mid, jnp.where(place == 2, low, 0.0)))
    split = split.astype(bf16)
    rows = grad.shape[0]

    def step(i, carry):
        base = i * blocks
        start = pl.multiple_of(base * LANES, LANES)
        part = dot(split[:, :UPPER], upper[:, pl.ds(start, blocks * LANES)])
        part = part + dot(split[:, UPPER:], lower[:, pl.ds(start, blocks * LANES)])
        part = jnp.sum(part, 0, keepdims=True)
        for j in range(blocks):
            removed[pl.ds(base + j, 1), :] = part[:, j * LANES : (j + 1) * LANES]
        return carry

    lax.fori_loop(0, rows // blocks, step, 0)
    projected = grad[...] * factor - removed[0:rows, :] * (1.0 / whole_len)
    new_first = BETA_ONE * first[...] + (1.0 - BETA_ONE) * projected
    new_second = BETA_TWO * second[...] + (1.0 - BETA_TWO) * projected * projected
    ratio = (
        new_first
        / (1.0 - BETA_ONE**STEP)
        / (jnp.sqrt(new_second / (1.0 - BETA_TWO**STEP)) + ADAM_EPS)
    )
    old = master[...]
    master_out[...] = old - LEARN_RATE * (ratio + WEIGHT_DECAY * old)
    first_out[...] = new_first
    second_out[...] = new_second


def dp_dims(count):
    zed = 4 if count % 4 == 0 else 1
    plane = count // zed
    ex = max(side for side in range(1, math.isqrt(plane) + 1) if plane % side == 0)
    return zed, plane // ex, ex


def moved(value, place, turn=(0, 0, 0), core=0, pairs_too=False):
    def step(index, by, size):
        return index ^ by if pairs_too and paired(size) else (index + by) % size

    pairs = []
    for section in range(2):
        for zed in range(place.z):
            for why in range(place.y):
                for ex in range(place.x):
                    source = (section * place.z + zed) * place.y * place.x + why * place.x + ex
                    there = ((section + core) % 2) * place.z + step(zed, turn[0], place.z)
                    target = (there * place.y + step(why, turn[1], place.y)) * place.x
                    pairs.append((source, target + step(ex, turn[2], place.x)))
    return lax.ppermute(value, ("section", "dp"), pairs)


def add(left, right, resident):
    vmem = pl.BlockSpec(memory_space=pltpu.VMEM)
    return pl.pallas_call(
        add_kernel,
        in_specs=[vmem, vmem] + [pl.BlockSpec(memory_space=pl.ANY)] * 2,
        out_specs=vmem,
        out_shape=jax.ShapeDtypeStruct(left.shape, left.dtype),
        compiler_params=pltpu.CompilerParams(vmem_limit_bytes=2 * 1024 * 1024),
        name="add",
    )(left, right, *resident)


def butterfly(value, place, resident):
    value = add(value, moved(value, place, core=1), resident)
    for axis, size in ((2, place.x), (1, place.y), (0, place.z)):
        span = 1
        while span < size:
            pairs = []
            for index in range(2 * place.count):
                section, rest = divmod(index, place.count)
                at = [rest // (place.y * place.x), rest // place.x % place.y, rest % place.x]
                at[axis] ^= span
                pairs.append((index, section * place.count + (at[0] * place.y + at[1]) * place.x + at[2]))
            value = add(value, lax.ppermute(value, ("section", "dp"), pairs), resident)
            span *= 2
    return value


def whole(shape):
    return pl.BlockSpec(shape, lambda *_: (0,) * len(shape))


def params(megabytes):
    return pltpu.CompilerParams(
        vmem_limit_bytes=megabytes * 1024 * 1024, dimension_semantics=("arbitrary",)
    )


BLOCK_SHAPES = [(D, D)] * 4 + [(D, FF), (FF, D)]
SAVED = [
    ((ROWS, D), f32),
    ((ROWS, D), bf16),
    ((ROWS, D), bf16),
    ((ROWS, D), bf16),
    ((HEADS * ROWS, ROWS), f32),
    ((ROWS, D), bf16),
    ((ROWS, D), f32),
    ((ROWS, FF), bf16),
    ((ROWS, FF), f32),
]
MIDDLE = ((ROWS, D), bf16)
WORK = pl.CostEstimate(flops=3_000_000_000, bytes_accessed=30_000_000, transcendentals=1_000_000)
VMEM = pl.BlockSpec(memory_space=pltpu.VMEM)
SMEM = pl.BlockSpec(memory_space=pltpu.SMEM)
ANY = pl.BlockSpec(memory_space=pl.ANY)


def group_of(per):
    return GROUP if per % GROUP == 0 else 1


def flat_scratch(place):
    flat_rows = place.count * place.shard_rows + SPARE
    return [
        pltpu.VMEM((flat_rows, LANES), f32),
        pltpu.VMEM((flat_rows, LANES), f32),
        pltpu.VMEM((FF + 32, LANES), f32),
    ]


def front(place, per, own, other, patches):
    outs = pl.pallas_call(
        functools.partial(front_kernel, place, per),
        in_specs=[VMEM] * (len(own) + len(other) + 1),
        out_specs=[VMEM] * (len(SAVED) + 1 + len(BLOCK_SHAPES) + 1),
        out_shape=[
            jax.ShapeDtypeStruct((per * shape[0], shape[1]), kind) for shape, kind in SAVED + [MIDDLE]
        ]
        + [jax.ShapeDtypeStruct(shape, bf16) for shape in BLOCK_SHAPES]
        + [jax.ShapeDtypeStruct((VEC_ROWS, FF), f32)],
        scratch_shapes=flat_scratch(place)
        + [pltpu.VMEM((PDIM, D), bf16), pltpu.VMEM((ROWS, D), f32), pltpu.VMEM((per * ROWS, D), f32)],
        compiler_params=pltpu.CompilerParams(vmem_limit_bytes=20 * 1024 * 1024),
        cost_estimate=WORK,
        name="front",
    )(*own, *other, patches)
    return outs[:9], outs[9], outs[10:]


def grad_kind(place):
    return jax.ShapeDtypeStruct((place.count, place.sent_rows, LANES), bf16)


def late(place, per, image_total, labels, replay, own, other, middle, old_logits):
    eight = -(-per // 8) * 8
    return pl.pallas_call(
        functools.partial(late_kernel, place, per, image_total),
        in_specs=[SMEM] * 2 + [VMEM] * (len(own) + len(other) + 2),
        out_specs=[VMEM] * 3,
        out_shape=[
            jax.ShapeDtypeStruct((per * ROWS, D), bf16),
            grad_kind(place),
            jax.ShapeDtypeStruct((1, LANES), f32),
        ],
        scratch_shapes=flat_scratch(place)
        + [pltpu.VMEM((8, 256, LANES), f32)]
        + [pltpu.VMEM(shape, bf16) for shape in BLOCK_SHAPES]
        + [
            pltpu.VMEM((VEC_ROWS, FF), f32),
            pltpu.VMEM((D, CPAD), bf16),
            pltpu.VMEM((1, CPAD), f32),
            pltpu.VMEM((eight, D), f32),
            pltpu.VMEM((per * ROWS, D), f32),
        ],
        compiler_params=pltpu.CompilerParams(vmem_limit_bytes=16 * 1024 * 1024),
        cost_estimate=WORK,
        name="late",
    )(labels, replay, *own, *other, middle, old_logits)


def back(place, per, grad_middle, kept, patches, weights, late_grad):
    return pl.pallas_call(
        functools.partial(back_kernel, place, per),
        in_specs=[VMEM] * (1 + len(kept) + 1 + len(weights) + 1),
        out_specs=[VMEM] * 2,
        out_shape=[grad_kind(place)] * 2,
        scratch_shapes=flat_scratch(place)
        + [pltpu.VMEM((per * ROWS, D), bf16)] * 6
        + [pltpu.VMEM((per * ROWS, FF), bf16)],
        compiler_params=pltpu.CompilerParams(vmem_limit_bytes=20 * 1024 * 1024),
        cost_estimate=WORK,
        name="back",
    )(grad_middle, *kept, patches, *weights, late_grad)


def body(
    patches, labels, replay, old_logits, basis_count, master, first_moment, second_moment, basis
):
    chips = lax.axis_size("dp")
    shard_len = master.shape[1]
    shard_rows = shard_len // LANES
    place = Place(dp_dims(chips), shard_rows)
    images = patches.shape[0]
    per = images // 2
    section = lax.axis_index("section")
    turns = place.turns()

    shard = pl.pallas_call(
        shard_kernel,
        grid=(1,),
        in_specs=[SMEM, whole((shard_rows, LANES))],
        out_specs=whole((place.sent_rows, LANES)),
        out_shape=jax.ShapeDtypeStruct((place.sent_rows, LANES), bf16),
        compiler_params=pltpu.CompilerParams(vmem_limit_bytes=2 * 1024 * 1024),
        name="shard",
    )(
        pltpu.with_memory_space_constraint(replay, pltpu.HBM),
        pltpu.with_memory_space_constraint(master.reshape(shard_rows, LANES), pltpu.HBM),
    )
    mine = lax.dynamic_slice_in_dim(patches, section * per, per, 0)
    early, late_part = shard[: place.first_rows], shard[place.first_rows :]
    column = [early] + [moved(early, place, (d, 0, 0)) for d in range(1, place.z)]
    plane = [moved(late_part, place, (0, a, b)) if a + b else late_part for a, b in turns]
    column[1], mine = lax.optimization_barrier((column[1], mine))
    column, plane = jnp.stack(column), jnp.stack(plane)
    own = [moved(column, place, (0, a, b)) if a + b else column for a, b in turns]
    own += [moved(plane, place, (d, 0, 0)) if d else plane for d in range(place.z)]
    other = [moved(piece, place, core=1) for piece in own]

    kept, middle, weights = front(place, per, own, other, mine)
    grad_middle, late_grad, loss = late(
        place, per, float(images * chips), labels, replay, own, other, middle, old_logits
    )
    keep, give = back(place, per, grad_middle, kept, mine, weights, late_grad)

    given = moved(give, place, core=1)

    def kinds(lead, rows, count):
        shape = (*lead, place.z, rows, LANES)
        return [jax.ShapeDtypeStruct(shape, bf16 if i else f32) for i in range(count)]

    one_rows, two_rows = place.half_rows, place.sent_rows - place.half_rows
    parts = pl.pallas_call(
        functools.partial(split_kernel, place),
        in_specs=[VMEM] * 2,
        out_specs=[VMEM] * (place.y + place.x),
        out_shape=kinds((place.x,), one_rows, place.y) + kinds((place.y,), two_rows, place.x),
        compiler_params=pltpu.CompilerParams(vmem_limit_bytes=12 * 1024 * 1024),
        name="split",
    )(keep, given)
    ones, twos = parts[: place.y], parts[place.y :]
    rows_basis = pltpu.with_memory_space_constraint(basis.reshape(KB, shard_len), pltpu.HBM)

    def fetch(first, last, after):
        return pl.pallas_call(
            functools.partial(fetch_kernel, first, last),
            in_specs=[ANY, ANY],
            out_specs=ANY,
            out_shape=pltpu.VMEM((last - first, shard_len), bf16),
            scratch_shapes=[pltpu.SemaphoreType.DMA],
            compiler_params=pltpu.CompilerParams(vmem_limit_bytes=2 * 1024 * 1024),
            cost_estimate=pl.CostEstimate(
                flops=0, bytes_accessed=4 * (last - first) * shard_len, transcendentals=0
            ),
            name="fetch",
        )(after, rows_basis)

    upper = fetch(0, UPPER, ones[-1])

    def along_y(values):
        return [moved(values[i], place, (0, i, 0), pairs_too=True) for i in range(1, place.y)]

    def along_x(values):
        return [moved(values[i], place, (0, 0, i), pairs_too=True) for i in range(1, place.x)]

    arrived = along_y(ones) + along_x(twos)
    parts = pl.pallas_call(
        functools.partial(turn_kernel, place),
        in_specs=[VMEM, VMEM, ANY] + [VMEM] * len(arrived),
        out_specs=[VMEM] * (place.y + place.x),
        out_shape=kinds((), one_rows, place.x) + kinds((), two_rows, place.y),
        compiler_params=pltpu.CompilerParams(vmem_limit_bytes=2 * 1024 * 1024),
        name="turn",
    )(ones[0], twos[0], upper, *arrived)
    ones, twos = parts[: place.x], parts[place.x :]
    arrived = along_x(ones) + along_y(twos)
    piece_shape = (place.sent_rows, LANES)
    first, *rest = pl.pallas_call(
        functools.partial(plane_kernel, place),
        in_specs=[VMEM, VMEM, ANY] + [VMEM] * len(arrived),
        out_specs=[VMEM] * place.z,
        out_shape=[jax.ShapeDtypeStruct(piece_shape, bf16 if d else f32) for d in range(place.z)],
        compiler_params=pltpu.CompilerParams(vmem_limit_bytes=2 * 1024 * 1024),
        name="plane",
    )(ones[0], twos[0], upper, *arrived)
    resident = (upper, fetch(UPPER, KB, rest[0]))
    pieces = [moved(rest[d - 1], place, (d, 0, 0), pairs_too=True) for d in range(1, place.z)]

    def divisor(most):
        return max(n for n in range(1, most + 1) if shard_rows % n == 0)

    flat_kind = jax.ShapeDtypeStruct((shard_rows, LANES), f32)
    grad, sums = pl.pallas_call(
        functools.partial(inner_kernel, divisor(26)),
        in_specs=[VMEM] * (place.z + 3),
        out_specs=[VMEM] * 2,
        out_shape=[flat_kind, jax.ShapeDtypeStruct((1, SUMS), f32)],
        scratch_shapes=[pltpu.VMEM((KB, LANES), f32)],
        compiler_params=pltpu.CompilerParams(vmem_limit_bytes=2 * 1024 * 1024),
        name="inner",
    )(first, *pieces, *resident, loss)
    sums = butterfly(sums, place, resident)
    padded_rows = -(-shard_rows // 8) * 8
    loss_parts, norm, coefficients, new_master, new_first, new_second = pl.pallas_call(
        functools.partial(update_kernel, divisor(312), float(2 * shard_len * chips)),
        in_specs=[SMEM] + [VMEM] * 8,
        out_specs=[SMEM, SMEM] + [VMEM] * 4,
        out_shape=[
            jax.ShapeDtypeStruct((3,), f32),
            jax.ShapeDtypeStruct((1,), f32),
            jax.ShapeDtypeStruct((TASKS, KMAX), f32),
        ]
        + [flat_kind] * 3,
        scratch_shapes=[pltpu.VMEM((padded_rows, LANES), f32)],
        compiler_params=pltpu.CompilerParams(vmem_limit_bytes=2 * 1024 * 1024),
        name="update",
    )(
        basis_count,
        sums,
        *resident,
        grad,
        loss,
        master.reshape(shard_rows, LANES),
        first_moment.reshape(shard_rows, LANES),
        second_moment.reshape(shard_rows, LANES),
    )
    return (
        loss_parts,
        norm[0],
        coefficients,
        new_master.reshape(1, shard_len),
        new_first.reshape(1, shard_len),
        new_second.reshape(1, shard_len),
    )


def solution(mesh):
    in_specs = (
        P("dp", None, None),
        P("dp"),
        P("dp"),
        P("dp", None),
        P(),
        P("section", "dp"),
        P("section", "dp"),
        P("section", "dp"),
        P(None, "section", "dp"),
    )
    out_specs = (P(), P(), P(), P("section", "dp"), P("section", "dp"), P("section", "dp"))
    return jax.shard_map(body, mesh=mesh, in_specs=in_specs, out_specs=out_specs, check_vma=False)
```

```python
import functools
import math

import jax
import jax.numpy as jnp
from jax import lax
from jax.experimental import pallas as pl
from jax.experimental.pallas import tpu as pltpu
from jax.sharding import PartitionSpec as P

HEADS = 3
HD = 64
D = 192
FF = 768
PDIM = 768
PATCHES = 196
TOKENS = PATCHES + 1
ROWS = 208
CLS = PATCHES
GROUP = 4
CLASSES = 1000
CPAD = 1024
TASKS = 2
KMAX = 200
KB = TASKS * KMAX
UPPER = 256
STEP = 10
LANES = 128
HALF = 64
SPARE = 512
SUMS = 512

NORM_EPS = 1e-06
CLIP_NORM = 0.02
LEARN_RATE = 0.05
BETA_ONE = 0.9
BETA_TWO = 0.999
ADAM_EPS = 1e-08
WEIGHT_DECAY = 0.05
SCALE = HD ** (-0.5)
MASKED = -1e30

BLOCK_AT = dict(
    gain_one=0,
    bias_one=3,
    w_qkv=6,
    b_qkv=1734,
    w_out=1740,
    b_out=2316,
    gain_two=2319,
    bias_two=2322,
    w_up=2325,
    b_up=4629,
    w_down=4641,
    b_down=6945,
)
W_PATCH, B_PATCH, CLS_TOKEN, POS_EMBED = 6948, 9252, 9255, 9258
GAIN_LAST, BIAS_LAST, W_HEAD, B_HEAD = 6948, 6951, 6954, 9954
VECTORS = ("gain_one", "bias_one", "b_q", "b_v", "b_out", "gain_two", "bias_two", "b_up", "b_down")
VEC_ROWS = 16

f32 = jnp.float32
bf16 = jnp.bfloat16


def dot(left, right, left_dim=1, right_dim=0):
    return lax.dot_general(
        left, right, (((left_dim,), (right_dim,)), ((), ())), preferred_element_type=f32
    )


def low_lanes(shape):
    return lax.broadcasted_iota(jnp.int32, shape, 1) < HALF


def swap_halves(value):
    return pltpu.roll(value, HALF, 1)


def head_masks():
    lane = lax.broadcasted_iota(jnp.int32, (1, D), 1)
    return [jnp.logical_and(lane >= h * HD, lane < (h + 1) * HD) for h in range(HEADS)]


def by_head(value):
    return jnp.concatenate([jnp.where(m, value, 0.0) for m in head_masks()], 0)


def from_heads(value):
    rows = value.shape[0] // HEADS
    parts = [value[h * rows : (h + 1) * rows] for h in range(HEADS)]
    masks = head_masks()
    return jnp.where(masks[0], parts[0], jnp.where(masks[1], parts[1], parts[2]))


def normalise(rows_in):
    mean = jnp.sum(rows_in, -1, keepdims=True) * (1.0 / D)
    centred = rows_in - mean
    variance = jnp.sum(centred * centred, -1, keepdims=True) * (1.0 / D)
    scale = lax.rsqrt(variance + NORM_EPS)
    return centred * scale, scale


def normalise_back(grad, gain, unit, scale):
    grad_unit = grad * gain
    first = jnp.sum(grad_unit, -1, keepdims=True) * (1.0 / D)
    second = jnp.sum(grad_unit * unit, -1, keepdims=True) * (1.0 / D)
    return scale * (grad_unit - first - unit * second)


def gelu_parts(pre):
    cdf = 0.5 * (1.0 + lax.erf(pre * math.sqrt(0.5)))
    slope = cdf + pre * (jnp.exp(-0.5 * pre * pre) * (1.0 / math.sqrt(2.0 * math.pi)))
    return pre * cdf, slope


def column_sums(value):
    return jnp.sum(value.astype(f32), 0, keepdims=True)


def strided(ref, start, count, stride):
    if count == 1 or stride == 1:
        return ref[pl.ds(start, count), :]
    return ref[pl.ds(start, count, stride=stride), :]


class Flat:
    def __init__(self, even, odd, mix, odd_rows):
        self.even, self.odd, self.mix, self.odd_rows = even, odd, mix, odd_rows

    def shift(self):
        step = 192
        for at in range(0, self.odd_rows, step):
            here = self.even[at : at + step, :]
            after = self.even[at + 1 : at + 1 + step, :]
            self.odd[at : at + step, :] = swap_halves(jnp.where(low_lanes(here.shape), after, here))

    def rows_at(self, half, count, stride):
        return strided(self.odd if half % 2 else self.even, half // 2, count, stride)

    def blocks(self, half, width, rows, cols):
        for at in range(0, cols, LANES):
            start = half + at // HALF
            if rows == 1 or width % 2 == 0:
                value = self.rows_at(start, rows, width // 2)
            else:
                pairs = (rows + 1) // 2
                self.mix[pl.ds(0, pairs, stride=2), :] = self.rows_at(start, pairs, width)
                self.mix[pl.ds(1, pairs, stride=2), :] = self.rows_at(start + width, pairs, width)
                value = self.mix[0:rows, :]
            yield at, min(LANES, cols - at), value

    def read(self, dest, half, width, rows, cols):
        for at, wide, value in self.blocks(half, width, rows, cols):
            dest[0:rows, at : at + wide] = value[:, :wide].astype(dest.dtype)

    def read_row(self, dest, row, half, cols):
        for at, wide, value in self.blocks(half, 2, 1, cols):
            dest[row : row + 1, at : at + wide] = value[:, :wide]

    def clear(self):
        rows = self.odd_rows + 16
        self.even[...] = jnp.zeros(self.even.shape, f32)
        self.odd[0:rows, :] = jnp.zeros((rows, LANES), f32)

    def put_rows(self, half, count, stride, value):
        ref, start = (self.odd, half // 2 + 8) if half % 2 else (self.even, half // 2)
        if count == 1 or stride == 1:
            ref[pl.ds(start, count), :] = value
        else:
            ref[pl.ds(start, count, stride=stride), :] = value

    def write(self, value, half, width, cols):
        rows = value.shape[0]
        for at in range(0, cols, LANES):
            wide = min(LANES, cols - at)
            part = value[:, at : at + wide]
            if wide < LANES:
                part = jnp.concatenate([part, jnp.zeros((rows, LANES - wide), f32)], 1)
            start = half + at // HALF
            if rows == 1 or width % 2 == 0:
                self.put_rows(start, rows, width // 2, part)
            else:
                pairs = (rows + 1) // 2
                self.mix[0:rows, :] = part
                self.put_rows(start, pairs, width, self.mix[pl.ds(0, pairs, stride=2), :])
                self.put_rows(start + width, pairs, width, self.mix[pl.ds(1, pairs, stride=2), :])

    def merged(self, at, count):
        if at >= self.odd_rows:
            return self.even[at : at + count, :]
        here = self.odd[at + 8 : at + 8 + count, :]
        before = self.odd[at + 7 : at + 7 + count, :]
        moved_back = swap_halves(jnp.where(low_lanes(here.shape), here, before))
        return self.even[at : at + count, :] + moved_back


def paired(size):
    return size & (size - 1) == 0


class Place:
    def __init__(self, dims, shard_rows):
        self.z, self.y, self.x = dims
        self.count = self.z * self.y * self.x
        self.shard_rows = shard_rows
        self.sent_rows = -(-(shard_rows + 1) // 16) * 16
        self.first_rows = self.sent_rows * 13 // 20 // 16 * 16

        self.half_rows = self.sent_rows // 32 * 16

    def split(self, index):
        plane = self.y * self.x
        return index // plane, lax.rem(index, plane) // self.x, lax.rem(index, self.x)

    def turns(self):
        return [(a, b) for a in range(self.y) for b in range(self.x)]


def load_section(place, pieces, wanted, flat):
    own, other = pieces
    section = lax.axis_index("section")
    zed, why, ex = place.split(lax.axis_index("dp"))
    rows = place.shard_rows

    def copy(refs):
        for turn, (a, b) in enumerate(place.turns()):
            for d in range(place.z):
                shard = lax.rem(zed + (place.z - d), place.z) * (place.y * place.x)
                shard = shard + lax.rem(why + (place.y - a), place.y) * place.x
                shard = shard + lax.rem(ex + (place.x - b), place.x)
                start = shard * rows
                if rows % 8 == 0:
                    start = pl.multiple_of(start, 8)
                cut = place.first_rows
                flat.even[pl.ds(start, cut), :] = refs[turn][d].astype(f32)
                value = refs[len(place.turns()) + d][turn].astype(f32)
                after = start + cut
                if rows % 8 == 0:
                    after = pl.multiple_of(after, 8)
                flat.even[pl.ds(after, rows - cut), :] = value[: rows - cut]

    @pl.when(section == wanted)
    def _():
        copy(own)

    @pl.when(section != wanted)
    def _():
        copy(other)

    flat.shift()


def read_block(flat, weights, vec):
    at = BLOCK_AT
    w_q, w_k, w_v, w_out, w_up, w_down = weights
    for place, dest in enumerate((w_q, w_k, w_v)):
        flat.read(dest, at["w_qkv"] + 3 * place, 9, D, D)
    flat.read(w_out, at["w_out"], 3, D, D)
    flat.read(w_up, at["w_up"], 12, D, FF)
    flat.read(w_down, at["w_down"], 3, FF, D)
    starts = dict(at, b_q=at["b_qkv"], b_v=at["b_qkv"] + 3)
    for row, name in enumerate(VECTORS):
        flat.read_row(vec, row, starts[name], FF if name == "b_up" else D)


def vector(vec, name):
    row = VECTORS.index(name)
    return vec[row : row + 1, 0 : FF if name == "b_up" else D]


def write_vectors(flat, sums):
    at = BLOCK_AT
    starts = dict(at, b_q=at["b_qkv"], b_v=at["b_qkv"] + 3)
    for name, value in sums.items():
        flat.write(value, starts[name], 2, value.shape[1])


def send_out(place, flat, write):
    zed, why, ex = place.split(lax.axis_index("dp"))
    rows, spare = place.shard_rows, place.sent_rows - place.shard_rows
    for shard in range(place.count):
        zk, yk, xk = shard // (place.y * place.x), shard // place.x % place.y, shard % place.x
        there = ((zk, zed, place.z), (yk, why, place.y), (xk, ex, place.x))
        d, a, b = [to ^ at if paired(size) else lax.rem(to + size - at, size) for to, at, size in there]
        value = flat.merged(shard * rows, rows)
        value = jnp.concatenate([value, jnp.zeros((spare, LANES), f32)], 0)
        write((a * place.x + b) * place.z + d, value.astype(bf16))


def shard_kernel(replay, master, out):
    rows = master.shape[0]
    count = sum(replay[i].astype(f32) for i in range(replay.shape[0]))
    tail = jnp.full((out.shape[0] - rows, LANES), count, f32)
    out[...] = jnp.concatenate([master[...], tail], 0).astype(bf16)


def front_kernel(place, per, *refs):
    parts = len(place.turns()) + place.z
    own, other, refs = refs[:parts], refs[parts : 2 * parts], refs[2 * parts :]
    patches, kept, middle_out, weights = refs[0], refs[1:10], refs[10], refs[11:18]
    even, odd, mix, w_patch, added, tokens = refs[18:]
    vec = weights[-1]
    flat = Flat(even, odd, mix, place.count * place.shard_rows)
    load_section(place, (own, other), 0, flat)
    read_block(flat, weights[:-1], vec)
    flat.read(w_patch, W_PATCH, 3, PDIM, D)
    flat.read_row(vec, 9, B_PATCH, D)
    flat.read_row(vec, 10, CLS_TOKEN, D)
    added[...] = jnp.zeros(added.shape, f32)
    tokens[...] = jnp.zeros(tokens.shape, f32)
    for at, wide, value in flat.blocks(POS_EMBED, 3, TOKENS + 1, D):
        added[0:PATCHES, at : at + wide] = value[1:TOKENS, :wide] + vec[9:10, at : at + wide]
        added[CLS : CLS + 1, at : at + wide] = value[0:1, :wide] + vec[10:11, at : at + wide]
    group = group_of(per)
    for step in range(0, per, group):
        cut = slice(step * ROWS, (step + group) * ROWS)
        front_images(step, cut, patches, kept, middle_out, weights, w_patch, added, tokens)


def front_images(step, cut, patches, kept, middle_out, weights, w_patch, added, tokens):
    x_out, q_out, k_out, v_out, probs_out, mixed_out, hidden_out, act_out, slope_out = kept
    w_q, w_k, w_v, w_out, w_up, w_down, vec = weights
    group = (cut.stop - cut.start) // ROWS
    spans = [slice(i * ROWS, (i + 1) * ROWS) for i in range(group)]
    for i, at in enumerate(spans):
        tokens[cut.start + at.start : cut.start + at.start + PATCHES, :] = dot(patches[step + i], w_patch[...])
    x = tokens[cut, :] + jnp.concatenate([added[...]] * group, 0)
    x_out[cut, :] = x
    unit, _ = normalise(x)
    normed = (unit * vector(vec, "gain_one") + vector(vec, "bias_one")).astype(bf16)
    q = (dot(normed, w_q[...]) + vector(vec, "b_q")).astype(bf16)
    k = dot(normed, w_k[...]).astype(bf16)
    v = (dot(normed, w_v[...]) + vector(vec, "b_v")).astype(bf16)
    q_out[cut, :], k_out[cut, :], v_out[cut, :] = q, k, v
    q_scaled = q.astype(f32) * SCALE
    column = lax.broadcasted_iota(jnp.int32, (1, ROWS), 1)
    scores = [dot(by_head(q_scaled[at]).astype(bf16), k[at], 1, 1) for at in spans]
    scores = [jnp.where(column < TOKENS, value, MASKED) for value in scores]
    raised = [jnp.exp(value - jnp.max(value, -1, keepdims=True)) for value in scores]
    probs = [value * (1.0 / jnp.sum(value, -1, keepdims=True)) for value in raised]
    for i, value in enumerate(probs):
        probs_out[(step + i) * HEADS * ROWS : (step + i + 1) * HEADS * ROWS, :] = value
    mixed = [from_heads(dot(value.astype(bf16), v[at])) for value, at in zip(probs, spans)]
    mixed = jnp.concatenate(mixed, 0).astype(bf16)
    mixed_out[cut, :] = mixed
    hidden = x + dot(mixed, w_out[...]) + vector(vec, "b_out")
    hidden_out[cut, :] = hidden
    unit, _ = normalise(hidden)
    normed = (unit * vector(vec, "gain_two") + vector(vec, "bias_two")).astype(bf16)
    pre = dot(normed, w_up[...]) + vector(vec, "b_up")
    act, slope = gelu_parts(pre)
    act = act.astype(bf16)
    act_out[cut, :], slope_out[cut, :] = act, slope
    middle = hidden + dot(act, w_down[...]) + vector(vec, "b_down")
    middle_out[cut, :] = middle.astype(bf16)


def read_head(flat, wide, w_head, b_head):
    first = W_HEAD // 2
    lane = lax.broadcasted_iota(jnp.int32, (16, LANES), 1)
    for phase in range(16):
        start, off = first + CLASSES * phase // LANES, CLASSES * phase % LANES
        got = [strided(flat.even, start + j, 16, 125) for j in range(9 if off else 8)]
        if off:
            got = [pltpu.roll(g, LANES - off, 1) for g in got]
        for j in range(8):
            value = jnp.where(lane < LANES - off, got[j], got[j + 1]) if off else got[j]
            wide[j, pl.ds(phase, 16, stride=16), :] = value
    lane = lax.broadcasted_iota(jnp.int32, (1, LANES), 1)
    for j in range(8):
        keep = lane + j * LANES < CLASSES
        w_head[:, j * LANES : (j + 1) * LANES] = jnp.where(keep, wide[j, 0:D, :], 0.0).astype(bf16)
        value = flat.even[B_HEAD // 2 + j : B_HEAD // 2 + j + 1, :]
        b_head[0:1, j * LANES : (j + 1) * LANES] = jnp.where(keep, value, 0.0)


def write_head(flat, wide, grad_w, grad_b):
    first = W_HEAD // 2
    for j in range(8):
        wide[j, 0:D, :] = grad_w[:, j * LANES : (j + 1) * LANES]
        wide[j, D:, :] = jnp.zeros((wide.shape[1] - D, LANES), f32)
    lane = lax.broadcasted_iota(jnp.int32, (16, LANES), 1)
    for phase in range(16):
        start, off = first + CLASSES * phase // LANES, CLASSES * phase % LANES
        got = [wide[j, pl.ds(phase, 16, stride=16), :] for j in range(8)]
        if off:
            got = [pltpu.roll(g, off, 1) for g in got]
        for j in range(9 if off else 8):
            if not off:
                value = got[j]
            else:
                before = got[j - 1] if j else jnp.zeros((16, LANES), f32)
                value = jnp.where(lane < off, before, got[j] if j < 8 else 0.0)
            flat.even[pl.ds(start + j, 16, stride=125), :] += value
    for j in range(8):
        row = B_HEAD // 2 + j
        flat.even[row : row + 1, :] += grad_b[:, j * LANES : (j + 1) * LANES]


def late_kernel(place, per, image_total, labels, replay, *refs):
    section = lax.axis_index("section")
    parts = len(place.turns()) + place.z
    odd_rows = -(-(W_HEAD // 2 + 1) // place.shard_rows) * place.shard_rows
    own, other, refs = refs[:parts], refs[parts : 2 * parts], refs[2 * parts :]
    middle, old_logits, back_out, grad_out, loss_out = refs[:5]
    even, odd, mix, wide, w_q, w_k, w_v, w_out, w_up, w_down, vec, w_head, b_head, few, many = refs[5:]
    flat = Flat(even, odd, mix, odd_rows)
    load_section(place, (own, other), 1, flat)
    read_block(flat, (w_q, w_k, w_v, w_out, w_up, w_down), vec)
    flat.read_row(vec, 9, GAIN_LAST, D)
    flat.read_row(vec, 10, BIAS_LAST, D)
    read_head(flat, wide, w_head, b_head)
    gain_last, bias_last = vec[9:10, 0:D], vec[10:11, 0:D]
    carried = jnp.zeros((1, LANES), f32)
    carrier = place.shard_rows - place.first_rows
    for ref in own[len(place.turns()) :]:
        for turn in range(len(place.turns())):
            carried = carried + ref[turn].astype(f32)[carrier : carrier + 1]
    replay_count = carried[:, 0:1]

    x = middle[...].astype(f32)
    unit, scale = normalise(x)
    normed_f = unit * vector(vec, "gain_one") + vector(vec, "bias_one")
    normed = normed_f.astype(bf16)
    k = dot(normed, w_k[...]).astype(bf16)
    v = (dot(normed, w_v[...]) + vector(vec, "b_v")).astype(bf16)

    def class_rows(value):
        few[...] = jnp.zeros(few.shape, f32)
        for i in range(per):
            few[i : i + 1, :] = value[i * ROWS + CLS : i * ROWS + CLS + 1, :]
        return few[...]

    eight = few.shape[0]
    image = lax.broadcasted_iota(jnp.int32, (eight, 1), 0)
    real = image < per
    x_top = class_rows(x)
    top_normed = class_rows(normed_f).astype(bf16)
    q = (dot(top_normed, w_q[...]) + vector(vec, "b_q")).astype(bf16)
    q_heads = by_head(jnp.where(real, q.astype(f32) * SCALE, 0.0)).astype(bf16)
    scores = dot(q_heads, k, 1, 1)
    column = lax.broadcasted_iota(jnp.int32, scores.shape, 1)
    owner = lax.rem(lax.broadcasted_iota(jnp.int32, scores.shape, 0), eight) * ROWS
    inside = jnp.logical_and(column >= owner, column < owner + TOKENS)
    scores = jnp.where(inside, scores, MASKED)
    raised = jnp.where(inside, jnp.exp(scores - jnp.max(scores, -1, keepdims=True)), 0.0)
    total = jnp.sum(raised, -1, keepdims=True)
    probs = raised * (1.0 / jnp.where(total > 0.0, total, 1.0))
    probs_low = probs.astype(bf16)
    mixed = from_heads(dot(probs_low, v)).astype(bf16)
    hidden = x_top + dot(mixed, w_out[...]) + vector(vec, "b_out")
    unit_two, scale_two = normalise(hidden)
    normed_two = (unit_two * vector(vec, "gain_two") + vector(vec, "bias_two")).astype(bf16)
    act, slope = gelu_parts(dot(normed_two, w_up[...]) + vector(vec, "b_up"))
    act = act.astype(bf16)
    final = hidden + dot(act, w_down[...]) + vector(vec, "b_down")

    unit_last, scale_last = normalise(final)
    top = (unit_last * gain_last + bias_last).astype(bf16)
    classes = lax.broadcasted_iota(jnp.int32, (eight, CPAD), 1)
    logits = dot(top, w_head[...]) + b_head[...]
    logits = jnp.where(classes < CLASSES, logits, MASKED)
    highest = jnp.max(logits, -1, keepdims=True)
    log_total = highest + jnp.log(jnp.sum(jnp.exp(logits - highest), -1, keepdims=True))
    label = jnp.zeros((eight, 1), jnp.int32)
    again = jnp.zeros((eight, 1), f32)
    for i in range(per):
        label = jnp.where(image == i, labels[section * per + i], label)
        again = jnp.where(image == i, replay[section * per + i].astype(f32), again)
    picked = jnp.logical_and(classes == label, real)
    entropy = jnp.where(real, log_total, 0.0) - jnp.sum(jnp.where(picked, logits, 0.0), -1, keepdims=True)
    wanted = jnp.where(section == 0, old_logits[0:per, :], old_logits[per : 2 * per, :])
    if per < eight:
        wanted = jnp.concatenate([wanted, jnp.zeros((eight - per, CLASSES), f32)], 0)
    wanted = jnp.concatenate([wanted, jnp.zeros((eight, CPAD - CLASSES), f32)], 1)
    distance = jnp.where(jnp.logical_and(classes < CLASSES, real), logits - wanted, 0.0)
    squares = again * (jnp.sum(distance * distance, -1, keepdims=True) * (1.0 / CLASSES))
    lane = lax.broadcasted_iota(jnp.int32, (1, LANES), 1)
    entropy_sum = jnp.sum(entropy, 0, keepdims=True)
    replay_sum = jnp.sum(squares, 0, keepdims=True)
    loss_out[...] = jnp.where(lane == 0, entropy_sum, jnp.where(lane == 1, replay_sum, replay_count))

    grad = (jnp.exp(logits - log_total) - jnp.where(picked, 1.0, 0.0)) * (1.0 / image_total)
    grad = grad + again * 2.0 * distance / (CLASSES * replay_count)
    grad = jnp.where(jnp.logical_and(classes < CLASSES, real), grad, 0.0)
    grad_low = grad.astype(bf16)
    flat.clear()
    write_head(flat, wide, dot(top, grad_low, 0, 0), column_sums(grad_low))
    sums = {}
    grad = dot(grad_low, w_head[...], 1, 1)
    flat.write(column_sums(grad * unit_last), GAIN_LAST, 2, D)
    flat.write(column_sums(grad), BIAS_LAST, 2, D)
    grad = normalise_back(grad, gain_last, unit_last, scale_last)

    at = BLOCK_AT
    grad_down = grad.astype(bf16)
    flat.write(dot(act, grad_down, 0, 0), at["w_down"], 3, D)
    sums["b_down"] = column_sums(grad_down)
    grad_up = (dot(grad_down, w_down[...], 1, 1) * slope).astype(bf16)
    flat.write(dot(normed_two, grad_up, 0, 0), at["w_up"], 12, FF)
    sums["b_up"] = column_sums(grad_up)
    grad_two = dot(grad_up, w_up[...], 1, 1)
    sums["gain_two"], sums["bias_two"] = column_sums(grad_two * unit_two), column_sums(grad_two)
    grad_hidden = grad + normalise_back(grad_two, vector(vec, "gain_two"), unit_two, scale_two)
    branch = grad_hidden.astype(bf16)
    flat.write(dot(mixed, branch, 0, 0), at["w_out"], 3, D)
    sums["b_out"] = column_sums(branch)
    mixed_heads = by_head(dot(branch, w_out[...], 1, 1).astype(bf16).astype(f32)).astype(bf16)
    grad_probs = dot(mixed_heads, v, 1, 1)
    grad_v = dot(probs_low, mixed_heads, 0, 0).astype(bf16)
    inner = jnp.sum(grad_probs * probs, -1, keepdims=True)
    grad_scores = (probs * (grad_probs - inner)).astype(bf16)
    grad_q = (from_heads(dot(grad_scores, k)) * SCALE).astype(bf16)
    grad_k = dot(grad_scores, q_heads, 0, 0).astype(bf16)
    flat.write(dot(top_normed, grad_q, 0, 0), at["w_qkv"], 9, D)
    flat.write(dot(normed, grad_k, 0, 0), at["w_qkv"] + 3, 9, D)
    flat.write(dot(normed, grad_v, 0, 0), at["w_qkv"] + 6, 9, D)
    sums["b_q"], sums["b_v"] = column_sums(grad_q), column_sums(grad_v)
    many[...] = dot(grad_k, w_k[...], 1, 1) + dot(grad_v, w_v[...], 1, 1)
    top_back = dot(grad_q, w_q[...], 1, 1)
    for i in range(per):
        many[i * ROWS + CLS : i * ROWS + CLS + 1, :] += top_back[i : i + 1, :]
    grad_one = many[...]
    sums["gain_one"], sums["bias_one"] = column_sums(grad_one * unit), column_sums(grad_one)
    many[...] = normalise_back(grad_one, vector(vec, "gain_one"), unit, scale)
    for i in range(per):
        many[i * ROWS + CLS : i * ROWS + CLS + 1, :] += grad_hidden[i : i + 1, :]
    back_out[...] = many[...].astype(bf16)
    write_vectors(flat, sums)

    def store(at, value):
        grad_out[at] = value

    send_out(place, flat, store)


def back_kernel(place, per, *refs):
    grad_in, kept, patches, weights = refs[0], refs[1:10], refs[10], refs[11:18]
    late_grad, keep_out, give_out = refs[18:21]
    even, odd, mix, *operands = refs[21:]
    s_normed, s_q, s_k, s_v, s_branch, s_two, s_up = operands
    vec = weights[-1]
    group = group_of(per)
    sums = {}
    embedded = []
    positions = jnp.zeros((ROWS, D), f32)
    for step in range(0, per, group):
        cut = slice(step * ROWS, (step + group) * ROWS)
        vectors, grad_x = back_images(step, cut, grad_in, kept, weights, operands)
        sums = {name: sums[name] + value if sums else value for name, value in vectors.items()}
        for i in range(group):
            embedded.append(grad_x[i * ROWS : i * ROWS + PATCHES].astype(bf16))
            positions = positions + grad_x[i * ROWS : (i + 1) * ROWS]

    at = BLOCK_AT
    flat = Flat(even, odd, mix, place.count * place.shard_rows)
    flat.clear()
    normed = s_normed[...]
    for part, ref in enumerate((s_q, s_k, s_v)):
        flat.write(dot(normed, ref[...], 0, 0), at["w_qkv"] + 3 * part, 9, D)
    flat.write(dot(kept[5][...], s_branch[...], 0, 0), at["w_out"], 3, D)
    flat.write(dot(s_two[...], s_up[...], 0, 0), at["w_up"], 12, FF)
    flat.write(dot(kept[7][...], grad_in[...], 0, 0), at["w_down"], 3, D)
    grad_patch = sum(dot(patches[i], value, 0, 0) for i, value in enumerate(embedded))
    flat.write(grad_patch, W_PATCH, 3, D)
    sums["b_q"], sums["b_v"] = column_sums(s_q[...]), column_sums(s_v[...])
    sums["b_out"], sums["b_up"] = column_sums(s_branch[...]), column_sums(s_up[...])
    sums["b_down"] = column_sums(grad_in[...])
    write_vectors(flat, sums)
    flat.write(sum(column_sums(value) for value in embedded), B_PATCH, 2, D)
    token = positions[CLS : CLS + 1, :]
    flat.write(token, CLS_TOKEN, 2, D)
    natural = jnp.concatenate([token, positions[0:PATCHES, :], jnp.zeros((1, D), f32)], 0)
    flat.write(natural, POS_EMBED, 3, D)

    section = lax.axis_index("section")

    @pl.when(section == 0)
    def _():
        def store(at, value):
            keep_out[at] = value
            give_out[at] = late_grad[at]

        send_out(place, flat, store)

    @pl.when(section != 0)
    def _():
        def store(at, value):
            give_out[at] = value
            keep_out[at] = late_grad[at]

        send_out(place, flat, store)


def back_images(step, cut, grad_in, kept, weights, operands):
    x_in, q_in, k_in, v_in, probs_in, mixed_in, hidden_in, act_in, slope_in = kept
    w_q, w_k, w_v, w_out, w_up, w_down, vec = weights
    s_normed, s_q, s_k, s_v, s_branch, s_two, s_up = operands
    group = (cut.stop - cut.start) // ROWS
    spans = [slice(i * ROWS, (i + 1) * ROWS) for i in range(group)]
    sums = {}
    grad_low = grad_in[cut, :]
    grad_up = (dot(grad_low, w_down[...], 1, 1) * slope_in[cut, :]).astype(bf16)
    s_up[cut, :] = grad_up
    unit, scale = normalise(hidden_in[cut, :])
    s_two[cut, :] = (unit * vector(vec, "gain_two") + vector(vec, "bias_two")).astype(bf16)
    grad_two = dot(grad_up, w_up[...], 1, 1)
    sums["gain_two"], sums["bias_two"] = column_sums(grad_two * unit), column_sums(grad_two)
    grad_hidden = grad_low.astype(f32) + normalise_back(grad_two, vector(vec, "gain_two"), unit, scale)
    branch = grad_hidden.astype(bf16)
    s_branch[cut, :] = branch
    grad_mixed = dot(branch, w_out[...], 1, 1).astype(bf16).astype(f32)
    mixed_heads = [by_head(grad_mixed[at]).astype(bf16) for at in spans]
    q_scaled = q_in[cut, :].astype(f32) * SCALE
    q_heads = [by_head(q_scaled[at]).astype(bf16) for at in spans]
    k, v = k_in[cut, :], v_in[cut, :]
    probs = [
        probs_in[(step + i) * HEADS * ROWS : (step + i + 1) * HEADS * ROWS, :] for i in range(group)
    ]
    grad_probs = [dot(value, v[at], 1, 1) for value, at in zip(mixed_heads, spans)]
    grad_v = [dot(value.astype(bf16), right, 0, 0) for value, right in zip(probs, mixed_heads)]
    inner = [jnp.sum(one * two, -1, keepdims=True) for one, two in zip(grad_probs, probs)]
    grad_scores = [(two * (one - less)).astype(bf16) for one, two, less in zip(grad_probs, probs, inner)]
    grad_q = [from_heads(dot(value, k[at])) * SCALE for value, at in zip(grad_scores, spans)]
    grad_k = [dot(value, right, 0, 0) for value, right in zip(grad_scores, q_heads)]
    grad_q, grad_k, grad_v = [jnp.concatenate(value, 0).astype(bf16) for value in (grad_q, grad_k, grad_v)]
    s_q[cut, :], s_k[cut, :], s_v[cut, :] = grad_q, grad_k, grad_v
    unit, scale = normalise(x_in[cut, :])
    s_normed[cut, :] = (unit * vector(vec, "gain_one") + vector(vec, "bias_one")).astype(bf16)
    grad_one = dot(grad_q, w_q[...], 1, 1) + dot(grad_k, w_k[...], 1, 1) + dot(grad_v, w_v[...], 1, 1)
    sums["gain_one"], sums["bias_one"] = column_sums(grad_one * unit), column_sums(grad_one)
    return sums, grad_hidden + normalise_back(grad_one, vector(vec, "gain_one"), unit, scale)


def fetch_kernel(first, last, _, basis, kept, sem):
    copy = pltpu.make_async_copy(basis.at[pl.ds(first, last - first)], kept, sem)
    copy.start()
    copy.wait()


def add_kernel(left, right, _, __, total):
    total[...] = left[...] + right[...]


def split_kernel(place, keep, given, *outs):
    cut = place.half_rows
    for place_y in range(place.y):
        for place_x in range(place.x):
            for d in range(place.z):
                at = (place_y * place.x + place_x) * place.z + d
                total = keep[at].astype(f32) + given[at].astype(f32)
                one, two = outs[place_y], outs[place.y + place_x]
                one[place_x, d] = total[:cut].astype(one.dtype)
                two[place_y, d] = total[cut:].astype(two.dtype)


def turn_kernel(place, one, two, _, *refs):
    count = place.y + place.x
    arrived, outs = refs[: count - 2], refs[count - 2 :]
    for own, came, parts in (
        (one, arrived[: place.y - 1], outs[: place.x]),
        (two, arrived[place.y - 1 :], outs[place.x :]),
    ):
        for step, out in enumerate(parts):
            for d in range(place.z):
                total = own[step, d]
                for ref in came:
                    total = total + ref[step, d].astype(f32)
                out[d] = total.astype(out.dtype)


def plane_kernel(place, one, two, _, *refs):
    arrived, (whole_out, *outs) = refs[: -place.z], refs[-place.z :]
    for d in range(place.z):
        upper, lower = one[d], two[d]
        for ref in arrived[: place.x - 1]:
            upper = upper + ref[d].astype(f32)
        for ref in arrived[place.x - 1 :]:
            lower = lower + ref[d].astype(f32)
        out = outs[d - 1] if d else whole_out
        out[0 : place.half_rows, :] = upper.astype(out.dtype)
        out[place.half_rows :, :] = lower.astype(out.dtype)


def inner_kernel(blocks, *refs):
    first, pieces, (upper, lower, loss, grad_out, sums_out, total) = refs[0], refs[1:-6], refs[-6:]
    shard_rows = grad_out.shape[0]
    value = first[...]
    for ref in pieces:
        value = value + ref[...].astype(f32)
    grad_out[...] = value[:shard_rows]
    total[...] = jnp.zeros(total.shape, f32)

    def step(i, carry):
        base = i * blocks
        rows = [jnp.broadcast_to(grad_out[pl.ds(base + j, 1), :], (8, LANES)) for j in range(blocks)]
        start = pl.multiple_of(base * LANES, LANES)
        for at in range(0, KB, 16):
            basis, row = (upper, at) if at < UPPER else (lower, at - UPPER)
            part = basis[row : row + 16, pl.ds(start, blocks * LANES)].astype(f32)
            for half in range(0, 16, 8):
                acc = total[at + half : at + half + 8, :]
                for j in range(blocks):
                    acc = acc + part[half : half + 8, j * LANES : (j + 1) * LANES] * rows[j]
                total[at + half : at + half + 8, :] = acc
        return carry

    lax.fori_loop(0, shard_rows // blocks, step, 0)
    coefs = jnp.sum(total[...].T, 0, keepdims=True)
    grad = grad_out[...]
    squares = jnp.sum(jnp.sum(grad * grad, 0, keepdims=True), 1, keepdims=True)
    lane = lax.broadcasted_iota(jnp.int32, (1, SUMS - KB), 1)
    rest = jnp.where(lane == 0, squares, 0.0)
    rest = rest + jnp.where(lane == 1, loss[0:1, 0:1], 0.0) + jnp.where(lane == 2, loss[0:1, 1:2], 0.0)
    sums_out[:, 0:KB] = coefs
    sums_out[:, KB:SUMS] = rest


def update_kernel(blocks, whole_len, counts, sums, upper, lower, grad, loss, master, first, second, *refs):
    loss_out, norm_out, coef_out, master_out, first_out, second_out, removed = refs
    norm = jnp.sqrt(sums[0:1, KB : KB + 1])
    factor = jnp.minimum(1.0, CLIP_NORM / (norm + 1e-06))
    lane = lax.broadcasted_iota(jnp.int32, (1, KB), 1)
    limit = jnp.where(lane < KMAX, counts[0], counts[1] + KMAX)
    row = jnp.where(lane < limit, sums[:, 0:KB] * factor, 0.0)
    coef_out[0:1, :] = row[:, 0:KMAX]
    coef_out[1:2, :] = row[:, KMAX:KB]
    norm_out[0] = jnp.sum(norm)
    loss_out[0] = jnp.sum(sums[0:1, KB + 1 : KB + 2])
    loss_out[1] = jnp.sum(sums[0:1, KB + 2 : KB + 3])
    loss_out[2] = jnp.sum(loss[0:1, 2:3])
    high = row.astype(bf16).astype(f32)
    mid = (row - high).astype(bf16).astype(f32)
    low = row - high - mid
    place = lax.broadcasted_iota(jnp.int32, (16, KB), 0)
    split = jnp.where(place == 0, high, jnp.where(place == 1, mid, jnp.where(place == 2, low, 0.0)))
    split = split.astype(bf16)
    rows = grad.shape[0]

    def step(i, carry):
        base = i * blocks
        start = pl.multiple_of(base * LANES, LANES)
        part = dot(split[:, :UPPER], upper[:, pl.ds(start, blocks * LANES)])
        part = part + dot(split[:, UPPER:], lower[:, pl.ds(start, blocks * LANES)])
        part = jnp.sum(part, 0, keepdims=True)
        for j in range(blocks):
            removed[pl.ds(base + j, 1), :] = part[:, j * LANES : (j + 1) * LANES]
        return carry

    lax.fori_loop(0, rows // blocks, step, 0)
    projected = grad[...] * factor - removed[0:rows, :] * (1.0 / whole_len)
    new_first = BETA_ONE * first[...] + (1.0 - BETA_ONE) * projected
    new_second = BETA_TWO * second[...] + (1.0 - BETA_TWO) * projected * projected
    ratio = (
        new_first
        / (1.0 - BETA_ONE**STEP)
        / (jnp.sqrt(new_second / (1.0 - BETA_TWO**STEP)) + ADAM_EPS)
    )
    old = master[...]
    master_out[...] = old - LEARN_RATE * (ratio + WEIGHT_DECAY * old)
    first_out[...] = new_first
    second_out[...] = new_second


def dp_dims(count):
    zed = 4 if count % 4 == 0 else 1
    plane = count // zed
    ex = max(side for side in range(1, math.isqrt(plane) + 1) if plane % side == 0)
    return zed, plane // ex, ex


def moved(value, place, turn=(0, 0, 0), core=0, pairs_too=False):
    def step(index, by, size):
        return index ^ by if pairs_too and paired(size) else (index + by) % size

    pairs = []
    for section in range(2):
        for zed in range(place.z):
            for why in range(place.y):
                for ex in range(place.x):
                    source = (section * place.z + zed) * place.y * place.x + why * place.x + ex
                    there = ((section + core) % 2) * place.z + step(zed, turn[0], place.z)
                    target = (there * place.y + step(why, turn[1], place.y)) * place.x
                    pairs.append((source, target + step(ex, turn[2], place.x)))
    return lax.ppermute(value, ("section", "dp"), pairs)


def add(left, right, resident):
    vmem = pl.BlockSpec(memory_space=pltpu.VMEM)
    return pl.pallas_call(
        add_kernel,
        in_specs=[vmem, vmem] + [pl.BlockSpec(memory_space=pl.ANY)] * 2,
        out_specs=vmem,
        out_shape=jax.ShapeDtypeStruct(left.shape, left.dtype),
        compiler_params=pltpu.CompilerParams(vmem_limit_bytes=2 * 1024 * 1024),
        name="add",
    )(left, right, *resident)


def butterfly(value, place, resident):
    value = add(value, moved(value, place, core=1), resident)
    for axis, size in ((2, place.x), (1, place.y), (0, place.z)):
        span = 1
        while span < size:
            pairs = []
            for index in range(2 * place.count):
                section, rest = divmod(index, place.count)
                at = [rest // (place.y * place.x), rest // place.x % place.y, rest % place.x]
                at[axis] ^= span
                pairs.append((index, section * place.count + (at[0] * place.y + at[1]) * place.x + at[2]))
            value = add(value, lax.ppermute(value, ("section", "dp"), pairs), resident)
            span *= 2
    return value


def whole(shape):
    return pl.BlockSpec(shape, lambda *_: (0,) * len(shape))


def params(megabytes):
    return pltpu.CompilerParams(
        vmem_limit_bytes=megabytes * 1024 * 1024, dimension_semantics=("arbitrary",)
    )


BLOCK_SHAPES = [(D, D)] * 4 + [(D, FF), (FF, D)]
SAVED = [
    ((ROWS, D), f32),
    ((ROWS, D), bf16),
    ((ROWS, D), bf16),
    ((ROWS, D), bf16),
    ((HEADS * ROWS, ROWS), f32),
    ((ROWS, D), bf16),
    ((ROWS, D), f32),
    ((ROWS, FF), bf16),
    ((ROWS, FF), f32),
]
MIDDLE = ((ROWS, D), bf16)
WORK = pl.CostEstimate(flops=3_000_000_000, bytes_accessed=30_000_000, transcendentals=1_000_000)
VMEM = pl.BlockSpec(memory_space=pltpu.VMEM)
SMEM = pl.BlockSpec(memory_space=pltpu.SMEM)
ANY = pl.BlockSpec(memory_space=pl.ANY)


def group_of(per):
    return GROUP if per % GROUP == 0 else 1


def flat_scratch(place):
    flat_rows = place.count * place.shard_rows + SPARE
    return [
        pltpu.VMEM((flat_rows, LANES), f32),
        pltpu.VMEM((flat_rows, LANES), f32),
        pltpu.VMEM((FF + 32, LANES), f32),
    ]


def front(place, per, own, other, patches):
    outs = pl.pallas_call(
        functools.partial(front_kernel, place, per),
        in_specs=[VMEM] * (len(own) + len(other) + 1),
        out_specs=[VMEM] * (len(SAVED) + 1 + len(BLOCK_SHAPES) + 1),
        out_shape=[
            jax.ShapeDtypeStruct((per * shape[0], shape[1]), kind) for shape, kind in SAVED + [MIDDLE]
        ]
        + [jax.ShapeDtypeStruct(shape, bf16) for shape in BLOCK_SHAPES]
        + [jax.ShapeDtypeStruct((VEC_ROWS, FF), f32)],
        scratch_shapes=flat_scratch(place)
        + [pltpu.VMEM((PDIM, D), bf16), pltpu.VMEM((ROWS, D), f32), pltpu.VMEM((per * ROWS, D), f32)],
        compiler_params=pltpu.CompilerParams(vmem_limit_bytes=20 * 1024 * 1024),
        cost_estimate=WORK,
        name="front",
    )(*own, *other, patches)
    return outs[:9], outs[9], outs[10:]


def grad_kind(place):
    return jax.ShapeDtypeStruct((place.count, place.sent_rows, LANES), bf16)


def late(place, per, image_total, labels, replay, own, other, middle, old_logits):
    eight = -(-per // 8) * 8
    return pl.pallas_call(
        functools.partial(late_kernel, place, per, image_total),
        in_specs=[SMEM] * 2 + [VMEM] * (len(own) + len(other) + 2),
        out_specs=[VMEM] * 3,
        out_shape=[
            jax.ShapeDtypeStruct((per * ROWS, D), bf16),
            grad_kind(place),
            jax.ShapeDtypeStruct((1, LANES), f32),
        ],
        scratch_shapes=flat_scratch(place)
        + [pltpu.VMEM((8, 256, LANES), f32)]
        + [pltpu.VMEM(shape, bf16) for shape in BLOCK_SHAPES]
        + [
            pltpu.VMEM((VEC_ROWS, FF), f32),
            pltpu.VMEM((D, CPAD), bf16),
            pltpu.VMEM((1, CPAD), f32),
            pltpu.VMEM((eight, D), f32),
            pltpu.VMEM((per * ROWS, D), f32),
        ],
        compiler_params=pltpu.CompilerParams(vmem_limit_bytes=16 * 1024 * 1024),
        cost_estimate=WORK,
        name="late",
    )(labels, replay, *own, *other, middle, old_logits)


def back(place, per, grad_middle, kept, patches, weights, late_grad):
    return pl.pallas_call(
        functools.partial(back_kernel, place, per),
        in_specs=[VMEM] * (1 + len(kept) + 1 + len(weights) + 1),
        out_specs=[VMEM] * 2,
        out_shape=[grad_kind(place)] * 2,
        scratch_shapes=flat_scratch(place)
        + [pltpu.VMEM((per * ROWS, D), bf16)] * 6
        + [pltpu.VMEM((per * ROWS, FF), bf16)],
        compiler_params=pltpu.CompilerParams(vmem_limit_bytes=20 * 1024 * 1024),
        cost_estimate=WORK,
        name="back",
    )(grad_middle, *kept, patches, *weights, late_grad)


def body(
    patches, labels, replay, old_logits, basis_count, master, first_moment, second_moment, basis
):
    chips = lax.axis_size("dp")
    shard_len = master.shape[1]
    shard_rows = shard_len // LANES
    place = Place(dp_dims(chips), shard_rows)
    images = patches.shape[0]
    per = images // 2
    section = lax.axis_index("section")
    turns = place.turns()

    shard = pl.pallas_call(
        shard_kernel,
        grid=(1,),
        in_specs=[SMEM, whole((shard_rows, LANES))],
        out_specs=whole((place.sent_rows, LANES)),
        out_shape=jax.ShapeDtypeStruct((place.sent_rows, LANES), bf16),
        compiler_params=pltpu.CompilerParams(vmem_limit_bytes=2 * 1024 * 1024),
        name="shard",
    )(
        pltpu.with_memory_space_constraint(replay, pltpu.HBM),
        pltpu.with_memory_space_constraint(master.reshape(shard_rows, LANES), pltpu.HBM),
    )
    mine = lax.dynamic_slice_in_dim(patches, section * per, per, 0)
    early, late_part = shard[: place.first_rows], shard[place.first_rows :]
    column = [early] + [moved(early, place, (d, 0, 0)) for d in range(1, place.z)]
    plane = [moved(late_part, place, (0, a, b)) if a + b else late_part for a, b in turns]
    plane[1], mine = lax.optimization_barrier((plane[1], mine))
    column, plane = jnp.stack(column), jnp.stack(plane)
    own = [moved(column, place, (0, a, b)) if a + b else column for a, b in turns]
    own += [moved(plane, place, (d, 0, 0)) if d else plane for d in range(place.z)]
    other = [moved(piece, place, core=1) for piece in own]

    kept, middle, weights = front(place, per, own, other, mine)
    grad_middle, late_grad, loss = late(
        place, per, float(images * chips), labels, replay, own, other, middle, old_logits
    )
    keep, give = back(place, per, grad_middle, kept, mine, weights, late_grad)

    given = moved(give, place, core=1)

    def kinds(lead, rows, count):
        shape = (*lead, place.z, rows, LANES)
        return [jax.ShapeDtypeStruct(shape, bf16 if i else f32) for i in range(count)]

    one_rows, two_rows = place.half_rows, place.sent_rows - place.half_rows
    parts = pl.pallas_call(
        functools.partial(split_kernel, place),
        in_specs=[VMEM] * 2,
        out_specs=[VMEM] * (place.y + place.x),
        out_shape=kinds((place.x,), one_rows, place.y) + kinds((place.y,), two_rows, place.x),
        compiler_params=pltpu.CompilerParams(vmem_limit_bytes=12 * 1024 * 1024),
        name="split",
    )(keep, given)
    ones, twos = parts[: place.y], parts[place.y :]
    rows_basis = pltpu.with_memory_space_constraint(basis.reshape(KB, shard_len), pltpu.HBM)

    def fetch(first, last, after):
        return pl.pallas_call(
            functools.partial(fetch_kernel, first, last),
            in_specs=[ANY, ANY],
            out_specs=ANY,
            out_shape=pltpu.VMEM((last - first, shard_len), bf16),
            scratch_shapes=[pltpu.SemaphoreType.DMA],
            compiler_params=pltpu.CompilerParams(vmem_limit_bytes=2 * 1024 * 1024),
            cost_estimate=pl.CostEstimate(
                flops=0, bytes_accessed=4 * (last - first) * shard_len, transcendentals=0
            ),
            name="fetch",
        )(after, rows_basis)

    upper = fetch(0, UPPER, ones[-1])

    def along_y(values):
        return [moved(values[i], place, (0, i, 0), pairs_too=True) for i in range(1, place.y)]

    def along_x(values):
        return [moved(values[i], place, (0, 0, i), pairs_too=True) for i in range(1, place.x)]

    arrived = along_y(ones) + along_x(twos)
    parts = pl.pallas_call(
        functools.partial(turn_kernel, place),
        in_specs=[VMEM, VMEM, ANY] + [VMEM] * len(arrived),
        out_specs=[VMEM] * (place.y + place.x),
        out_shape=kinds((), one_rows, place.x) + kinds((), two_rows, place.y),
        compiler_params=pltpu.CompilerParams(vmem_limit_bytes=2 * 1024 * 1024),
        name="turn",
    )(ones[0], twos[0], upper, *arrived)
    ones, twos = parts[: place.x], parts[place.x :]
    arrived = along_x(ones) + along_y(twos)
    piece_shape = (place.sent_rows, LANES)
    first, *rest = pl.pallas_call(
        functools.partial(plane_kernel, place),
        in_specs=[VMEM, VMEM, ANY] + [VMEM] * len(arrived),
        out_specs=[VMEM] * place.z,
        out_shape=[jax.ShapeDtypeStruct(piece_shape, bf16 if d else f32) for d in range(place.z)],
        compiler_params=pltpu.CompilerParams(vmem_limit_bytes=2 * 1024 * 1024),
        name="plane",
    )(ones[0], twos[0], upper, *arrived)
    resident = (upper, fetch(UPPER, KB, rest[0]))
    pieces = [moved(rest[d - 1], place, (d, 0, 0), pairs_too=True) for d in range(1, place.z)]

    def divisor(most):
        return max(n for n in range(1, most + 1) if shard_rows % n == 0)

    flat_kind = jax.ShapeDtypeStruct((shard_rows, LANES), f32)
    grad, sums = pl.pallas_call(
        functools.partial(inner_kernel, divisor(26)),
        in_specs=[VMEM] * (place.z + 3),
        out_specs=[VMEM] * 2,
        out_shape=[flat_kind, jax.ShapeDtypeStruct((1, SUMS), f32)],
        scratch_shapes=[pltpu.VMEM((KB, LANES), f32)],
        compiler_params=pltpu.CompilerParams(vmem_limit_bytes=2 * 1024 * 1024),
        name="inner",
    )(first, *pieces, *resident, loss)
    sums = butterfly(sums, place, resident)
    padded_rows = -(-shard_rows // 8) * 8
    loss_parts, norm, coefficients, new_master, new_first, new_second = pl.pallas_call(
        functools.partial(update_kernel, divisor(312), float(2 * shard_len * chips)),
        in_specs=[SMEM] + [VMEM] * 8,
        out_specs=[SMEM, SMEM] + [VMEM] * 4,
        out_shape=[
            jax.ShapeDtypeStruct((3,), f32),
            jax.ShapeDtypeStruct((1,), f32),
            jax.ShapeDtypeStruct((TASKS, KMAX), f32),
        ]
        + [flat_kind] * 3,
        scratch_shapes=[pltpu.VMEM((padded_rows, LANES), f32)],
        compiler_params=pltpu.CompilerParams(vmem_limit_bytes=2 * 1024 * 1024),
        name="update",
    )(
        basis_count,
        sums,
        *resident,
        grad,
        loss,
        master.reshape(shard_rows, LANES),
        first_moment.reshape(shard_rows, LANES),
        second_moment.reshape(shard_rows, LANES),
    )
    return (
        loss_parts,
        norm[0],
        coefficients,
        new_master.reshape(1, shard_len),
        new_first.reshape(1, shard_len),
        new_second.reshape(1, shard_len),
    )


def solution(mesh):
    in_specs = (
        P("dp", None, None),
        P("dp"),
        P("dp"),
        P("dp", None),
        P(),
        P("section", "dp"),
        P("section", "dp"),
        P("section", "dp"),
        P(None, "section", "dp"),
    )
    out_specs = (P(), P(), P(), P("section", "dp"), P("section", "dp"), P("section", "dp"))
    return jax.shard_map(body, mesh=mesh, in_specs=in_specs, out_specs=out_specs, check_vma=False)
```
